32 devices in a mesh: seq: 8 (over z, x), row: 4 (over y, core).
Axes of the slice: x: 2, y: 2, z: 4, core: 2. Of those that a mesh axis runs over, the one named last changes fastest.
Arguments:
- tokens: bfloat16 [4, 1024, 1536], P('row', 'seq'), may hold values from -6 to 6
- segments: int32 [4, 1024], P('row', 'seq'), may hold values from 0 to 3, as said below
- joint_matrix: bfloat16 [1536, 2048], P(('seq', 'row')), may hold values from -0.21875 to 0.21875
- joint_bias: bfloat16 [2048], P(('seq', 'row')), may hold values from -3 to 3
- merge_matrix: bfloat16 [1536, 1536], P(None, ('seq', 'row')), may hold values from -0.625 to 0.625
- norm_first: bfloat16 [1536], P(('seq', 'row')), may hold values from 0.5 to 1.5
- norm_second: bfloat16 [1536], P(('seq', 'row')), may hold values from 0.5 to 1.5
- gate_matrix: bfloat16 [1536, 8960], P(('seq', 'row')), may hold values from -0.15625 to 0.15625
- up_matrix: bfloat16 [1536, 8960], P(('seq', 'row')), may hold values from -0.15625 to 0.15625
- down_matrix: bfloat16 [8960, 1536], P(None, ('seq', 'row')), may hold values from -0.25 to 0.25
- cotangent: bfloat16 [4, 1024, 1536], P('row', 'seq'), may hold values from -8 to 8
Outputs:
- output: bfloat16 [4, 1024, 1536], P('row', 'seq')
- tokens_grad: float32 [4, 1024, 1536], P('row', 'seq')
- joint_grad: float32 [1536, 2048], P(('seq', 'row'))
- bias_grad: float32 [2048], P(('seq', 'row'))
- merge_grad: float32 [1536, 1536], P(None, ('seq', 'row'))
- first_grad: float32 [1536], P(('seq', 'row'))
- second_grad: float32 [1536], P(('seq', 'row'))
- gate_grad: float32 [1536, 8960], P(('seq', 'row'))
- up_grad: float32 [1536, 8960], P(('seq', 'row'))
- down_grad: float32 [8960, 1536], P(None, ('seq', 'row'))
The draws below stay inside these ranges and needn't reach their ends.
Inputs may be any that keep to these rules, and one draw needn't show every extreme that they name: `segments`: in each row the document numbers never fall and every number from 0 to 3 occurs; document 2 begins within the first 128 tokens of the row and ends within its last 128.
All inputs are finite; a program needn't handle non-finite values.
Results may differ from the reference program's by a relative error of at most 0.02.
Values may be sent and summed in bfloat16 or wider, within the bound.
A program may use at most 448 MiB of HBM per device.

```python
import math
import jax
import jax.numpy as jnp
from jax import lax

D = 1536
HEADS = 12
KV_HEADS = 2
HEAD_DIM = 128
FF = 8960
TOK_DEV = 128
LENGTH = 1024
ROWS = 4
JOINT_WIDTH = 2048


def draw_segments(key, part):
    key = jax.random.fold_in(key, 7)
    first_key, second_key, third_key = jax.random.split(key, 3)
    opening = jax.random.randint(first_key, (ROWS, 1), 2, TOK_DEV, dtype=jnp.int32)
    early = jax.random.randint(second_key, (ROWS, 1), 1, opening, dtype=jnp.int32)
    closing = jax.random.randint(third_key, (ROWS, 1), LENGTH - TOK_DEV + 1, LENGTH, dtype=jnp.int32)
    places = jnp.arange(LENGTH, dtype=jnp.int32)[None, :]
    return (places >= early).astype(jnp.int32) + (places >= opening).astype(jnp.int32) + (places >= closing).astype(jnp.int32)


def spiked(drawn, rng, source, target, blocks, factor):
    def block_of(axis_at):
        return (jnp.arange(drawn.shape[axis_at]) // (drawn.shape[axis_at] // blocks)).reshape((-1,) + (1,) * (drawn.ndim - 1 - axis_at))

    near = jax.random.permutation(rng, blocks)[block_of(target)]
    second = (block_of(target) + blocks // 2) % blocks
    return jnp.where((block_of(source) == near) | (block_of(source) == second), factor * drawn, drawn)


def block_scale(rng, shape, cuts, low, high):
    factor_of = 1.0
    for dim, shards_of in cuts:
        draws = jax.random.uniform(jax.random.fold_in(jax.random.fold_in(rng, 6), dim), (shards_of,), jnp.float32, low / len(cuts), high / len(cuts))
        factor_of = factor_of * jnp.repeat(jnp.exp(draws), shape[dim] // shards_of).reshape((-1,) + (1,) * (len(shape) - 1 - dim))
    return factor_of


def normal_values(own_key, shape, spread, bound, cuts=(), kind=jnp.bfloat16):
    level = block_scale(own_key, shape, cuts, -0.22, 0.18) if cuts else 1.0
    result = jax.random.normal(own_key, shape, jnp.float32) * spread * level
    return jnp.minimum(jnp.maximum(result, -bound), bound).astype(kind)


def heavy_noise(own_key, extent, deviation, bound, cuts, heavy, kind=jnp.bfloat16):
    drawn = deviation * jax.random.normal(own_key, extent, jnp.float32)
    if cuts:
        drawn = drawn * block_scale(own_key, extent, cuts, -0.22, 0.18)
    return jnp.clip(spiked(drawn, jax.random.fold_in(own_key, 3), *heavy), -bound, bound).astype(kind)


def setup_inputs(seed: int = 0) -> dict:
    splits = jax.random.split(jax.random.key(seed), 12)
    tokens = normal_values(splits[0], (ROWS, LENGTH, D), 1.0, 6.0, ((0, 4), (1, 8)))
    segments = draw_segments(jax.random.fold_in(splits[11], 71), 0)
    joint_matrix = normal_values(splits[2], (D, JOINT_WIDTH), (D // 2) ** -0.5, 0.21875, ((0, 32),))
    joint_bias = normal_values(splits[3], (JOINT_WIDTH,), 0.5, 3.0, ((0, 32),))
    merge_matrix = normal_values(splits[4], (HEADS * HEAD_DIM, D), (HEADS * HEAD_DIM // 16) ** -0.5, 0.625, ((1, 32),))
    norm_first = jnp.clip(1.0 + 0.1 * jax.random.normal(splits[5], (D,), jnp.float32), 0.5, 1.5).astype(jnp.bfloat16)
    norm_second = jnp.clip(1.0 + 0.1 * jax.random.normal(splits[6], (D,), jnp.float32), 0.5, 1.5).astype(jnp.bfloat16)
    gate_matrix = normal_values(splits[7], (D, FF), D ** -0.5, 0.15625, ((0, 32),))
    up_matrix = normal_values(splits[8], (D, FF), D ** -0.5, 0.15625, ((0, 32),))
    down_matrix = normal_values(splits[9], (FF, D), (FF // 16) ** -0.5, 0.25, ((1, 32),))
    cotangent = heavy_noise(splits[10], (ROWS, LENGTH, D), 1.0, 8.0, ((0, 4), (1, 8)), (1, 2, 8, 2.0))
    return dict(tokens=tokens, segments=segments, joint_matrix=joint_matrix, joint_bias=joint_bias, merge_matrix=merge_matrix, norm_first=norm_first, norm_second=norm_second, gate_matrix=gate_matrix, up_matrix=up_matrix, down_matrix=down_matrix, cotangent=cotangent)


eps = 1e-06
theta = 1000000.0
neg = -1e+30
high = lax.Precision.HIGHEST

@jax.custom_vjp
def low(v):
    return lax.optimization_barrier(v.astype(jnp.bfloat16)).astype(jnp.float32)

@jax.custom_vjp
def low_back(v):
    return v

def low_keep(v):
    return (low(v), None)

def low_pass(kept, grad):
    return (grad,)

def back_keep(v):
    return (v, None)

def back_low(kept, grad):
    return (low(grad),)
low.defvjp(low_keep, low_pass)
low_back.defvjp(back_keep, back_low)

def normed(values, gain):
    return values * lax.rsqrt(lax.optimization_barrier(jnp.mean(values * values, axis=-1, keepdims=True)) + eps) * gain

def turn_half(values):
    middle = values.shape[-1] // 2
    return jnp.concatenate([-values[..., middle:], values[..., :middle]], axis=-1)

def row_positions(labels):
    length = labels.shape[0]
    places = jnp.arange(length, dtype=jnp.int32)
    change = jnp.concatenate([jnp.ones((1,), dtype=jnp.bool_), labels[1:] != labels[:-1]])
    starts = lax.cummax(jnp.where(change, places, 0).astype(jnp.int32), axis=0)
    return (places - starts).astype(jnp.int32)

def rotary(positions, width):
    inverse = jnp.power(jnp.float32(theta), -(jnp.arange(width // 2, dtype=jnp.float32) * (2.0 / width)))
    angle = positions.astype(jnp.float32)[:, None] * inverse[None, :]
    angle = jnp.concatenate([angle, angle], axis=1)[:, None, :]
    return (jnp.cos(angle), jnp.sin(angle))

def attention(query, keys, values, labels):
    length = query.shape[0]
    group = HEADS // KV_HEADS
    block = math.gcd(length, 512)
    scale = 1.0 / math.sqrt(HEAD_DIM)
    places = jnp.arange(length, dtype=jnp.int32)

    def one_block(start):
        rows = lax.dynamic_slice_in_dim(query, start, block, 0).reshape(block, KV_HEADS, group, HEAD_DIM)
        scores = low_back(jnp.einsum('qkgd,skd->kgqs', rows, keys, precision=high) * scale)
        row_places = start + jnp.arange(block, dtype=jnp.int32)
        row_labels = lax.dynamic_slice_in_dim(labels, start, block, 0)
        allowed = (row_places[:, None] >= places[None, :]) & (row_labels[:, None] == labels[None, :])
        scores = jnp.where(allowed[None, None], scores, neg)
        top = lax.optimization_barrier(jnp.max(scores, axis=-1, keepdims=True))
        raised = jnp.exp(scores - top)
        shares = low(raised / lax.optimization_barrier(jnp.sum(raised, axis=-1, keepdims=True)))
        summed = jnp.einsum('kgqs,skd->qkgd', shares, values, precision=high)
        return summed.reshape(block, HEADS * HEAD_DIM)
    starts = jnp.arange(length // block, dtype=jnp.int32) * block
    return lax.map(jax.checkpoint(one_block), starts).reshape(length, HEADS * HEAD_DIM)

def layer_row(inputs, labels, joint_matrix, joint_bias, merge_matrix, norm_first, norm_second, gate_matrix, up_matrix, down_matrix):
    length = inputs.shape[0]
    query_width = HEADS * HEAD_DIM
    key_width = KV_HEADS * HEAD_DIM
    normal_first = low(normed(inputs, norm_first))
    joint = low_back(jnp.dot(normal_first, joint_matrix, precision=high) + joint_bias)
    cosine, sine = rotary(row_positions(labels), HEAD_DIM)
    query = joint[:, :query_width].reshape(length, HEADS, HEAD_DIM)
    keys = joint[:, query_width:query_width + key_width].reshape(length, KV_HEADS, HEAD_DIM)
    values = low(joint[:, query_width + key_width:].reshape(length, KV_HEADS, HEAD_DIM))
    query = low(query * cosine + turn_half(query) * sine)
    keys = low(keys * cosine + turn_half(keys) * sine)
    attended = low(low_back(attention(query, keys, values, labels)))
    mixed = inputs + low_back(jnp.dot(attended, merge_matrix, precision=high))
    normal_second = low(normed(mixed, norm_second))
    gate = low_back(jnp.dot(normal_second, gate_matrix, precision=high))
    upper = low_back(jnp.dot(normal_second, up_matrix, precision=high))
    hidden = low(jax.nn.silu(gate) * upper)
    return mixed + jnp.dot(hidden, down_matrix, precision=high)

def reference(tokens, segments, joint_matrix, joint_bias, merge_matrix, norm_first, norm_second, gate_matrix, up_matrix, down_matrix, cotangent):
    floats = jnp.float32

    def forward(inputs, joint_matrix, joint_bias, merge_matrix, norm_first, norm_second, gate_matrix, up_matrix, down_matrix):

        def one_row(pair):
            return layer_row(pair[0], pair[1], joint_matrix, joint_bias, merge_matrix, norm_first, norm_second, gate_matrix, up_matrix, down_matrix)
        return lax.map(jax.checkpoint(one_row), (inputs, segments))
    output, pullback = jax.vjp(forward, tokens.astype(floats), joint_matrix.astype(floats), joint_bias.astype(floats), merge_matrix.astype(floats), norm_first.astype(floats), norm_second.astype(floats), gate_matrix.astype(floats), up_matrix.astype(floats), down_matrix.astype(floats))
    grads = pullback(cotangent.astype(floats))
    return (output.astype(jnp.bfloat16), grads[0], grads[1], grads[2], grads[3], grads[4], grads[5], grads[6], grads[7], grads[8])
```

```python
import math

import jax
import jax.numpy as jnp
from jax import lax
from jax.sharding import Mesh, PartitionSpec as P

HEADS = 12
KV_HEADS = 2
HEAD_DIM = 128
GROUP = HEADS // KV_HEADS
QUERY_WIDTH = HEADS * HEAD_DIM
KEY_WIDTH = KV_HEADS * HEAD_DIM
SCALE = 1.0 / math.sqrt(HEAD_DIM)

eps = 1e-06
theta = 1000000.0
neg = -1e30
last_pair = (((1,), (1,)), ((), ()))
first_pair = (((0,), (0,)), ((), ()))
floats = jnp.float32
halves = jnp.bfloat16

AXES = ("z", "x", "y", "c")
SEQ = ("z", "x")
ROW = ("y", "c")
TEAM = ("z", "y")


def turn_half(values):
    middle = values.shape[-1] // 2
    return jnp.concatenate([-values[..., middle:], values[..., :middle]], axis=-1)


def unturn_half(values):
    middle = values.shape[-1] // 2
    return jnp.concatenate([values[..., middle:], -values[..., :middle]], axis=-1)


def row_positions(labels):
    length = labels.shape[0]
    places = jnp.arange(length, dtype=jnp.int32)
    change = jnp.concatenate([jnp.ones((1,), dtype=jnp.bool_), labels[1:] != labels[:-1]])
    starts = lax.cummax(jnp.where(change, places, 0), axis=0)
    return places - starts


def rotary(positions, width):
    inverse = jnp.power(
        jnp.float32(theta), -(jnp.arange(width // 2, dtype=jnp.float32) * (2.0 / width))
    )
    angle = positions.astype(jnp.float32)[:, None] * inverse[None, :]
    angle = jnp.concatenate([angle, angle], axis=1)[:, None, :]
    return (jnp.cos(angle), jnp.sin(angle))


def to_groups(values):
    length = values.shape[0]
    return (
        values.reshape(length, KV_HEADS, GROUP, HEAD_DIM)
        .transpose(1, 2, 0, 3)
        .reshape(KV_HEADS, GROUP * length, HEAD_DIM)
    )


def from_groups(values, length):
    return (
        values.reshape(KV_HEADS, GROUP, length, HEAD_DIM)
        .transpose(2, 0, 1, 3)
        .reshape(length, QUERY_WIDTH)
    )


def norm_parts(values):
    return lax.rsqrt(jnp.mean(values * values, axis=-1, keepdims=True) + eps)


def norm_back(upstream, values, scale, gain):
    scaled = upstream * gain
    inner = jnp.mean(scaled * values, axis=-1, keepdims=True)
    part = scale * scaled - values * (scale * scale * scale) * inner
    gain_grad = jnp.sum(upstream * values * scale, axis=0)
    return part, gain_grad


def body(
    tokens,
    segments,
    joint_matrix,
    joint_bias,
    merge_matrix,
    norm_first,
    norm_second,
    gate_matrix,
    up_matrix,
    down_matrix,
    cotangent,
):
    residual = tokens[0].astype(floats)
    length, model = residual.shape
    depth = joint_matrix.shape[0]
    joint_width = joint_matrix.shape[1]
    hidden_width = gate_matrix.shape[1]
    z_count = lax.axis_size("z")
    team = lax.axis_size(TEAM)
    share = hidden_width // team
    own_labels = segments[0]
    labels = lax.all_gather(own_labels, SEQ, axis=0, tiled=True)
    offset = lax.axis_index(SEQ) * length
    places = offset + jnp.arange(length, dtype=jnp.int32)
    positions = lax.dynamic_slice_in_dim(row_positions(labels), offset, length, 0)
    cosine, sine = rotary(positions, HEAD_DIM)

    small = jnp.concatenate([joint_bias, norm_first, norm_second])
    small = jnp.pad(small, (0, -small.shape[0] % depth)).reshape(depth, -1)
    small_width = small.shape[1]
    packed = jnp.concatenate([joint_matrix, merge_matrix.T, small], axis=1)
    packed = lax.all_gather(packed, AXES, axis=0, tiled=True)
    joint_all = packed[:, :joint_width]
    merge_turned = packed[:, joint_width : joint_width + model]
    small = packed[:, joint_width + model :].reshape(-1, depth * small_width).astype(floats)
    bias_depth = joint_bias.shape[0]
    bias_all = small[:, :bias_depth].reshape(-1)
    gain_first = small[:, bias_depth : bias_depth + depth].reshape(-1)
    gain_second = small[:, bias_depth + depth : bias_depth + 2 * depth].reshape(-1)

    stacked = jnp.stack([gate_matrix, up_matrix, down_matrix.T], axis=1)
    stacked = stacked.reshape(depth, 3, team, share).transpose(2, 0, 1, 3)
    stacked = stacked.reshape(team, depth, 3 * share)
    stacked = lax.all_to_all(stacked, TEAM, split_axis=0, concat_axis=0, tiled=True)
    stacked = stacked.reshape(z_count, 1, team // z_count, 1, depth, 3 * share)
    stacked = lax.all_gather(stacked, "x", axis=1, tiled=True)
    stacked = lax.all_gather(stacked, "c", axis=3, tiled=True)
    stacked = stacked.reshape(model, 3 * share)
    both_all, down_turned = stacked[:, : 2 * share], stacked[:, 2 * share :]
    outer_grad = cotangent[0]
    team_outer = lax.all_gather(outer_grad, TEAM, axis=0, tiled=True)

    scale_first = norm_parts(residual)
    normal_first = (residual * scale_first * gain_first).astype(halves)
    joint = jnp.dot(normal_first, joint_all, preferred_element_type=floats) + bias_all
    query = joint[:, :QUERY_WIDTH].reshape(length, HEADS, HEAD_DIM)
    keys = joint[:, QUERY_WIDTH : QUERY_WIDTH + KEY_WIDTH].reshape(length, KV_HEADS, HEAD_DIM)
    values = joint[:, QUERY_WIDTH + KEY_WIDTH :].astype(halves)
    query = (query * cosine + turn_half(query) * sine).astype(halves)
    keys = (keys * cosine + turn_half(keys) * sine).astype(halves).reshape(length, KEY_WIDTH)
    query_group = to_groups(query)
    pair = lax.all_gather(jnp.concatenate([keys, values], axis=1), SEQ, axis=0, tiled=True)
    count = pair.shape[0]
    key_all = pair[:, :KEY_WIDTH].reshape(count, KV_HEADS, HEAD_DIM)
    value_all = pair[:, KEY_WIDTH:].reshape(count, KV_HEADS, HEAD_DIM)
    allowed = (places[:, None] >= jnp.arange(count, dtype=jnp.int32)[None, :]) & (
        own_labels[:, None] == labels[None, :]
    )
    allowed = jnp.tile(allowed, (GROUP, 1))[None]
    scores = jnp.einsum("krd,nkd->krn", query_group, key_all, preferred_element_type=floats)
    scores = jnp.where(allowed, scores * SCALE, neg)
    top = jnp.max(scores, axis=-1, keepdims=True)
    weights = jnp.where(allowed, jnp.exp(scores - top), 0.0)
    total = jnp.sum(weights, axis=-1, keepdims=True)
    shares = weights / total
    shares_half = shares.astype(halves)
    attended = jnp.einsum("krn,nkd->krd", shares_half, value_all, preferred_element_type=floats)
    attended_half = from_groups(attended, length).astype(halves)
    mixed = residual + lax.dot_general(
        attended_half, merge_turned, last_pair, preferred_element_type=floats
    )
    scale_second = norm_parts(mixed)
    normal_half = (mixed * scale_second * gain_second).astype(halves)

    team_normal = lax.all_gather(normal_half, TEAM, axis=0, tiled=True)
    both = jnp.dot(team_normal, both_all, preferred_element_type=floats)
    gate, upper = both[:, :share], both[:, share:]
    sig = jax.nn.sigmoid(gate)
    silu = gate * sig
    hidden_half = (silu * upper).astype(halves)
    branch = lax.dot_general(hidden_half, down_turned, last_pair, preferred_element_type=floats)
    hidden_grad = jnp.dot(team_outer, down_turned, preferred_element_type=floats)
    gate_half = (hidden_grad * upper * sig * (1.0 + gate * (1.0 - sig))).astype(halves)
    upper_half = (hidden_grad * silu).astype(halves)
    both_half = jnp.concatenate([gate_half, upper_half], axis=1)
    normal_grad = lax.dot_general(both_half, both_all, last_pair, preferred_element_type=floats)
    branch = lax.psum_scatter(branch.astype(halves), TEAM, scatter_dimension=0, tiled=True)
    normal_grad = lax.psum_scatter(normal_grad.astype(halves), TEAM, scatter_dimension=0, tiled=True)
    output = (mixed + branch.astype(floats)).astype(halves)[None]
    both_grad = lax.dot_general(team_normal, both_half, first_pair, preferred_element_type=floats)
    down_grad = lax.dot_general(team_outer, hidden_half, first_pair, preferred_element_type=floats)
    grads = jnp.concatenate([both_grad, down_grad], axis=1).astype(halves)
    grads = grads.reshape(z_count, 2, team // z_count, 2, depth, 3 * share)
    grads = lax.psum_scatter(grads, "c", scatter_dimension=3, tiled=True)
    grads = lax.psum_scatter(grads, "x", scatter_dimension=1, tiled=True)
    grads = grads.reshape(team, depth, 3 * share)
    grads = lax.all_to_all(grads, TEAM, split_axis=0, concat_axis=0, tiled=True)
    grads = grads.reshape(team, depth, 3, share).transpose(2, 1, 0, 3)
    grads = grads.reshape(3, depth, hidden_width).astype(floats)

    normal_grad = normal_grad.astype(floats)
    mixed_part, second_local = norm_back(normal_grad, mixed, scale_second, gain_second)
    mixed_grad = outer_grad.astype(floats) + mixed_part
    mixed_half = mixed_grad.astype(halves)
    merge_local = lax.dot_general(
        mixed_half, attended_half, first_pair, preferred_element_type=floats
    )
    attended_grad = jnp.dot(mixed_half, merge_turned, preferred_element_type=floats).astype(halves)
    grad_group = to_groups(attended_grad.reshape(length, HEADS, HEAD_DIM))
    mass_grad = jnp.einsum("krd,nkd->krn", grad_group, value_all, preferred_element_type=floats)
    row_dots = jnp.sum(shares * mass_grad, axis=-1, keepdims=True)
    score_half = (shares * (mass_grad - row_dots)).astype(halves)
    query_sum = (
        jnp.einsum("krn,nkd->krd", score_half, key_all, preferred_element_type=floats) * SCALE
    )
    key_grad = (
        jnp.einsum("krn,krd->nkd", score_half, query_group, preferred_element_type=floats) * SCALE
    )
    value_grad = jnp.einsum("krn,krd->nkd", shares_half, grad_group, preferred_element_type=floats)
    pair_sums = jnp.concatenate(
        [key_grad.reshape(count, KEY_WIDTH), value_grad.reshape(count, KEY_WIDTH)], axis=1
    )
    pair_mine = lax.psum_scatter(
        pair_sums.astype(halves), SEQ, scatter_dimension=0, tiled=True
    ).astype(floats)
    key_back = pair_mine[:, :KEY_WIDTH].reshape(length, KV_HEADS, HEAD_DIM)
    value_back = pair_mine[:, KEY_WIDTH:]
    query_back = from_groups(query_sum, length).reshape(length, HEADS, HEAD_DIM)
    query_back = query_back * cosine + unturn_half(query_back * sine)
    key_back = key_back * cosine + unturn_half(key_back * sine)
    joint_back = jnp.concatenate(
        [query_back.reshape(length, QUERY_WIDTH), key_back.reshape(length, KEY_WIDTH), value_back],
        axis=1,
    ).astype(halves)
    joint_local = lax.dot_general(
        normal_first, joint_back, first_pair, preferred_element_type=floats
    )
    bias_local = jnp.sum(joint_back.astype(floats), axis=0)
    normal_back = lax.dot_general(joint_back, joint_all, last_pair, preferred_element_type=floats)
    residual_part, first_local = norm_back(normal_back, residual, scale_first, gain_first)
    tokens_grad = (mixed_grad + residual_part)[None]

    small_back = jnp.concatenate(
        [
            bias_local.reshape(-1, bias_depth),
            first_local.reshape(-1, depth),
            second_local.reshape(-1, depth),
        ],
        axis=1,
    )
    small_back = jnp.pad(small_back, ((0, 0), (0, depth * small_width - small_back.shape[1])))
    small_back = small_back.reshape(-1, small_width)
    packed_grad = jnp.concatenate([joint_local, merge_local, small_back], axis=1).astype(halves)
    packed_grad = lax.psum_scatter(packed_grad, AXES, scatter_dimension=0, tiled=True).astype(floats)
    joint_grad = packed_grad[:, :joint_width]
    merge_grad = packed_grad[:, joint_width : joint_width + model].T
    small_back = packed_grad[:, joint_width + model :].reshape(-1)
    bias_grad = small_back[:bias_depth]
    first_grad = small_back[bias_depth : bias_depth + depth]
    second_grad = small_back[bias_depth + depth : bias_depth + 2 * depth]
    return (
        output,
        tokens_grad,
        joint_grad,
        bias_grad,
        merge_grad,
        first_grad,
        second_grad,
        grads[0],
        grads[1],
        grads[2].T,
    )


def solution(mesh):
    seq, row = mesh.shape["seq"], mesh.shape["row"]
    fine = Mesh(mesh.devices.reshape(seq // 2, 2, row // 2, 2), AXES)
    whole = ("z", "x", "y", "c")
    placed = (
        P(ROW, SEQ, None),
        P(ROW, SEQ),
        P(whole, None),
        P(whole),
        P(None, whole),
        P(whole),
        P(whole),
        P(whole, None),
        P(whole, None),
        P(None, whole),
        P(ROW, SEQ, None),
    )
    return jax.shard_map(
        body,
        mesh=fine,
        in_specs=placed,
        out_specs=(
            P(ROW, SEQ, None),
            P(ROW, SEQ, None),
            P(whole, None),
            P(whole),
            P(None, whole),
            P(whole),
            P(whole),
            P(whole, None),
            P(whole, None),
            P(None, whole),
        ),
        check_vma=False,
    )
```

```python
import functools
import math

import jax
import jax.numpy as jnp
from jax import lax
from jax.experimental import pallas as pl
from jax.experimental.pallas import tpu as pltpu
from jax.sharding import Mesh, PartitionSpec as P

HEADS = 12
KV_HEADS = 2
HEAD_DIM = 128
GROUP = HEADS // KV_HEADS
QUERY_WIDTH = HEADS * HEAD_DIM
KEY_WIDTH = KV_HEADS * HEAD_DIM
SCALE = 1.0 / math.sqrt(HEAD_DIM)

eps = 1e-06
theta = 1000000.0
neg = -1e30
last_pair = (((1,), (1,)), ((), ()))
first_pair = (((0,), (0,)), ((), ()))
floats = jnp.float32
halves = jnp.bfloat16

AXES = ("z", "x", "y", "c")
SEQ = ("z", "x")
ROW = ("y", "c")
TEAM = ("z", "y")


def turn_half(values):
    middle = values.shape[-1] // 2
    return jnp.concatenate([-values[..., middle:], values[..., :middle]], axis=-1)


def unturn_half(values):
    middle = values.shape[-1] // 2
    return jnp.concatenate([values[..., middle:], -values[..., :middle]], axis=-1)


def row_positions(labels):
    length = labels.shape[0]
    places = jnp.arange(length, dtype=jnp.int32)
    change = jnp.concatenate([jnp.ones((1,), dtype=jnp.bool_), labels[1:] != labels[:-1]])
    starts = lax.cummax(jnp.where(change, places, 0), axis=0)
    return places - starts


def rotary(positions, width):
    inverse = jnp.power(
        jnp.float32(theta), -(jnp.arange(width // 2, dtype=jnp.float32) * (2.0 / width))
    )
    angle = positions.astype(jnp.float32)[:, None] * inverse[None, :]
    angle = jnp.concatenate([angle, angle], axis=1)[:, None, :]
    return (jnp.cos(angle), jnp.sin(angle))


def to_groups(values):
    length = values.shape[0]
    return (
        values.reshape(length, KV_HEADS, GROUP, HEAD_DIM)
        .transpose(1, 2, 0, 3)
        .reshape(KV_HEADS, GROUP * length, HEAD_DIM)
    )


def from_groups(values, length):
    return (
        values.reshape(KV_HEADS, GROUP, length, HEAD_DIM)
        .transpose(2, 0, 1, 3)
        .reshape(length, QUERY_WIDTH)
    )


def norm_parts(values):
    return lax.rsqrt(jnp.mean(values * values, axis=-1, keepdims=True) + eps)


def norm_back(upstream, values, scale, gain):
    scaled = upstream * gain
    inner = jnp.mean(scaled * values, axis=-1, keepdims=True)
    part = scale * scaled - values * (scale * scale * scale) * inner
    gain_grad = jnp.sum(upstream * values * scale, axis=0)
    return part, gain_grad


MESH = pl.DeviceIdType.MESH
VMEM_LIMIT = 60 * 2**20


def coordinates():
    return tuple(lax.axis_index(name) for name in AXES)


class Courier:
    def __init__(self, sends, receives):
        self.sends, self.receives, self.copies, self.settled = sends, receives, [], 0

    def copy(self, source, target, device):
        place = len(self.copies)
        made = pltpu.make_async_remote_copy(
            src_ref=source,
            dst_ref=target,
            send_sem=self.sends.at[place],
            recv_sem=self.receives.at[place],
            device_id=device,
            device_id_type=MESH,
        )
        made.start()
        self.copies.append(made)
        return made

    def finish(self):
        for made in self.copies[self.settled :]:
            made.wait_send()
        self.settled = len(self.copies)


def meet(devices):
    barrier = pltpu.get_barrier_semaphore()
    for device in devices:
        pl.semaphore_signal(barrier, inc=1, device_id=device, device_id_type=MESH)
    pl.semaphore_wait(barrier, len(devices))


def cuts_of(width, step):
    return [(start, min(step, width - start)) for start in range(0, width, step)]


def forward_kernel(
    nz,
    stack_ref,
    normal_ref,
    outer_ref,
    branch_ref,
    back_ref,
    grads_ref,
    w,
    xn,
    ct,
    hid,
    gb,
    ub,
    part,
    ybuf,
    zsend,
    zbuf,
    cbuf,
    xbuf,
    gbuf,
    sends,
    receives,
    locals_,
):
    z, x, y, c = coordinates()
    length, model = normal_ref.shape
    share = w.shape[-1]
    block = model // nz
    courier = Courier(sends, receives)
    across_x, across_y, across_c = (z, 1 - x, y, c), (z, x, 1 - y, c), (z, x, y, 1 - c)

    def source(dz):
        return lax.rem(z + nz - dz, nz)

    team = [(dz, dy) for dz in range(nz) for dy in range(2)]
    meet(
        [(lax.rem(z + dz, nz), x, lax.rem(y + dy, 2), c) for dz, dy in team[1:]]
        + [across_x, across_c]
    )

    def columns(tz, ty):
        return pl.ds(pl.multiple_of((tz * 2 + ty) * share, 128), share)

    own = pltpu.make_async_copy(
        stack_ref.at[:, :, columns(z, y)], w.at[:, z, x * 2 + y, c], locals_.at[0]
    )
    own.start()
    direct = {}
    for dz, dy in team[1:]:
        tz, ty = lax.rem(z + dz, nz), lax.rem(y + dy, 2)
        direct[dz, dy] = courier.copy(
            stack_ref.at[:, :, columns(tz, ty)], w.at[:, z, x * 2 + y, c], (tz, x, ty, c)
        )

    rows_mine, rows_other = pl.ds(y * length, length), pl.ds((1 - y) * length, length)
    arriving = {}
    for mine, team_buffer, name in ((outer_ref, ct, "outer"), (normal_ref, xn, "normal")):
        team_buffer[z, rows_mine, :] = mine[...]
        along = {}
        for dz in range(1, nz):
            along[dz] = courier.copy(
                mine, team_buffer.at[z, rows_mine], (lax.rem(z + dz, nz), x, y, c)
            )
        side = {0: courier.copy(mine, team_buffer.at[z, rows_mine], across_y)}
        arriving[name] = (along, side)
    for dz in range(1, nz):
        for team_buffer, name in ((ct, "outer"), (xn, "normal")):
            along, side = arriving[name]
            along[dz].wait_recv()
            spot = team_buffer.at[source(dz), rows_mine]
            side[dz] = courier.copy(spot, spot, across_y)

    crossed, handed = {}, []
    own.wait()
    for dz, dy in team:
        if (dz, dy) != (0, 0):
            direct[dz, dy].wait_recv()
        sy = lax.rem(y + dy, 2)
        spot = w.at[:, source(dz), x * 2 + sy, c]
        crossed[dz, dy] = courier.copy(spot, spot, across_x)
        handed.append(courier.copy(spot, spot, across_c))
    for dz, dy in team:
        crossed[dz, dy].wait_recv()
        sy = lax.rem(y + dy, 2)
        spot = w.at[:, source(dz), (1 - x) * 2 + sy, c]
        handed.append(courier.copy(spot, spot, across_c))
    for made in handed:
        made.wait_recv()
    for name in ("outer", "normal"):
        for made in arriving[name][1].values():
            made.wait_recv()
    courier.finish()

    def weight(which, start, size):
        return w[which, :, :, :, :, start : start + size].reshape(model, size)

    scatter = []
    for dz in range(nz):
        group = source(dz)
        for start, size in cuts_of(share, 256):
            normal = xn[group]
            outer = ct[group]
            gate = jnp.dot(normal, weight(0, start, size), preferred_element_type=floats)
            upper = jnp.dot(normal, weight(1, start, size), preferred_element_type=floats)
            hidden_back = jnp.dot(outer, weight(2, start, size), preferred_element_type=floats)
            sig = 1.0 / (1.0 + jnp.exp(-gate))
            silu = gate * sig
            spot = (group, slice(None), slice(start, start + size))
            hid[spot] = (silu * upper).astype(halves)
            gb[spot] = (hidden_back * upper * (sig * (1.0 + gate * (1.0 - sig)))).astype(halves)
            ub[spot] = (hidden_back * silu).astype(halves)
        half = nz // 2

        @pl.loop(0, 2)
        def _(step):
            rows = pl.ds(step * half, half)
            lanes = pl.ds(pl.multiple_of(step * (model // 2), 128), model // 2)

            def turned(which):
                return w[which, rows].reshape(model // 2, share)

            part[0, group, :, lanes] = (
                lax.dot_general(gb[group], turned(0), last_pair, preferred_element_type=floats)
                + lax.dot_general(ub[group], turned(1), last_pair, preferred_element_type=floats)
            ).astype(halves)
            part[1, group, :, lanes] = lax.dot_general(
                hid[group], turned(2), last_pair, preferred_element_type=floats
            ).astype(halves)

        for which in range(2):
            scatter.append(
                courier.copy(
                    part.at[which, group, rows_other], ybuf.at[which, group], across_y
                )
            )

    final = {}
    for dz in range(nz):
        group = source(dz)
        for which in range(2):
            scatter[2 * dz + which].wait_recv()
            total = part[which, group, rows_mine, :].astype(floats) + ybuf[which, group].astype(floats)
            if dz == 0:
                (back_ref, branch_ref)[which][...] = total
            else:
                zsend[which, dz - 1] = total.astype(halves)
                final[which, dz] = courier.copy(
                    zsend.at[which, dz - 1], zbuf.at[which, dz - 1], (group, x, y, c)
                )

    lines = 2 * length * nz
    moved = {}
    orders = [(dz + nz // 2) % nz for dz in range(nz)]
    for dz in orders:
        group = lax.rem(z + dz, nz)
        lanes = pl.ds(pl.multiple_of(group * block, 128), block)
        normal_turned = xn[:, :, lanes].reshape(lines, block).T
        outer_turned = ct[:, :, lanes].reshape(lines, block).T
        for which, left, right in ((0, normal_turned, gb), (1, normal_turned, ub), (2, outer_turned, hid)):
            for start, size in cuts_of(share, 512):
                w[which, group, :, :, :, start : start + size] = (
                    jnp.dot(
                        left,
                        right[:, :, start : start + size].reshape(lines, size),
                        preferred_element_type=floats,
                    )
                    .astype(halves)
                    .reshape(4, 2, -1, size)
                )
        moved[dz] = courier.copy(w.at[:, group, :, 1 - c], cbuf.at[dz], across_c)
    crossing = {}
    for dz in orders:
        group = lax.rem(z + dz, nz)
        moved[dz].wait_recv()
        for which in range(3):
            w[which, group, :, c] = (
                w[which, group, :, c].astype(floats) + cbuf[dz, which].astype(floats)
            ).astype(halves)
        crossing[dz] = courier.copy(
            w.at[:, group, pl.ds((1 - x) * 2, 2), c], xbuf.at[dz], across_x
        )
    arrived = []
    for dz in orders:
        group = lax.rem(z + dz, nz)
        crossing[dz].wait_recv()
        for dy in range(2):
            ty = lax.rem(y + dy, 2)
            for which in range(3):
                total = w[which, group, x * 2 + ty, c].astype(floats) + xbuf[dz, which, ty].astype(floats)
                if (dz, dy) == (0, 0):
                    gbuf[z * 2 + y, which] = total.astype(halves)
                else:
                    w[which, group, x * 2 + ty, c] = total.astype(halves)
            if (dz, dy) != (0, 0):
                arrived.append(
                    courier.copy(
                        w.at[:, group, x * 2 + ty, c], gbuf.at[z * 2 + y], (group, x, ty, c)
                    )
                )
    for which, target in ((0, back_ref), (1, branch_ref)):
        for dz in range(1, nz):
            final[which, dz].wait_recv()
            target[...] += zbuf[which, dz - 1].astype(floats)
    for made in arrived:
        made.wait_recv()
    for member in range(2 * nz):
        for which in range(3):
            grads_ref[which, :, member * share : (member + 1) * share] = gbuf[member, which]
    courier.finish()


def padded_share(hidden_width, team):
    return -(-hidden_width // (team * 128)) * 128


def feed_forward_kernel(normal_half, outer_grad, gate_matrix, up_matrix, down_matrix):
    length, model = normal_half.shape
    depth, hidden_width = gate_matrix.shape
    nz = lax.axis_size("z")
    share = padded_share(hidden_width, 2 * nz)
    stack = jnp.stack([gate_matrix, up_matrix, down_matrix.T])
    stack = jnp.pad(stack, ((0, 0), (0, 0), (0, 2 * nz * share - hidden_width)))
    vmem = pl.BlockSpec(memory_space=pltpu.VMEM)
    lines = 2 * length
    copies = 31 + 14 + 14 + 15
    branch, back, grads = pl.pallas_call(
        functools.partial(forward_kernel, nz),
        name="feed_forward",
        out_shape=(
            jax.ShapeDtypeStruct((length, model), floats),
            jax.ShapeDtypeStruct((length, model), floats),
            jax.ShapeDtypeStruct((3, depth, 2 * nz * share), halves),
        ),
        in_specs=[pl.BlockSpec(memory_space=pl.ANY), vmem, vmem],
        out_specs=(vmem, vmem, vmem),
        scratch_shapes=[
            pltpu.VMEM((3, nz, 4, 2, depth, share), halves),
            pltpu.VMEM((nz, lines, model), halves),
            pltpu.VMEM((nz, lines, model), halves),
            pltpu.VMEM((nz, lines, share), halves),
            pltpu.VMEM((nz, lines, share), halves),
            pltpu.VMEM((nz, lines, share), halves),
            pltpu.VMEM((2, nz, lines, model), halves),
            pltpu.VMEM((2, nz, length, model), halves),
            pltpu.VMEM((2, nz - 1, length, model), halves),
            pltpu.VMEM((2, nz - 1, length, model), halves),
            pltpu.VMEM((nz, 3, 4, depth, share), halves),
            pltpu.VMEM((nz, 3, 2, depth, share), halves),
            pltpu.VMEM((2 * nz, 3, depth, share), halves),
            pltpu.SemaphoreType.DMA((copies,)),
            pltpu.SemaphoreType.DMA((copies,)),
            pltpu.SemaphoreType.DMA((1,)),
        ],
        compiler_params=pltpu.CompilerParams(
            collective_id=0, has_side_effects=True, vmem_limit_bytes=VMEM_LIMIT
        ),
    )(stack, normal_half, outer_grad)
    return branch, back, grads[:, :, :hidden_width].astype(floats)


def feed_forward_plain(normal_half, outer_grad, gate_matrix, up_matrix, down_matrix):
    model = normal_half.shape[1]
    depth, hidden_width = gate_matrix.shape
    z_count = lax.axis_size("z")
    team = lax.axis_size(TEAM)
    share = hidden_width // team
    stacked = jnp.stack([gate_matrix, up_matrix, down_matrix.T], axis=1)
    stacked = stacked.reshape(depth, 3, team, share).transpose(2, 0, 1, 3)
    stacked = stacked.reshape(team, depth, 3 * share)
    stacked = lax.all_to_all(stacked, TEAM, split_axis=0, concat_axis=0, tiled=True)
    stacked = stacked.reshape(z_count, 1, team // z_count, 1, depth, 3 * share)
    stacked = lax.all_gather(stacked, "x", axis=1, tiled=True)
    stacked = lax.all_gather(stacked, "c", axis=3, tiled=True)
    stacked = stacked.reshape(model, 3 * share)
    both_all, down_turned = stacked[:, : 2 * share], stacked[:, 2 * share :]
    team_outer = lax.all_gather(outer_grad, TEAM, axis=0, tiled=True)
    team_normal = lax.all_gather(normal_half, TEAM, axis=0, tiled=True)
    both = jnp.dot(team_normal, both_all, preferred_element_type=floats)
    gate, upper = both[:, :share], both[:, share:]
    sig = jax.nn.sigmoid(gate)
    silu = gate * sig
    hidden_half = (silu * upper).astype(halves)
    branch = lax.dot_general(hidden_half, down_turned, last_pair, preferred_element_type=floats)
    hidden_grad = jnp.dot(team_outer, down_turned, preferred_element_type=floats)
    gate_half = (hidden_grad * upper * sig * (1.0 + gate * (1.0 - sig))).astype(halves)
    upper_half = (hidden_grad * silu).astype(halves)
    both_half = jnp.concatenate([gate_half, upper_half], axis=1)
    normal_grad = lax.dot_general(both_half, both_all, last_pair, preferred_element_type=floats)
    branch = lax.psum_scatter(branch.astype(halves), TEAM, scatter_dimension=0, tiled=True)
    normal_grad = lax.psum_scatter(normal_grad.astype(halves), TEAM, scatter_dimension=0, tiled=True)
    both_grad = lax.dot_general(team_normal, both_half, first_pair, preferred_element_type=floats)
    down_grad = lax.dot_general(team_outer, hidden_half, first_pair, preferred_element_type=floats)
    grads = jnp.concatenate([both_grad, down_grad], axis=1).astype(halves)
    grads = grads.reshape(z_count, 2, team // z_count, 2, depth, 3 * share)
    grads = lax.psum_scatter(grads, "c", scatter_dimension=3, tiled=True)
    grads = lax.psum_scatter(grads, "x", scatter_dimension=1, tiled=True)
    grads = grads.reshape(team, depth, 3 * share)
    grads = lax.all_to_all(grads, TEAM, split_axis=0, concat_axis=0, tiled=True)
    grads = grads.reshape(team, depth, 3, share).transpose(2, 1, 0, 3)
    grads = grads.reshape(3, depth, hidden_width).astype(floats)
    return branch.astype(floats), normal_grad.astype(floats), grads


def body(
    tokens,
    segments,
    joint_matrix,
    joint_bias,
    merge_matrix,
    norm_first,
    norm_second,
    gate_matrix,
    up_matrix,
    down_matrix,
    cotangent,
):
    residual = tokens[0].astype(floats)
    length, model = residual.shape
    depth = joint_matrix.shape[0]
    joint_width = joint_matrix.shape[1]
    own_labels = segments[0]
    labels = lax.all_gather(own_labels, SEQ, axis=0, tiled=True)
    offset = lax.axis_index(SEQ) * length
    places = offset + jnp.arange(length, dtype=jnp.int32)
    positions = lax.dynamic_slice_in_dim(row_positions(labels), offset, length, 0)
    cosine, sine = rotary(positions, HEAD_DIM)

    small = jnp.concatenate([joint_bias, norm_first, norm_second])
    small = jnp.pad(small, (0, -small.shape[0] % depth)).reshape(depth, -1)
    small_width = small.shape[1]
    packed = jnp.concatenate([joint_matrix, merge_matrix.T, small], axis=1)
    packed = lax.all_gather(packed, AXES, axis=0, tiled=True)
    joint_all = packed[:, :joint_width]
    merge_turned = packed[:, joint_width : joint_width + model]
    small = packed[:, joint_width + model :].reshape(-1, depth * small_width).astype(floats)
    bias_depth = joint_bias.shape[0]
    bias_all = small[:, :bias_depth].reshape(-1)
    gain_first = small[:, bias_depth : bias_depth + depth].reshape(-1)
    gain_second = small[:, bias_depth + depth : bias_depth + 2 * depth].reshape(-1)

    outer_grad = cotangent[0]

    scale_first = norm_parts(residual)
    normal_first = (residual * scale_first * gain_first).astype(halves)
    joint = jnp.dot(normal_first, joint_all, preferred_element_type=floats) + bias_all
    query = joint[:, :QUERY_WIDTH].reshape(length, HEADS, HEAD_DIM)
    keys = joint[:, QUERY_WIDTH : QUERY_WIDTH + KEY_WIDTH].reshape(length, KV_HEADS, HEAD_DIM)
    values = joint[:, QUERY_WIDTH + KEY_WIDTH :].astype(halves)
    query = (query * cosine + turn_half(query) * sine).astype(halves)
    keys = (keys * cosine + turn_half(keys) * sine).astype(halves).reshape(length, KEY_WIDTH)
    query_group = to_groups(query)
    pair = lax.all_gather(jnp.concatenate([keys, values], axis=1), SEQ, axis=0, tiled=True)
    count = pair.shape[0]
    key_all = pair[:, :KEY_WIDTH].reshape(count, KV_HEADS, HEAD_DIM)
    value_all = pair[:, KEY_WIDTH:].reshape(count, KV_HEADS, HEAD_DIM)
    allowed = (places[:, None] >= jnp.arange(count, dtype=jnp.int32)[None, :]) & (
        own_labels[:, None] == labels[None, :]
    )
    allowed = jnp.tile(allowed, (GROUP, 1))[None]
    scores = jnp.einsum("krd,nkd->krn", query_group, key_all, preferred_element_type=floats)
    scores = jnp.where(allowed, scores * SCALE, neg)
    top = jnp.max(scores, axis=-1, keepdims=True)
    weights = jnp.where(allowed, jnp.exp(scores - top), 0.0)
    total = jnp.sum(weights, axis=-1, keepdims=True)
    shares = weights / total
    shares_half = shares.astype(halves)
    attended = jnp.einsum("krn,nkd->krd", shares_half, value_all, preferred_element_type=floats)
    attended_half = from_groups(attended, length).astype(halves)
    mixed = residual + lax.dot_general(
        attended_half, merge_turned, last_pair, preferred_element_type=floats
    )
    scale_second = norm_parts(mixed)
    normal_half = (mixed * scale_second * gain_second).astype(halves)

    if depth % 16 == 0:
        feed_forward = feed_forward_kernel
    else:
        feed_forward = feed_forward_plain
    branch, normal_grad, grads = feed_forward(
        normal_half, outer_grad, gate_matrix, up_matrix, down_matrix
    )
    output = (mixed + branch).astype(halves)[None]

    mixed_part, second_local = norm_back(normal_grad, mixed, scale_second, gain_second)
    mixed_grad = outer_grad.astype(floats) + mixed_part
    mixed_half = mixed_grad.astype(halves)
    merge_local = lax.dot_general(
        mixed_half, attended_half, first_pair, preferred_element_type=floats
    )
    attended_grad = jnp.dot(mixed_half, merge_turned, preferred_element_type=floats).astype(halves)
    grad_group = to_groups(attended_grad.reshape(length, HEADS, HEAD_DIM))
    mass_grad = jnp.einsum("krd,nkd->krn", grad_group, value_all, preferred_element_type=floats)
    row_dots = jnp.sum(shares * mass_grad, axis=-1, keepdims=True)
    score_half = (shares * (mass_grad - row_dots)).astype(halves)
    query_sum = (
        jnp.einsum("krn,nkd->krd", score_half, key_all, preferred_element_type=floats) * SCALE
    )
    key_grad = (
        jnp.einsum("krn,krd->nkd", score_half, query_group, preferred_element_type=floats) * SCALE
    )
    value_grad = jnp.einsum("krn,krd->nkd", shares_half, grad_group, preferred_element_type=floats)
    pair_sums = jnp.concatenate(
        [key_grad.reshape(count, KEY_WIDTH), value_grad.reshape(count, KEY_WIDTH)], axis=1
    )
    pair_mine = lax.psum_scatter(
        pair_sums.astype(halves), SEQ, scatter_dimension=0, tiled=True
    ).astype(floats)
    key_back = pair_mine[:, :KEY_WIDTH].reshape(length, KV_HEADS, HEAD_DIM)
    value_back = pair_mine[:, KEY_WIDTH:]
    query_back = from_groups(query_sum, length).reshape(length, HEADS, HEAD_DIM)
    query_back = query_back * cosine + unturn_half(query_back * sine)
    key_back = key_back * cosine + unturn_half(key_back * sine)
    joint_back = jnp.concatenate(
        [query_back.reshape(length, QUERY_WIDTH), key_back.reshape(length, KEY_WIDTH), value_back],
        axis=1,
    ).astype(halves)
    joint_local = lax.dot_general(
        normal_first, joint_back, first_pair, preferred_element_type=floats
    )
    bias_local = jnp.sum(joint_back.astype(floats), axis=0)
    normal_back = lax.dot_general(joint_back, joint_all, last_pair, preferred_element_type=floats)
    residual_part, first_local = norm_back(normal_back, residual, scale_first, gain_first)
    tokens_grad = (mixed_grad + residual_part)[None]

    small_back = jnp.concatenate(
        [
            bias_local.reshape(-1, bias_depth),
            first_local.reshape(-1, depth),
            second_local.reshape(-1, depth),
        ],
        axis=1,
    )
    small_back = jnp.pad(small_back, ((0, 0), (0, depth * small_width - small_back.shape[1])))
    small_back = small_back.reshape(-1, small_width)
    packed_grad = jnp.concatenate([joint_local, merge_local, small_back], axis=1).astype(halves)
    packed_grad = lax.psum_scatter(packed_grad, AXES, scatter_dimension=0, tiled=True).astype(floats)
    joint_grad = packed_grad[:, :joint_width]
    merge_grad = packed_grad[:, joint_width : joint_width + model].T
    small_back = packed_grad[:, joint_width + model :].reshape(-1)
    bias_grad = small_back[:bias_depth]
    first_grad = small_back[bias_depth : bias_depth + depth]
    second_grad = small_back[bias_depth + depth : bias_depth + 2 * depth]
    return (
        output,
        tokens_grad,
        joint_grad,
        bias_grad,
        merge_grad,
        first_grad,
        second_grad,
        grads[0],
        grads[1],
        grads[2].T,
    )


def solution(mesh):
    seq, row = mesh.shape["seq"], mesh.shape["row"]
    fine = Mesh(mesh.devices.reshape(seq // 2, 2, row // 2, 2), AXES)
    whole = ("z", "x", "y", "c")
    placed = (
        P(ROW, SEQ, None),
        P(ROW, SEQ),
        P(whole, None),
        P(whole),
        P(None, whole),
        P(whole),
        P(whole),
        P(whole, None),
        P(whole, None),
        P(None, whole),
        P(ROW, SEQ, None),
    )
    return jax.shard_map(
        body,
        mesh=fine,
        in_specs=placed,
        out_specs=(
            P(ROW, SEQ, None),
            P(ROW, SEQ, None),
            P(whole, None),
            P(whole),
            P(None, whole),
            P(whole),
            P(whole),
            P(whole, None),
            P(whole, None),
            P(None, whole),
        ),
        check_vma=False,
    )
```

```python
import functools
import math

import jax
import jax.numpy as jnp
from jax import lax
from jax.experimental import pallas as pl
from jax.experimental.pallas import tpu as pltpu
from jax.sharding import Mesh, PartitionSpec as P

HEADS = 12
KV_HEADS = 2
HEAD_DIM = 128
MODEL = HEADS * HEAD_DIM
GROUP = HEADS // KV_HEADS
QUERY_WIDTH = HEADS * HEAD_DIM
KEY_WIDTH = KV_HEADS * HEAD_DIM
SCALE = 1.0 / math.sqrt(HEAD_DIM)

eps = 1e-06
theta = 1000000.0
neg = -1e30
last_pair = (((1,), (1,)), ((), ()))
first_pair = (((0,), (0,)), ((), ()))
floats = jnp.float32
halves = jnp.bfloat16

AXES = ("z", "x", "y", "c")
SEQ = ("z", "x")
ROW = ("y", "c")
TEAM = ("z", "y")


def turn_half(values):
    middle = values.shape[-1] // 2
    return jnp.concatenate([-values[..., middle:], values[..., :middle]], axis=-1)


def unturn_half(values):
    middle = values.shape[-1] // 2
    return jnp.concatenate([values[..., middle:], -values[..., :middle]], axis=-1)


def row_positions(labels):
    length = labels.shape[0]
    places = jnp.arange(length, dtype=jnp.int32)
    change = jnp.concatenate([jnp.ones((1,), dtype=jnp.bool_), labels[1:] != labels[:-1]])
    starts = lax.cummax(jnp.where(change, places, 0), axis=0)
    return places - starts


def rotary(positions, width):
    inverse = jnp.power(
        jnp.float32(theta), -(jnp.arange(width // 2, dtype=jnp.float32) * (2.0 / width))
    )
    angle = positions.astype(jnp.float32)[:, None] * inverse[None, :]
    angle = jnp.concatenate([angle, angle], axis=1)[:, None, :]
    return (jnp.cos(angle), jnp.sin(angle))


def to_groups(values):
    length = values.shape[0]
    return (
        values.reshape(length, KV_HEADS, GROUP, HEAD_DIM)
        .transpose(1, 2, 0, 3)
        .reshape(KV_HEADS, GROUP * length, HEAD_DIM)
    )


def from_groups(values, length):
    return (
        values.reshape(KV_HEADS, GROUP, length, HEAD_DIM)
        .transpose(2, 0, 1, 3)
        .reshape(length, QUERY_WIDTH)
    )


def norm_parts(values):
    return lax.rsqrt(jnp.mean(values * values, axis=-1, keepdims=True) + eps)


def norm_back(upstream, values, scale, gain):
    scaled = upstream * gain
    inner = jnp.mean(scaled * values, axis=-1, keepdims=True)
    part = scale * scaled - values * (scale * scale * scale) * inner
    gain_grad = jnp.sum(upstream * values * scale, axis=0, keepdims=True)
    return part, gain_grad


MESH = pl.DeviceIdType.MESH
VMEM_LIMIT = 60 * 2**20


def coordinates():
    return tuple(lax.axis_index(name) for name in AXES)


class Courier:
    def __init__(self, sends, receives):
        self.sends, self.receives, self.copies, self.settled = sends, receives, [], 0

    def copy(self, source, target, device):
        place = len(self.copies)
        made = pltpu.make_async_remote_copy(
            src_ref=source,
            dst_ref=target,
            send_sem=self.sends.at[place],
            recv_sem=self.receives.at[place],
            device_id=device,
            device_id_type=MESH,
        )
        made.start()
        self.copies.append(made)
        return made

    def finish(self):
        for made in self.copies[self.settled :]:
            made.wait_send()
        self.settled = len(self.copies)


def meet(devices):
    barrier = pltpu.get_barrier_semaphore()
    for device in devices:
        pl.semaphore_signal(barrier, inc=1, device_id=device, device_id_type=MESH)
    pl.semaphore_wait(barrier, len(devices))


def cuts_of(width, step):
    return [(start, min(step, width - start)) for start in range(0, width, step)]


class Gather:
    def __init__(self, courier, place, source, buffer, order):
        self.courier, self.place, self.order = courier, place, order
        self.source, self.buffer = source, buffer
        self.hops = [{}, {}, {}, {}]

    def line(self, dz):
        nz = self.place.nz
        return lax.rem(self.place.z + nz - dz, nz)

    def start(self):
        p = self.place
        spot = self.buffer.at[p.z, p.x, p.y, p.c]
        for dz in range(1, p.nz):
            device = (lax.rem(p.z + dz, p.nz), p.x, p.y, p.c)
            self.hops[0][dz] = self.courier.copy(self.source, spot, device)

    def hop(self, number, dz):
        p, group = self.place, self.line(dz)
        if dz or number > 1:
            self.hops[number - 1][dz].wait_recv()
        if number == 1:
            spot = self.buffer.at[group, p.x, p.y, p.c]
            device = p.across[self.order[0]]
        elif number == 2:
            if self.order[0] == "y":
                spot = self.buffer.at[group, p.x, :, p.c]
            else:
                spot = self.buffer.at[group, :, p.y, p.c]
            device = p.across[self.order[1]]
        else:
            spot = self.buffer.at[group, :, :, p.c]
            device = p.across["c"]
        self.hops[number][dz] = self.courier.copy(spot, spot, device)

    def hop_all(self, number):
        for dz in range(self.place.nz):
            self.hop(number, dz)

    def done(self):
        for made in self.hops[3].values():
            made.wait_recv()


class Place:
    def __init__(self, nz):
        self.nz = nz
        self.z, self.x, self.y, self.c = z, x, y, c = coordinates()
        self.across = {"x": (z, 1 - x, y, c), "y": (z, x, 1 - y, c), "c": (z, x, y, 1 - c)}

    def line(self, dz, dy=0):
        y = lax.rem(self.y + dy, 2) if dy else self.y
        return (lax.rem(self.z + dz, self.nz), self.x, y, self.c)

    def peers(self):
        team = [self.line(dz, dy) for dz in range(self.nz) for dy in range(2)]
        return team[1:] + [self.across["x"], self.across["c"]]


def spread(values, piece, width):
    devices, lanes = values.shape
    at = lax.broadcasted_iota(jnp.int32, (lanes, width), 1)
    inner = lax.broadcasted_iota(jnp.int32, (lanes, width), 0)
    chosen = (lax.rem(at, piece) == inner).astype(floats).astype(halves)
    repeated = jnp.dot(values.astype(halves), chosen, preferred_element_type=floats)
    owner = lax.div(lax.broadcasted_iota(jnp.int32, (devices, width), 1), piece)
    mine = owner == lax.broadcasted_iota(jnp.int32, (devices, width), 0)
    return jnp.sum(jnp.where(mine, repeated, 0.0), axis=0, keepdims=True)


def attention_kernel(
    nz,
    stack_ref,
    joint_ref,
    merge_ref,
    small_ref,
    label_ref,
    inverse_ref,
    tokens_ref,
    outer_ref,
    w_ref,
    ct_ref,
    kv_out,
    query_out,
    merge_out,
    xn1_ref,
    xn2_ref,
    mixed_ref,
    gain_ref,
    turn_ref,
    query_ref,
    pair_ref,
    share_ref,
    out_ref,
    joint_kv,
    joint_q,
    merge,
    small,
    bias_mask,
    qjoint,
    pair_own,
    sends,
    receives,
    locals_,
):
    place = Place(nz)
    z, x, y, c = place.z, place.x, place.y, place.c
    length, model = tokens_ref.shape
    depth, joint_width = joint_ref.shape
    share = w_ref.shape[-1]
    courier = Courier(sends, receives)
    devices = 8 * nz
    meet(place.peers())

    own_copies = []

    def keep(source, target):
        made = pltpu.make_async_copy(source, target, locals_.at[len(own_copies)])
        made.start()
        own_copies.append(made)
        return made

    def columns(tz, ty):
        return pl.ds(pl.multiple_of((tz * 2 + ty) * share, 128), share)

    half = QUERY_WIDTH // 2
    blocks = {
        "small": (small_ref, small, "yx"),
        "kv": (joint_ref.at[:, QUERY_WIDTH:], joint_kv, "xy"),
        "q0": (joint_ref.at[:, :half], joint_q.at[0], "yx"),
        "q1": (joint_ref.at[:, half:QUERY_WIDTH], joint_q.at[1], "xy"),
        "m0": (merge_ref.at[:, :half], merge.at[0], "yx"),
        "m1": (merge_ref.at[:, half:], merge.at[1], "xy"),
    }
    gathers = {}
    own_waits = {}
    for name, (source, buffer, order) in blocks.items():
        own_waits[name] = keep(source, buffer.at[z, x, y, c])
        gathers[name] = Gather(courier, place, source, buffer, order)
    for name in ("small", "kv", "q0", "q1"):
        gathers[name].start()
    w_own = keep(stack_ref.at[:, :, columns(z, y)], w_ref.at[:, z, x, y, c])
    ct_own = keep(outer_ref, ct_ref.at[z, y])

    residual = tokens_ref[...].astype(floats)
    hat = residual * norm_parts(residual)

    for name in ("small", "kv"):
        own_waits[name].wait()
        gathers[name].hop_all(1)
    direct = {}
    for dz in list(range(1, nz)) + [0]:
        for dy in range(2):
            if dz or dy:
                ty = lax.rem(y + dy, 2)
                device = place.line(dz, dy)
                direct[dz, dy] = courier.copy(
                    stack_ref.at[:, :, columns(device[0], ty)], w_ref.at[:, z, x, y, c], device
                )
    for name in ("small", "kv"):
        gathers[name].hop_all(2)
    for name in ("q0", "q1"):
        own_waits[name].wait()
        gathers[name].hop_all(1)
    for name in ("small", "kv"):
        gathers[name].hop_all(3)
    for name in ("m0", "m1"):
        gathers[name].start()
    ct_along = {
        dz: courier.copy(outer_ref, ct_ref.at[z, y], place.line(dz)) for dz in range(1, nz)
    }
    for name in ("small", "kv"):
        gathers[name].done()

    pieces = small[...].reshape(devices * 8, 128).astype(halves)

    def row_of(which):
        at = lax.broadcasted_iota(jnp.int32, (devices, devices * 8), 1)
        wanted = lax.broadcasted_iota(jnp.int32, (devices, devices * 8), 0) * 8 + which
        chosen = (at == wanted).astype(floats).astype(halves)
        return jnp.dot(chosen, pieces, preferred_element_type=floats)

    gain_first = spread(row_of(1), depth, model)
    gain_second = spread(row_of(2), depth, model)
    bias = spread(row_of(0), joint_width // devices, joint_width)
    gain_ref[0:1, :] = gain_first
    gain_ref[1:2, :] = gain_second
    label = label_ref[...]
    start = jnp.zeros((length, 1), floats)
    block_at = (z * 2 + x) * length
    rows_at = block_at + lax.broadcasted_iota(jnp.int32, (length, length), 0)
    lanes_at = lax.broadcasted_iota(jnp.int32, (length, length), 1)
    for block in range(2 * nz):
        keys_label = small[block // 2, block % 2, y, c, 3:4, :]
        start = start + jnp.sum((keys_label < label).astype(floats), axis=1, keepdims=True)
        allowed = (keys_label == label) & (rows_at >= block * length + lanes_at)
        bias_mask[:, block * length : (block + 1) * length] = jnp.where(allowed, 0.0, neg)
    place_at = (block_at + lax.broadcasted_iota(jnp.int32, (length, 1), 0)).astype(floats)
    angle = (place_at - start) * inverse_ref[...]
    cosine = jnp.cos(angle)
    lane = lax.broadcasted_iota(jnp.int32, (length, HEAD_DIM), 1)
    sine = jnp.where(lane < HEAD_DIM // 2, -1.0, 1.0) * jnp.sin(angle)
    turn_ref[0] = cosine
    turn_ref[1] = sine

    def turned(values):
        return values * cosine + pltpu.roll(values, HEAD_DIM // 2, 1) * sine

    xn1_ref[...] = (hat * gain_first).astype(halves)
    pair = jnp.dot(
        xn1_ref[...], joint_kv[...].reshape(model, 2 * KEY_WIDTH), preferred_element_type=floats
    ) + bias[:, QUERY_WIDTH:]
    for head in range(KV_HEADS):
        lanes = slice(head * HEAD_DIM, (head + 1) * HEAD_DIM)
        pair_own[:, lanes] = turned(pair[:, lanes]).astype(halves)
    pair_own[:, KEY_WIDTH:] = pair[:, KEY_WIDTH:].astype(halves)
    pair_ref[z, x] = pair_own[...]
    pair_along = {
        dz: courier.copy(pair_own, pair_ref.at[z, x], place.line(dz)) for dz in range(1, nz)
    }
    pair_side = {0: courier.copy(pair_own, pair_ref.at[z, x], place.across["x"])}
    for name in ("q0", "q1"):
        gathers[name].hop_all(2)
    for dz in range(1, nz):
        pair_along[dz].wait_recv()
        spot = pair_ref.at[lax.rem(z + nz - dz, nz), x]
        pair_side[dz] = courier.copy(spot, spot, place.across["x"])
    for name in ("q0", "q1"):
        gathers[name].hop_all(3)
    for name in ("m0", "m1"):
        own_waits[name].wait()
        gathers[name].hop_all(1)
    for name in ("q0", "q1"):
        gathers[name].done()

    for part in range(2):
        qjoint[:, part * half : (part + 1) * half] = jnp.dot(
            xn1_ref[...], joint_q[part].reshape(model, half), preferred_element_type=floats
        ) + bias[:, part * half : (part + 1) * half]
    for head in range(HEADS):
        query_ref[head // GROUP, head % GROUP] = turned(
            qjoint[:, head * HEAD_DIM : (head + 1) * HEAD_DIM]
        ).astype(halves)

    w_cross, ct_side = {}, {}
    ct_own.wait()
    w_own.wait()
    for dz in range(nz):
        if dz:
            ct_along[dz].wait_recv()
        spot = ct_ref.at[lax.rem(z + nz - dz, nz), y]
        ct_side[dz] = courier.copy(spot, spot, place.across["y"])
    for name in ("m0", "m1"):
        gathers[name].hop_all(2)
    for made in pair_side.values():
        made.wait_recv()

    def cross(dz):
        for dy in range(2):
            if dz or dy:
                direct[dz, dy].wait_recv()
        spot = w_ref.at[:, lax.rem(z + nz - dz, nz), x, :, c]
        w_cross[dz] = courier.copy(spot, spot, place.across["x"])

    cross(0)
    cross(1)

    heads = 2

    @pl.loop(0, HEADS // heads)
    def _(step):
        kv = lax.div(step, GROUP // heads)
        pack = lax.rem(step, GROUP // heads)
        key_lanes = pl.ds(pl.multiple_of(kv * HEAD_DIM, 128), HEAD_DIM)
        value_lanes = pl.ds(pl.multiple_of(KEY_WIDTH + kv * HEAD_DIM, 128), HEAD_DIM)
        total_keys = 2 * nz * length
        query = query_ref[kv, pl.ds(pack * heads, heads)].reshape(heads * length, HEAD_DIM)
        keys = pair_ref[:, :, :, key_lanes].reshape(total_keys, HEAD_DIM)
        values = pair_ref[:, :, :, value_lanes].reshape(total_keys, HEAD_DIM)
        scores = lax.dot_general(query, keys, last_pair, preferred_element_type=floats)
        scores = scores.reshape(heads, length, total_keys) * SCALE + bias_mask[...][None]
        top = jnp.max(scores, axis=-1, keepdims=True)
        raised = jnp.exp(scores - top)
        shares = raised / jnp.sum(raised, axis=-1, keepdims=True)
        shares = shares.reshape(heads * length, total_keys).astype(halves)
        share_ref[kv, pl.ds(pack * heads, heads)] = shares.reshape(heads, length, total_keys)
        summed = jnp.dot(shares, values, preferred_element_type=floats)
        for index in range(heads):
            lanes = pl.ds(pl.multiple_of((step * heads + index) * HEAD_DIM, 128), HEAD_DIM)
            out_ref[:, lanes] = summed[index * length : (index + 1) * length]

    for name in ("m0", "m1"):
        gathers[name].hop_all(3)
    for dz in range(2, nz):
        cross(dz)
    for name in ("m0", "m1"):
        gathers[name].done()
    saves = [
        keep(joint_kv, kv_out),
        keep(joint_q, query_out),
        keep(merge, merge_out),
    ]
    attended = out_ref[...].astype(halves)
    mixed = tokens_ref[...].astype(floats)
    for part in range(2):
        mixed = mixed + lax.dot_general(
            attended[:, part * half : (part + 1) * half],
            merge[part].reshape(model, half),
            last_pair,
            preferred_element_type=floats,
        )
    mixed_ref[...] = mixed
    xn2_ref[...] = (mixed * norm_parts(mixed) * gain_second).astype(halves)

    hand = []
    for dz in range(nz):
        w_cross[dz].wait_recv()
        spot = w_ref.at[:, lax.rem(z + nz - dz, nz), :, :, c]
        hand.append(courier.copy(spot, spot, place.across["c"]))
    for made in hand:
        made.wait_recv()
    for made in ct_side.values():
        made.wait_recv()
    for made in saves:
        made.wait()
    courier.finish()


def feed_kernel(
    nz,
    w_ref,
    ct_ref,
    normal_ref,
    back_ref,
    branch_ref,
    grads_ref,
    w,
    xn,
    ct,
    hid,
    gb,
    ub,
    part,
    ybuf,
    zsend,
    zbuf,
    cbuf,
    sends,
    receives,
    locals_,
):
    place = Place(nz)
    z, x, y, c = place.z, place.x, place.y, place.c
    length, model = normal_ref.shape
    share = w.shape[-1]
    block = model // nz
    lines = 2 * length * nz
    courier = Courier(sends, receives)

    def source(dz):
        return lax.rem(z + nz - dz, nz)

    meet([place.line(dz) for dz in range(1, nz)] + [place.across["y"], place.across["c"]])
    along = {
        dz: courier.copy(normal_ref, xn.at[z, y], place.line(dz)) for dz in range(1, nz)
    }
    side = {0: courier.copy(normal_ref, xn.at[z, y], place.across["y"])}
    loads = [
        pltpu.make_async_copy(w_ref.at[which], w.at[which], locals_.at[which])
        for which in range(3)
    ] + [pltpu.make_async_copy(ct_ref, ct, locals_.at[3])]
    for made in loads:
        made.start()
    xn[z, y] = normal_ref[...]
    for made in loads:
        made.wait()

    def weight(which, start, size):
        return w[which, :, :, :, :, :, start : start + size].reshape(model, size)

    def pass_on(dz):
        along[dz].wait_recv()
        spot = xn.at[source(dz), y]
        side[dz] = courier.copy(spot, spot, place.across["y"])

    half = nz // 2
    scatter = []
    for dz in range(nz):
        group = source(dz)
        if dz + 1 < nz:
            pass_on(dz + 1)
        side[dz].wait_recv()
        for start, size in cuts_of(share, 256):
            normal = xn[group].reshape(2 * length, model)
            outer = ct[group].reshape(2 * length, model)
            gate = jnp.dot(normal, weight(0, start, size), preferred_element_type=floats)
            upper = jnp.dot(normal, weight(1, start, size), preferred_element_type=floats)
            hidden_back = jnp.dot(outer, weight(2, start, size), preferred_element_type=floats)
            sig = 1.0 / (1.0 + jnp.exp(-gate))
            silu = gate * sig
            spot = (group, slice(None), slice(start, start + size))
            hid[spot] = (silu * upper).astype(halves)
            gb[spot] = (hidden_back * upper * (sig * (1.0 + gate * (1.0 - sig)))).astype(halves)
            ub[spot] = (hidden_back * silu).astype(halves)

        @pl.loop(0, 2)
        def _(step):
            rows = pl.ds(step * half, half)
            lanes = pl.ds(pl.multiple_of(step * (model // 2), 128), model // 2)

            def turned(which):
                return w[which, rows].reshape(model // 2, share)

            both = lax.dot_general(
                gb[group], turned(0), last_pair, preferred_element_type=floats
            ) + lax.dot_general(ub[group], turned(1), last_pair, preferred_element_type=floats)
            part[group, :, :, lanes] = both.astype(halves).reshape(2, length, model // 2)

        scatter.append(
            courier.copy(part.at[group, 1 - y], ybuf.at[group], place.across["y"])
        )

    final = {}
    for dz in [(dz + nz // 2) % nz for dz in range(nz)]:
        group = source(dz)
        scatter[dz].wait_recv()
        total = part[group, y].astype(floats) + ybuf[group].astype(floats)
        if dz == 0:
            back_ref[...] = total
        else:
            zsend[dz - 1] = total.astype(halves)
            final[dz] = courier.copy(zsend.at[dz - 1], zbuf.at[dz - 1], (group, x, y, c))

    for group in range(nz):

        @pl.loop(0, 2)
        def _(step):
            rows = pl.ds(step * half, half)
            lanes = pl.ds(pl.multiple_of(step * (model // 2), 128), model // 2)
            product = lax.dot_general(
                hid[group],
                w[2, rows].reshape(model // 2, share),
                last_pair,
                preferred_element_type=floats,
            )
            branch_ref[group, :, :, lanes] = product.astype(halves).reshape(2, length, model // 2)

    saves, handed = [], []
    for group in range(nz):
        lanes = slice(group * block, (group + 1) * block)
        normal_turned = xn[:, :, :, lanes].reshape(lines, block).T
        outer_turned = ct[:, :, :, lanes].reshape(lines, block).T
        for which, left, right in (
            (0, normal_turned, gb),
            (1, normal_turned, ub),
            (2, outer_turned, hid),
        ):
            for start, size in cuts_of(share, 512):
                w[which, group, :, :, :, :, start : start + size] = (
                    jnp.dot(
                        left,
                        right[:, :, start : start + size].reshape(lines, size),
                        preferred_element_type=floats,
                    )
                    .astype(halves)
                    .reshape(2, 2, 2, -1, size)
                )
        handed.append(
            courier.copy(w.at[:, group, :, :, 1 - c], cbuf.at[group], place.across["c"])
        )
    for group in range(nz):
        handed[group].wait_recv()
        for which in range(3):
            w[which, group, :, :, c] = (
                w[which, group, :, :, c].astype(floats) + cbuf[group, which].astype(floats)
            ).astype(halves)
        made = pltpu.make_async_copy(
            w.at[:, group, :, :, c], grads_ref.at[:, group], locals_.at[4 + group]
        )
        made.start()
        saves.append(made)
    for dz in range(1, nz):
        final[dz].wait_recv()
        back_ref[...] += zbuf[dz - 1].astype(floats)
    for made in saves:
        made.wait()
    courier.finish()


class Scatter:
    def __init__(self, courier, place, parts, core_in, second_in, first_in, line_in, order):
        self.courier, self.place, self.order = courier, place, order
        self.parts, self.line_in = parts, line_in
        self.arrivals = [core_in, second_in, first_in]
        self.hops = [{}, {}, {}, {}]

    def spots(self, group):
        p = self.place
        if self.order == "xy":
            second = ((group, p.x, slice(None), p.c), (group, 1 - p.x, slice(None), p.c))
            first = ((group, p.x, p.y, p.c), (group, p.x, 1 - p.y, p.c))
        else:
            second = ((group, slice(None), p.y, p.c), (group, slice(None), 1 - p.y, p.c))
            first = ((group, p.x, p.y, p.c), (group, 1 - p.x, p.y, p.c))
        every = slice(None)
        core = ((group, every, every, p.c), (group, every, every, 1 - p.c))
        return [core, second, first]

    def hop(self, number, dz):
        p = self.place
        group = lax.rem(p.z + dz, p.nz)
        spots = self.spots(group)
        if number:
            self.hops[number - 1][dz].wait_recv()
            kept = spots[number - 1][0]
            self.parts[kept] = (
                self.parts[kept].astype(floats) + self.arrivals[number - 1][dz].astype(floats)
            ).astype(self.parts.dtype)
        if number < 3:
            device = p.across[("c" + self.order)[number]]
            self.hops[number][dz] = self.courier.copy(
                self.parts.at[spots[number][1]], self.arrivals[number].at[dz], device
            )
        elif dz:
            self.hops[3][dz] = self.courier.copy(
                self.parts.at[spots[2][0]], self.line_in.at[dz - 1], p.line(dz)
            )

    def hop_all(self, number):
        for dz in [(dz + self.place.nz // 2) % self.place.nz for dz in range(self.place.nz)]:
            self.hop(number, dz)

    def total(self):
        p = self.place
        result = self.parts[p.z, p.x, p.y, p.c].astype(floats)
        for dz in range(1, p.nz):
            self.hops[3][dz].wait_recv()
            result = result + self.line_in[dz - 1].astype(floats)
        return result


def gather_pieces(values, piece, devices):
    width = values.shape[1]
    owner = lax.div(lax.broadcasted_iota(jnp.int32, (devices, width), 1), piece)
    mine = owner == lax.broadcasted_iota(jnp.int32, (devices, width), 0)
    at = lax.broadcasted_iota(jnp.int32, (width, 128), 0)
    inner = lax.broadcasted_iota(jnp.int32, (width, 128), 1)
    chosen = (lax.rem(at, piece) == inner).astype(floats)
    rows = jnp.where(mine, values, 0.0)
    return jnp.dot(rows, chosen, preferred_element_type=floats, precision=lax.Precision.HIGHEST)


def back_kernel(
    nz,
    grads_in,
    branch_ref,
    kv_ref,
    q_ref,
    m_ref,
    back_ref,
    mixed_ref,
    outer_ref,
    tokens_ref,
    xn1_ref,
    gain_ref,
    turn_ref,
    query_ref,
    pair_ref,
    share_ref,
    out_ref,
    output_ref,
    tokens_grad_ref,
    joint_grad_ref,
    merge_grad_ref,
    small_grad_ref,
    grads_ref,
    weight,
    weight_kv,
    gown,
    gin,
    branch_own,
    branch_in,
    branch_line,
    merge_part,
    merge_c,
    merge_s,
    merge_f,
    merge_z,
    query_part,
    query_c,
    query_s,
    query_f,
    query_z,
    kv_part,
    kv_c,
    kv_s,
    kv_f,
    kv_z,
    small_part,
    small_c,
    small_s,
    small_f,
    small_z,
    pair_sum,
    pair_half,
    pair_side,
    pair_line,
    joint_back,
    attended_back,
    query_back,
    mixed_grad,
    sends,
    receives,
    locals_,
):
    place = Place(nz)
    z, x, y, c = place.z, place.x, place.y, place.c
    length, model = tokens_ref.shape
    share = gown.shape[-1]
    half = QUERY_WIDTH // 2
    block = model // nz
    depth = grads_in.shape[-2]
    devices = 8 * nz
    total_keys = 2 * nz * length
    orders = [(dz + nz // 2) % nz for dz in range(nz)]
    courier = Courier(sends, receives)
    meet(place.peers())

    def group_of(dz):
        return lax.rem(z + dz, nz)

    copies = []

    def load(source, target):
        made = pltpu.make_async_copy(source, target, locals_.at[len(copies)])
        made.start()
        copies.append(made)
        return made

    merge_load = load(m_ref, weight)
    kv_load = load(kv_ref, weight_kv)
    branch_load = load(branch_ref.at[:, y], branch_own)
    gown_load = load(grads_in.at[:, :, x], gown)

    g_cross = {
        dz: courier.copy(grads_in.at[:, group_of(dz), 1 - x], gin.at[dz], place.across["x"])
        for dz in orders
    }
    b_cross = {
        dz: courier.copy(branch_ref.at[group_of(dz), 1 - y], branch_in.at[dz], place.across["y"])
        for dz in orders
    }

    mixed = mixed_ref[...]
    second_scale = norm_parts(mixed)
    part, second_local = norm_back(back_ref[...], mixed, second_scale, gain_ref[1:2, :])
    grad = outer_ref[...].astype(floats) + part
    mixed_grad[...] = grad
    mixed_half = grad.astype(halves)

    def scatter(arrays, order):
        return Scatter(courier, place, *arrays, order)

    merges = [
        scatter([ref.at[i] for ref in (merge_part, merge_c, merge_s, merge_f, merge_z)], order)
        for i, order in ((0, "xy"), (1, "yx"))
    ]
    attended = out_ref[...].astype(halves)
    mixed_turned = mixed_half.T
    for group in range(nz):
        for i in range(2):
            merge_part[i, group] = (
                jnp.dot(
                    mixed_turned[group * block : (group + 1) * block],
                    attended[:, i * half : (i + 1) * half],
                    preferred_element_type=floats,
                )
                .astype(halves)
                .reshape(2, 2, 2, depth, half)
            )
    for made in merges:
        made.hop_all(0)
    merge_load.wait()
    for i in range(2):
        attended_back[:, i * half : (i + 1) * half] = jnp.dot(
            mixed_half, weight[i].reshape(model, half), preferred_element_type=floats
        ).astype(halves)
    query_load = load(q_ref, weight)

    branch_load.wait()
    gown_load.wait()
    b_line, g_line = {}, []
    for dz in orders:
        group = group_of(dz)
        b_cross[dz].wait_recv()
        branch_own[group] = (
            branch_own[group].astype(floats) + branch_in[dz].astype(floats)
        ).astype(halves)
        if dz:
            b_line[dz] = courier.copy(
                branch_own.at[group], branch_line.at[dz - 1], place.line(dz)
            )
    mine = pl.ds(pl.multiple_of((z * 2 + y) * share, 128), share)
    kept = []

    def grads_on(dz):
        group = group_of(dz)
        g_cross[dz].wait_recv()
        for which in range(3):
            gown[which, group] = (
                gown[which, group].astype(floats) + gin[dz, which].astype(floats)
            ).astype(halves)
        for dy in range(2):
            ty = lax.rem(y + dy, 2)
            if dz or dy:
                g_line.append(
                    courier.copy(
                        gown.at[:, group, ty], grads_ref.at[:, :, mine], (group, x, ty, c)
                    )
                )
            else:
                kept.append(load(gown.at[:, group, ty], grads_ref.at[:, :, mine]))

    grads_on(orders[0])
    for made in merges:
        made.hop_all(1)

    heads = 2
    pair_sum[...] = jnp.zeros_like(pair_sum)

    @pl.loop(0, HEADS // heads)
    def _(step):
        kv = lax.div(step, GROUP // heads)
        pack = lax.rem(step, GROUP // heads)
        key_lanes = pl.ds(pl.multiple_of(kv * HEAD_DIM, 128), HEAD_DIM)
        value_lanes = pl.ds(pl.multiple_of(KEY_WIDTH + kv * HEAD_DIM, 128), HEAD_DIM)
        rows = heads * length
        query = query_ref[kv, pl.ds(pack * heads, heads)].reshape(rows, HEAD_DIM)
        keys = pair_ref[:, :, :, key_lanes].reshape(total_keys, HEAD_DIM)
        values = pair_ref[:, :, :, value_lanes].reshape(total_keys, HEAD_DIM)
        lanes = [
            pl.ds(pl.multiple_of((step * heads + index) * HEAD_DIM, 128), HEAD_DIM)
            for index in range(heads)
        ]
        upstream = jnp.concatenate([attended_back[:, at] for at in lanes], axis=0)
        summed = jnp.concatenate([out_ref[:, at] for at in lanes], axis=0)
        delta = jnp.sum(upstream.astype(floats) * summed, axis=-1, keepdims=True)
        mass = lax.dot_general(upstream, values, last_pair, preferred_element_type=floats)
        shares = share_ref[kv, pl.ds(pack * heads, heads)].reshape(rows, total_keys)
        scores = (shares.astype(floats) * (mass - delta)).astype(halves)
        query_sum = jnp.dot(scores, keys, preferred_element_type=floats) * SCALE
        for index in range(heads):
            query_back[:, lanes[index]] = query_sum[index * length : (index + 1) * length]
        pair_sum[:, key_lanes] += jnp.dot(scores.T, query, preferred_element_type=floats) * SCALE
        pair_sum[:, value_lanes] += jnp.dot(shares.T, upstream, preferred_element_type=floats)

    pair_half[...] = pair_sum[...].astype(halves).reshape(nz, 2, length, 2 * KEY_WIDTH)
    p_cross = {
        dz: courier.copy(pair_half.at[group_of(dz), 1 - x], pair_side.at[dz], place.across["x"])
        for dz in orders
    }
    grads_on(orders[1])
    cosine, sine = turn_ref[0], turn_ref[1]

    def unturned(values):
        return values * cosine + pltpu.roll(values * sine, HEAD_DIM // 2, 1)

    for head in range(HEADS):
        lanes = slice(head * HEAD_DIM, (head + 1) * HEAD_DIM)
        joint_back[:, lanes] = unturned(query_back[:, lanes]).astype(halves)
    p_line = {}
    for dz in orders:
        group = group_of(dz)
        p_cross[dz].wait_recv()
        pair_half[group, x] = (
            pair_half[group, x].astype(floats) + pair_side[dz].astype(floats)
        ).astype(halves)
        if dz:
            p_line[dz] = courier.copy(
                pair_half.at[group, x], pair_line.at[dz - 1], place.line(dz)
            )
    queries = [
        scatter([ref.at[i] for ref in (query_part, query_c, query_s, query_f, query_z)], order)
        for i, order in ((0, "xy"), (1, "yx"))
    ]
    keys_values = scatter([kv_part, kv_c, kv_s, kv_f, kv_z], "yx")
    smalls = scatter([small_part, small_c, small_s, small_f, small_z], "xy")
    turned = xn1_ref[...].T
    for group in range(nz):
        for i in range(2):
            query_part[i, group] = (
                jnp.dot(
                    turned[group * block : (group + 1) * block],
                    joint_back[:, i * half : (i + 1) * half],
                    preferred_element_type=floats,
                )
                .astype(halves)
                .reshape(2, 2, 2, depth, half)
            )
    for made in queries:
        made.hop_all(0)
    for made in merges:
        made.hop_all(2)
    total = pair_half[z, x].astype(floats)
    for dz in range(1, nz):
        p_line[dz].wait_recv()
        total = total + pair_line[dz - 1].astype(floats)
    for head in range(KV_HEADS):
        lanes = slice(head * HEAD_DIM, (head + 1) * HEAD_DIM)
        joint_back[:, QUERY_WIDTH + head * HEAD_DIM : QUERY_WIDTH + (head + 1) * HEAD_DIM] = (
            unturned(total[:, lanes]).astype(halves)
        )
    joint_back[:, QUERY_WIDTH + KEY_WIDTH :] = total[:, KEY_WIDTH:].astype(halves)
    for group in range(nz):
        kv_part[group] = (
            jnp.dot(
                turned[group * block : (group + 1) * block],
                joint_back[:, QUERY_WIDTH:],
                preferred_element_type=floats,
            )
            .astype(halves)
            .reshape(2, 2, 2, depth, 2 * KEY_WIDTH)
        )
    keys_values.hop_all(0)
    for made in queries:
        made.hop_all(1)
    grads_on(orders[2])

    query_load.wait()
    kv_load.wait()
    normal_back = lax.dot_general(
        joint_back[:, QUERY_WIDTH:],
        weight_kv[...].reshape(model, 2 * KEY_WIDTH),
        last_pair,
        preferred_element_type=floats,
    )
    for i in range(2):
        normal_back = normal_back + lax.dot_general(
            joint_back[:, i * half : (i + 1) * half],
            weight[i].reshape(model, half),
            last_pair,
            preferred_element_type=floats,
        )
    residual = tokens_ref[...].astype(floats)
    part, first_local = norm_back(normal_back, residual, norm_parts(residual), gain_ref[0:1, :])
    tokens_grad_ref[...] = mixed_grad[...] + part
    bias_local = jnp.sum(joint_back[...].astype(floats), axis=0, keepdims=True)

    pieces = jnp.zeros((devices * 8, 128), floats)
    for which, values in ((0, bias_local), (1, first_local), (2, second_local)):
        mine_rows = gather_pieces(values, values.shape[1] // devices, devices)
        at = lax.broadcasted_iota(jnp.int32, (devices * 8, devices), 0)
        wanted = lax.broadcasted_iota(jnp.int32, (devices * 8, devices), 1) * 8 + which
        pieces = pieces + jnp.dot(
            (at == wanted).astype(floats),
            mine_rows,
            preferred_element_type=floats,
            precision=lax.Precision.HIGHEST,
        )
    small_part[...] = pieces.reshape(nz, 2, 2, 2, 8, 128)
    smalls.hop_all(0)
    keys_values.hop_all(1)
    smalls.hop_all(1)
    for made in queries:
        made.hop_all(2)
    keys_values.hop_all(2)
    smalls.hop_all(2)
    for dz in orders[3:]:
        grads_on(dz)
    for made in merges + queries + [keys_values, smalls]:
        made.hop_all(3)
    total = mixed_ref[...] + branch_own[z].astype(floats)
    for dz in range(1, nz):
        b_line[dz].wait_recv()
        total = total + branch_line[dz - 1].astype(floats)
    output_ref[...] = total.astype(halves)
    for i in range(2):
        merge_grad_ref[:, i * half : (i + 1) * half] = merges[i].total()
        joint_grad_ref[:, i * half : (i + 1) * half] = queries[i].total()
    joint_grad_ref[:, QUERY_WIDTH:] = keys_values.total()
    small_grad_ref[...] = smalls.total()
    for made in g_line:
        made.wait_recv()
    for made in kept:
        made.wait()
    courier.finish()


def padded_share(hidden_width, team):
    return -(-hidden_width // (team * 128)) * 128


def body_kernels(
    tokens,
    segments,
    joint_matrix,
    joint_bias,
    merge_matrix,
    norm_first,
    norm_second,
    gate_matrix,
    up_matrix,
    down_matrix,
    cotangent,
):
    length, model = tokens.shape[1:]
    depth, joint_width = joint_matrix.shape
    hidden_width = gate_matrix.shape[1]
    nz = lax.axis_size("z")
    share = padded_share(hidden_width, 2 * nz)
    half = QUERY_WIDTH // 2
    pair_width = 2 * KEY_WIDTH
    keys = 2 * nz * length
    vmem = pl.BlockSpec(memory_space=pltpu.VMEM)
    anywhere = pl.BlockSpec(memory_space=pl.ANY)
    blocks = (nz, 2, 2, 2)

    def shape(dims, kind=halves):
        return jax.ShapeDtypeStruct(dims, kind)

    def semaphores(count, loads):
        return [
            pltpu.SemaphoreType.DMA((count,)),
            pltpu.SemaphoreType.DMA((count,)),
            pltpu.SemaphoreType.DMA((loads,)),
        ]

    def params(number):
        return pltpu.CompilerParams(
            collective_id=number, has_side_effects=True, vmem_limit_bytes=VMEM_LIMIT
        )

    stack = jnp.stack([gate_matrix, up_matrix, down_matrix.T])
    stack = jnp.pad(stack, ((0, 0), (0, 0), (0, 2 * nz * share - hidden_width)))

    def lane_row(values):
        return jnp.pad(values.astype(floats), (0, 128 - values.shape[0]))

    own_labels = segments[0]
    empty = jnp.zeros((128,), floats)
    small = jnp.stack(
        [lane_row(v) for v in (joint_bias, norm_first, norm_second, own_labels)] + [empty] * 4
    )
    inverse = jnp.power(floats(theta), -(jnp.arange(HEAD_DIM // 2, dtype=floats) * (2.0 / HEAD_DIM)))
    inverse = jnp.concatenate([inverse, inverse])[None]
    labels = own_labels.astype(floats)[:, None]
    outer = cotangent[0]
    (
        w,
        team_outer,
        kv_all,
        q_all,
        m_all,
        xn1,
        xn2,
        mixed,
        gains,
        turns,
        queries,
        pair,
        shares,
        summed,
    ) = pl.pallas_call(
        functools.partial(attention_kernel, nz),
        name="attention_forward",
        out_shape=(
            shape((3,) + blocks + (depth, share)),
            shape((nz, 2, length, model)),
            shape(blocks + (depth, pair_width)),
            shape((2,) + blocks + (depth, half)),
            shape((2,) + blocks + (depth, half)),
            shape((length, model)),
            shape((length, model)),
            shape((length, model), floats),
            shape((8, model), floats),
            shape((2, length, HEAD_DIM), floats),
            shape((KV_HEADS, GROUP, length, HEAD_DIM)),
            shape((nz, 2, length, pair_width)),
            shape((KV_HEADS, GROUP, length, keys)),
            shape((length, QUERY_WIDTH), floats),
        ),
        in_specs=[anywhere] * 3 + [vmem] * 5,
        out_specs=(anywhere,) * 5 + (vmem,) * 9,
        scratch_shapes=[
            pltpu.VMEM(blocks + (depth, pair_width), halves),
            pltpu.VMEM((2,) + blocks + (depth, half), halves),
            pltpu.VMEM((2,) + blocks + (depth, half), halves),
            pltpu.VMEM(blocks + (8, 128), floats),
            pltpu.VMEM((length, keys), floats),
            pltpu.VMEM((length, QUERY_WIDTH), floats),
            pltpu.VMEM((length, pair_width), halves),
        ]
        + semaphores(119, 11),
        compiler_params=params(0),
    )(stack, joint_matrix, merge_matrix.T, small, labels, inverse, tokens[0], outer)

    lines = 2 * length
    back, branch, grads = pl.pallas_call(
        functools.partial(feed_kernel, nz),
        name="feed_forward",
        out_shape=(
            shape((length, model), floats),
            shape((nz, 2, length, model)),
            shape((3, nz, 2, 2, depth, share)),
        ),
        in_specs=[anywhere, anywhere, vmem],
        out_specs=(vmem, vmem, anywhere),
        scratch_shapes=[
            pltpu.VMEM((3,) + blocks + (depth, share), halves),
            pltpu.VMEM((nz, 2, length, model), halves),
            pltpu.VMEM((nz, 2, length, model), halves),
            pltpu.VMEM((nz, lines, share), halves),
            pltpu.VMEM((nz, lines, share), halves),
            pltpu.VMEM((nz, lines, share), halves),
            pltpu.VMEM((nz, 2, length, model), halves),
            pltpu.VMEM((nz, length, model), halves),
            pltpu.VMEM((nz - 1, length, model), halves),
            pltpu.VMEM((nz - 1, length, model), halves),
            pltpu.VMEM((nz, 3, 2, 2, depth, share), halves),
        ]
        + semaphores(18, 8),
        compiler_params=params(1),
    )(w, team_outer, xn2)

    def sums(rows, width, kind=halves, lead=()):
        return [
            pltpu.VMEM(lead + blocks + (rows, width), kind),
            pltpu.VMEM(lead + (nz, 2, 2, rows, width), kind),
            pltpu.VMEM(lead + (nz, 2, rows, width), kind),
            pltpu.VMEM(lead + (nz, rows, width), kind),
            pltpu.VMEM(lead + (nz - 1, rows, width), kind),
        ]

    output, tokens_grad, joint_grad, merge_grad, small_grad, grads = pl.pallas_call(
        functools.partial(back_kernel, nz),
        name="attention_backward",
        out_shape=(
            shape((length, model)),
            shape((length, model), floats),
            shape((depth, joint_width), floats),
            shape((depth, QUERY_WIDTH), floats),
            shape((8, 128), floats),
            shape((3, depth, 2 * nz * share)),
        ),
        in_specs=[anywhere] * 5 + [vmem] * 11,
        out_specs=(vmem,) * 5 + (anywhere,),
        scratch_shapes=[
            pltpu.VMEM((2,) + blocks + (depth, half), halves),
            pltpu.VMEM(blocks + (depth, pair_width), halves),
            pltpu.VMEM((3, nz, 2, depth, share), halves),
            pltpu.VMEM((nz, 3, 2, depth, share), halves),
            pltpu.VMEM((nz, length, model), halves),
            pltpu.VMEM((nz, length, model), halves),
            pltpu.VMEM((nz - 1, length, model), halves),
        ]
        + sums(depth, half, lead=(2,))
        + sums(depth, half, lead=(2,))
        + sums(depth, pair_width)
        + sums(8, 128, floats)
        + [
            pltpu.VMEM((keys, pair_width), floats),
            pltpu.VMEM((nz, 2, length, pair_width), halves),
            pltpu.VMEM((nz, length, pair_width), halves),
            pltpu.VMEM((nz - 1, length, pair_width), halves),
            pltpu.VMEM((length, joint_width), halves),
            pltpu.VMEM((length, QUERY_WIDTH), halves),
            pltpu.VMEM((length, QUERY_WIDTH), floats),
            pltpu.VMEM((length, model), floats),
        ]
        + semaphores(115, 6),
        compiler_params=params(2),
    )(
        grads,
        branch,
        kv_all,
        q_all,
        m_all,
        back,
        mixed,
        outer,
        tokens[0],
        xn1,
        gains,
        turns,
        queries,
        pair,
        shares,
        summed,
    )
    grads = grads[:, :, :hidden_width].astype(floats)
    return (
        output[None],
        tokens_grad[None],
        joint_grad,
        small_grad[0, : joint_bias.shape[0]],
        merge_grad.T,
        small_grad[1, :depth],
        small_grad[2, :depth],
        grads[0],
        grads[1],
        grads[2].T,
    )


def body_plain(
    tokens,
    segments,
    joint_matrix,
    joint_bias,
    merge_matrix,
    norm_first,
    norm_second,
    gate_matrix,
    up_matrix,
    down_matrix,
    cotangent,
):
    residual = tokens[0].astype(floats)
    length, model = residual.shape
    depth = joint_matrix.shape[0]
    joint_width = joint_matrix.shape[1]
    hidden_width = gate_matrix.shape[1]
    z_count = lax.axis_size("z")
    team = lax.axis_size(TEAM)
    share = hidden_width // team
    own_labels = segments[0]
    labels = lax.all_gather(own_labels, SEQ, axis=0, tiled=True)
    offset = lax.axis_index(SEQ) * length
    places = offset + jnp.arange(length, dtype=jnp.int32)
    positions = lax.dynamic_slice_in_dim(row_positions(labels), offset, length, 0)
    cosine, sine = rotary(positions, HEAD_DIM)

    small = jnp.concatenate([joint_bias, norm_first, norm_second])
    small = jnp.pad(small, (0, -small.shape[0] % depth)).reshape(depth, -1)
    small_width = small.shape[1]
    packed = jnp.concatenate([joint_matrix, merge_matrix.T, small], axis=1)
    packed = lax.all_gather(packed, AXES, axis=0, tiled=True)
    joint_all = packed[:, :joint_width]
    merge_turned = packed[:, joint_width : joint_width + model]
    small = packed[:, joint_width + model :].reshape(-1, depth * small_width).astype(floats)
    bias_depth = joint_bias.shape[0]
    bias_all = small[:, :bias_depth].reshape(-1)
    gain_first = small[:, bias_depth : bias_depth + depth].reshape(-1)
    gain_second = small[:, bias_depth + depth : bias_depth + 2 * depth].reshape(-1)

    stacked = jnp.stack([gate_matrix, up_matrix, down_matrix.T], axis=1)
    stacked = stacked.reshape(depth, 3, team, share).transpose(2, 0, 1, 3)
    stacked = stacked.reshape(team, depth, 3 * share)
    stacked = lax.all_to_all(stacked, TEAM, split_axis=0, concat_axis=0, tiled=True)
    stacked = stacked.reshape(z_count, 1, team // z_count, 1, depth, 3 * share)
    stacked = lax.all_gather(stacked, "x", axis=1, tiled=True)
    stacked = lax.all_gather(stacked, "c", axis=3, tiled=True)
    stacked = stacked.reshape(model, 3 * share)
    both_all, down_turned = stacked[:, : 2 * share], stacked[:, 2 * share :]
    outer_grad = cotangent[0]
    team_outer = lax.all_gather(outer_grad, TEAM, axis=0, tiled=True)

    scale_first = norm_parts(residual)
    normal_first = (residual * scale_first * gain_first).astype(halves)
    joint = jnp.dot(normal_first, joint_all, preferred_element_type=floats) + bias_all
    query = joint[:, :QUERY_WIDTH].reshape(length, HEADS, HEAD_DIM)
    keys = joint[:, QUERY_WIDTH : QUERY_WIDTH + KEY_WIDTH].reshape(length, KV_HEADS, HEAD_DIM)
    values = joint[:, QUERY_WIDTH + KEY_WIDTH :].astype(halves)
    query = (query * cosine + turn_half(query) * sine).astype(halves)
    keys = (keys * cosine + turn_half(keys) * sine).astype(halves).reshape(length, KEY_WIDTH)
    query_group = to_groups(query)
    pair = lax.all_gather(jnp.concatenate([keys, values], axis=1), SEQ, axis=0, tiled=True)
    count = pair.shape[0]
    key_all = pair[:, :KEY_WIDTH].reshape(count, KV_HEADS, HEAD_DIM)
    value_all = pair[:, KEY_WIDTH:].reshape(count, KV_HEADS, HEAD_DIM)
    allowed = (places[:, None] >= jnp.arange(count, dtype=jnp.int32)[None, :]) & (
        own_labels[:, None] == labels[None, :]
    )
    allowed = jnp.tile(allowed, (GROUP, 1))[None]
    scores = jnp.einsum("krd,nkd->krn", query_group, key_all, preferred_element_type=floats)
    scores = jnp.where(allowed, scores * SCALE, neg)
    top = jnp.max(scores, axis=-1, keepdims=True)
    weights = jnp.where(allowed, jnp.exp(scores - top), 0.0)
    total = jnp.sum(weights, axis=-1, keepdims=True)
    shares = weights / total
    shares_half = shares.astype(halves)
    attended = jnp.einsum("krn,nkd->krd", shares_half, value_all, preferred_element_type=floats)
    attended_half = from_groups(attended, length).astype(halves)
    mixed = residual + lax.dot_general(
        attended_half, merge_turned, last_pair, preferred_element_type=floats
    )
    scale_second = norm_parts(mixed)
    normal_half = (mixed * scale_second * gain_second).astype(halves)

    team_normal = lax.all_gather(normal_half, TEAM, axis=0, tiled=True)
    both = jnp.dot(team_normal, both_all, preferred_element_type=floats)
    gate, upper = both[:, :share], both[:, share:]
    sig = jax.nn.sigmoid(gate)
    silu = gate * sig
    hidden_half = (silu * upper).astype(halves)
    branch = lax.dot_general(hidden_half, down_turned, last_pair, preferred_element_type=floats)
    hidden_grad = jnp.dot(team_outer, down_turned, preferred_element_type=floats)
    gate_half = (hidden_grad * upper * sig * (1.0 + gate * (1.0 - sig))).astype(halves)
    upper_half = (hidden_grad * silu).astype(halves)
    both_half = jnp.concatenate([gate_half, upper_half], axis=1)
    normal_grad = lax.dot_general(both_half, both_all, last_pair, preferred_element_type=floats)
    branch = lax.psum_scatter(branch.astype(halves), TEAM, scatter_dimension=0, tiled=True)
    normal_grad = lax.psum_scatter(normal_grad.astype(halves), TEAM, scatter_dimension=0, tiled=True)
    output = (mixed + branch.astype(floats)).astype(halves)[None]
    both_grad = lax.dot_general(team_normal, both_half, first_pair, preferred_element_type=floats)
    down_grad = lax.dot_general(team_outer, hidden_half, first_pair, preferred_element_type=floats)
    grads = jnp.concatenate([both_grad, down_grad], axis=1).astype(halves)
    grads = grads.reshape(z_count, 2, team // z_count, 2, depth, 3 * share)
    grads = lax.psum_scatter(grads, "c", scatter_dimension=3, tiled=True)
    grads = lax.psum_scatter(grads, "x", scatter_dimension=1, tiled=True)
    grads = grads.reshape(team, depth, 3 * share)
    grads = lax.all_to_all(grads, TEAM, split_axis=0, concat_axis=0, tiled=True)
    grads = grads.reshape(team, depth, 3, share).transpose(2, 1, 0, 3)
    grads = grads.reshape(3, depth, hidden_width).astype(floats)

    normal_grad = normal_grad.astype(floats)
    mixed_part, second_local = norm_back(normal_grad, mixed, scale_second, gain_second)
    mixed_grad = outer_grad.astype(floats) + mixed_part
    mixed_half = mixed_grad.astype(halves)
    merge_local = lax.dot_general(
        mixed_half, attended_half, first_pair, preferred_element_type=floats
    )
    attended_grad = jnp.dot(mixed_half, merge_turned, preferred_element_type=floats).astype(halves)
    grad_group = to_groups(attended_grad.reshape(length, HEADS, HEAD_DIM))
    mass_grad = jnp.einsum("krd,nkd->krn", grad_group, value_all, preferred_element_type=floats)
    row_dots = jnp.sum(shares * mass_grad, axis=-1, keepdims=True)
    score_half = (shares * (mass_grad - row_dots)).astype(halves)
    query_sum = (
        jnp.einsum("krn,nkd->krd", score_half, key_all, preferred_element_type=floats) * SCALE
    )
    key_grad = (
        jnp.einsum("krn,krd->nkd", score_half, query_group, preferred_element_type=floats) * SCALE
    )
    value_grad = jnp.einsum("krn,krd->nkd", shares_half, grad_group, preferred_element_type=floats)
    pair_sums = jnp.concatenate(
        [key_grad.reshape(count, KEY_WIDTH), value_grad.reshape(count, KEY_WIDTH)], axis=1
    )
    pair_mine = lax.psum_scatter(
        pair_sums.astype(halves), SEQ, scatter_dimension=0, tiled=True
    ).astype(floats)
    key_back = pair_mine[:, :KEY_WIDTH].reshape(length, KV_HEADS, HEAD_DIM)
    value_back = pair_mine[:, KEY_WIDTH:]
    query_back = from_groups(query_sum, length).reshape(length, HEADS, HEAD_DIM)
    query_back = query_back * cosine + unturn_half(query_back * sine)
    key_back = key_back * cosine + unturn_half(key_back * sine)
    joint_back = jnp.concatenate(
        [query_back.reshape(length, QUERY_WIDTH), key_back.reshape(length, KEY_WIDTH), value_back],
        axis=1,
    ).astype(halves)
    joint_local = lax.dot_general(
        normal_first, joint_back, first_pair, preferred_element_type=floats
    )
    bias_local = jnp.sum(joint_back.astype(floats), axis=0)
    normal_back = lax.dot_general(joint_back, joint_all, last_pair, preferred_element_type=floats)
    residual_part, first_local = norm_back(normal_back, residual, scale_first, gain_first)
    tokens_grad = (mixed_grad + residual_part)[None]

    small_back = jnp.concatenate(
        [
            bias_local.reshape(-1, bias_depth),
            first_local.reshape(-1, depth),
            second_local.reshape(-1, depth),
        ],
        axis=1,
    )
    small_back = jnp.pad(small_back, ((0, 0), (0, depth * small_width - small_back.shape[1])))
    small_back = small_back.reshape(-1, small_width)
    packed_grad = jnp.concatenate([joint_local, merge_local, small_back], axis=1).astype(halves)
    packed_grad = lax.psum_scatter(packed_grad, AXES, scatter_dimension=0, tiled=True).astype(floats)
    joint_grad = packed_grad[:, :joint_width]
    merge_grad = packed_grad[:, joint_width : joint_width + model].T
    small_back = packed_grad[:, joint_width + model :].reshape(-1)
    bias_grad = small_back[:bias_depth]
    first_grad = small_back[bias_depth : bias_depth + depth]
    second_grad = small_back[bias_depth + depth : bias_depth + 2 * depth]
    return (
        output,
        tokens_grad,
        joint_grad,
        bias_grad,
        merge_grad,
        first_grad,
        second_grad,
        grads[0],
        grads[1],
        grads[2].T,
    )


def solution(mesh):
    seq, row = mesh.shape["seq"], mesh.shape["row"]
    fine = Mesh(mesh.devices.reshape(seq // 2, 2, row // 2, 2), AXES)
    whole = ("z", "x", "y", "c")
    placed = (
        P(ROW, SEQ, None),
        P(ROW, SEQ),
        P(whole, None),
        P(whole),
        P(None, whole),
        P(whole),
        P(whole),
        P(whole, None),
        P(whole, None),
        P(None, whole),
        P(ROW, SEQ, None),
    )
    depth = MODEL // mesh.size
    return jax.shard_map(
        body_kernels if depth % 16 == 0 else body_plain,
        mesh=fine,
        in_specs=placed,
        out_specs=(
            P(ROW, SEQ, None),
            P(ROW, SEQ, None),
            P(whole, None),
            P(whole),
            P(None, whole),
            P(whole),
            P(whole),
            P(whole, None),
            P(whole, None),
            P(None, whole),
        ),
        check_vma=False,
    )
```

```python
import functools
import math

import jax
import jax.numpy as jnp
from jax import lax
from jax.experimental import pallas as pl
from jax.experimental.pallas import tpu as pltpu
from jax.sharding import Mesh, PartitionSpec as P

HEADS = 12
KV_HEADS = 2
HEAD_DIM = 128
MODEL = HEADS * HEAD_DIM
GROUP = HEADS // KV_HEADS
QUERY_WIDTH = HEADS * HEAD_DIM
KEY_WIDTH = KV_HEADS * HEAD_DIM
SCALE = 1.0 / math.sqrt(HEAD_DIM)

eps = 1e-06
theta = 1000000.0
neg = -1e30
last_pair = (((1,), (1,)), ((), ()))
first_pair = (((0,), (0,)), ((), ()))
floats = jnp.float32
halves = jnp.bfloat16

AXES = ("z", "x", "y", "c")
SEQ = ("z", "x")
ROW = ("y", "c")
TEAM = ("z", "y")


def turn_half(values):
    middle = values.shape[-1] // 2
    return jnp.concatenate([-values[..., middle:], values[..., :middle]], axis=-1)


def unturn_half(values):
    middle = values.shape[-1] // 2
    return jnp.concatenate([values[..., middle:], -values[..., :middle]], axis=-1)


def row_positions(labels):
    length = labels.shape[0]
    places = jnp.arange(length, dtype=jnp.int32)
    change = jnp.concatenate([jnp.ones((1,), dtype=jnp.bool_), labels[1:] != labels[:-1]])
    starts = lax.cummax(jnp.where(change, places, 0), axis=0)
    return places - starts


def rotary(positions, width):
    inverse = jnp.power(
        jnp.float32(theta), -(jnp.arange(width // 2, dtype=jnp.float32) * (2.0 / width))
    )
    angle = positions.astype(jnp.float32)[:, None] * inverse[None, :]
    angle = jnp.concatenate([angle, angle], axis=1)[:, None, :]
    return (jnp.cos(angle), jnp.sin(angle))


def to_groups(values):
    length = values.shape[0]
    return (
        values.reshape(length, KV_HEADS, GROUP, HEAD_DIM)
        .transpose(1, 2, 0, 3)
        .reshape(KV_HEADS, GROUP * length, HEAD_DIM)
    )


def from_groups(values, length):
    return (
        values.reshape(KV_HEADS, GROUP, length, HEAD_DIM)
        .transpose(2, 0, 1, 3)
        .reshape(length, QUERY_WIDTH)
    )


def norm_parts(values):
    return lax.rsqrt(jnp.mean(values * values, axis=-1, keepdims=True) + eps)


def norm_back(upstream, values, scale, gain):
    scaled = upstream * gain
    inner = jnp.mean(scaled * values, axis=-1, keepdims=True)
    part = scale * scaled - values * (scale * scale * scale) * inner
    gain_grad = jnp.sum(upstream * values * scale, axis=0, keepdims=True)
    return part, gain_grad


MESH = pl.DeviceIdType.MESH
VMEM_LIMIT = 60 * 2**20


def coordinates():
    return tuple(lax.axis_index(name) for name in AXES)


class Sent:
    def __init__(self, raw, when):
        self.raw, self.when = raw, when

    def under(self, act):
        if self.when is None:
            act()
        else:
            pl.when(self.when)(act)

    def start(self):
        self.under(self.raw.start)

    def wait_recv(self):
        self.under(self.raw.wait_recv)

    def wait_send(self):
        self.under(self.raw.wait_send)


class Courier:
    def __init__(self, sends, receives):
        self.sends, self.receives, self.copies = sends, receives, []

    def make(self, source, target, device, when=None):
        place = len(self.copies)
        raw = pltpu.make_async_remote_copy(
            src_ref=source,
            dst_ref=target,
            send_sem=self.sends.at[place],
            recv_sem=self.receives.at[place],
            device_id=device,
            device_id_type=MESH,
        )
        made = Sent(raw, when)
        self.copies.append(made)
        return made

    def copy(self, source, target, device, when=None):
        made = self.make(source, target, device, when)
        made.start()
        return made

    def finish(self):
        for made in self.copies:
            made.wait_send()


def meet(devices):
    barrier = pltpu.get_barrier_semaphore()
    for device in devices:
        pl.semaphore_signal(barrier, inc=1, device_id=device, device_id_type=MESH)
    pl.semaphore_wait(barrier, len(devices))


def cuts_of(width, step):
    return [(start, min(step, width - start)) for start in range(0, width, step)]


class Line:
    def __init__(self, courier, place, spot):
        self.courier, self.place, self.spot = courier, place, spot
        self.sent = {}

    def items(self):
        p = self.place
        found = [(0, 0, p.z, None)]
        for step in range(1, p.nz):
            found.append((step, 1, lax.max(p.z - step, 0), p.z >= step))
            found.append((step, -1, lax.min(p.z + step, p.nz - 1), p.z + step < p.nz))
        return found

    def send(self, step, way, group, also=None):
        p = self.place
        inside = p.z < p.nz - 1 if way == 1 else p.z > 0
        if also is not None:
            inside = inside & also
        spot = self.spot(group)
        self.sent[step, way] = self.courier.copy(spot, spot, p.line_at(way), inside)

    def start(self):
        self.send(0, 1, self.place.z)
        self.send(0, -1, self.place.z)

    def arrive(self, step, way, group, exists):
        made = self.sent[step - 1, way]

        @pl.when(exists)
        def _():
            made.raw.wait_recv()

        if step < self.place.nz - 1:
            self.send(step, way, group, exists)


class Gather:
    def __init__(self, courier, place, source, buffer):
        self.courier, self.place = courier, place
        self.source, self.buffer = source, buffer
        self.line = Line(courier, place, lambda group: buffer.at[group, :, place.y, place.c])
        self.side, self.core = {}, {}

    def start(self):
        p = self.place
        self.cross = self.courier.copy(
            self.source, self.buffer.at[p.z, p.x, p.y, p.c], p.across["x"]
        )

    def along(self):
        self.cross.wait_recv()
        self.line.start()
        self.sideways(self.line.items()[0])

    def sideways(self, item):
        step, way, group, exists = item
        p = self.place
        spot = self.buffer.at[group, :, p.y, p.c]
        self.side[step, way] = self.courier.copy(spot, spot, p.across["y"], exists)

    def pass_on(self, step):
        for item in self.line.items():
            if item[0] == step:
                self.line.arrive(*item)
                self.sideways(item)

    def to_core(self):
        p = self.place
        for item in self.line.items():
            step, way, group, exists = item
            self.side[step, way].wait_recv()
            spot = self.buffer.at[group, :, :, p.c]
            self.core[step, way] = self.courier.copy(spot, spot, p.across["c"], exists)

    def done(self):
        for made in self.core.values():
            made.wait_recv()


class Place:
    def __init__(self, nz):
        self.nz = nz
        self.z, self.x, self.y, self.c = z, x, y, c = coordinates()
        self.across = {"x": (z, 1 - x, y, c), "y": (z, x, 1 - y, c), "c": (z, x, y, 1 - c)}

    def line(self, dz, dy=0):
        y = lax.rem(self.y + dy, 2) if dy else self.y
        return (lax.rem(self.z + dz, self.nz), self.x, y, self.c)

    def line_at(self, way):
        return (lax.rem(self.z + self.nz + way, self.nz), self.x, self.y, self.c)

    def peers(self):
        team = [self.line(dz, dy) for dz in range(self.nz) for dy in range(2)]
        return team[1:] + [self.across["x"], self.across["c"]]


def spread(values, piece, width):
    devices, lanes = values.shape
    at = lax.broadcasted_iota(jnp.int32, (lanes, width), 1)
    inner = lax.broadcasted_iota(jnp.int32, (lanes, width), 0)
    chosen = (lax.rem(at, piece) == inner).astype(floats).astype(halves)
    repeated = jnp.dot(values.astype(halves), chosen, preferred_element_type=floats)
    owner = lax.div(lax.broadcasted_iota(jnp.int32, (devices, width), 1), piece)
    mine = owner == lax.broadcasted_iota(jnp.int32, (devices, width), 0)
    return jnp.sum(jnp.where(mine, repeated, 0.0), axis=0, keepdims=True)


def attention_kernel(
    nz,
    stack_ref,
    joint_ref,
    merge_ref,
    small_ref,
    inverse_ref,
    tokens_ref,
    outer_ref,
    w_ref,
    ct_ref,
    kv_out,
    query_out,
    merge_out,
    xn1_ref,
    xn2_ref,
    mixed_ref,
    gain_ref,
    turn_ref,
    query_ref,
    pair_ref,
    share_ref,
    out_ref,
    joint_kv,
    joint_q,
    merge,
    small,
    bias_mask,
    tokens_all,
    mixed_send,
    mixed_in,
    sends,
    receives,
    locals_,
):
    place = Place(nz)
    z, x, y, c = place.z, place.x, place.y, place.c
    length, model = tokens_ref.shape
    depth = joint_ref.shape[1]
    share = w_ref.shape[-1]
    half = GROUP * HEAD_DIM
    both = 2 * length
    total_keys = nz * both
    courier = Courier(sends, receives)
    devices = 8 * nz
    joint_width = 2 * joint_ref.shape[2]
    meet(place.peers())

    own_copies = []

    def keep(source, target):
        made = pltpu.make_async_copy(source, target, locals_.at[len(own_copies)])
        made.start()
        own_copies.append(made)
        return made

    def columns(tz, ty):
        return pl.ds(pl.multiple_of((tz * 2 + ty) * share, 128), share)

    gathers, own_waits = {}, {}

    def begin(name, own, other, buffer):
        own_waits[name] = keep(own, buffer.at[z, x, y, c])
        gathers[name] = Gather(courier, place, other, buffer)
        gathers[name].start()

    begin("small", small_ref, small_ref, small)
    begin("kv", joint_ref.at[x, :, half:], joint_ref.at[1 - x, :, half:], joint_kv)
    token_cross = courier.copy(tokens_ref, tokens_all.at[x], place.across["x"])
    begin("q", joint_ref.at[x, :, :half], joint_ref.at[1 - x, :, :half], joint_q)
    begin("m", merge_ref.at[x], merge_ref.at[1 - x], merge)
    tokens_all[x] = tokens_ref[...]
    w_own = keep(stack_ref.at[:, :, columns(z, y)], w_ref.at[:, z, x, y, c])
    ct_own = keep(outer_ref, ct_ref.at[z, y])

    direct, w_cross, w_hand = {}, {}, {}

    def give(dz, dy):
        device = place.line(dz, dy)
        direct[dz, dy] = courier.copy(
            stack_ref.at[:, :, columns(device[0], device[2])], w_ref.at[:, z, x, y, c], device
        )

    def w_spot(dz, dy, side):
        return w_ref.at[:, lax.rem(z + nz - dz, nz), side, lax.rem(y + dy, 2), c]

    def take(dz, dy):
        if dz or dy:
            direct[dz, dy].wait_recv()
        spot = w_spot(dz, dy, x)
        w_cross[dz, dy] = courier.copy(spot, spot, place.across["x"])
        w_hand[dz, dy, 0] = courier.copy(spot, spot, place.across["c"])

    def hand(dz, dy):
        w_cross[dz, dy].wait_recv()
        spot = w_spot(dz, dy, 1 - x)
        w_hand[dz, dy, 1] = courier.copy(spot, spot, place.across["c"])

    give(0, 1)
    give(2, 0)
    for name in ("small", "kv"):
        own_waits[name].wait()
        gathers[name].along()
    token_cross.wait_recv()
    tokens_both = tokens_all[...].reshape(both, model).astype(floats)
    hat = tokens_both * norm_parts(tokens_both)
    for name in ("small", "kv"):
        gathers[name].pass_on(1)
    own_waits["q"].wait()
    gathers["q"].along()
    for step in range(2, nz):
        for name in ("small", "kv"):
            gathers[name].pass_on(step)
    for name in ("small", "kv"):
        gathers[name].to_core()
    w_own.wait()
    take(0, 0)
    for step in range(1, nz):
        gathers["q"].pass_on(step)
    for name in ("small", "kv"):
        gathers[name].done()
    take(0, 1)
    give(2, 1)
    own_waits["m"].wait()

    pieces = small[...].reshape(devices * 8, 128).astype(halves)

    def row_of(which):
        at = lax.broadcasted_iota(jnp.int32, (devices, devices * 8), 1)
        wanted = lax.broadcasted_iota(jnp.int32, (devices, devices * 8), 0) * 8 + which
        chosen = (at == wanted).astype(floats).astype(halves)
        return jnp.dot(chosen, pieces, preferred_element_type=floats)

    gain_first = spread(row_of(1), depth, model)
    gain_second = spread(row_of(2), depth, model)
    bias = spread(row_of(0), joint_width // devices, joint_width)
    gain_ref[0:1, :] = gain_first
    gain_ref[1:2, :] = gain_second

    def mine(first, width):
        return jnp.where(x == 0, bias[:, first : first + width], bias[:, first + width : first + 2 * width])

    bias_query = mine(0, half)
    bias_key = mine(QUERY_WIDTH, HEAD_DIM)
    bias_value = mine(QUERY_WIDTH + KEY_WIDTH, HEAD_DIM)
    label = jnp.concatenate([small[z, side, y, c].T[:, 3:4] for side in range(2)], axis=0)
    start = jnp.zeros((both, 1), floats)
    rows_at = z * both + lax.broadcasted_iota(jnp.int32, (both, length), 0)
    lanes_at = lax.broadcasted_iota(jnp.int32, (both, length), 1)
    for block in range(2 * nz):
        keys_label = small[block // 2, block % 2, y, c, 3:4, :]
        start = start + jnp.sum((keys_label < label).astype(floats), axis=1, keepdims=True)
        allowed = (keys_label == label) & (rows_at >= block * length + lanes_at)
        bias_mask[:, block * length : (block + 1) * length] = jnp.where(allowed, 0.0, neg)
    place_at = (z * both + lax.broadcasted_iota(jnp.int32, (both, 1), 0)).astype(floats)
    angle = (place_at - start) * inverse_ref[...]
    cosine = jnp.cos(angle)
    lane = lax.broadcasted_iota(jnp.int32, (both, HEAD_DIM), 1)
    sine = jnp.where(lane < HEAD_DIM // 2, -1.0, 1.0) * jnp.sin(angle)
    turn_ref[0] = cosine
    turn_ref[1] = sine

    def turned(values):
        return values * cosine + pltpu.roll(values, HEAD_DIM // 2, 1) * sine

    xn1_ref[...] = (hat * gain_first).astype(halves)
    pair = jnp.dot(
        xn1_ref[...], joint_kv[...].reshape(model, 2 * HEAD_DIM), preferred_element_type=floats
    )
    pair_ref[z, :, :HEAD_DIM] = turned(pair[:, :HEAD_DIM] + bias_key).astype(halves)
    pair_ref[z, :, HEAD_DIM:] = (pair[:, HEAD_DIM:] + bias_value).astype(halves)
    pairs = Line(courier, place, lambda group: pair_ref.at[group])
    pairs.start()
    gathers["q"].to_core()
    gathers["m"].along()
    for item in pairs.items()[1:3]:
        pairs.arrive(*item)
    take(2, 0)
    give(1, 0)
    for item in pairs.items()[3:]:
        pairs.arrive(*item)
    gathers["m"].pass_on(1)
    gathers["q"].done()

    query = jnp.dot(xn1_ref[...], joint_q[...].reshape(model, half), preferred_element_type=floats)
    query = query + bias_query
    for head in range(GROUP):
        query_ref[head] = turned(query[:, head * HEAD_DIM : (head + 1) * HEAD_DIM]).astype(halves)
    for step in range(2, nz):
        gathers["m"].pass_on(step)
    take(2, 1)
    give(1, 1)
    give(3, 0)
    outers = Line(courier, place, lambda group: ct_ref.at[group, y])
    ct_side = {}

    def ct_on(item):
        step, way, group, exists = item
        if step:
            outers.arrive(*item)
        spot = ct_ref.at[group, y]
        ct_side[step, way] = courier.copy(spot, spot, place.across["y"], exists)

    ct_own.wait()
    ct_on(outers.items()[0])
    gathers["m"].to_core()
    hand(0, 0)
    hand(0, 1)

    def attend(first, last):
        @pl.loop(first, last)
        def _(head):
            keys = pair_ref[:, :, :HEAD_DIM].reshape(total_keys, HEAD_DIM)
            values = pair_ref[:, :, HEAD_DIM:].reshape(total_keys, HEAD_DIM)
            scores = lax.dot_general(
                query_ref[head], keys, last_pair, preferred_element_type=floats
            )
            scores = scores * SCALE + bias_mask[...]
            top = jnp.max(scores, axis=-1, keepdims=True)
            raised = jnp.exp(scores - top)
            shares = (raised / jnp.sum(raised, axis=-1, keepdims=True)).astype(halves)
            share_ref[head] = shares
            lanes = pl.ds(pl.multiple_of(head * HEAD_DIM, 128), HEAD_DIM)
            out_ref[:, lanes] = jnp.dot(shares, values, preferred_element_type=floats)

    attend(0, GROUP // 2)
    take(1, 0)
    give(3, 1)
    attend(GROUP // 2, GROUP)
    outers.start()
    gathers["m"].done()
    saves = [keep(joint_kv, kv_out), keep(joint_q, query_out), keep(merge, merge_out)]
    merged = lax.dot_general(
        out_ref[...].astype(halves),
        merge[...].reshape(model, half),
        last_pair,
        preferred_element_type=floats,
    )
    mixed_ref[...] = jnp.where(x == 0, merged[:length], merged[length:])
    mixed_send[...] = jnp.where(x == 0, merged[length:], merged[:length]).astype(halves)
    mixed_cross = courier.copy(mixed_send, mixed_in, place.across["x"])
    take(1, 1)
    hand(2, 0)
    for item in outers.items()[1:3]:
        ct_on(item)
    mixed_cross.wait_recv()
    mixed = tokens_ref[...].astype(floats) + (mixed_ref[...] + mixed_in[...].astype(floats))
    mixed_ref[...] = mixed
    xn2_ref[...] = (mixed * norm_parts(mixed) * gain_second).astype(halves)
    take(3, 0)
    hand(2, 1)
    for item in outers.items()[3:5]:
        ct_on(item)
    hand(1, 0)
    take(3, 1)
    for item in outers.items()[5:]:
        ct_on(item)
    for spot in ((1, 1), (3, 0), (3, 1)):
        hand(*spot)
    for made in w_hand.values():
        made.wait_recv()
    for made in ct_side.values():
        made.wait_recv()
    for made in saves:
        made.wait()
    courier.finish()


def feed_kernel(
    nz,
    w_ref,
    ct_ref,
    normal_ref,
    back_ref,
    branch_ref,
    grads_ref,
    w,
    xn,
    ct,
    hid,
    gb,
    ub,
    part,
    ybuf,
    zsend,
    zbuf,
    cbuf,
    sends,
    receives,
    locals_,
):
    place = Place(nz)
    z, x, y, c = place.z, place.x, place.y, place.c
    length, model = normal_ref.shape
    share = w.shape[-1]
    block = model // nz
    lines = 2 * length * nz
    courier = Courier(sends, receives)

    def source(dz):
        return lax.rem(z + nz - dz, nz)

    meet([place.line(dz) for dz in range(1, nz)] + [place.across["y"], place.across["c"]])
    along = {
        dz: courier.copy(normal_ref, xn.at[z, y], place.line(dz)) for dz in range(1, nz)
    }
    side = {0: courier.copy(normal_ref, xn.at[z, y], place.across["y"])}
    loads = [
        pltpu.make_async_copy(w_ref.at[which], w.at[which], locals_.at[which])
        for which in range(3)
    ] + [pltpu.make_async_copy(ct_ref, ct, locals_.at[3])]
    for made in loads:
        made.start()
    xn[z, y] = normal_ref[...]
    for made in loads:
        made.wait()

    def weight(which, start, size):
        return w[which, :, :, :, :, :, start : start + size].reshape(model, size)

    def pass_on(dz):
        along[dz].wait_recv()
        spot = xn.at[source(dz), y]
        side[dz] = courier.copy(spot, spot, place.across["y"])

    half = nz // 2
    scatter = []
    for dz in range(nz):
        group = source(dz)
        if dz + 1 < nz:
            pass_on(dz + 1)
        side[dz].wait_recv()
        for start, size in cuts_of(share, 256):
            normal = xn[group].reshape(2 * length, model)
            outer = ct[group].reshape(2 * length, model)
            gate = jnp.dot(normal, weight(0, start, size), preferred_element_type=floats)
            upper = jnp.dot(normal, weight(1, start, size), preferred_element_type=floats)
            hidden_back = jnp.dot(outer, weight(2, start, size), preferred_element_type=floats)
            sig = 1.0 / (1.0 + jnp.exp(-gate))
            silu = gate * sig
            spot = (group, slice(None), slice(start, start + size))
            hid[spot] = (silu * upper).astype(halves)
            gb[spot] = (hidden_back * upper * (sig * (1.0 + gate * (1.0 - sig)))).astype(halves)
            ub[spot] = (hidden_back * silu).astype(halves)

        @pl.loop(0, 2)
        def _(step):
            rows = pl.ds(step * half, half)
            lanes = pl.ds(pl.multiple_of(step * (model // 2), 128), model // 2)

            def turned(which):
                return w[which, rows].reshape(model // 2, share)

            both = lax.dot_general(
                gb[group], turned(0), last_pair, preferred_element_type=floats
            ) + lax.dot_general(ub[group], turned(1), last_pair, preferred_element_type=floats)
            part[group, :, :, lanes] = both.astype(halves).reshape(2, length, model // 2)

        scatter.append(
            courier.copy(part.at[group, 1 - y], ybuf.at[group], place.across["y"])
        )

    final = {}
    for dz in [(dz + nz // 2) % nz for dz in range(nz)]:
        group = source(dz)
        scatter[dz].wait_recv()
        total = part[group, y].astype(floats) + ybuf[group].astype(floats)
        if dz == 0:
            back_ref[...] = total
        else:
            zsend[dz - 1] = total.astype(halves)
            final[dz] = courier.copy(zsend.at[dz - 1], zbuf.at[dz - 1], (group, x, y, c))

    for group in range(nz):

        @pl.loop(0, 2)
        def _(step):
            rows = pl.ds(step * half, half)
            lanes = pl.ds(pl.multiple_of(step * (model // 2), 128), model // 2)
            product = lax.dot_general(
                hid[group],
                w[2, rows].reshape(model // 2, share),
                last_pair,
                preferred_element_type=floats,
            )
            branch_ref[group, :, :, lanes] = product.astype(halves).reshape(2, length, model // 2)

    saves, handed = [], []
    for group in range(nz):
        lanes = slice(group * block, (group + 1) * block)
        normal_turned = xn[:, :, :, lanes].reshape(lines, block).T
        outer_turned = ct[:, :, :, lanes].reshape(lines, block).T
        for which, left, right in (
            (0, normal_turned, gb),
            (1, normal_turned, ub),
            (2, outer_turned, hid),
        ):
            for start, size in cuts_of(share, 512):
                w[which, group, :, :, :, :, start : start + size] = (
                    jnp.dot(
                        left,
                        right[:, :, start : start + size].reshape(lines, size),
                        preferred_element_type=floats,
                    )
                    .astype(halves)
                    .reshape(2, 2, 2, -1, size)
                )
        handed.append(
            courier.copy(w.at[:, group, :, :, 1 - c], cbuf.at[group], place.across["c"])
        )
    for group in range(nz):
        handed[group].wait_recv()
        for which in range(3):
            w[which, group, :, :, c] = (
                w[which, group, :, :, c].astype(floats) + cbuf[group, which].astype(floats)
            ).astype(halves)
        made = pltpu.make_async_copy(
            w.at[:, group, :, :, c], grads_ref.at[:, group], locals_.at[4 + group]
        )
        made.start()
        saves.append(made)
    for dz in range(1, nz):
        final[dz].wait_recv()
        back_ref[...] += zbuf[dz - 1].astype(floats)
    for made in saves:
        made.wait()
    courier.finish()


class LineSum:
    def __init__(self, courier, place, parts, spot, above, below):
        self.courier, self.place, self.parts, self.spot = courier, place, parts, spot
        self.arrivals = {1: above, -1: below}
        self.sent = {}

    def add(self, target, way):
        nz = self.place.nz
        spot = self.spot(target)
        arrived = self.arrivals[way][target - 1 if way == 1 else target]
        self.parts[spot] = (self.parts[spot].astype(floats) + arrived.astype(floats)).astype(
            self.parts.dtype
        )

    def forward(self, target, way):
        p = self.place
        moving = p.z < target if way == 1 else p.z > target
        fed = p.z > 0 if way == 1 else p.z < p.nz - 1
        made = self.courier.make(
            self.parts.at[self.spot(target)],
            self.arrivals[way].at[target - 1 if way == 1 else target],
            p.line_at(way),
            moving,
        )
        self.sent[target, way] = made

        @pl.when(moving & fed)
        def _():
            made.raw.wait_recv()
            self.add(target, way)

        made.start()

    def forward_all(self):
        nz = self.place.nz
        for step in range(nz - 1):
            self.forward(nz - 1 - step, 1)
            self.forward(step, -1)

    def finish(self):
        p = self.place
        for (target, way), made in self.sent.items():
            fed = p.z > 0 if way == 1 else p.z < p.nz - 1

            @pl.when((p.z == target) & fed)
            def _(target=target, way=way, made=made):
                made.raw.wait_recv()
                self.add(target, way)


class Scatter:
    def __init__(self, courier, place, parts, core_in, side_in, above, below, last_in):
        self.courier, self.place, self.parts = courier, place, parts
        self.core_in, self.side_in, self.last_in = core_in, side_in, last_in
        every = slice(None)
        self.line = LineSum(
            courier, place, parts, lambda group: (group, every, place.y, place.c), above, below
        )
        self.groups = []
        for step in range((place.nz + 1) // 2):
            self.groups += [place.nz - 1 - step, step]
        self.core, self.side = {}, {}

    def to_core(self, group):
        p = self.place
        self.core[group] = self.courier.copy(
            self.parts.at[group, :, :, 1 - p.c], self.core_in.at[group], p.across["c"]
        )

    def add(self, spot, arrived):
        self.parts[spot] = (self.parts[spot].astype(floats) + arrived.astype(floats)).astype(
            self.parts.dtype
        )

    def sideways(self):
        p = self.place
        every = slice(None)
        for group in self.groups:
            self.core[group].wait_recv()
            self.add((group, every, every, p.c), self.core_in[group])
            self.side[group] = self.courier.copy(
                self.parts.at[group, :, 1 - p.y, p.c], self.side_in.at[group], p.across["y"]
            )

    def along(self):
        p = self.place
        for group in self.groups:
            self.side[group].wait_recv()
            self.add((group, slice(None), p.y, p.c), self.side_in[group])
        self.line.forward_all()

    def across(self):
        p = self.place
        self.line.finish()
        self.last = self.courier.copy(
            self.parts.at[p.z, 1 - p.x, p.y, p.c], self.last_in, p.across["x"]
        )

    def own(self):
        p = self.place
        return self.parts[p.z, p.x, p.y, p.c].astype(floats)

    def other(self):
        self.last.wait_recv()
        return self.last_in[...].astype(floats)


def gather_pieces(values, piece, devices):
    width = values.shape[1]
    owner = lax.div(lax.broadcasted_iota(jnp.int32, (devices, width), 1), piece)
    mine = owner == lax.broadcasted_iota(jnp.int32, (devices, width), 0)
    at = lax.broadcasted_iota(jnp.int32, (width, 128), 0)
    inner = lax.broadcasted_iota(jnp.int32, (width, 128), 1)
    chosen = (lax.rem(at, piece) == inner).astype(floats)
    rows = jnp.where(mine, values, 0.0)
    return jnp.dot(rows, chosen, preferred_element_type=floats, precision=lax.Precision.HIGHEST)


def back_kernel(
    nz,
    grads_in,
    branch_ref,
    kv_ref,
    q_ref,
    m_ref,
    back_ref,
    mixed_ref,
    outer_ref,
    tokens_ref,
    xn1_ref,
    gain_ref,
    turn_ref,
    query_ref,
    pair_ref,
    share_ref,
    out_ref,
    output_ref,
    tokens_grad_ref,
    joint_grad_ref,
    merge_grad_ref,
    small_grad_ref,
    grads_ref,
    weight_m,
    weight_q,
    weight_kv,
    gown,
    gin,
    branch_own,
    branch_in,
    branch_above,
    branch_below,
    *rest,
):
    merge_bufs, query_bufs, kv_bufs, small_bufs = (rest[6 * i : 6 * i + 6] for i in range(4))
    (
        pair_sum,
        pair_half,
        pair_above,
        pair_below,
        joint_back,
        attended_back,
        mixed_both,
        back_send,
        back_in,
        sends,
        receives,
        locals_,
    ) = rest[24:]
    place = Place(nz)
    z, x, y, c = place.z, place.x, place.y, place.c
    length, model = tokens_ref.shape
    share = gown.shape[-1]
    half = GROUP * HEAD_DIM
    both = 2 * length
    block = model // nz
    depth = grads_in.shape[-2]
    devices = 8 * nz
    total_keys = nz * both
    orders = [(dz + nz // 2) % nz for dz in range(nz)]
    courier = Courier(sends, receives)
    meet(place.peers())

    def group_of(dz):
        return lax.rem(z + dz, nz)

    copies = []

    def load(source, target):
        made = pltpu.make_async_copy(source, target, locals_.at[len(copies)])
        made.start()
        copies.append(made)
        return made

    merge_load = load(m_ref, weight_m)
    branch_load = load(branch_ref.at[:, y], branch_own)
    gown_load = load(grads_in.at[:, :, x], gown)
    query_load = load(q_ref, weight_q)
    kv_load = load(kv_ref, weight_kv)

    b_cross = {
        group: courier.copy(branch_ref.at[group, 1 - y], branch_in.at[group], place.across["y"])
        for group in range(nz)
    }
    g_cross, g_line, kept = {}, [], []

    def grads_across(dz):
        g_cross[dz] = courier.copy(
            grads_in.at[:, group_of(dz), 1 - x], gin.at[dz], place.across["x"]
        )

    mixed = mixed_ref[...]
    second_scale = norm_parts(mixed)
    part, second_local = norm_back(back_ref[...], mixed, second_scale, gain_ref[1:2, :])
    grad = outer_ref[...].astype(floats) + part
    tokens_grad_ref[...] = grad
    mixed_both[x] = grad.astype(halves)
    mixed_cross = courier.copy(mixed_both.at[x], mixed_both.at[x], place.across["x"])
    grads_across(orders[0])
    mixed_cross.wait_recv()
    grads_across(orders[1])

    merge_load.wait()
    upstream_both = mixed_both[...].reshape(both, model)
    attended_back[...] = jnp.dot(
        upstream_both, weight_m[...].reshape(model, half), preferred_element_type=floats
    ).astype(halves)
    merges = Scatter(courier, place, *merge_bufs)
    queries = Scatter(courier, place, *query_bufs)
    keys_values = Scatter(courier, place, *kv_bufs)
    smalls = Scatter(courier, place, *small_bufs)

    def product_rows(scatter, left, right):
        for group in scatter.groups:
            scatter.parts[group] = (
                jnp.dot(
                    left[group * block : (group + 1) * block], right, preferred_element_type=floats
                )
                .astype(halves)
                .reshape(2, 2, 2, depth, right.shape[1])
            )
            scatter.to_core(group)

    product_rows(merges, upstream_both.T, out_ref[...].astype(halves))

    def attend(first, last):
        @pl.loop(first, last)
        def _(head):
            query = query_ref[head]
            keys = pair_ref[:, :, :HEAD_DIM].reshape(total_keys, HEAD_DIM)
            values = pair_ref[:, :, HEAD_DIM:].reshape(total_keys, HEAD_DIM)
            lanes = pl.ds(pl.multiple_of(head * HEAD_DIM, 128), HEAD_DIM)
            upstream = attended_back[:, lanes]
            delta = jnp.sum(upstream.astype(floats) * out_ref[:, lanes], axis=-1, keepdims=True)
            mass = lax.dot_general(upstream, values, last_pair, preferred_element_type=floats)
            shares = share_ref[head]
            scores = (shares.astype(floats) * (mass - delta)).astype(halves)
            query_sum = jnp.dot(scores, keys, preferred_element_type=floats) * SCALE
            cosine, sine = turn_ref[0], turn_ref[1]
            joint_back[:, lanes] = (
                query_sum * cosine + pltpu.roll(query_sum * sine, HEAD_DIM // 2, 1)
            ).astype(halves)
            pair_sum[:, :HEAD_DIM] += (
                jnp.dot(scores.T, query, preferred_element_type=floats) * SCALE
            )
            pair_sum[:, HEAD_DIM:] += jnp.dot(shares.T, upstream, preferred_element_type=floats)

    pair_sum[...] = jnp.zeros_like(pair_sum)
    attend(0, GROUP // 2)

    gown_load.wait()
    mine = pl.ds(pl.multiple_of((z * 2 + y) * share, 128), share)

    def grads_on(dz):
        group = group_of(dz)
        g_cross[dz].wait_recv()
        for which in range(3):
            gown[which, group] = (
                gown[which, group].astype(floats) + gin[dz, which].astype(floats)
            ).astype(halves)
        for dy in range(2):
            ty = lax.rem(y + dy, 2)
            if dz or dy:
                g_line.append(
                    courier.copy(
                        gown.at[:, group, ty], grads_ref.at[:, :, mine], (group, x, ty, c)
                    )
                )
            else:
                kept.append(load(gown.at[:, group, ty], grads_ref.at[:, :, mine]))

    grads_on(orders[0])
    grads_across(orders[2])
    merges.sideways()
    attend(GROUP // 2, GROUP)

    pair_half[...] = pair_sum[...].astype(halves).reshape(nz, both, 2 * HEAD_DIM)
    pairs = LineSum(courier, place, pair_half, lambda group: (group,), pair_above, pair_below)
    pairs.forward(nz - 1, 1)
    pairs.forward(0, -1)
    turned = xn1_ref[...].T
    product_rows(queries, turned, joint_back[:, :half])
    for step in range(1, nz - 1):
        pairs.forward(nz - 1 - step, 1)
        pairs.forward(step, -1)
    branch_load.wait()
    for group in range(nz):
        b_cross[group].wait_recv()
        branch_own[group] = (
            branch_own[group].astype(floats) + branch_in[group].astype(floats)
        ).astype(halves)
    pairs.finish()
    total = pair_half[z].astype(floats)
    key_total = total[:, :HEAD_DIM]
    joint_back[:, half : half + HEAD_DIM] = (
        key_total * turn_ref[0] + pltpu.roll(key_total * turn_ref[1], HEAD_DIM // 2, 1)
    ).astype(halves)
    joint_back[:, half + HEAD_DIM :] = total[:, HEAD_DIM:].astype(halves)
    product_rows(keys_values, turned, joint_back[:, half:])
    query_load.wait()
    kv_load.wait()
    normal_back = lax.dot_general(
        joint_back[:, :half],
        weight_q[...].reshape(model, half),
        last_pair,
        preferred_element_type=floats,
    ) + lax.dot_general(
        joint_back[:, half:],
        weight_kv[...].reshape(model, 2 * HEAD_DIM),
        last_pair,
        preferred_element_type=floats,
    )
    back_send[...] = jnp.where(x == 0, normal_back[length:], normal_back[:length]).astype(halves)
    back_cross = courier.copy(back_send, back_in, place.across["x"])
    normal_own = jnp.where(x == 0, normal_back[:length], normal_back[length:])
    queries.sideways()
    keys_values.sideways()
    grads_on(orders[1])
    grads_across(orders[3])
    merges.along()

    back_cross.wait_recv()
    normal_own = normal_own + back_in[...].astype(floats)
    residual = tokens_ref[...].astype(floats)
    part, first_local = norm_back(normal_own, residual, norm_parts(residual), gain_ref[0:1, :])
    tokens_grad_ref[...] += part

    local = jnp.sum(joint_back[...].astype(floats), axis=0, keepdims=True)
    pieces_of = []
    for first, width in ((0, half), (half, HEAD_DIM), (half + HEAD_DIM, HEAD_DIM)):
        for side in range(2):
            pieces_of.append(jnp.where(x == side, local[:, first : first + width], 0.0))
    bias_local = jnp.concatenate(pieces_of, axis=1)
    pieces = jnp.zeros((devices * 8, 128), floats)
    for which, values in ((0, bias_local), (1, first_local), (2, second_local)):
        mine_rows = gather_pieces(values, values.shape[1] // devices, devices)
        at = lax.broadcasted_iota(jnp.int32, (devices * 8, devices), 0)
        wanted = lax.broadcasted_iota(jnp.int32, (devices * 8, devices), 1) * 8 + which
        pieces = pieces + jnp.dot(
            (at == wanted).astype(floats),
            mine_rows,
            preferred_element_type=floats,
            precision=lax.Precision.HIGHEST,
        )
    smalls.parts[...] = pieces.reshape(nz, 2, 2, 2, 8, 128)
    for group in smalls.groups:
        smalls.to_core(group)
    keys_values.along()
    queries.along()
    smalls.sideways()
    grads_on(orders[2])
    branches = LineSum(
        courier, place, branch_own, lambda group: (group,), branch_above, branch_below
    )
    branches.forward_all()
    smalls.along()
    merges.across()
    grads_on(orders[3])
    keys_values.across()
    queries.across()
    smalls.across()
    branches.finish()
    output_ref[...] = (mixed_ref[...] + branch_own[z].astype(floats)).astype(halves)
    merge_grad_ref[x] = merges.own()
    merge_grad_ref[1 - x] = merges.other()
    joint_grad_ref[x, :, :half] = queries.own()
    joint_grad_ref[1 - x, :, :half] = queries.other()
    joint_grad_ref[x, :, half:] = keys_values.own()
    joint_grad_ref[1 - x, :, half:] = keys_values.other()
    small_grad_ref[...] = smalls.own() + smalls.other()
    for made in g_line:
        made.wait_recv()
    for made in kept:
        made.wait()
    courier.finish()


def padded_share(hidden_width, team):
    return -(-hidden_width // (team * 128)) * 128


def body_kernels(
    tokens,
    segments,
    joint_matrix,
    joint_bias,
    merge_matrix,
    norm_first,
    norm_second,
    gate_matrix,
    up_matrix,
    down_matrix,
    cotangent,
):
    length, model = tokens.shape[1:]
    depth, joint_width = joint_matrix.shape
    hidden_width = gate_matrix.shape[1]
    nz = lax.axis_size("z")
    share = padded_share(hidden_width, 2 * nz)
    half = GROUP * HEAD_DIM
    pair_width = 2 * HEAD_DIM
    both = 2 * length
    keys = nz * both
    vmem = pl.BlockSpec(memory_space=pltpu.VMEM)
    anywhere = pl.BlockSpec(memory_space=pl.ANY)
    blocks = (nz, 2, 2, 2)

    def shape(dims, kind=halves):
        return jax.ShapeDtypeStruct(dims, kind)

    def semaphores(count, loads):
        return [
            pltpu.SemaphoreType.DMA((count,)),
            pltpu.SemaphoreType.DMA((count,)),
            pltpu.SemaphoreType.DMA((loads,)),
        ]

    def params(number):
        return pltpu.CompilerParams(
            collective_id=number, has_side_effects=True, vmem_limit_bytes=VMEM_LIMIT
        )

    stack = jnp.stack([gate_matrix, up_matrix, down_matrix.T])
    stack = jnp.pad(stack, ((0, 0), (0, 0), (0, 2 * nz * share - hidden_width)))

    def lane_row(values):
        return jnp.pad(values.astype(floats), (0, 128 - values.shape[0]))

    own_labels = segments[0]
    empty = jnp.zeros((128,), floats)
    small = jnp.stack(
        [lane_row(v) for v in (joint_bias, norm_first, norm_second, own_labels)] + [empty] * 4
    )
    inverse = jnp.power(floats(theta), -(jnp.arange(HEAD_DIM // 2, dtype=floats) * (2.0 / HEAD_DIM)))
    inverse = jnp.concatenate([inverse, inverse])[None]
    joint_halves = jnp.stack(
        [
            jnp.concatenate(
                [
                    joint_matrix[:, side * half : (side + 1) * half],
                    joint_matrix[:, QUERY_WIDTH + side * HEAD_DIM :][:, :HEAD_DIM],
                    joint_matrix[:, QUERY_WIDTH + KEY_WIDTH + side * HEAD_DIM :][:, :HEAD_DIM],
                ],
                axis=1,
            )
            for side in range(2)
        ]
    )
    merge_halves = merge_matrix.T.reshape(depth, 2, half).transpose(1, 0, 2)
    outer = cotangent[0]
    (
        w,
        team_outer,
        kv_all,
        q_all,
        m_all,
        xn1,
        xn2,
        mixed,
        gains,
        turns,
        queries,
        pair,
        shares,
        summed,
    ) = pl.pallas_call(
        functools.partial(attention_kernel, nz),
        name="attention_forward",
        out_shape=(
            shape((3,) + blocks + (depth, share)),
            shape((nz, 2, length, model)),
            shape(blocks + (depth, pair_width)),
            shape(blocks + (depth, half)),
            shape(blocks + (depth, half)),
            shape((both, model)),
            shape((length, model)),
            shape((length, model), floats),
            shape((8, model), floats),
            shape((2, both, HEAD_DIM), floats),
            shape((GROUP, both, HEAD_DIM)),
            shape((nz, both, pair_width)),
            shape((GROUP, both, keys)),
            shape((both, half), floats),
        ),
        in_specs=[anywhere] * 3 + [vmem] * 4,
        out_specs=(anywhere,) * 5 + (vmem,) * 9,
        scratch_shapes=[
            pltpu.VMEM(blocks + (depth, pair_width), halves),
            pltpu.VMEM(blocks + (depth, half), halves),
            pltpu.VMEM(blocks + (depth, half), halves),
            pltpu.VMEM(blocks + (8, 128), floats),
            pltpu.VMEM((both, keys), floats),
            pltpu.VMEM((2, length, model), halves),
            pltpu.VMEM((length, model), halves),
            pltpu.VMEM((length, model), halves),
        ]
        + semaphores(136, 9),
        compiler_params=params(0),
    )(stack, joint_halves, merge_halves, small, inverse, tokens[0], outer)

    lines = 2 * length
    back, branch, grads = pl.pallas_call(
        functools.partial(feed_kernel, nz),
        name="feed_forward",
        out_shape=(
            shape((length, model), floats),
            shape((nz, 2, length, model)),
            shape((3, nz, 2, 2, depth, share)),
        ),
        in_specs=[anywhere, anywhere, vmem],
        out_specs=(vmem, vmem, anywhere),
        scratch_shapes=[
            pltpu.VMEM((3,) + blocks + (depth, share), halves),
            pltpu.VMEM((nz, 2, length, model), halves),
            pltpu.VMEM((nz, 2, length, model), halves),
            pltpu.VMEM((nz, lines, share), halves),
            pltpu.VMEM((nz, lines, share), halves),
            pltpu.VMEM((nz, lines, share), halves),
            pltpu.VMEM((nz, 2, length, model), halves),
            pltpu.VMEM((nz, length, model), halves),
            pltpu.VMEM((nz - 1, length, model), halves),
            pltpu.VMEM((nz - 1, length, model), halves),
            pltpu.VMEM((nz, 3, 2, 2, depth, share), halves),
        ]
        + semaphores(18, 8),
        compiler_params=params(1),
    )(w, team_outer, xn2)

    def sums(rows, width, kind=halves):
        return [
            pltpu.VMEM(blocks + (rows, width), kind),
            pltpu.VMEM((nz, 2, 2, rows, width), kind),
            pltpu.VMEM((nz, 2, rows, width), kind),
            pltpu.VMEM((nz - 1, 2, rows, width), kind),
            pltpu.VMEM((nz - 1, 2, rows, width), kind),
            pltpu.VMEM((rows, width), kind),
        ]

    output, tokens_grad, joint_grad, merge_grad, small_grad, grads = pl.pallas_call(
        functools.partial(back_kernel, nz),
        name="attention_backward",
        out_shape=(
            shape((length, model)),
            shape((length, model), floats),
            shape((2, depth, half + pair_width), floats),
            shape((2, depth, half), floats),
            shape((8, 128), floats),
            shape((3, depth, 2 * nz * share)),
        ),
        in_specs=[anywhere] * 5 + [vmem] * 11,
        out_specs=(vmem,) * 5 + (anywhere,),
        scratch_shapes=[
            pltpu.VMEM(blocks + (depth, half), halves),
            pltpu.VMEM(blocks + (depth, half), halves),
            pltpu.VMEM(blocks + (depth, pair_width), halves),
            pltpu.VMEM((3, nz, 2, depth, share), halves),
            pltpu.VMEM((nz, 3, 2, depth, share), halves),
            pltpu.VMEM((nz, length, model), halves),
            pltpu.VMEM((nz, length, model), halves),
            pltpu.VMEM((nz - 1, length, model), halves),
            pltpu.VMEM((nz - 1, length, model), halves),
        ]
        + sums(depth, half)
        + sums(depth, half)
        + sums(depth, pair_width)
        + sums(8, 128, floats)
        + [
            pltpu.VMEM((keys, pair_width), floats),
            pltpu.VMEM((nz, both, pair_width), halves),
            pltpu.VMEM((nz - 1, both, pair_width), halves),
            pltpu.VMEM((nz - 1, both, pair_width), halves),
            pltpu.VMEM((both, half + pair_width), halves),
            pltpu.VMEM((both, half), halves),
            pltpu.VMEM((2, length, model), halves),
            pltpu.VMEM((length, model), halves),
            pltpu.VMEM((length, model), halves),
        ]
        + semaphores(89, 6),
        compiler_params=params(2),
    )(
        grads,
        branch,
        kv_all,
        q_all,
        m_all,
        back,
        mixed,
        outer,
        tokens[0],
        xn1,
        gains,
        turns,
        queries,
        pair,
        shares,
        summed,
    )
    joint_grad = jnp.concatenate(
        [
            joint_grad[side, :, first : first + width]
            for first, width in ((0, half), (half, HEAD_DIM), (half + HEAD_DIM, HEAD_DIM))
            for side in range(2)
        ],
        axis=1,
    )
    merge_grad = merge_grad.transpose(1, 0, 2).reshape(depth, QUERY_WIDTH)
    grads = grads[:, :, :hidden_width].astype(floats)
    return (
        output[None],
        tokens_grad[None],
        joint_grad,
        small_grad[0, : joint_bias.shape[0]],
        merge_grad.T,
        small_grad[1, :depth],
        small_grad[2, :depth],
        grads[0],
        grads[1],
        grads[2].T,
    )


def body_plain(
    tokens,
    segments,
    joint_matrix,
    joint_bias,
    merge_matrix,
    norm_first,
    norm_second,
    gate_matrix,
    up_matrix,
    down_matrix,
    cotangent,
):
    residual = tokens[0].astype(floats)
    length, model = residual.shape
    depth = joint_matrix.shape[0]
    joint_width = joint_matrix.shape[1]
    hidden_width = gate_matrix.shape[1]
    z_count = lax.axis_size("z")
    team = lax.axis_size(TEAM)
    share = hidden_width // team
    own_labels = segments[0]
    labels = lax.all_gather(own_labels, SEQ, axis=0, tiled=True)
    offset = lax.axis_index(SEQ) * length
    places = offset + jnp.arange(length, dtype=jnp.int32)
    positions = lax.dynamic_slice_in_dim(row_positions(labels), offset, length, 0)
    cosine, sine = rotary(positions, HEAD_DIM)

    small = jnp.concatenate([joint_bias, norm_first, norm_second])
    small = jnp.pad(small, (0, -small.shape[0] % depth)).reshape(depth, -1)
    small_width = small.shape[1]
    packed = jnp.concatenate([joint_matrix, merge_matrix.T, small], axis=1)
    packed = lax.all_gather(packed, AXES, axis=0, tiled=True)
    joint_all = packed[:, :joint_width]
    merge_turned = packed[:, joint_width : joint_width + model]
    small = packed[:, joint_width + model :].reshape(-1, depth * small_width).astype(floats)
    bias_depth = joint_bias.shape[0]
    bias_all = small[:, :bias_depth].reshape(-1)
    gain_first = small[:, bias_depth : bias_depth + depth].reshape(-1)
    gain_second = small[:, bias_depth + depth : bias_depth + 2 * depth].reshape(-1)

    stacked = jnp.stack([gate_matrix, up_matrix, down_matrix.T], axis=1)
    stacked = stacked.reshape(depth, 3, team, share).transpose(2, 0, 1, 3)
    stacked = stacked.reshape(team, depth, 3 * share)
    stacked = lax.all_to_all(stacked, TEAM, split_axis=0, concat_axis=0, tiled=True)
    stacked = stacked.reshape(z_count, 1, team // z_count, 1, depth, 3 * share)
    stacked = lax.all_gather(stacked, "x", axis=1, tiled=True)
    stacked = lax.all_gather(stacked, "c", axis=3, tiled=True)
    stacked = stacked.reshape(model, 3 * share)
    both_all, down_turned = stacked[:, : 2 * share], stacked[:, 2 * share :]
    outer_grad = cotangent[0]
    team_outer = lax.all_gather(outer_grad, TEAM, axis=0, tiled=True)

    scale_first = norm_parts(residual)
    normal_first = (residual * scale_first * gain_first).astype(halves)
    joint = jnp.dot(normal_first, joint_all, preferred_element_type=floats) + bias_all
    query = joint[:, :QUERY_WIDTH].reshape(length, HEADS, HEAD_DIM)
    keys = joint[:, QUERY_WIDTH : QUERY_WIDTH + KEY_WIDTH].reshape(length, KV_HEADS, HEAD_DIM)
    values = joint[:, QUERY_WIDTH + KEY_WIDTH :].astype(halves)
    query = (query * cosine + turn_half(query) * sine).astype(halves)
    keys = (keys * cosine + turn_half(keys) * sine).astype(halves).reshape(length, KEY_WIDTH)
    query_group = to_groups(query)
    pair = lax.all_gather(jnp.concatenate([keys, values], axis=1), SEQ, axis=0, tiled=True)
    count = pair.shape[0]
    key_all = pair[:, :KEY_WIDTH].reshape(count, KV_HEADS, HEAD_DIM)
    value_all = pair[:, KEY_WIDTH:].reshape(count, KV_HEADS, HEAD_DIM)
    allowed = (places[:, None] >= jnp.arange(count, dtype=jnp.int32)[None, :]) & (
        own_labels[:, None] == labels[None, :]
    )
    allowed = jnp.tile(allowed, (GROUP, 1))[None]
    scores = jnp.einsum("krd,nkd->krn", query_group, key_all, preferred_element_type=floats)
    scores = jnp.where(allowed, scores * SCALE, neg)
    top = jnp.max(scores, axis=-1, keepdims=True)
    weights = jnp.where(allowed, jnp.exp(scores - top), 0.0)
    total = jnp.sum(weights, axis=-1, keepdims=True)
    shares = weights / total
    shares_half = shares.astype(halves)
    attended = jnp.einsum("krn,nkd->krd", shares_half, value_all, preferred_element_type=floats)
    attended_half = from_groups(attended, length).astype(halves)
    mixed = residual + lax.dot_general(
        attended_half, merge_turned, last_pair, preferred_element_type=floats
    )
    scale_second = norm_parts(mixed)
    normal_half = (mixed * scale_second * gain_second).astype(halves)

    team_normal = lax.all_gather(normal_half, TEAM, axis=0, tiled=True)
    both = jnp.dot(team_normal, both_all, preferred_element_type=floats)
    gate, upper = both[:, :share], both[:, share:]
    sig = jax.nn.sigmoid(gate)
    silu = gate * sig
    hidden_half = (silu * upper).astype(halves)
    branch = lax.dot_general(hidden_half, down_turned, last_pair, preferred_element_type=floats)
    hidden_grad = jnp.dot(team_outer, down_turned, preferred_element_type=floats)
    gate_half = (hidden_grad * upper * sig * (1.0 + gate * (1.0 - sig))).astype(halves)
    upper_half = (hidden_grad * silu).astype(halves)
    both_half = jnp.concatenate([gate_half, upper_half], axis=1)
    normal_grad = lax.dot_general(both_half, both_all, last_pair, preferred_element_type=floats)
    branch = lax.psum_scatter(branch.astype(halves), TEAM, scatter_dimension=0, tiled=True)
    normal_grad = lax.psum_scatter(normal_grad.astype(halves), TEAM, scatter_dimension=0, tiled=True)
    output = (mixed + branch.astype(floats)).astype(halves)[None]
    both_grad = lax.dot_general(team_normal, both_half, first_pair, preferred_element_type=floats)
    down_grad = lax.dot_general(team_outer, hidden_half, first_pair, preferred_element_type=floats)
    grads = jnp.concatenate([both_grad, down_grad], axis=1).astype(halves)
    grads = grads.reshape(z_count, 2, team // z_count, 2, depth, 3 * share)
    grads = lax.psum_scatter(grads, "c", scatter_dimension=3, tiled=True)
    grads = lax.psum_scatter(grads, "x", scatter_dimension=1, tiled=True)
    grads = grads.reshape(team, depth, 3 * share)
    grads = lax.all_to_all(grads, TEAM, split_axis=0, concat_axis=0, tiled=True)
    grads = grads.reshape(team, depth, 3, share).transpose(2, 1, 0, 3)
    grads = grads.reshape(3, depth, hidden_width).astype(floats)

    normal_grad = normal_grad.astype(floats)
    mixed_part, second_local = norm_back(normal_grad, mixed, scale_second, gain_second)
    mixed_grad = outer_grad.astype(floats) + mixed_part
    mixed_half = mixed_grad.astype(halves)
    merge_local = lax.dot_general(
        mixed_half, attended_half, first_pair, preferred_element_type=floats
    )
    attended_grad = jnp.dot(mixed_half, merge_turned, preferred_element_type=floats).astype(halves)
    grad_group = to_groups(attended_grad.reshape(length, HEADS, HEAD_DIM))
    mass_grad = jnp.einsum("krd,nkd->krn", grad_group, value_all, preferred_element_type=floats)
    row_dots = jnp.sum(shares * mass_grad, axis=-1, keepdims=True)
    score_half = (shares * (mass_grad - row_dots)).astype(halves)
    query_sum = (
        jnp.einsum("krn,nkd->krd", score_half, key_all, preferred_element_type=floats) * SCALE
    )
    key_grad = (
        jnp.einsum("krn,krd->nkd", score_half, query_group, preferred_element_type=floats) * SCALE
    )
    value_grad = jnp.einsum("krn,krd->nkd", shares_half, grad_group, preferred_element_type=floats)
    pair_sums = jnp.concatenate(
        [key_grad.reshape(count, KEY_WIDTH), value_grad.reshape(count, KEY_WIDTH)], axis=1
    )
    pair_mine = lax.psum_scatter(
        pair_sums.astype(halves), SEQ, scatter_dimension=0, tiled=True
    ).astype(floats)
    key_back = pair_mine[:, :KEY_WIDTH].reshape(length, KV_HEADS, HEAD_DIM)
    value_back = pair_mine[:, KEY_WIDTH:]
    query_back = from_groups(query_sum, length).reshape(length, HEADS, HEAD_DIM)
    query_back = query_back * cosine + unturn_half(query_back * sine)
    key_back = key_back * cosine + unturn_half(key_back * sine)
    joint_back = jnp.concatenate(
        [query_back.reshape(length, QUERY_WIDTH), key_back.reshape(length, KEY_WIDTH), value_back],
        axis=1,
    ).astype(halves)
    joint_local = lax.dot_general(
        normal_first, joint_back, first_pair, preferred_element_type=floats
    )
    bias_local = jnp.sum(joint_back.astype(floats), axis=0)
    normal_back = lax.dot_general(joint_back, joint_all, last_pair, preferred_element_type=floats)
    residual_part, first_local = norm_back(normal_back, residual, scale_first, gain_first)
    tokens_grad = (mixed_grad + residual_part)[None]

    small_back = jnp.concatenate(
        [
            bias_local.reshape(-1, bias_depth),
            first_local.reshape(-1, depth),
            second_local.reshape(-1, depth),
        ],
        axis=1,
    )
    small_back = jnp.pad(small_back, ((0, 0), (0, depth * small_width - small_back.shape[1])))
    small_back = small_back.reshape(-1, small_width)
    packed_grad = jnp.concatenate([joint_local, merge_local, small_back], axis=1).astype(halves)
    packed_grad = lax.psum_scatter(packed_grad, AXES, scatter_dimension=0, tiled=True).astype(floats)
    joint_grad = packed_grad[:, :joint_width]
    merge_grad = packed_grad[:, joint_width : joint_width + model].T
    small_back = packed_grad[:, joint_width + model :].reshape(-1)
    bias_grad = small_back[:bias_depth]
    first_grad = small_back[bias_depth : bias_depth + depth]
    second_grad = small_back[bias_depth + depth : bias_depth + 2 * depth]
    return (
        output,
        tokens_grad,
        joint_grad,
        bias_grad,
        merge_grad,
        first_grad,
        second_grad,
        grads[0],
        grads[1],
        grads[2].T,
    )


def solution(mesh):
    seq, row = mesh.shape["seq"], mesh.shape["row"]
    fine = Mesh(mesh.devices.reshape(seq // 2, 2, row // 2, 2), AXES)
    whole = ("z", "x", "y", "c")
    placed = (
        P(ROW, SEQ, None),
        P(ROW, SEQ),
        P(whole, None),
        P(whole),
        P(None, whole),
        P(whole),
        P(whole),
        P(whole, None),
        P(whole, None),
        P(None, whole),
        P(ROW, SEQ, None),
    )
    depth = MODEL // mesh.size
    return jax.shard_map(
        body_kernels if depth % 16 == 0 else body_plain,
        mesh=fine,
        in_specs=placed,
        out_specs=(
            P(ROW, SEQ, None),
            P(ROW, SEQ, None),
            P(whole, None),
            P(whole),
            P(None, whole),
            P(whole),
            P(whole),
            P(whole, None),
            P(whole, None),
            P(None, whole),
        ),
        check_vma=False,
    )
```

```python
import functools
import math

import jax
import jax.numpy as jnp
import numpy as np
from jax import lax
from jax.experimental import pallas as pl
from jax.experimental.pallas import tpu as pltpu
from jax.sharding import Mesh, PartitionSpec as P

HEADS = 12
KV_HEADS = 2
HEAD_DIM = 128
MODEL = HEADS * HEAD_DIM
GROUP = HEADS // KV_HEADS
QUERY_WIDTH = HEADS * HEAD_DIM
KEY_WIDTH = KV_HEADS * HEAD_DIM
KV_PIECES = [(QUERY_WIDTH, HEAD_DIM), (QUERY_WIDTH + KEY_WIDTH, HEAD_DIM)]
SCALE = 1.0 / math.sqrt(HEAD_DIM)

eps = 1e-06
theta = 1000000.0
neg = -1e30
last_pair = (((1,), (1,)), ((), ()))
first_pair = (((0,), (0,)), ((), ()))
floats = jnp.float32
halves = jnp.bfloat16

AXES = ("z", "x", "y", "c")
SEQ = ("z", "x")
ROW = ("y", "c")
TEAM = ("z", "y")


def turn_half(values):
    middle = values.shape[-1] // 2
    return jnp.concatenate([-values[..., middle:], values[..., :middle]], axis=-1)


def unturn_half(values):
    middle = values.shape[-1] // 2
    return jnp.concatenate([values[..., middle:], -values[..., :middle]], axis=-1)


def row_positions(labels):
    length = labels.shape[0]
    places = jnp.arange(length, dtype=jnp.int32)
    change = jnp.concatenate([jnp.ones((1,), dtype=jnp.bool_), labels[1:] != labels[:-1]])
    starts = lax.cummax(jnp.where(change, places, 0), axis=0)
    return places - starts


def rotary(positions, width):
    inverse = jnp.power(
        jnp.float32(theta), -(jnp.arange(width // 2, dtype=jnp.float32) * (2.0 / width))
    )
    angle = positions.astype(jnp.float32)[:, None] * inverse[None, :]
    angle = jnp.concatenate([angle, angle], axis=1)[:, None, :]
    return (jnp.cos(angle), jnp.sin(angle))


def to_groups(values):
    length = values.shape[0]
    return (
        values.reshape(length, KV_HEADS, GROUP, HEAD_DIM)
        .transpose(1, 2, 0, 3)
        .reshape(KV_HEADS, GROUP * length, HEAD_DIM)
    )


def from_groups(values, length):
    return (
        values.reshape(KV_HEADS, GROUP, length, HEAD_DIM)
        .transpose(2, 0, 1, 3)
        .reshape(length, QUERY_WIDTH)
    )


def norm_parts(values):
    return lax.rsqrt(jnp.mean(values * values, axis=-1, keepdims=True) + eps)


def norm_back(upstream, values, scale, gain):
    scaled = upstream * gain
    inner = jnp.mean(scaled * values, axis=-1, keepdims=True)
    part = scale * scaled - values * (scale * scale * scale) * inner
    gain_grad = jnp.sum(upstream * values * scale, axis=0, keepdims=True)
    return part, gain_grad


MESH = pl.DeviceIdType.MESH
VMEM_LIMIT = 60 * 2**20


def coordinates():
    return tuple(lax.axis_index(name) for name in AXES)


class Sent:
    def __init__(self, raw, when):
        self.raw, self.when = raw, when

    def under(self, act):
        if self.when is None:
            act()
        else:
            pl.when(self.when)(act)

    def start(self):
        self.under(self.raw.start)

    def wait_recv(self):
        self.under(self.raw.wait_recv)

    def wait_send(self):
        self.under(self.raw.wait_send)


class Courier:
    def __init__(self, sends, receives):
        self.sends, self.receives, self.copies = sends, receives, []

    def make(self, source, target, device, when=None):
        place = len(self.copies)
        raw = pltpu.make_async_remote_copy(
            src_ref=source,
            dst_ref=target,
            send_sem=self.sends.at[place],
            recv_sem=self.receives.at[place],
            device_id=device,
            device_id_type=MESH,
        )
        made = Sent(raw, when)
        self.copies.append(made)
        return made

    def copy(self, source, target, device, when=None):
        made = self.make(source, target, device, when)
        made.start()
        return made

    def finish(self):
        for made in self.copies:
            made.wait_send()


def meet(devices):
    barrier = pltpu.get_barrier_semaphore()
    for device in devices:
        pl.semaphore_signal(barrier, inc=1, device_id=device, device_id_type=MESH)
    pl.semaphore_wait(barrier, len(devices))


def far_first(nz):
    return sorted(range(nz), key=lambda dz: (dz == 0, abs(2 * dz - nz)))


def cuts_of(width, step):
    return [(start, min(step, width - start)) for start in range(0, width, step)]


class Line:
    def __init__(self, courier, place, spot):
        self.courier, self.place, self.spot = courier, place, spot
        self.sent = {}

    def items(self):
        p = self.place
        found = [(0, 0, p.z, None)]
        for step in range(1, p.nz):
            found.append((step, 1, lax.max(p.z - step, 0), p.z >= step))
            found.append((step, -1, lax.min(p.z + step, p.nz - 1), p.z + step < p.nz))
        return found

    def send(self, step, way, group, also=None):
        p = self.place
        inside = p.z < p.nz - 1 if way == 1 else p.z > 0
        if also is not None:
            inside = inside & also
        spot = self.spot(group)
        self.sent[step, way] = self.courier.copy(spot, spot, p.line_at(way), inside)

    def start(self):
        self.send(0, 1, self.place.z)
        self.send(0, -1, self.place.z)

    def arrive(self, step, way, group, exists):
        made = self.sent[step - 1, way]

        @pl.when(exists)
        def _():
            made.raw.wait_recv()

        if step < self.place.nz - 1:
            self.send(step, way, group, exists)


class Gather:
    def __init__(self, courier, place, source, buffer):
        self.courier, self.place = courier, place
        self.source, self.buffer = source, buffer
        self.line = Line(courier, place, lambda group: buffer.at[group, :, place.y, place.c])
        self.side, self.core = {}, {}

    def start(self):
        p = self.place
        spot = self.buffer.at[p.z, p.x, p.y, p.c]
        self.cross = [
            self.courier.copy(source, spot.at[:, lanes], p.across["x"])
            for source, lanes in self.source
        ]

    def along(self):
        for made in self.cross:
            made.wait_recv()
        self.line.start()
        self.sideways(self.line.items()[0])

    def sideways(self, item):
        step, way, group, exists = item
        p = self.place
        spot = self.buffer.at[group, :, p.y, p.c]
        self.side[step, way] = self.courier.copy(spot, spot, p.across["y"], exists)

    def pass_on(self, step):
        for item in self.line.items():
            if item[0] == step:
                self.line.arrive(*item)
                self.sideways(item)

    def to_core(self):
        p = self.place
        for item in self.line.items():
            step, way, group, exists = item
            self.side[step, way].wait_recv()
            spot = self.buffer.at[group, :, :, p.c]
            self.core[step, way] = self.courier.copy(spot, spot, p.across["c"], exists)

    def done(self):
        for made in self.core.values():
            made.wait_recv()


class Place:
    def __init__(self, nz):
        self.nz = nz
        self.z, self.x, self.y, self.c = z, x, y, c = coordinates()
        self.across = {"x": (z, 1 - x, y, c), "y": (z, x, 1 - y, c), "c": (z, x, y, 1 - c)}

    def line(self, dz, dy=0):
        y = lax.rem(self.y + dy, 2) if dy else self.y
        return (lax.rem(self.z + dz, self.nz), self.x, y, self.c)

    def line_at(self, way):
        return (lax.rem(self.z + self.nz + way, self.nz), self.x, self.y, self.c)

    def peers(self):
        team = [self.line(dz, dy) for dz in range(self.nz) for dy in range(2)]
        return team[1:] + [self.across["x"], self.across["c"]]


def spread(values, piece, width):
    devices, lanes = values.shape
    at = lax.broadcasted_iota(jnp.int32, (lanes, width), 1)
    inner = lax.broadcasted_iota(jnp.int32, (lanes, width), 0)
    chosen = (lax.rem(at, piece) == inner).astype(floats).astype(halves)
    repeated = jnp.dot(values.astype(halves), chosen, preferred_element_type=floats)
    owner = lax.div(lax.broadcasted_iota(jnp.int32, (devices, width), 1), piece)
    mine = owner == lax.broadcasted_iota(jnp.int32, (devices, width), 0)
    return jnp.sum(jnp.where(mine, repeated, 0.0), axis=0, keepdims=True)


def attention_kernel(
    nz,
    stack_ref,
    joint_ref,
    merge_ref,
    small_ref,
    inverse_ref,
    tokens_ref,
    outer_ref,
    w_ref,
    ct_ref,
    kv_out,
    query_out,
    merge_out,
    xn1_ref,
    xn2_ref,
    mixed_ref,
    gain_ref,
    turn_ref,
    query_ref,
    pair_ref,
    share_ref,
    out_ref,
    joint_kv,
    joint_q,
    merge,
    small,
    bias_mask,
    tokens_all,
    mixed_send,
    mixed_in,
    sends,
    receives,
    locals_,
):
    place = Place(nz)
    z, x, y, c = place.z, place.x, place.y, place.c
    length, model = tokens_ref.shape
    depth, joint_width = joint_ref.shape
    share = w_ref.shape[-1]
    half = GROUP * HEAD_DIM
    both = 2 * length
    total_keys = nz * both
    courier = Courier(sends, receives)
    devices = 8 * nz
    meet(place.peers())

    own_copies = []

    def keep(source, target):
        made = pltpu.make_async_copy(source, target, locals_.at[len(own_copies)])
        made.start()
        own_copies.append(made)
        return made

    def columns(tz, ty):
        return pl.ds(pl.multiple_of((tz * 2 + ty) * share, 128), share)

    gathers, own_waits = {}, {}

    def begin(name, ref, pieces, buffer):
        def from_side(side):
            found = []
            at = 0
            for first, width in pieces:
                lanes = pl.ds(pl.multiple_of(first + side * width, 128), width)
                found.append((ref.at[:, lanes], slice(at, at + width)))
                at += width
            return found

        spot = buffer.at[z, x, y, c]
        own_waits[name] = [keep(own, spot.at[:, lanes]) for own, lanes in from_side(x)]
        gathers[name] = Gather(courier, place, from_side(1 - x), buffer)
        gathers[name].start()

    own_waits["small"] = [keep(small_ref, small.at[z, x, y, c])]
    gathers["small"] = Gather(courier, place, [(small_ref, slice(None))], small)
    gathers["small"].start()
    begin("kv", joint_ref, KV_PIECES, joint_kv)
    token_cross = courier.copy(tokens_ref, tokens_all.at[x], place.across["x"])
    begin("q", joint_ref, [(0, half)], joint_q)
    begin("m", merge_ref, [(0, half)], merge)
    tokens_all[x] = tokens_ref[...]
    w_own = keep(stack_ref.at[:, :, columns(z, y)], w_ref.at[:, z, x, y, c])
    ct_own = keep(outer_ref, ct_ref.at[z, y])

    direct, w_cross, w_hand = {}, {}, {}

    def give(dz, dy):
        device = place.line(dz, dy)
        direct[dz, dy] = courier.copy(
            stack_ref.at[:, :, columns(device[0], device[2])], w_ref.at[:, z, x, y, c], device
        )

    def w_spot(dz, dy, side):
        return w_ref.at[:, lax.rem(z + nz - dz, nz), side, lax.rem(y + dy, 2), c]

    def take(dz, dy):
        if dz or dy:
            direct[dz, dy].wait_recv()
        spot = w_spot(dz, dy, x)
        w_cross[dz, dy] = courier.copy(spot, spot, place.across["x"])
        w_hand[dz, dy, 0] = courier.copy(spot, spot, place.across["c"])

    def hand(dz, dy):
        w_cross[dz, dy].wait_recv()
        spot = w_spot(dz, dy, 1 - x)
        w_hand[dz, dy, 1] = courier.copy(spot, spot, place.across["c"])

    give(0, 1)
    give(2, 0)
    for name in ("small", "kv"):
        for made in own_waits[name]:
            made.wait()
        gathers[name].along()
    token_cross.wait_recv()
    tokens_both = tokens_all[...].reshape(both, model).astype(floats)
    hat = tokens_both * norm_parts(tokens_both)
    for name in ("small", "kv"):
        gathers[name].pass_on(1)
    for made in own_waits["q"] + own_waits["m"]:
        made.wait()
    gathers["q"].along()
    for step in range(2, nz):
        for name in ("small", "kv"):
            gathers[name].pass_on(step)
    for name in ("small", "kv"):
        gathers[name].to_core()
    w_own.wait()
    take(0, 0)
    for step in range(1, nz):
        gathers["q"].pass_on(step)
    for name in ("small", "kv"):
        gathers[name].done()
    take(0, 1)
    give(2, 1)

    pieces = small[...].reshape(devices * 8, 128).astype(halves)

    def row_of(which):
        at = lax.broadcasted_iota(jnp.int32, (devices, devices * 8), 1)
        wanted = lax.broadcasted_iota(jnp.int32, (devices, devices * 8), 0) * 8 + which
        chosen = (at == wanted).astype(floats).astype(halves)
        return jnp.dot(chosen, pieces, preferred_element_type=floats)

    gain_first = spread(row_of(1), depth, model)
    gain_second = spread(row_of(2), depth, model)
    bias = spread(row_of(0), joint_width // devices, joint_width)
    gain_ref[0:1, :] = gain_first
    gain_ref[1:2, :] = gain_second

    def mine(first, width):
        return jnp.where(x == 0, bias[:, first : first + width], bias[:, first + width : first + 2 * width])

    bias_query = mine(0, half)
    bias_key = mine(QUERY_WIDTH, HEAD_DIM)
    bias_value = mine(QUERY_WIDTH + KEY_WIDTH, HEAD_DIM)
    label = jnp.concatenate([small[z, side, y, c].T[:, 3:4] for side in range(2)], axis=0)
    start = jnp.zeros((both, 1), floats)
    rows_at = z * both + lax.broadcasted_iota(jnp.int32, (both, length), 0)
    lanes_at = lax.broadcasted_iota(jnp.int32, (both, length), 1)
    for block in range(2 * nz):
        keys_label = small[block // 2, block % 2, y, c, 3:4, :]
        start = start + jnp.sum((keys_label < label).astype(floats), axis=1, keepdims=True)
        allowed = (keys_label == label) & (rows_at >= block * length + lanes_at)
        bias_mask[:, block * length : (block + 1) * length] = jnp.where(allowed, 0.0, neg)
    place_at = (z * both + lax.broadcasted_iota(jnp.int32, (both, 1), 0)).astype(floats)
    angle = (place_at - start) * inverse_ref[...]
    cosine = jnp.cos(angle)
    lane = lax.broadcasted_iota(jnp.int32, (both, HEAD_DIM), 1)
    sine = jnp.where(lane < HEAD_DIM // 2, -1.0, 1.0) * jnp.sin(angle)
    turn_ref[0] = cosine
    turn_ref[1] = sine

    def turned(values):
        return values * cosine + pltpu.roll(values, HEAD_DIM // 2, 1) * sine

    xn1_ref[...] = (hat * gain_first).astype(halves)
    pair = jnp.dot(
        xn1_ref[...], joint_kv[...].reshape(model, 2 * HEAD_DIM), preferred_element_type=floats
    )
    pair_ref[z, :, :HEAD_DIM] = turned(pair[:, :HEAD_DIM] + bias_key).astype(halves)
    pair_ref[z, :, HEAD_DIM:] = (pair[:, HEAD_DIM:] + bias_value).astype(halves)
    pairs = Line(courier, place, lambda group: pair_ref.at[group])
    pairs.start()
    gathers["q"].to_core()
    gathers["m"].along()
    for item in pairs.items()[1:3]:
        pairs.arrive(*item)
    take(2, 0)
    give(1, 0)
    for item in pairs.items()[3:]:
        pairs.arrive(*item)
    gathers["m"].pass_on(1)
    gathers["q"].done()

    query = jnp.dot(xn1_ref[...], joint_q[...].reshape(model, half), preferred_element_type=floats)
    query = query + bias_query
    for head in range(GROUP):
        query_ref[head] = turned(query[:, head * HEAD_DIM : (head + 1) * HEAD_DIM]).astype(halves)
    for step in range(2, nz):
        gathers["m"].pass_on(step)
    take(2, 1)
    give(1, 1)
    give(3, 0)
    outers = Line(courier, place, lambda group: ct_ref.at[group, y])
    ct_side = {}

    def ct_on(item):
        step, way, group, exists = item
        if step:
            outers.arrive(*item)
        spot = ct_ref.at[group, y]
        ct_side[step, way] = courier.copy(spot, spot, place.across["y"], exists)

    ct_own.wait()
    ct_on(outers.items()[0])
    gathers["m"].to_core()
    hand(0, 0)
    hand(0, 1)

    def attend(first, last):
        @pl.loop(first, last)
        def _(head):
            keys = pair_ref[:, :, :HEAD_DIM].reshape(total_keys, HEAD_DIM)
            values = pair_ref[:, :, HEAD_DIM:].reshape(total_keys, HEAD_DIM)
            scores = lax.dot_general(
                query_ref[head], keys, last_pair, preferred_element_type=floats
            )
            scores = scores * SCALE + bias_mask[...]
            top = jnp.max(scores, axis=-1, keepdims=True)
            raised = jnp.exp(scores - top)
            shares = (raised / jnp.sum(raised, axis=-1, keepdims=True)).astype(halves)
            share_ref[head] = shares
            lanes = pl.ds(pl.multiple_of(head * HEAD_DIM, 128), HEAD_DIM)
            out_ref[:, lanes] = jnp.dot(shares, values, preferred_element_type=floats)

    attend(0, GROUP // 2)
    take(1, 0)
    give(3, 1)
    attend(GROUP // 2, GROUP)
    outers.start()
    gathers["m"].done()
    saves = [keep(joint_kv, kv_out), keep(joint_q, query_out), keep(merge, merge_out)]
    merged = lax.dot_general(
        out_ref[...].astype(halves),
        merge[...].reshape(model, half),
        last_pair,
        preferred_element_type=floats,
    )
    mixed_ref[...] = jnp.where(x == 0, merged[:length], merged[length:])
    mixed_send[...] = jnp.where(x == 0, merged[length:], merged[:length]).astype(halves)
    mixed_cross = courier.copy(mixed_send, mixed_in, place.across["x"])
    take(1, 1)
    hand(2, 0)
    for item in outers.items()[1:3]:
        ct_on(item)
    mixed_cross.wait_recv()
    mixed = tokens_ref[...].astype(floats) + (mixed_ref[...] + mixed_in[...].astype(floats))
    mixed_ref[...] = mixed
    xn2_ref[...] = (mixed * norm_parts(mixed) * gain_second).astype(halves)
    take(3, 0)
    hand(2, 1)
    for item in outers.items()[3:5]:
        ct_on(item)
    hand(1, 0)
    take(3, 1)
    for item in outers.items()[5:]:
        ct_on(item)
    for spot in ((1, 1), (3, 0), (3, 1)):
        hand(*spot)
    for made in w_hand.values():
        made.wait_recv()
    for made in ct_side.values():
        made.wait_recv()
    for made in saves:
        made.wait()
    courier.finish()


def feed_kernel(
    nz,
    w_ref,
    ct_ref,
    normal_ref,
    back_ref,
    branch_ref,
    done_ref,
    grads_ref,
    w,
    xn,
    ct,
    hid,
    gb,
    ub,
    part,
    ybuf,
    zsend,
    zbuf,
    cbuf,
    xbuf,
    sends,
    receives,
    locals_,
):
    place = Place(nz)
    z, x, y, c = place.z, place.x, place.y, place.c
    length, model = normal_ref.shape
    share = w.shape[-1]
    block = model // nz
    lines = 2 * length * nz
    courier = Courier(sends, receives)

    def source(dz):
        return lax.rem(z + nz - dz, nz)

    meet([place.line(dz) for dz in range(1, nz)] + [place.across[name] for name in "xyc"])
    along = {
        dz: courier.copy(normal_ref, xn.at[z, y], place.line(dz)) for dz in range(1, nz)
    }
    side = {0: courier.copy(normal_ref, xn.at[z, y], place.across["y"])}
    loads = [
        pltpu.make_async_copy(w_ref.at[which], w.at[which], locals_.at[which])
        for which in range(3)
    ] + [pltpu.make_async_copy(ct_ref, ct, locals_.at[3])]
    for made in loads:
        made.start()
    xn[z, y] = normal_ref[...]
    for made in loads:
        made.wait()

    def weight(which, start, size):
        return w[which, :, :, :, :, :, start : start + size].reshape(model, size)

    def pass_on(dz):
        along[dz].wait_recv()
        spot = xn.at[source(dz), y]
        side[dz] = courier.copy(spot, spot, place.across["y"])

    half = nz // 2
    scatter = []
    for dz in range(nz):
        group = source(dz)
        if dz + 1 < nz:
            pass_on(dz + 1)
        side[dz].wait_recv()
        for start, size in cuts_of(share, 256):
            normal = xn[group].reshape(2 * length, model)
            outer = ct[group].reshape(2 * length, model)
            gate = jnp.dot(normal, weight(0, start, size), preferred_element_type=floats)
            upper = jnp.dot(normal, weight(1, start, size), preferred_element_type=floats)
            hidden_back = jnp.dot(outer, weight(2, start, size), preferred_element_type=floats)
            sig = 1.0 / (1.0 + jnp.exp(-gate))
            silu = gate * sig
            spot = (group, slice(None), slice(start, start + size))
            hid[spot] = (silu * upper).astype(halves)
            gb[spot] = (hidden_back * upper * (sig * (1.0 + gate * (1.0 - sig)))).astype(halves)
            ub[spot] = (hidden_back * silu).astype(halves)

        @pl.loop(0, 2)
        def _(step):
            rows = pl.ds(step * half, half)
            lanes = pl.ds(pl.multiple_of(step * (model // 2), 128), model // 2)

            def turned(which):
                return w[which, rows].reshape(model // 2, share)

            both = lax.dot_general(
                gb[group], turned(0), last_pair, preferred_element_type=floats
            ) + lax.dot_general(ub[group], turned(1), last_pair, preferred_element_type=floats)
            part[group, :, :, lanes] = both.astype(halves).reshape(2, length, model // 2)

        scatter.append(
            courier.copy(part.at[group, 1 - y], ybuf.at[group], place.across["y"])
        )

    final = {}

    def sum_on(dz):
        group = source(dz)
        scatter[dz].wait_recv()
        total = part[group, y].astype(floats) + ybuf[group].astype(floats)
        if dz == 0:
            back_ref[...] = total
        else:
            zsend[dz - 1] = total.astype(halves)
            final[dz] = courier.copy(zsend.at[dz - 1], zbuf.at[dz - 1], (group, x, y, c))

    for group in range(nz):

        @pl.loop(0, 2)
        def _(step):
            rows = pl.ds(step * half, half)
            lanes = pl.ds(pl.multiple_of(step * (model // 2), 128), model // 2)
            product = lax.dot_general(
                hid[group],
                w[2, rows].reshape(model // 2, share),
                last_pair,
                preferred_element_type=floats,
            )
            branch_ref[group, :, :, lanes] = product.astype(halves).reshape(2, length, model // 2)

    orders = far_first(nz)
    early = 2
    handed, crossed, saves = {}, {}, []

    def save(source, target):
        made = pltpu.make_async_copy(source, target, locals_.at[4 + len(saves)])
        made.start()
        saves.append(made)

    def product(dz):
        group = lax.rem(z + dz, nz)
        lanes = pl.ds(pl.multiple_of(group * block, 128), block)
        normal_turned = xn[:, :, :, lanes].reshape(lines, block).T
        outer_turned = ct[:, :, :, lanes].reshape(lines, block).T
        for which, left, right in (
            (0, normal_turned, gb),
            (1, normal_turned, ub),
            (2, outer_turned, hid),
        ):
            for start, size in cuts_of(share, 512):
                w[which, group, :, :, :, :, start : start + size] = (
                    jnp.dot(
                        left,
                        right[:, :, start : start + size].reshape(lines, size),
                        preferred_element_type=floats,
                    )
                    .astype(halves)
                    .reshape(2, 2, 2, -1, size)
                )
        handed[dz] = courier.copy(
            w.at[:, group, :, :, 1 - c], cbuf.at[dz], place.across["c"]
        )

    def settle(position):
        dz = orders[position]
        group = lax.rem(z + dz, nz)
        handed[dz].wait_recv()
        for which in range(3):
            w[which, group, :, :, c] = (
                w[which, group, :, :, c].astype(floats) + cbuf[dz, which].astype(floats)
            ).astype(halves)
        if position < early:
            crossed[position] = courier.copy(
                w.at[:, group, 1 - x, :, c], xbuf.at[position], place.across["x"]
            )
        else:
            save(w.at[:, group, :, :, c], grads_ref.at[:, position - early])

    for position in range(nz):
        product(orders[position])
        sum_on(position)
        if position:
            settle(position - 1)
    settle(nz - 1)
    for position in range(early):
        group = lax.rem(z + orders[position], nz)
        crossed[position].wait_recv()
        for which in range(3):
            w[which, group, x, :, c] = (
                w[which, group, x, :, c].astype(floats) + xbuf[position, which].astype(floats)
            ).astype(halves)
        save(w.at[:, group, x, :, c], done_ref.at[:, position])
    for dz in range(1, nz):
        final[dz].wait_recv()
        back_ref[...] += zbuf[dz - 1].astype(floats)
    for made in saves:
        made.wait()
    courier.finish()


class LineSum:
    def __init__(self, courier, place, parts, spot, above, below):
        self.courier, self.place, self.parts, self.spot = courier, place, parts, spot
        self.arrivals = {1: above, -1: below}
        self.sent = {}

    def add(self, target, way):
        nz = self.place.nz
        spot = self.spot(target)
        arrived = self.arrivals[way][target - 1 if way == 1 else target]
        self.parts[spot] = (self.parts[spot].astype(floats) + arrived.astype(floats)).astype(
            self.parts.dtype
        )

    def forward(self, target, way):
        p = self.place
        moving = p.z < target if way == 1 else p.z > target
        fed = p.z > 0 if way == 1 else p.z < p.nz - 1
        made = self.courier.make(
            self.parts.at[self.spot(target)],
            self.arrivals[way].at[target - 1 if way == 1 else target],
            p.line_at(way),
            moving,
        )
        self.sent[target, way] = made

        @pl.when(moving & fed)
        def _():
            made.raw.wait_recv()
            self.add(target, way)

        made.start()

    def forward_step(self, step):
        self.forward(self.place.nz - 1 - step, 1)
        self.forward(step, -1)

    def finish(self):
        p = self.place
        for (target, way), made in self.sent.items():
            fed = p.z > 0 if way == 1 else p.z < p.nz - 1

            @pl.when((p.z == target) & fed)
            def _(target=target, way=way, made=made):
                made.raw.wait_recv()
                self.add(target, way)


class Scatter:
    def __init__(self, courier, place, parts, core_in, side_in, above, below, last_in):
        self.courier, self.place, self.parts = courier, place, parts
        self.core_in, self.side_in, self.last_in = core_in, side_in, last_in
        every = slice(None)
        self.line = LineSum(
            courier, place, parts, lambda group: (group, every, place.y, place.c), above, below
        )
        self.groups = []
        for step in range((place.nz + 1) // 2):
            self.groups += [place.nz - 1 - step, step]
        self.core, self.side = {}, {}

    def to_core(self, group):
        p = self.place
        self.core[group] = self.courier.copy(
            self.parts.at[group, :, :, 1 - p.c], self.core_in.at[group], p.across["c"]
        )

    def add(self, spot, arrived):
        self.parts[spot] = (self.parts[spot].astype(floats) + arrived.astype(floats)).astype(
            self.parts.dtype
        )

    def sideways(self):
        p = self.place
        every = slice(None)
        for group in self.groups:
            self.core[group].wait_recv()
            self.add((group, every, every, p.c), self.core_in[group])
            self.side[group] = self.courier.copy(
                self.parts.at[group, :, 1 - p.y, p.c], self.side_in.at[group], p.across["y"]
            )

    def along(self):
        p = self.place
        for group in self.groups:
            self.side[group].wait_recv()
            self.add((group, slice(None), p.y, p.c), self.side_in[group])

    def across(self):
        p = self.place
        self.line.finish()
        self.last = self.courier.copy(
            self.parts.at[p.z, 1 - p.x, p.y, p.c], self.last_in, p.across["x"]
        )

    def own(self):
        p = self.place
        return self.parts[p.z, p.x, p.y, p.c].astype(floats)

    def other(self):
        self.last.wait_recv()
        return self.last_in[...].astype(floats)


def gather_pieces(values, piece, devices):
    width = values.shape[1]
    owner = lax.div(lax.broadcasted_iota(jnp.int32, (devices, width), 1), piece)
    mine = owner == lax.broadcasted_iota(jnp.int32, (devices, width), 0)
    at = lax.broadcasted_iota(jnp.int32, (width, 128), 0)
    inner = lax.broadcasted_iota(jnp.int32, (width, 128), 1)
    chosen = (lax.rem(at, piece) == inner).astype(floats)
    rows = jnp.where(mine, values, 0.0)
    return jnp.dot(rows, chosen, preferred_element_type=floats, precision=lax.Precision.HIGHEST)


def back_kernel(
    nz,
    done_ref,
    grads_in,
    branch_ref,
    kv_ref,
    q_ref,
    m_ref,
    back_ref,
    mixed_ref,
    outer_ref,
    tokens_ref,
    xn1_ref,
    gain_ref,
    turn_ref,
    query_ref,
    pair_ref,
    share_ref,
    out_ref,
    output_ref,
    tokens_grad_ref,
    joint_grad_ref,
    merge_grad_ref,
    small_grad_ref,
    grads_ref,
    weight_m,
    weight_q,
    weight_kv,
    gown,
    gin,
    branch_own,
    branch_in,
    branch_above,
    branch_below,
    *rest,
):
    merge_bufs, query_bufs, kv_bufs, small_bufs = (rest[6 * i : 6 * i + 6] for i in range(4))
    (
        pair_sum,
        pair_half,
        pair_above,
        pair_below,
        joint_back,
        attended_back,
        mixed_both,
        back_send,
        back_in,
        sends,
        receives,
        locals_,
    ) = rest[24:]
    place = Place(nz)
    z, x, y, c = place.z, place.x, place.y, place.c
    length, model = tokens_ref.shape
    share = gown.shape[-1]
    half = GROUP * HEAD_DIM
    both = 2 * length
    block = model // nz
    depth = grads_in.shape[-2]
    devices = 8 * nz
    total_keys = nz * both
    orders = far_first(nz)
    courier = Courier(sends, receives)
    meet(place.peers())

    def group_of(dz):
        return lax.rem(z + dz, nz)

    copies = []

    def load(source, target):
        made = pltpu.make_async_copy(source, target, locals_.at[len(copies)])
        made.start()
        copies.append(made)
        return made

    merge_load = load(m_ref, weight_m)
    branch_load = load(branch_ref.at[:, y], branch_own)
    gown_load = load(grads_in.at[:, :, x], gown)
    early = 2
    late = orders[early:]
    query_load = load(q_ref, weight_q)
    kv_load = load(kv_ref, weight_kv)

    b_cross = {
        group: courier.copy(branch_ref.at[group, 1 - y], branch_in.at[group], place.across["y"])
        for group in range(nz)
    }
    g_cross, g_line, kept = {}, [], []

    def grads_across(dz):
        g_cross[dz] = courier.copy(
            grads_in.at[:, late.index(dz), 1 - x], gin.at[late.index(dz)], place.across["x"]
        )

    mine = pl.ds(pl.multiple_of((z * 2 + y) * share, 128), share)

    def grads_line(dz, rows):
        for dy in range(2):
            ty = lax.rem(y + dy, 2)
            if dz or dy:
                g_line.append(
                    courier.copy(
                        rows.at[:, ty], grads_ref.at[:, :, mine], (group_of(dz), x, ty, c)
                    )
                )
            else:
                kept.append(load(rows.at[:, ty], grads_ref.at[:, :, mine]))

    for position in range(early):
        grads_line(orders[position], done_ref.at[:, position])

    mixed = mixed_ref[...]
    second_scale = norm_parts(mixed)
    part, second_local = norm_back(back_ref[...], mixed, second_scale, gain_ref[1:2, :])
    grad = outer_ref[...].astype(floats) + part
    tokens_grad_ref[...] = grad
    mixed_both[x] = grad.astype(halves)
    mixed_cross = courier.copy(mixed_both.at[x], mixed_both.at[x], place.across["x"])
    mixed_cross.wait_recv()
    for dz in late:
        grads_across(dz)

    merge_load.wait()
    upstream_both = mixed_both[...].reshape(both, model)
    attended_back[...] = jnp.dot(
        upstream_both, weight_m[...].reshape(model, half), preferred_element_type=floats
    ).astype(halves)
    merges = Scatter(courier, place, *merge_bufs)
    queries = Scatter(courier, place, *query_bufs)
    keys_values = Scatter(courier, place, *kv_bufs)
    smalls = Scatter(courier, place, *small_bufs)

    def product_rows(scatter, left, right):
        for group in scatter.groups:
            scatter.parts[group] = (
                jnp.dot(
                    left[group * block : (group + 1) * block], right, preferred_element_type=floats
                )
                .astype(halves)
                .reshape(2, 2, 2, depth, right.shape[1])
            )
            scatter.to_core(group)

    product_rows(merges, upstream_both.T, out_ref[...].astype(halves))

    def attend(first, last):
        @pl.loop(first, last)
        def _(head):
            query = query_ref[head]
            keys = pair_ref[:, :, :HEAD_DIM].reshape(total_keys, HEAD_DIM)
            values = pair_ref[:, :, HEAD_DIM:].reshape(total_keys, HEAD_DIM)
            lanes = pl.ds(pl.multiple_of(head * HEAD_DIM, 128), HEAD_DIM)
            upstream = attended_back[:, lanes]
            delta = jnp.sum(upstream.astype(floats) * out_ref[:, lanes], axis=-1, keepdims=True)
            mass = lax.dot_general(upstream, values, last_pair, preferred_element_type=floats)
            shares = share_ref[head]
            scores = (shares.astype(floats) * (mass - delta)).astype(halves)
            query_sum = jnp.dot(scores, keys, preferred_element_type=floats) * SCALE
            cosine, sine = turn_ref[0], turn_ref[1]
            joint_back[:, lanes] = (
                query_sum * cosine + pltpu.roll(query_sum * sine, HEAD_DIM // 2, 1)
            ).astype(halves)
            pair_sum[:, :HEAD_DIM] += (
                jnp.dot(scores.T, query, preferred_element_type=floats) * SCALE
            )
            pair_sum[:, HEAD_DIM:] += jnp.dot(shares.T, upstream, preferred_element_type=floats)

    def grads_on(dz):
        at = late.index(dz)
        g_cross[dz].wait_recv()
        for which in range(3):
            gown[which, at] = (
                gown[which, at].astype(floats) + gin[at, which].astype(floats)
            ).astype(halves)
        grads_line(dz, gown.at[:, at])

    pair_sum[...] = jnp.zeros_like(pair_sum)
    attend(0, GROUP // 2)
    merges.sideways()

    attend(GROUP // 2, GROUP)

    pair_half[...] = pair_sum[...].astype(halves).reshape(nz, both, 2 * HEAD_DIM)
    pairs = LineSum(courier, place, pair_half, lambda group: (group,), pair_above, pair_below)
    pairs.forward(nz - 1, 1)
    pairs.forward(0, -1)
    turned = xn1_ref[...].T
    product_rows(queries, turned, joint_back[:, :half])
    for step in range(1, nz - 1):
        pairs.forward(nz - 1 - step, 1)
        pairs.forward(step, -1)
    branch_load.wait()
    for group in range(nz):
        b_cross[group].wait_recv()
        branch_own[group] = (
            branch_own[group].astype(floats) + branch_in[group].astype(floats)
        ).astype(halves)
    pairs.finish()
    total = pair_half[z].astype(floats)
    key_total = total[:, :HEAD_DIM]
    joint_back[:, half : half + HEAD_DIM] = (
        key_total * turn_ref[0] + pltpu.roll(key_total * turn_ref[1], HEAD_DIM // 2, 1)
    ).astype(halves)
    joint_back[:, half + HEAD_DIM :] = total[:, HEAD_DIM:].astype(halves)
    product_rows(keys_values, turned, joint_back[:, half:])
    query_load.wait()
    kv_load.wait()
    normal_back = lax.dot_general(
        joint_back[:, :half],
        weight_q[...].reshape(model, half),
        last_pair,
        preferred_element_type=floats,
    ) + lax.dot_general(
        joint_back[:, half:],
        weight_kv[...].reshape(model, 2 * HEAD_DIM),
        last_pair,
        preferred_element_type=floats,
    )
    back_send[...] = jnp.where(x == 0, normal_back[length:], normal_back[:length]).astype(halves)
    back_cross = courier.copy(back_send, back_in, place.across["x"])
    normal_own = jnp.where(x == 0, normal_back[:length], normal_back[length:])
    queries.sideways()
    keys_values.sideways()
    gown_load.wait()
    for dz in late[:1]:
        grads_on(dz)

    back_cross.wait_recv()
    normal_own = normal_own + back_in[...].astype(floats)
    residual = tokens_ref[...].astype(floats)
    part, first_local = norm_back(normal_own, residual, norm_parts(residual), gain_ref[0:1, :])
    tokens_grad_ref[...] += part

    local = jnp.sum(joint_back[...].astype(floats), axis=0, keepdims=True)
    pieces_of = []
    for first, width in ((0, half), (half, HEAD_DIM), (half + HEAD_DIM, HEAD_DIM)):
        for side in range(2):
            pieces_of.append(jnp.where(x == side, local[:, first : first + width], 0.0))
    bias_local = jnp.concatenate(pieces_of, axis=1)
    pieces = jnp.zeros((devices * 8, 128), floats)
    for which, values in ((0, bias_local), (1, first_local), (2, second_local)):
        mine_rows = gather_pieces(values, values.shape[1] // devices, devices)
        at = lax.broadcasted_iota(jnp.int32, (devices * 8, devices), 0)
        wanted = lax.broadcasted_iota(jnp.int32, (devices * 8, devices), 1) * 8 + which
        pieces = pieces + jnp.dot(
            (at == wanted).astype(floats),
            mine_rows,
            preferred_element_type=floats,
            precision=lax.Precision.HIGHEST,
        )
    smalls.parts[...] = pieces.reshape(nz, 2, 2, 2, 8, 128)
    for group in smalls.groups:
        smalls.to_core(group)
    for dz in late[1:]:
        grads_on(dz)
    smalls.sideways()
    for made in (merges, queries, keys_values):
        made.along()
    branches = LineSum(
        courier, place, branch_own, lambda group: (group,), branch_above, branch_below
    )
    smalls.along()
    for step in range(nz - 1):
        for line in (smalls.line, keys_values.line, queries.line, merges.line, branches):
            line.forward_step(step)
    for made in (merges, queries, keys_values, smalls):
        made.across()
    branches.finish()
    output_ref[...] = (mixed_ref[...] + branch_own[z].astype(floats)).astype(halves)
    for ref, made, pieces in (
        (merge_grad_ref, merges, [(0, half)]),
        (joint_grad_ref, queries, [(0, half)]),
        (joint_grad_ref, keys_values, KV_PIECES),
    ):
        for side, values in ((x, made.own()), (1 - x, made.other())):
            at = 0
            for first, width in pieces:
                lanes = pl.ds(pl.multiple_of(first + side * width, 128), width)
                ref[:, lanes] = values[:, at : at + width]
                at += width
    small_grad_ref[...] = smalls.own() + smalls.other()
    for made in g_line:
        made.wait_recv()
    for made in kept:
        made.wait()
    courier.finish()


def padded_share(hidden_width, team):
    return -(-hidden_width // (team * 128)) * 128


def body_kernels(
    tokens,
    segments,
    joint_matrix,
    joint_bias,
    merge_matrix,
    norm_first,
    norm_second,
    gate_matrix,
    up_matrix,
    down_matrix,
    cotangent,
):
    length, model = tokens.shape[1:]
    depth, joint_width = joint_matrix.shape
    hidden_width = gate_matrix.shape[1]
    nz = lax.axis_size("z")
    share = padded_share(hidden_width, 2 * nz)
    half = GROUP * HEAD_DIM
    pair_width = 2 * HEAD_DIM
    both = 2 * length
    keys = nz * both
    vmem = pl.BlockSpec(memory_space=pltpu.VMEM)
    anywhere = pl.BlockSpec(memory_space=pl.ANY)
    blocks = (nz, 2, 2, 2)

    def shape(dims, kind=halves):
        return jax.ShapeDtypeStruct(dims, kind)

    def semaphores(count, loads):
        return [
            pltpu.SemaphoreType.DMA((count,)),
            pltpu.SemaphoreType.DMA((count,)),
            pltpu.SemaphoreType.DMA((loads,)),
        ]

    def params(number):
        return pltpu.CompilerParams(
            collective_id=number, has_side_effects=True, vmem_limit_bytes=VMEM_LIMIT
        )

    stack = jnp.stack([gate_matrix, up_matrix, down_matrix.T])
    stack = jnp.pad(stack, ((0, 0), (0, 0), (0, 2 * nz * share - hidden_width)))

    def lane_row(values):
        return jnp.pad(values.astype(floats), (0, 128 - values.shape[0]))

    own_labels = segments[0]
    empty = jnp.zeros((128,), floats)
    small = jnp.stack(
        [lane_row(v) for v in (joint_bias, norm_first, norm_second, own_labels)] + [empty] * 4
    )
    inverse = theta ** -(np.arange(HEAD_DIM // 2) * (2.0 / HEAD_DIM))
    inverse = jnp.asarray(np.tile(inverse, 2)[None], floats)
    outer = cotangent[0]
    (
        w,
        team_outer,
        kv_all,
        q_all,
        m_all,
        xn1,
        xn2,
        mixed,
        gains,
        turns,
        queries,
        pair,
        shares,
        summed,
    ) = pl.pallas_call(
        functools.partial(attention_kernel, nz),
        name="attention_forward",
        out_shape=(
            shape((3,) + blocks + (depth, share)),
            shape((nz, 2, length, model)),
            shape(blocks + (depth, pair_width)),
            shape(blocks + (depth, half)),
            shape(blocks + (depth, half)),
            shape((both, model)),
            shape((length, model)),
            shape((length, model), floats),
            shape((8, model), floats),
            shape((2, both, HEAD_DIM), floats),
            shape((GROUP, both, HEAD_DIM)),
            shape((nz, both, pair_width)),
            shape((GROUP, both, keys)),
            shape((both, half), floats),
        ),
        in_specs=[anywhere] * 3 + [vmem] * 4,
        out_specs=(anywhere,) * 5 + (vmem,) * 9,
        scratch_shapes=[
            pltpu.VMEM(blocks + (depth, pair_width), halves),
            pltpu.VMEM(blocks + (depth, half), halves),
            pltpu.VMEM(blocks + (depth, half), halves),
            pltpu.VMEM(blocks + (8, 128), floats),
            pltpu.VMEM((both, keys), floats),
            pltpu.VMEM((2, length, model), halves),
            pltpu.VMEM((length, model), halves),
            pltpu.VMEM((length, model), halves),
        ]
        + semaphores(137, 10),
        compiler_params=params(0),
    )(stack, joint_matrix, merge_matrix.T, small, inverse, tokens[0], outer)

    lines = 2 * length
    back, branch, done, grads = pl.pallas_call(
        functools.partial(feed_kernel, nz),
        name="feed_forward",
        out_shape=(
            shape((length, model), floats),
            shape((nz, 2, length, model)),
            shape((3, 2, 2, depth, share)),
            shape((3, nz - 2, 2, 2, depth, share)),
        ),
        in_specs=[anywhere, anywhere, vmem],
        out_specs=(vmem, vmem, anywhere, anywhere),
        scratch_shapes=[
            pltpu.VMEM((3,) + blocks + (depth, share), halves),
            pltpu.VMEM((nz, 2, length, model), halves),
            pltpu.VMEM((nz, 2, length, model), halves),
            pltpu.VMEM((nz, lines, share), halves),
            pltpu.VMEM((nz, lines, share), halves),
            pltpu.VMEM((nz, lines, share), halves),
            pltpu.VMEM((nz, 2, length, model), halves),
            pltpu.VMEM((nz, length, model), halves),
            pltpu.VMEM((nz - 1, length, model), halves),
            pltpu.VMEM((nz - 1, length, model), halves),
            pltpu.VMEM((nz, 3, 2, 2, depth, share), halves),
            pltpu.VMEM((2, 3, 2, depth, share), halves),
        ]
        + semaphores(22, 8),
        compiler_params=params(1),
    )(w, team_outer, xn2)

    def sums(rows, width, kind=halves):
        return [
            pltpu.VMEM(blocks + (rows, width), kind),
            pltpu.VMEM((nz, 2, 2, rows, width), kind),
            pltpu.VMEM((nz, 2, rows, width), kind),
            pltpu.VMEM((nz - 1, 2, rows, width), kind),
            pltpu.VMEM((nz - 1, 2, rows, width), kind),
            pltpu.VMEM((rows, width), kind),
        ]

    output, tokens_grad, joint_grad, merge_grad, small_grad, grads = pl.pallas_call(
        functools.partial(back_kernel, nz),
        name="attention_backward",
        out_shape=(
            shape((length, model)),
            shape((length, model), floats),
            shape((depth, joint_width), floats),
            shape((depth, QUERY_WIDTH), floats),
            shape((8, 128), floats),
            shape((3, depth, 2 * nz * share)),
        ),
        in_specs=[anywhere] * 6 + [vmem] * 11,
        out_specs=(vmem,) * 5 + (anywhere,),
        scratch_shapes=[
            pltpu.VMEM(blocks + (depth, half), halves),
            pltpu.VMEM(blocks + (depth, half), halves),
            pltpu.VMEM(blocks + (depth, pair_width), halves),
            pltpu.VMEM((3, nz - 2, 2, depth, share), halves),
            pltpu.VMEM((nz - 2, 3, 2, depth, share), halves),
            pltpu.VMEM((nz, length, model), halves),
            pltpu.VMEM((nz, length, model), halves),
            pltpu.VMEM((nz - 1, length, model), halves),
            pltpu.VMEM((nz - 1, length, model), halves),
        ]
        + sums(depth, half)
        + sums(depth, half)
        + sums(depth, pair_width)
        + sums(8, 128, floats)
        + [
            pltpu.VMEM((keys, pair_width), floats),
            pltpu.VMEM((nz, both, pair_width), halves),
            pltpu.VMEM((nz - 1, both, pair_width), halves),
            pltpu.VMEM((nz - 1, both, pair_width), halves),
            pltpu.VMEM((both, half + pair_width), halves),
            pltpu.VMEM((both, half), halves),
            pltpu.VMEM((2, length, model), halves),
            pltpu.VMEM((length, model), halves),
            pltpu.VMEM((length, model), halves),
        ]
        + semaphores(90, 6),
        compiler_params=params(2),
    )(
        done,
        grads,
        branch,
        kv_all,
        q_all,
        m_all,
        back,
        mixed,
        outer,
        tokens[0],
        xn1,
        gains,
        turns,
        queries,
        pair,
        shares,
        summed,
    )
    grads = [grads[which, :, :hidden_width].astype(floats) for which in range(3)]
    return (
        output[None],
        tokens_grad[None],
        joint_grad,
        small_grad[0, : joint_bias.shape[0]],
        merge_grad.T,
        small_grad[1, :depth],
        small_grad[2, :depth],
        grads[0],
        grads[1],
        grads[2].T,
    )


def body_plain(
    tokens,
    segments,
    joint_matrix,
    joint_bias,
    merge_matrix,
    norm_first,
    norm_second,
    gate_matrix,
    up_matrix,
    down_matrix,
    cotangent,
):
    residual = tokens[0].astype(floats)
    length, model = residual.shape
    depth = joint_matrix.shape[0]
    joint_width = joint_matrix.shape[1]
    hidden_width = gate_matrix.shape[1]
    z_count = lax.axis_size("z")
    team = lax.axis_size(TEAM)
    share = hidden_width // team
    own_labels = segments[0]
    labels = lax.all_gather(own_labels, SEQ, axis=0, tiled=True)
    offset = lax.axis_index(SEQ) * length
    places = offset + jnp.arange(length, dtype=jnp.int32)
    positions = lax.dynamic_slice_in_dim(row_positions(labels), offset, length, 0)
    cosine, sine = rotary(positions, HEAD_DIM)

    small = jnp.concatenate([joint_bias, norm_first, norm_second])
    small = jnp.pad(small, (0, -small.shape[0] % depth)).reshape(depth, -1)
    small_width = small.shape[1]
    packed = jnp.concatenate([joint_matrix, merge_matrix.T, small], axis=1)
    packed = lax.all_gather(packed, AXES, axis=0, tiled=True)
    joint_all = packed[:, :joint_width]
    merge_turned = packed[:, joint_width : joint_width + model]
    small = packed[:, joint_width + model :].reshape(-1, depth * small_width).astype(floats)
    bias_depth = joint_bias.shape[0]
    bias_all = small[:, :bias_depth].reshape(-1)
    gain_first = small[:, bias_depth : bias_depth + depth].reshape(-1)
    gain_second = small[:, bias_depth + depth : bias_depth + 2 * depth].reshape(-1)

    stacked = jnp.stack([gate_matrix, up_matrix, down_matrix.T], axis=1)
    stacked = stacked.reshape(depth, 3, team, share).transpose(2, 0, 1, 3)
    stacked = stacked.reshape(team, depth, 3 * share)
    stacked = lax.all_to_all(stacked, TEAM, split_axis=0, concat_axis=0, tiled=True)
    stacked = stacked.reshape(z_count, 1, team // z_count, 1, depth, 3 * share)
    stacked = lax.all_gather(stacked, "x", axis=1, tiled=True)
    stacked = lax.all_gather(stacked, "c", axis=3, tiled=True)
    stacked = stacked.reshape(model, 3 * share)
    both_all, down_turned = stacked[:, : 2 * share], stacked[:, 2 * share :]
    outer_grad = cotangent[0]
    team_outer = lax.all_gather(outer_grad, TEAM, axis=0, tiled=True)

    scale_first = norm_parts(residual)
    normal_first = (residual * scale_first * gain_first).astype(halves)
    joint = jnp.dot(normal_first, joint_all, preferred_element_type=floats) + bias_all
    query = joint[:, :QUERY_WIDTH].reshape(length, HEADS, HEAD_DIM)
    keys = joint[:, QUERY_WIDTH : QUERY_WIDTH + KEY_WIDTH].reshape(length, KV_HEADS, HEAD_DIM)
    values = joint[:, QUERY_WIDTH + KEY_WIDTH :].astype(halves)
    query = (query * cosine + turn_half(query) * sine).astype(halves)
    keys = (keys * cosine + turn_half(keys) * sine).astype(halves).reshape(length, KEY_WIDTH)
    query_group = to_groups(query)
    pair = lax.all_gather(jnp.concatenate([keys, values], axis=1), SEQ, axis=0, tiled=True)
    count = pair.shape[0]
    key_all = pair[:, :KEY_WIDTH].reshape(count, KV_HEADS, HEAD_DIM)
    value_all = pair[:, KEY_WIDTH:].reshape(count, KV_HEADS, HEAD_DIM)
    allowed = (places[:, None] >= jnp.arange(count, dtype=jnp.int32)[None, :]) & (
        own_labels[:, None] == labels[None, :]
    )
    allowed = jnp.tile(allowed, (GROUP, 1))[None]
    scores = jnp.einsum("krd,nkd->krn", query_group, key_all, preferred_element_type=floats)
    scores = jnp.where(allowed, scores * SCALE, neg)
    top = jnp.max(scores, axis=-1, keepdims=True)
    weights = jnp.where(allowed, jnp.exp(scores - top), 0.0)
    total = jnp.sum(weights, axis=-1, keepdims=True)
    shares = weights / total
    shares_half = shares.astype(halves)
    attended = jnp.einsum("krn,nkd->krd", shares_half, value_all, preferred_element_type=floats)
    attended_half = from_groups(attended, length).astype(halves)
    mixed = residual + lax.dot_general(
        attended_half, merge_turned, last_pair, preferred_element_type=floats
    )
    scale_second = norm_parts(mixed)
    normal_half = (mixed * scale_second * gain_second).astype(halves)

    team_normal = lax.all_gather(normal_half, TEAM, axis=0, tiled=True)
    both = jnp.dot(team_normal, both_all, preferred_element_type=floats)
    gate, upper = both[:, :share], both[:, share:]
    sig = jax.nn.sigmoid(gate)
    silu = gate * sig
    hidden_half = (silu * upper).astype(halves)
    branch = lax.dot_general(hidden_half, down_turned, last_pair, preferred_element_type=floats)
    hidden_grad = jnp.dot(team_outer, down_turned, preferred_element_type=floats)
    gate_half = (hidden_grad * upper * sig * (1.0 + gate * (1.0 - sig))).astype(halves)
    upper_half = (hidden_grad * silu).astype(halves)
    both_half = jnp.concatenate([gate_half, upper_half], axis=1)
    normal_grad = lax.dot_general(both_half, both_all, last_pair, preferred_element_type=floats)
    branch = lax.psum_scatter(branch.astype(halves), TEAM, scatter_dimension=0, tiled=True)
    normal_grad = lax.psum_scatter(normal_grad.astype(halves), TEAM, scatter_dimension=0, tiled=True)
    output = (mixed + branch.astype(floats)).astype(halves)[None]
    both_grad = lax.dot_general(team_normal, both_half, first_pair, preferred_element_type=floats)
    down_grad = lax.dot_general(team_outer, hidden_half, first_pair, preferred_element_type=floats)
    grads = jnp.concatenate([both_grad, down_grad], axis=1).astype(halves)
    grads = grads.reshape(z_count, 2, team // z_count, 2, depth, 3 * share)
    grads = lax.psum_scatter(grads, "c", scatter_dimension=3, tiled=True)
    grads = lax.psum_scatter(grads, "x", scatter_dimension=1, tiled=True)
    grads = grads.reshape(team, depth, 3 * share)
    grads = lax.all_to_all(grads, TEAM, split_axis=0, concat_axis=0, tiled=True)
    grads = grads.reshape(team, depth, 3, share).transpose(2, 1, 0, 3)
    grads = grads.reshape(3, depth, hidden_width).astype(floats)

    normal_grad = normal_grad.astype(floats)
    mixed_part, second_local = norm_back(normal_grad, mixed, scale_second, gain_second)
    mixed_grad = outer_grad.astype(floats) + mixed_part
    mixed_half = mixed_grad.astype(halves)
    merge_local = lax.dot_general(
        mixed_half, attended_half, first_pair, preferred_element_type=floats
    )
    attended_grad = jnp.dot(mixed_half, merge_turned, preferred_element_type=floats).astype(halves)
    grad_group = to_groups(attended_grad.reshape(length, HEADS, HEAD_DIM))
    mass_grad = jnp.einsum("krd,nkd->krn", grad_group, value_all, preferred_element_type=floats)
    row_dots = jnp.sum(shares * mass_grad, axis=-1, keepdims=True)
    score_half = (shares * (mass_grad - row_dots)).astype(halves)
    query_sum = (
        jnp.einsum("krn,nkd->krd", score_half, key_all, preferred_element_type=floats) * SCALE
    )
    key_grad = (
        jnp.einsum("krn,krd->nkd", score_half, query_group, preferred_element_type=floats) * SCALE
    )
    value_grad = jnp.einsum("krn,krd->nkd", shares_half, grad_group, preferred_element_type=floats)
    pair_sums = jnp.concatenate(
        [key_grad.reshape(count, KEY_WIDTH), value_grad.reshape(count, KEY_WIDTH)], axis=1
    )
    pair_mine = lax.psum_scatter(
        pair_sums.astype(halves), SEQ, scatter_dimension=0, tiled=True
    ).astype(floats)
    key_back = pair_mine[:, :KEY_WIDTH].reshape(length, KV_HEADS, HEAD_DIM)
    value_back = pair_mine[:, KEY_WIDTH:]
    query_back = from_groups(query_sum, length).reshape(length, HEADS, HEAD_DIM)
    query_back = query_back * cosine + unturn_half(query_back * sine)
    key_back = key_back * cosine + unturn_half(key_back * sine)
    joint_back = jnp.concatenate(
        [query_back.reshape(length, QUERY_WIDTH), key_back.reshape(length, KEY_WIDTH), value_back],
        axis=1,
    ).astype(halves)
    joint_local = lax.dot_general(
        normal_first, joint_back, first_pair, preferred_element_type=floats
    )
    bias_local = jnp.sum(joint_back.astype(floats), axis=0)
    normal_back = lax.dot_general(joint_back, joint_all, last_pair, preferred_element_type=floats)
    residual_part, first_local = norm_back(normal_back, residual, scale_first, gain_first)
    tokens_grad = (mixed_grad + residual_part)[None]

    small_back = jnp.concatenate(
        [
            bias_local.reshape(-1, bias_depth),
            first_local.reshape(-1, depth),
            second_local.reshape(-1, depth),
        ],
        axis=1,
    )
    small_back = jnp.pad(small_back, ((0, 0), (0, depth * small_width - small_back.shape[1])))
    small_back = small_back.reshape(-1, small_width)
    packed_grad = jnp.concatenate([joint_local, merge_local, small_back], axis=1).astype(halves)
    packed_grad = lax.psum_scatter(packed_grad, AXES, scatter_dimension=0, tiled=True).astype(floats)
    joint_grad = packed_grad[:, :joint_width]
    merge_grad = packed_grad[:, joint_width : joint_width + model].T
    small_back = packed_grad[:, joint_width + model :].reshape(-1)
    bias_grad = small_back[:bias_depth]
    first_grad = small_back[bias_depth : bias_depth + depth]
    second_grad = small_back[bias_depth + depth : bias_depth + 2 * depth]
    return (
        output,
        tokens_grad,
        joint_grad,
        bias_grad,
        merge_grad,
        first_grad,
        second_grad,
        grads[0],
        grads[1],
        grads[2].T,
    )


def solution(mesh):
    seq, row = mesh.shape["seq"], mesh.shape["row"]
    fine = Mesh(mesh.devices.reshape(seq // 2, 2, row // 2, 2), AXES)
    whole = ("z", "x", "y", "c")
    placed = (
        P(ROW, SEQ, None),
        P(ROW, SEQ),
        P(whole, None),
        P(whole),
        P(None, whole),
        P(whole),
        P(whole),
        P(whole, None),
        P(whole, None),
        P(None, whole),
        P(ROW, SEQ, None),
    )
    depth = MODEL // mesh.size
    return jax.shard_map(
        body_kernels if depth % 16 == 0 else body_plain,
        mesh=fine,
        in_specs=placed,
        out_specs=(
            P(ROW, SEQ, None),
            P(ROW, SEQ, None),
            P(whole, None),
            P(whole),
            P(None, whole),
            P(whole),
            P(whole),
            P(whole, None),
            P(whole, None),
            P(None, whole),
        ),
        check_vma=False,
    )
```

```python
import functools
import math

import jax
import jax.numpy as jnp
import numpy as np
from jax import lax
from jax.experimental import pallas as pl
from jax.experimental.pallas import tpu as pltpu
from jax.sharding import Mesh, PartitionSpec as P

HEADS = 12
KV_HEADS = 2
HEAD_DIM = 128
MODEL = HEADS * HEAD_DIM
GROUP = HEADS // KV_HEADS
QUERY_WIDTH = HEADS * HEAD_DIM
KEY_WIDTH = KV_HEADS * HEAD_DIM
KV_PIECES = [(QUERY_WIDTH, HEAD_DIM), (QUERY_WIDTH + KEY_WIDTH, HEAD_DIM)]
SCALE = 1.0 / math.sqrt(HEAD_DIM)

eps = 1e-06
theta = 1000000.0
neg = -1e30
last_pair = (((1,), (1,)), ((), ()))
first_pair = (((0,), (0,)), ((), ()))
floats = jnp.float32
halves = jnp.bfloat16

AXES = ("z", "x", "y", "c")
SEQ = ("z", "x")
ROW = ("y", "c")
TEAM = ("z", "y")


def turn_half(values):
    middle = values.shape[-1] // 2
    return jnp.concatenate([-values[..., middle:], values[..., :middle]], axis=-1)


def unturn_half(values):
    middle = values.shape[-1] // 2
    return jnp.concatenate([values[..., middle:], -values[..., :middle]], axis=-1)


def row_positions(labels):
    length = labels.shape[0]
    places = jnp.arange(length, dtype=jnp.int32)
    change = jnp.concatenate([jnp.ones((1,), dtype=jnp.bool_), labels[1:] != labels[:-1]])
    starts = lax.cummax(jnp.where(change, places, 0), axis=0)
    return places - starts


def rotary(positions, width):
    inverse = jnp.power(
        jnp.float32(theta), -(jnp.arange(width // 2, dtype=jnp.float32) * (2.0 / width))
    )
    angle = positions.astype(jnp.float32)[:, None] * inverse[None, :]
    angle = jnp.concatenate([angle, angle], axis=1)[:, None, :]
    return (jnp.cos(angle), jnp.sin(angle))


def to_groups(values):
    length = values.shape[0]
    return (
        values.reshape(length, KV_HEADS, GROUP, HEAD_DIM)
        .transpose(1, 2, 0, 3)
        .reshape(KV_HEADS, GROUP * length, HEAD_DIM)
    )


def from_groups(values, length):
    return (
        values.reshape(KV_HEADS, GROUP, length, HEAD_DIM)
        .transpose(2, 0, 1, 3)
        .reshape(length, QUERY_WIDTH)
    )


def norm_parts(values):
    return lax.rsqrt(jnp.mean(values * values, axis=-1, keepdims=True) + eps)


def norm_back(upstream, values, scale, gain):
    scaled = upstream * gain
    inner = jnp.mean(scaled * values, axis=-1, keepdims=True)
    part = scale * scaled - values * (scale * scale * scale) * inner
    gain_grad = jnp.sum(upstream * values * scale, axis=0, keepdims=True)
    return part, gain_grad


MESH = pl.DeviceIdType.MESH
VMEM_LIMIT = 60 * 2**20


def coordinates():
    return tuple(lax.axis_index(name) for name in AXES)


class Sent:
    def __init__(self, raw, when):
        self.raw, self.when = raw, when

    def under(self, act):
        if self.when is None:
            act()
        else:
            pl.when(self.when)(act)

    def start(self):
        self.under(self.raw.start)

    def wait_recv(self):
        self.under(self.raw.wait_recv)

    def wait_send(self):
        self.under(self.raw.wait_send)


class Courier:
    def __init__(self, sends, receives):
        self.sends, self.receives, self.copies = sends, receives, []

    def make(self, source, target, device, when=None):
        place = len(self.copies)
        raw = pltpu.make_async_remote_copy(
            src_ref=source,
            dst_ref=target,
            send_sem=self.sends.at[place],
            recv_sem=self.receives.at[place],
            device_id=device,
            device_id_type=MESH,
        )
        made = Sent(raw, when)
        self.copies.append(made)
        return made

    def copy(self, source, target, device, when=None):
        made = self.make(source, target, device, when)
        made.start()
        return made

    def finish(self):
        for made in self.copies:
            made.wait_send()


def meet(devices):
    barrier = pltpu.get_barrier_semaphore()
    for device in devices:
        pl.semaphore_signal(barrier, inc=1, device_id=device, device_id_type=MESH)
    pl.semaphore_wait(barrier, len(devices))


def far_first(nz):
    return sorted(range(nz), key=lambda dz: (dz == 0, abs(2 * dz - nz)))


def near_first(nz):
    return [sorted(range(nz), key=lambda group: (abs(group - at), -group)) for at in range(nz)]


def cuts_of(width, step):
    return [(start, min(step, width - start)) for start in range(0, width, step)]


class Line:
    def __init__(self, courier, place, spot):
        self.courier, self.place, self.spot = courier, place, spot
        self.sent = {}

    def items(self):
        p = self.place
        found = [(0, 0, p.z, None)]
        for step in range(1, p.nz):
            found.append((step, 1, lax.max(p.z - step, 0), p.z >= step))
            found.append((step, -1, lax.min(p.z + step, p.nz - 1), p.z + step < p.nz))
        return found

    def send(self, step, way, group, also=None):
        p = self.place
        inside = p.z < p.nz - 1 if way == 1 else p.z > 0
        if also is not None:
            inside = inside & also
        spot = self.spot(group)
        self.sent[step, way] = self.courier.copy(spot, spot, p.line_at(way), inside)

    def start(self):
        self.send(0, 1, self.place.z)
        self.send(0, -1, self.place.z)

    def arrive(self, step, way, group, exists):
        made = self.sent[step - 1, way]

        @pl.when(exists)
        def _():
            made.raw.wait_recv()

        if step < self.place.nz - 1:
            self.send(step, way, group, exists)


class Gather:
    def __init__(self, courier, place, source, buffer):
        self.courier, self.place = courier, place
        self.source, self.buffer = source, buffer
        self.line = Line(courier, place, lambda group: buffer.at[group, :, place.y, place.c])
        self.side, self.core = {}, {}

    def start(self):
        p = self.place
        spot = self.buffer.at[p.z, p.x, p.y, p.c]
        self.cross = [
            self.courier.copy(source, spot.at[:, lanes], p.across["x"])
            for source, lanes in self.source
        ]

    def along(self):
        for made in self.cross:
            made.wait_recv()
        self.line.start()
        self.sideways(self.line.items()[0])

    def sideways(self, item):
        step, way, group, exists = item
        p = self.place
        spot = self.buffer.at[group, :, p.y, p.c]
        self.side[step, way] = self.courier.copy(spot, spot, p.across["y"], exists)

    def pass_on(self, step):
        for item in self.line.items():
            if item[0] == step:
                self.line.arrive(*item)
                self.sideways(item)

    def to_core(self):
        p = self.place
        for item in self.line.items():
            step, way, group, exists = item
            self.side[step, way].wait_recv()
            spot = self.buffer.at[group, :, :, p.c]
            self.core[step, way] = self.courier.copy(spot, spot, p.across["c"], exists)

    def done(self):
        for made in self.core.values():
            made.wait_recv()


class Place:
    def __init__(self, nz):
        self.nz = nz
        self.z, self.x, self.y, self.c = z, x, y, c = coordinates()
        self.across = {"x": (z, 1 - x, y, c), "y": (z, x, 1 - y, c), "c": (z, x, y, 1 - c)}

    def line(self, dz, dy=0):
        y = lax.rem(self.y + dy, 2) if dy else self.y
        return (lax.rem(self.z + dz, self.nz), self.x, y, self.c)

    def line_at(self, way):
        return (lax.rem(self.z + self.nz + way, self.nz), self.x, self.y, self.c)

    def peers(self):
        team = [self.line(dz, dy) for dz in range(self.nz) for dy in range(2)]
        return team[1:] + [self.across["x"], self.across["c"]]


def spread(values, piece, width):
    devices, lanes = values.shape
    at = lax.broadcasted_iota(jnp.int32, (lanes, width), 1)
    inner = lax.broadcasted_iota(jnp.int32, (lanes, width), 0)
    chosen = (lax.rem(at, piece) == inner).astype(floats).astype(halves)
    repeated = jnp.dot(values.astype(halves), chosen, preferred_element_type=floats)
    owner = lax.div(lax.broadcasted_iota(jnp.int32, (devices, width), 1), piece)
    mine = owner == lax.broadcasted_iota(jnp.int32, (devices, width), 0)
    return jnp.sum(jnp.where(mine, repeated, 0.0), axis=0, keepdims=True)


def attention_kernel(
    nz,
    stack_ref,
    joint_ref,
    merge_ref,
    small_ref,
    inverse_ref,
    tokens_ref,
    outer_ref,
    w_ref,
    ct_ref,
    kv_out,
    query_out,
    merge_out,
    xn1_ref,
    xn2_ref,
    mixed_ref,
    gain_ref,
    turn_ref,
    query_ref,
    pair_ref,
    share_ref,
    out_ref,
    joint_kv,
    joint_q,
    merge,
    small,
    bias_mask,
    tokens_all,
    mixed_send,
    mixed_in,
    sends,
    receives,
    locals_,
):
    place = Place(nz)
    z, x, y, c = place.z, place.x, place.y, place.c
    length, model = tokens_ref.shape
    depth, joint_width = joint_ref.shape
    share = w_ref.shape[-1]
    half = GROUP * HEAD_DIM
    both = 2 * length
    total_keys = nz * both
    courier = Courier(sends, receives)
    devices = 8 * nz
    meet(place.peers())

    own_copies = []

    def keep(source, target):
        made = pltpu.make_async_copy(source, target, locals_.at[len(own_copies)])
        made.start()
        own_copies.append(made)
        return made

    def columns(tz, ty):
        return pl.ds(pl.multiple_of((tz * 2 + ty) * share, 128), share)

    gathers, own_waits = {}, {}

    def begin(name, ref, pieces, buffer):
        def from_side(side):
            found = []
            at = 0
            for first, width in pieces:
                lanes = pl.ds(pl.multiple_of(first + side * width, 128), width)
                found.append((ref.at[:, lanes], slice(at, at + width)))
                at += width
            return found

        spot = buffer.at[z, x, y, c]
        own_waits[name] = [keep(own, spot.at[:, lanes]) for own, lanes in from_side(x)]
        gathers[name] = Gather(courier, place, from_side(1 - x), buffer)
        gathers[name].start()

    own_waits["small"] = [keep(small_ref, small.at[z, x, y, c])]
    gathers["small"] = Gather(courier, place, [(small_ref, slice(None))], small)
    gathers["small"].start()
    begin("kv", joint_ref, KV_PIECES, joint_kv)
    token_cross = courier.copy(tokens_ref, tokens_all.at[x], place.across["x"])
    begin("q", joint_ref, [(0, half)], joint_q)
    begin("m", merge_ref, [(0, half)], merge)
    tokens_all[x] = tokens_ref[...]
    w_own = keep(stack_ref.at[:, :, columns(z, y)], w_ref.at[:, z, x, y, c])
    ct_own = keep(outer_ref, ct_ref.at[z, y])

    direct, w_cross, w_hand = {}, {}, {}

    def give(dz, dy):
        device = place.line(dz, dy)
        direct[dz, dy] = courier.copy(
            stack_ref.at[:, :, columns(device[0], device[2])], w_ref.at[:, z, x, y, c], device
        )

    def w_spot(dz, dy, side):
        return w_ref.at[:, lax.rem(z + nz - dz, nz), side, lax.rem(y + dy, 2), c]

    def take(dz, dy):
        if dz or dy:
            direct[dz, dy].wait_recv()
        spot = w_spot(dz, dy, x)
        w_cross[dz, dy] = courier.copy(spot, spot, place.across["x"])
        w_hand[dz, dy, 0] = courier.copy(spot, spot, place.across["c"])

    def hand(dz, dy):
        w_cross[dz, dy].wait_recv()
        spot = w_spot(dz, dy, 1 - x)
        w_hand[dz, dy, 1] = courier.copy(spot, spot, place.across["c"])

    give(0, 1)
    give(2, 0)
    for name in ("small", "kv"):
        for made in own_waits[name]:
            made.wait()
        gathers[name].along()
    token_cross.wait_recv()
    tokens_both = tokens_all[...].reshape(both, model).astype(floats)
    hat = tokens_both * norm_parts(tokens_both)
    for name in ("small", "kv"):
        gathers[name].pass_on(1)
    for made in own_waits["q"] + own_waits["m"]:
        made.wait()
    gathers["q"].along()
    for step in range(2, nz):
        for name in ("small", "kv"):
            gathers[name].pass_on(step)
    for name in ("small", "kv"):
        gathers[name].to_core()
    w_own.wait()
    take(0, 0)
    for step in range(1, nz):
        gathers["q"].pass_on(step)
    for name in ("small", "kv"):
        gathers[name].done()
    take(0, 1)
    give(2, 1)

    pieces = small[...].reshape(devices * 8, 128).astype(halves)

    def row_of(which):
        at = lax.broadcasted_iota(jnp.int32, (devices, devices * 8), 1)
        wanted = lax.broadcasted_iota(jnp.int32, (devices, devices * 8), 0) * 8 + which
        chosen = (at == wanted).astype(floats).astype(halves)
        return jnp.dot(chosen, pieces, preferred_element_type=floats)

    gain_first = spread(row_of(1), depth, model)
    gain_second = spread(row_of(2), depth, model)
    bias = spread(row_of(0), joint_width // devices, joint_width)
    gain_ref[0:1, :] = gain_first
    gain_ref[1:2, :] = gain_second

    def mine(first, width):
        return jnp.where(x == 0, bias[:, first : first + width], bias[:, first + width : first + 2 * width])

    bias_query = mine(0, half)
    bias_key = mine(QUERY_WIDTH, HEAD_DIM)
    bias_value = mine(QUERY_WIDTH + KEY_WIDTH, HEAD_DIM)
    label = jnp.concatenate([small[z, side, y, c].T[:, 3:4] for side in range(2)], axis=0)
    start = jnp.zeros((both, 1), floats)
    rows_at = z * both + lax.broadcasted_iota(jnp.int32, (both, length), 0)
    lanes_at = lax.broadcasted_iota(jnp.int32, (both, length), 1)
    for block in range(2 * nz):
        keys_label = small[block // 2, block % 2, y, c, 3:4, :]
        start = start + jnp.sum((keys_label < label).astype(floats), axis=1, keepdims=True)
        allowed = (keys_label == label) & (rows_at >= block * length + lanes_at)
        bias_mask[:, block * length : (block + 1) * length] = jnp.where(allowed, 0.0, neg)
    place_at = (z * both + lax.broadcasted_iota(jnp.int32, (both, 1), 0)).astype(floats)
    angle = (place_at - start) * inverse_ref[...]
    cosine = jnp.cos(angle)
    lane = lax.broadcasted_iota(jnp.int32, (both, HEAD_DIM), 1)
    sine = jnp.where(lane < HEAD_DIM // 2, -1.0, 1.0) * jnp.sin(angle)
    turn_ref[0] = cosine
    turn_ref[1] = sine

    def turned(values):
        return values * cosine + pltpu.roll(values, HEAD_DIM // 2, 1) * sine

    xn1_ref[...] = (hat * gain_first).astype(halves)
    pair = jnp.dot(
        xn1_ref[...], joint_kv[...].reshape(model, 2 * HEAD_DIM), preferred_element_type=floats
    )
    pair_ref[z, :, :HEAD_DIM] = turned(pair[:, :HEAD_DIM] + bias_key).astype(halves)
    pair_ref[z, :, HEAD_DIM:] = (pair[:, HEAD_DIM:] + bias_value).astype(halves)
    pairs = Line(courier, place, lambda group: pair_ref.at[group])
    pairs.start()
    gathers["q"].to_core()
    gathers["m"].along()
    for item in pairs.items()[1:3]:
        pairs.arrive(*item)
    take(2, 0)
    give(1, 0)
    for item in pairs.items()[3:]:
        pairs.arrive(*item)
    gathers["m"].pass_on(1)
    gathers["q"].done()

    query = jnp.dot(xn1_ref[...], joint_q[...].reshape(model, half), preferred_element_type=floats)
    query = query + bias_query
    for head in range(GROUP):
        query_ref[head] = turned(query[:, head * HEAD_DIM : (head + 1) * HEAD_DIM]).astype(halves)
    for step in range(2, nz):
        gathers["m"].pass_on(step)
    take(2, 1)
    give(1, 1)
    give(3, 0)
    outers = Line(courier, place, lambda group: ct_ref.at[group, y])
    ct_side = {}

    def ct_on(item):
        step, way, group, exists = item
        if step:
            outers.arrive(*item)
        spot = ct_ref.at[group, y]
        ct_side[step, way] = courier.copy(spot, spot, place.across["y"], exists)

    ct_own.wait()
    ct_on(outers.items()[0])
    gathers["m"].to_core()
    hand(0, 0)
    hand(0, 1)

    def attend(first, last):
        @pl.loop(first, last)
        def _(head):
            keys = pair_ref[:, :, :HEAD_DIM].reshape(total_keys, HEAD_DIM)
            values = pair_ref[:, :, HEAD_DIM:].reshape(total_keys, HEAD_DIM)
            scores = lax.dot_general(
                query_ref[head], keys, last_pair, preferred_element_type=floats
            )
            scores = scores * SCALE + bias_mask[...]
            top = jnp.max(scores, axis=-1, keepdims=True)
            raised = jnp.exp(scores - top)
            shares = (raised / jnp.sum(raised, axis=-1, keepdims=True)).astype(halves)
            share_ref[head] = shares
            lanes = pl.ds(pl.multiple_of(head * HEAD_DIM, 128), HEAD_DIM)
            out_ref[:, lanes] = jnp.dot(shares, values, preferred_element_type=floats)

    attend(0, GROUP // 2)
    take(1, 0)
    give(3, 1)
    attend(GROUP // 2, GROUP)
    outers.start()
    gathers["m"].done()
    saves = [keep(joint_kv, kv_out), keep(joint_q, query_out), keep(merge, merge_out)]
    merged = lax.dot_general(
        out_ref[...].astype(halves),
        merge[...].reshape(model, half),
        last_pair,
        preferred_element_type=floats,
    )
    mixed_ref[...] = jnp.where(x == 0, merged[:length], merged[length:])
    mixed_send[...] = jnp.where(x == 0, merged[length:], merged[:length]).astype(halves)
    mixed_cross = courier.copy(mixed_send, mixed_in, place.across["x"])
    take(1, 1)
    hand(2, 0)
    for item in outers.items()[1:3]:
        ct_on(item)
    mixed_cross.wait_recv()
    mixed = tokens_ref[...].astype(floats) + (mixed_ref[...] + mixed_in[...].astype(floats))
    mixed_ref[...] = mixed
    xn2_ref[...] = (mixed * norm_parts(mixed) * gain_second).astype(halves)
    take(3, 0)
    hand(2, 1)
    for item in outers.items()[3:5]:
        ct_on(item)
    hand(1, 0)
    take(3, 1)
    for item in outers.items()[5:]:
        ct_on(item)
    for spot in ((1, 1), (3, 0), (3, 1)):
        hand(*spot)
    for made in w_hand.values():
        made.wait_recv()
    for made in ct_side.values():
        made.wait_recv()
    for made in saves:
        made.wait()
    courier.finish()


def feed_kernel(
    nz,
    w_ref,
    ct_ref,
    normal_ref,
    back_ref,
    branch_ref,
    done_ref,
    grads_ref,
    w,
    xn,
    ct,
    hid,
    gb,
    ub,
    part,
    ybuf,
    zsend,
    zbuf,
    cbuf,
    xbuf,
    sends,
    receives,
    locals_,
):
    place = Place(nz)
    z, x, y, c = place.z, place.x, place.y, place.c
    length, model = normal_ref.shape
    share = w.shape[-1]
    block = model // nz
    lines = 2 * length * nz
    courier = Courier(sends, receives)

    def source(dz):
        return lax.rem(z + nz - dz, nz)

    meet([place.line(dz) for dz in range(1, nz)] + [place.across[name] for name in "xyc"])
    xn[z, y] = normal_ref[...]
    blocks = Line(courier, place, lambda group: xn.at[group, y])
    blocks.start()
    side = {}

    def pass_on(step):
        for item in blocks.items():
            if item[0] == step:
                way, group, exists = item[1:]
                if step:
                    blocks.arrive(*item)
                spot = xn.at[group, y]
                side[step, way] = courier.copy(spot, spot, place.across["y"], exists)

    pass_on(0)
    groups = near_first(nz)

    def group_at(number):
        return sum(jnp.where(z == at, groups[at][number], 0) for at in range(nz))

    def wait_for(number):
        for at in range(nz):
            gap = groups[at][number] - at
            made = side[abs(gap), 0 if gap == 0 else (1 if gap < 0 else -1)]
            pl.when(z == at)(made.raw.wait_recv)

    loads = [
        pltpu.make_async_copy(w_ref.at[which], w.at[which], locals_.at[which])
        for which in range(3)
    ] + [pltpu.make_async_copy(ct_ref, ct, locals_.at[3])]
    for made in loads:
        made.start()
    pass_on(1)
    for made in loads:
        made.wait()

    def weight(which, start, size):
        return w[which, :, :, :, :, :, start : start + size].reshape(model, size)

    half = nz // 2
    scatter = {}

    def scatter_on(dz):
        group = group_at(dz)
        scatter[dz] = courier.copy(
            part.at[group, 1 - y], ybuf.at[group], place.across["y"]
        )

    for dz in range(nz):
        group = group_at(dz)
        wait_for(dz)
        for start, size in cuts_of(share, 256):
            normal = xn[group].reshape(2 * length, model)
            outer = ct[group].reshape(2 * length, model)
            gate = jnp.dot(normal, weight(0, start, size), preferred_element_type=floats)
            upper = jnp.dot(normal, weight(1, start, size), preferred_element_type=floats)
            hidden_back = jnp.dot(outer, weight(2, start, size), preferred_element_type=floats)
            sig = 1.0 / (1.0 + jnp.exp(-gate))
            silu = gate * sig
            spot = (group, slice(None), slice(start, start + size))
            hid[spot] = (silu * upper).astype(halves)
            gb[spot] = (hidden_back * upper * (sig * (1.0 + gate * (1.0 - sig)))).astype(halves)
            ub[spot] = (hidden_back * silu).astype(halves)

        @pl.loop(0, 2)
        def _(step):
            rows = pl.ds(step * half, half)
            lanes = pl.ds(pl.multiple_of(step * (model // 2), 128), model // 2)

            def turned(which):
                return w[which, rows].reshape(model // 2, share)

            both = lax.dot_general(
                gb[group], turned(0), last_pair, preferred_element_type=floats
            ) + lax.dot_general(ub[group], turned(1), last_pair, preferred_element_type=floats)
            part[group, :, :, lanes] = both.astype(halves).reshape(2, length, model // 2)

        if dz:
            scatter_on(dz)
        if dz + 2 < nz:
            pass_on(dz + 2)

    scatter_on(0)

    final = {
        dz: courier.make(
            zsend.at[source(dz)], zbuf.at[dz - 1], (source(dz), x, y, c)
        )
        for dz in range(1, nz)
    }

    def sum_on(dz):
        group = group_at(dz)
        scatter[dz].wait_recv()
        total = part[group, y].astype(floats) + ybuf[group].astype(floats)
        if dz == 0:
            back_ref[...] = total
        else:
            zsend[group] = total.astype(halves)
            for apart, made in final.items():
                pl.when(source(apart) == group)(made.raw.start)

    for group in range(nz):

        @pl.loop(0, 2)
        def _(step):
            rows = pl.ds(step * half, half)
            lanes = pl.ds(pl.multiple_of(step * (model // 2), 128), model // 2)
            product = lax.dot_general(
                hid[group],
                w[2, rows].reshape(model // 2, share),
                last_pair,
                preferred_element_type=floats,
            )
            branch_ref[group, :, :, lanes] = product.astype(halves).reshape(2, length, model // 2)

    orders = far_first(nz)
    early = 2
    handed, crossed, saves = {}, {}, []

    def save(source, target):
        made = pltpu.make_async_copy(source, target, locals_.at[4 + len(saves)])
        made.start()
        saves.append(made)

    def product(dz):
        group = lax.rem(z + dz, nz)
        lanes = pl.ds(pl.multiple_of(group * block, 128), block)
        normal_turned = xn[:, :, :, lanes].reshape(lines, block).T
        outer_turned = ct[:, :, :, lanes].reshape(lines, block).T
        for which, left, right in (
            (0, normal_turned, gb),
            (1, normal_turned, ub),
            (2, outer_turned, hid),
        ):
            for start, size in cuts_of(share, 512):
                w[which, group, :, :, :, :, start : start + size] = (
                    jnp.dot(
                        left,
                        right[:, :, start : start + size].reshape(lines, size),
                        preferred_element_type=floats,
                    )
                    .astype(halves)
                    .reshape(2, 2, 2, -1, size)
                )
        handed[dz] = courier.copy(
            w.at[:, group, :, :, 1 - c], cbuf.at[dz], place.across["c"]
        )

    def settle(position):
        dz = orders[position]
        group = lax.rem(z + dz, nz)
        handed[dz].wait_recv()
        for which in range(3):
            w[which, group, :, :, c] = (
                w[which, group, :, :, c].astype(floats) + cbuf[dz, which].astype(floats)
            ).astype(halves)
        if position < early:
            crossed[position] = courier.copy(
                w.at[:, group, 1 - x, :, c], xbuf.at[position], place.across["x"]
            )
        else:
            save(w.at[:, group, :, :, c], grads_ref.at[:, position - early])

    for position in range(nz):
        product(orders[position])
        sum_on((position + 1) % nz)
        if position:
            settle(position - 1)
    settle(nz - 1)
    for position in range(early):
        group = lax.rem(z + orders[position], nz)
        crossed[position].wait_recv()
        for which in range(3):
            w[which, group, x, :, c] = (
                w[which, group, x, :, c].astype(floats) + xbuf[position, which].astype(floats)
            ).astype(halves)
        save(w.at[:, group, x, :, c], done_ref.at[:, position])
    for dz in range(1, nz):
        final[dz].wait_recv()
        back_ref[...] += zbuf[dz - 1].astype(floats)
    for made in saves:
        made.wait()
    courier.finish()


class LineSum:
    def __init__(self, courier, place, parts, spot, above, below):
        self.courier, self.place, self.parts, self.spot = courier, place, parts, spot
        self.arrivals = {1: above, -1: below}
        self.sent = {}

    def add(self, target, way):
        nz = self.place.nz
        spot = self.spot(target)
        arrived = self.arrivals[way][target - 1 if way == 1 else target]
        self.parts[spot] = (self.parts[spot].astype(floats) + arrived.astype(floats)).astype(
            self.parts.dtype
        )

    def forward(self, target, way):
        p = self.place
        moving = p.z < target if way == 1 else p.z > target
        fed = p.z > 0 if way == 1 else p.z < p.nz - 1
        made = self.courier.make(
            self.parts.at[self.spot(target)],
            self.arrivals[way].at[target - 1 if way == 1 else target],
            p.line_at(way),
            moving,
        )
        self.sent[target, way] = made

        @pl.when(moving & fed)
        def _():
            made.raw.wait_recv()
            self.add(target, way)

        made.start()

    def forward_step(self, step):
        self.forward(self.place.nz - 1 - step, 1)
        self.forward(step, -1)

    def finish(self):
        p = self.place
        for (target, way), made in self.sent.items():
            fed = p.z > 0 if way == 1 else p.z < p.nz - 1

            @pl.when((p.z == target) & fed)
            def _(target=target, way=way, made=made):
                made.raw.wait_recv()
                self.add(target, way)


class Scatter:
    def __init__(self, courier, place, parts, core_in, side_in, above, below, last_in):
        self.courier, self.place, self.parts = courier, place, parts
        self.core_in, self.side_in, self.last_in = core_in, side_in, last_in
        every = slice(None)
        self.line = LineSum(
            courier, place, parts, lambda group: (group, every, place.y, place.c), above, below
        )
        self.groups = []
        for step in range((place.nz + 1) // 2):
            self.groups += [place.nz - 1 - step, step]
        self.core, self.side = {}, {}

    def to_core(self, group):
        p = self.place
        self.core[group] = self.courier.copy(
            self.parts.at[group, :, :, 1 - p.c], self.core_in.at[group], p.across["c"]
        )

    def add(self, spot, arrived):
        self.parts[spot] = (self.parts[spot].astype(floats) + arrived.astype(floats)).astype(
            self.parts.dtype
        )

    def sideways(self):
        p = self.place
        every = slice(None)
        for group in self.groups:
            self.core[group].wait_recv()
            self.add((group, every, every, p.c), self.core_in[group])
            self.side[group] = self.courier.copy(
                self.parts.at[group, :, 1 - p.y, p.c], self.side_in.at[group], p.across["y"]
            )

    def along(self):
        p = self.place
        for group in self.groups:
            self.side[group].wait_recv()
            self.add((group, slice(None), p.y, p.c), self.side_in[group])

    def across(self):
        p = self.place
        self.line.finish()
        self.last = self.courier.copy(
            self.parts.at[p.z, 1 - p.x, p.y, p.c], self.last_in, p.across["x"]
        )

    def own(self):
        p = self.place
        return self.parts[p.z, p.x, p.y, p.c].astype(floats)

    def other(self):
        self.last.wait_recv()
        return self.last_in[...].astype(floats)


def gather_pieces(values, piece, devices):
    width = values.shape[1]
    owner = lax.div(lax.broadcasted_iota(jnp.int32, (devices, width), 1), piece)
    mine = owner == lax.broadcasted_iota(jnp.int32, (devices, width), 0)
    at = lax.broadcasted_iota(jnp.int32, (width, 128), 0)
    inner = lax.broadcasted_iota(jnp.int32, (width, 128), 1)
    chosen = (lax.rem(at, piece) == inner).astype(floats)
    rows = jnp.where(mine, values, 0.0)
    return jnp.dot(rows, chosen, preferred_element_type=floats, precision=lax.Precision.HIGHEST)


def back_kernel(
    nz,
    done_ref,
    grads_in,
    branch_ref,
    kv_ref,
    q_ref,
    m_ref,
    back_ref,
    mixed_ref,
    outer_ref,
    tokens_ref,
    xn1_ref,
    gain_ref,
    turn_ref,
    query_ref,
    pair_ref,
    share_ref,
    out_ref,
    output_ref,
    tokens_grad_ref,
    joint_grad_ref,
    merge_grad_ref,
    small_grad_ref,
    grads_ref,
    weight_m,
    weight_q,
    weight_kv,
    gown,
    gin,
    branch_own,
    branch_in,
    branch_above,
    branch_below,
    *rest,
):
    merge_bufs, query_bufs, kv_bufs, small_bufs = (rest[6 * i : 6 * i + 6] for i in range(4))
    (
        pair_sum,
        pair_half,
        pair_above,
        pair_below,
        joint_back,
        attended_back,
        mixed_both,
        back_send,
        back_in,
        sends,
        receives,
        locals_,
    ) = rest[24:]
    place = Place(nz)
    z, x, y, c = place.z, place.x, place.y, place.c
    length, model = tokens_ref.shape
    share = gown.shape[-1]
    half = GROUP * HEAD_DIM
    both = 2 * length
    block = model // nz
    depth = grads_in.shape[-2]
    devices = 8 * nz
    total_keys = nz * both
    orders = far_first(nz)
    courier = Courier(sends, receives)
    meet(place.peers())

    def group_of(dz):
        return lax.rem(z + dz, nz)

    copies = []

    def load(source, target):
        made = pltpu.make_async_copy(source, target, locals_.at[len(copies)])
        made.start()
        copies.append(made)
        return made

    merge_load = load(m_ref, weight_m)
    branch_load = load(branch_ref.at[:, y], branch_own)
    gown_load = load(grads_in.at[:, :, x], gown)
    early = 2
    late = orders[early:]
    query_load = load(q_ref, weight_q)
    kv_load = load(kv_ref, weight_kv)

    b_cross = {
        group: courier.copy(branch_ref.at[group, 1 - y], branch_in.at[group], place.across["y"])
        for group in range(nz)
    }
    g_cross, g_line, kept = {}, [], []

    def grads_across(dz):
        g_cross[dz] = courier.copy(
            grads_in.at[:, late.index(dz), 1 - x], gin.at[late.index(dz)], place.across["x"]
        )

    mine = pl.ds(pl.multiple_of((z * 2 + y) * share, 128), share)

    def grads_line(dz, rows):
        for dy in range(2):
            ty = lax.rem(y + dy, 2)
            if dz or dy:
                g_line.append(
                    courier.copy(
                        rows.at[:, ty], grads_ref.at[:, :, mine], (group_of(dz), x, ty, c)
                    )
                )
            else:
                kept.append(load(rows.at[:, ty], grads_ref.at[:, :, mine]))

    for position in range(early):
        grads_line(orders[position], done_ref.at[:, position])

    mixed = mixed_ref[...]
    second_scale = norm_parts(mixed)
    part, second_local = norm_back(back_ref[...], mixed, second_scale, gain_ref[1:2, :])
    grad = outer_ref[...].astype(floats) + part
    tokens_grad_ref[...] = grad
    mixed_both[x] = grad.astype(halves)
    mixed_cross = courier.copy(mixed_both.at[x], mixed_both.at[x], place.across["x"])
    mixed_cross.wait_recv()
    for dz in late:
        grads_across(dz)

    merge_load.wait()
    upstream_both = mixed_both[...].reshape(both, model)
    attended_back[...] = jnp.dot(
        upstream_both, weight_m[...].reshape(model, half), preferred_element_type=floats
    ).astype(halves)
    merges = Scatter(courier, place, *merge_bufs)
    queries = Scatter(courier, place, *query_bufs)
    keys_values = Scatter(courier, place, *kv_bufs)
    smalls = Scatter(courier, place, *small_bufs)

    def product_rows(scatter, left, right):
        for group in scatter.groups:
            scatter.parts[group] = (
                jnp.dot(
                    left[group * block : (group + 1) * block], right, preferred_element_type=floats
                )
                .astype(halves)
                .reshape(2, 2, 2, depth, right.shape[1])
            )
            scatter.to_core(group)

    product_rows(merges, upstream_both.T, out_ref[...].astype(halves))

    def attend(first, last):
        @pl.loop(first, last)
        def _(head):
            query = query_ref[head]
            keys = pair_ref[:, :, :HEAD_DIM].reshape(total_keys, HEAD_DIM)
            values = pair_ref[:, :, HEAD_DIM:].reshape(total_keys, HEAD_DIM)
            lanes = pl.ds(pl.multiple_of(head * HEAD_DIM, 128), HEAD_DIM)
            upstream = attended_back[:, lanes]
            delta = jnp.sum(upstream.astype(floats) * out_ref[:, lanes], axis=-1, keepdims=True)
            mass = lax.dot_general(upstream, values, last_pair, preferred_element_type=floats)
            shares = share_ref[head]
            scores = (shares.astype(floats) * (mass - delta)).astype(halves)
            query_sum = jnp.dot(scores, keys, preferred_element_type=floats) * SCALE
            cosine, sine = turn_ref[0], turn_ref[1]
            joint_back[:, lanes] = (
                query_sum * cosine + pltpu.roll(query_sum * sine, HEAD_DIM // 2, 1)
            ).astype(halves)
            pair_sum[:, :HEAD_DIM] += (
                jnp.dot(scores.T, query, preferred_element_type=floats) * SCALE
            )
            pair_sum[:, HEAD_DIM:] += jnp.dot(shares.T, upstream, preferred_element_type=floats)

    def grads_on(dz):
        at = late.index(dz)
        g_cross[dz].wait_recv()
        for which in range(3):
            gown[which, at] = (
                gown[which, at].astype(floats) + gin[at, which].astype(floats)
            ).astype(halves)
        grads_line(dz, gown.at[:, at])

    pair_sum[...] = jnp.zeros_like(pair_sum)
    attend(0, GROUP // 2)
    merges.sideways()

    attend(GROUP // 2, GROUP)

    pair_half[...] = pair_sum[...].astype(halves).reshape(nz, both, 2 * HEAD_DIM)
    pairs = LineSum(courier, place, pair_half, lambda group: (group,), pair_above, pair_below)
    pairs.forward(nz - 1, 1)
    pairs.forward(0, -1)
    turned = xn1_ref[...].T
    product_rows(queries, turned, joint_back[:, :half])
    for step in range(1, nz - 1):
        pairs.forward(nz - 1 - step, 1)
        pairs.forward(step, -1)
    branch_load.wait()
    for group in range(nz):
        b_cross[group].wait_recv()
        branch_own[group] = (
            branch_own[group].astype(floats) + branch_in[group].astype(floats)
        ).astype(halves)
    pairs.finish()
    total = pair_half[z].astype(floats)
    key_total = total[:, :HEAD_DIM]
    joint_back[:, half : half + HEAD_DIM] = (
        key_total * turn_ref[0] + pltpu.roll(key_total * turn_ref[1], HEAD_DIM // 2, 1)
    ).astype(halves)
    joint_back[:, half + HEAD_DIM :] = total[:, HEAD_DIM:].astype(halves)
    product_rows(keys_values, turned, joint_back[:, half:])
    query_load.wait()
    kv_load.wait()
    normal_back = lax.dot_general(
        joint_back[:, :half],
        weight_q[...].reshape(model, half),
        last_pair,
        preferred_element_type=floats,
    ) + lax.dot_general(
        joint_back[:, half:],
        weight_kv[...].reshape(model, 2 * HEAD_DIM),
        last_pair,
        preferred_element_type=floats,
    )
    back_send[...] = jnp.where(x == 0, normal_back[length:], normal_back[:length]).astype(halves)
    back_cross = courier.copy(back_send, back_in, place.across["x"])
    normal_own = jnp.where(x == 0, normal_back[:length], normal_back[length:])
    queries.sideways()
    keys_values.sideways()
    gown_load.wait()
    for dz in late[:1]:
        grads_on(dz)

    back_cross.wait_recv()
    normal_own = normal_own + back_in[...].astype(floats)
    residual = tokens_ref[...].astype(floats)
    part, first_local = norm_back(normal_own, residual, norm_parts(residual), gain_ref[0:1, :])
    tokens_grad_ref[...] += part

    local = jnp.sum(joint_back[...].astype(floats), axis=0, keepdims=True)
    pieces_of = []
    for first, width in ((0, half), (half, HEAD_DIM), (half + HEAD_DIM, HEAD_DIM)):
        for side in range(2):
            pieces_of.append(jnp.where(x == side, local[:, first : first + width], 0.0))
    bias_local = jnp.concatenate(pieces_of, axis=1)
    pieces = jnp.zeros((devices * 8, 128), floats)
    for which, values in ((0, bias_local), (1, first_local), (2, second_local)):
        mine_rows = gather_pieces(values, values.shape[1] // devices, devices)
        at = lax.broadcasted_iota(jnp.int32, (devices * 8, devices), 0)
        wanted = lax.broadcasted_iota(jnp.int32, (devices * 8, devices), 1) * 8 + which
        pieces = pieces + jnp.dot(
            (at == wanted).astype(floats),
            mine_rows,
            preferred_element_type=floats,
            precision=lax.Precision.HIGHEST,
        )
    smalls.parts[...] = pieces.reshape(nz, 2, 2, 2, 8, 128)
    for group in smalls.groups:
        smalls.to_core(group)
    for dz in late[1:]:
        grads_on(dz)
    smalls.sideways()
    for made in (merges, queries, keys_values):
        made.along()
    branches = LineSum(
        courier, place, branch_own, lambda group: (group,), branch_above, branch_below
    )
    smalls.along()
    for step in range(nz - 1):
        for line in (smalls.line, keys_values.line, queries.line, merges.line, branches):
            line.forward_step(step)
    for made in (merges, queries, keys_values, smalls):
        made.across()
    branches.finish()
    output_ref[...] = (mixed_ref[...] + branch_own[z].astype(floats)).astype(halves)
    for ref, made, pieces in (
        (merge_grad_ref, merges, [(0, half)]),
        (joint_grad_ref, queries, [(0, half)]),
        (joint_grad_ref, keys_values, KV_PIECES),
    ):
        for side, values in ((x, made.own()), (1 - x, made.other())):
            at = 0
            for first, width in pieces:
                lanes = pl.ds(pl.multiple_of(first + side * width, 128), width)
                ref[:, lanes] = values[:, at : at + width]
                at += width
    small_grad_ref[...] = smalls.own() + smalls.other()
    for made in g_line:
        made.wait_recv()
    for made in kept:
        made.wait()
    courier.finish()


def padded_share(hidden_width, team):
    return -(-hidden_width // (team * 128)) * 128


def body_kernels(
    tokens,
    segments,
    joint_matrix,
    joint_bias,
    merge_matrix,
    norm_first,
    norm_second,
    gate_matrix,
    up_matrix,
    down_matrix,
    cotangent,
):
    length, model = tokens.shape[1:]
    depth, joint_width = joint_matrix.shape
    hidden_width = gate_matrix.shape[1]
    nz = lax.axis_size("z")
    share = padded_share(hidden_width, 2 * nz)
    half = GROUP * HEAD_DIM
    pair_width = 2 * HEAD_DIM
    both = 2 * length
    keys = nz * both
    vmem = pl.BlockSpec(memory_space=pltpu.VMEM)
    anywhere = pl.BlockSpec(memory_space=pl.ANY)
    blocks = (nz, 2, 2, 2)

    def shape(dims, kind=halves):
        return jax.ShapeDtypeStruct(dims, kind)

    def semaphores(count, loads):
        return [
            pltpu.SemaphoreType.DMA((count,)),
            pltpu.SemaphoreType.DMA((count,)),
            pltpu.SemaphoreType.DMA((loads,)),
        ]

    def params(number):
        return pltpu.CompilerParams(
            collective_id=number, has_side_effects=True, vmem_limit_bytes=VMEM_LIMIT
        )

    stack = jnp.stack([gate_matrix, up_matrix, down_matrix.T])
    stack = jnp.pad(stack, ((0, 0), (0, 0), (0, 2 * nz * share - hidden_width)))

    def lane_row(values):
        return jnp.pad(values.astype(floats), (0, 128 - values.shape[0]))

    own_labels = segments[0]
    empty = jnp.zeros((128,), floats)
    small = jnp.stack(
        [lane_row(v) for v in (joint_bias, norm_first, norm_second, own_labels)] + [empty] * 4
    )
    inverse = theta ** -(np.arange(HEAD_DIM // 2) * (2.0 / HEAD_DIM))
    inverse = jnp.asarray(np.tile(inverse, 2)[None], floats)
    outer = cotangent[0]
    (
        w,
        team_outer,
        kv_all,
        q_all,
        m_all,
        xn1,
        xn2,
        mixed,
        gains,
        turns,
        queries,
        pair,
        shares,
        summed,
    ) = pl.pallas_call(
        functools.partial(attention_kernel, nz),
        name="attention_forward",
        out_shape=(
            shape((3,) + blocks + (depth, share)),
            shape((nz, 2, length, model)),
            shape(blocks + (depth, pair_width)),
            shape(blocks + (depth, half)),
            shape(blocks + (depth, half)),
            shape((both, model)),
            shape((length, model)),
            shape((length, model), floats),
            shape((8, model), floats),
            shape((2, both, HEAD_DIM), floats),
            shape((GROUP, both, HEAD_DIM)),
            shape((nz, both, pair_width)),
            shape((GROUP, both, keys)),
            shape((both, half), floats),
        ),
        in_specs=[anywhere] * 3 + [vmem] * 4,
        out_specs=(anywhere,) * 5 + (vmem,) * 9,
        scratch_shapes=[
            pltpu.VMEM(blocks + (depth, pair_width), halves),
            pltpu.VMEM(blocks + (depth, half), halves),
            pltpu.VMEM(blocks + (depth, half), halves),
            pltpu.VMEM(blocks + (8, 128), floats),
            pltpu.VMEM((both, keys), floats),
            pltpu.VMEM((2, length, model), halves),
            pltpu.VMEM((length, model), halves),
            pltpu.VMEM((length, model), halves),
        ]
        + semaphores(137, 10),
        compiler_params=params(0),
    )(stack, joint_matrix, merge_matrix.T, small, inverse, tokens[0], outer)

    lines = 2 * length
    back, branch, done, grads = pl.pallas_call(
        functools.partial(feed_kernel, nz),
        name="feed_forward",
        out_shape=(
            shape((length, model), floats),
            shape((nz, 2, length, model)),
            shape((3, 2, 2, depth, share)),
            shape((3, nz - 2, 2, 2, depth, share)),
        ),
        in_specs=[anywhere, anywhere, vmem],
        out_specs=(vmem, vmem, anywhere, anywhere),
        scratch_shapes=[
            pltpu.VMEM((3,) + blocks + (depth, share), halves),
            pltpu.VMEM((nz, 2, length, model), halves),
            pltpu.VMEM((nz, 2, length, model), halves),
            pltpu.VMEM((nz, lines, share), halves),
            pltpu.VMEM((nz, lines, share), halves),
            pltpu.VMEM((nz, lines, share), halves),
            pltpu.VMEM((nz, 2, length, model), halves),
            pltpu.VMEM((nz, length, model), halves),
            pltpu.VMEM((nz, length, model), halves),
            pltpu.VMEM((nz - 1, length, model), halves),
            pltpu.VMEM((nz, 3, 2, 2, depth, share), halves),
            pltpu.VMEM((2, 3, 2, depth, share), halves),
        ]
        + semaphores(30, 8),
        compiler_params=params(1),
    )(w, team_outer, xn2)

    def sums(rows, width, kind=halves):
        return [
            pltpu.VMEM(blocks + (rows, width), kind),
            pltpu.VMEM((nz, 2, 2, rows, width), kind),
            pltpu.VMEM((nz, 2, rows, width), kind),
            pltpu.VMEM((nz - 1, 2, rows, width), kind),
            pltpu.VMEM((nz - 1, 2, rows, width), kind),
            pltpu.VMEM((rows, width), kind),
        ]

    output, tokens_grad, joint_grad, merge_grad, small_grad, grads = pl.pallas_call(
        functools.partial(back_kernel, nz),
        name="attention_backward",
        out_shape=(
            shape((length, model)),
            shape((length, model), floats),
            shape((depth, joint_width), floats),
            shape((depth, QUERY_WIDTH), floats),
            shape((8, 128), floats),
            shape((3, depth, 2 * nz * share)),
        ),
        in_specs=[anywhere] * 6 + [vmem] * 11,
        out_specs=(vmem,) * 5 + (anywhere,),
        scratch_shapes=[
            pltpu.VMEM(blocks + (depth, half), halves),
            pltpu.VMEM(blocks + (depth, half), halves),
            pltpu.VMEM(blocks + (depth, pair_width), halves),
            pltpu.VMEM((3, nz - 2, 2, depth, share), halves),
            pltpu.VMEM((nz - 2, 3, 2, depth, share), halves),
            pltpu.VMEM((nz, length, model), halves),
            pltpu.VMEM((nz, length, model), halves),
            pltpu.VMEM((nz - 1, length, model), halves),
            pltpu.VMEM((nz - 1, length, model), halves),
        ]
        + sums(depth, half)
        + sums(depth, half)
        + sums(depth, pair_width)
        + sums(8, 128, floats)
        + [
            pltpu.VMEM((keys, pair_width), floats),
            pltpu.VMEM((nz, both, pair_width), halves),
            pltpu.VMEM((nz - 1, both, pair_width), halves),
            pltpu.VMEM((nz - 1, both, pair_width), halves),
            pltpu.VMEM((both, half + pair_width), halves),
            pltpu.VMEM((both, half), halves),
            pltpu.VMEM((2, length, model), halves),
            pltpu.VMEM((length, model), halves),
            pltpu.VMEM((length, model), halves),
        ]
        + semaphores(90, 6),
        compiler_params=params(2),
    )(
        done,
        grads,
        branch,
        kv_all,
        q_all,
        m_all,
        back,
        mixed,
        outer,
        tokens[0],
        xn1,
        gains,
        turns,
        queries,
        pair,
        shares,
        summed,
    )
    grads = [grads[which, :, :hidden_width].astype(floats) for which in range(3)]
    return (
        output[None],
        tokens_grad[None],
        joint_grad,
        small_grad[0, : joint_bias.shape[0]],
        merge_grad.T,
        small_grad[1, :depth],
        small_grad[2, :depth],
        grads[0],
        grads[1],
        grads[2].T,
    )


def body_plain(
    tokens,
    segments,
    joint_matrix,
    joint_bias,
    merge_matrix,
    norm_first,
    norm_second,
    gate_matrix,
    up_matrix,
    down_matrix,
    cotangent,
):
    residual = tokens[0].astype(floats)
    length, model = residual.shape
    depth = joint_matrix.shape[0]
    joint_width = joint_matrix.shape[1]
    hidden_width = gate_matrix.shape[1]
    z_count = lax.axis_size("z")
    team = lax.axis_size(TEAM)
    share = hidden_width // team
    own_labels = segments[0]
    labels = lax.all_gather(own_labels, SEQ, axis=0, tiled=True)
    offset = lax.axis_index(SEQ) * length
    places = offset + jnp.arange(length, dtype=jnp.int32)
    positions = lax.dynamic_slice_in_dim(row_positions(labels), offset, length, 0)
    cosine, sine = rotary(positions, HEAD_DIM)

    small = jnp.concatenate([joint_bias, norm_first, norm_second])
    small = jnp.pad(small, (0, -small.shape[0] % depth)).reshape(depth, -1)
    small_width = small.shape[1]
    packed = jnp.concatenate([joint_matrix, merge_matrix.T, small], axis=1)
    packed = lax.all_gather(packed, AXES, axis=0, tiled=True)
    joint_all = packed[:, :joint_width]
    merge_turned = packed[:, joint_width : joint_width + model]
    small = packed[:, joint_width + model :].reshape(-1, depth * small_width).astype(floats)
    bias_depth = joint_bias.shape[0]
    bias_all = small[:, :bias_depth].reshape(-1)
    gain_first = small[:, bias_depth : bias_depth + depth].reshape(-1)
    gain_second = small[:, bias_depth + depth : bias_depth + 2 * depth].reshape(-1)

    stacked = jnp.stack([gate_matrix, up_matrix, down_matrix.T], axis=1)
    stacked = stacked.reshape(depth, 3, team, share).transpose(2, 0, 1, 3)
    stacked = stacked.reshape(team, depth, 3 * share)
    stacked = lax.all_to_all(stacked, TEAM, split_axis=0, concat_axis=0, tiled=True)
    stacked = stacked.reshape(z_count, 1, team // z_count, 1, depth, 3 * share)
    stacked = lax.all_gather(stacked, "x", axis=1, tiled=True)
    stacked = lax.all_gather(stacked, "c", axis=3, tiled=True)
    stacked = stacked.reshape(model, 3 * share)
    both_all, down_turned = stacked[:, : 2 * share], stacked[:, 2 * share :]
    outer_grad = cotangent[0]
    team_outer = lax.all_gather(outer_grad, TEAM, axis=0, tiled=True)

    scale_first = norm_parts(residual)
    normal_first = (residual * scale_first * gain_first).astype(halves)
    joint = jnp.dot(normal_first, joint_all, preferred_element_type=floats) + bias_all
    query = joint[:, :QUERY_WIDTH].reshape(length, HEADS, HEAD_DIM)
    keys = joint[:, QUERY_WIDTH : QUERY_WIDTH + KEY_WIDTH].reshape(length, KV_HEADS, HEAD_DIM)
    values = joint[:, QUERY_WIDTH + KEY_WIDTH :].astype(halves)
    query = (query * cosine + turn_half(query) * sine).astype(halves)
    keys = (keys * cosine + turn_half(keys) * sine).astype(halves).reshape(length, KEY_WIDTH)
    query_group = to_groups(query)
    pair = lax.all_gather(jnp.concatenate([keys, values], axis=1), SEQ, axis=0, tiled=True)
    count = pair.shape[0]
    key_all = pair[:, :KEY_WIDTH].reshape(count, KV_HEADS, HEAD_DIM)
    value_all = pair[:, KEY_WIDTH:].reshape(count, KV_HEADS, HEAD_DIM)
    allowed = (places[:, None] >= jnp.arange(count, dtype=jnp.int32)[None, :]) & (
        own_labels[:, None] == labels[None, :]
    )
    allowed = jnp.tile(allowed, (GROUP, 1))[None]
    scores = jnp.einsum("krd,nkd->krn", query_group, key_all, preferred_element_type=floats)
    scores = jnp.where(allowed, scores * SCALE, neg)
    top = jnp.max(scores, axis=-1, keepdims=True)
    weights = jnp.where(allowed, jnp.exp(scores - top), 0.0)
    total = jnp.sum(weights, axis=-1, keepdims=True)
    shares = weights / total
    shares_half = shares.astype(halves)
    attended = jnp.einsum("krn,nkd->krd", shares_half, value_all, preferred_element_type=floats)
    attended_half = from_groups(attended, length).astype(halves)
    mixed = residual + lax.dot_general(
        attended_half, merge_turned, last_pair, preferred_element_type=floats
    )
    scale_second = norm_parts(mixed)
    normal_half = (mixed * scale_second * gain_second).astype(halves)

    team_normal = lax.all_gather(normal_half, TEAM, axis=0, tiled=True)
    both = jnp.dot(team_normal, both_all, preferred_element_type=floats)
    gate, upper = both[:, :share], both[:, share:]
    sig = jax.nn.sigmoid(gate)
    silu = gate * sig
    hidden_half = (silu * upper).astype(halves)
    branch = lax.dot_general(hidden_half, down_turned, last_pair, preferred_element_type=floats)
    hidden_grad = jnp.dot(team_outer, down_turned, preferred_element_type=floats)
    gate_half = (hidden_grad * upper * sig * (1.0 + gate * (1.0 - sig))).astype(halves)
    upper_half = (hidden_grad * silu).astype(halves)
    both_half = jnp.concatenate([gate_half, upper_half], axis=1)
    normal_grad = lax.dot_general(both_half, both_all, last_pair, preferred_element_type=floats)
    branch = lax.psum_scatter(branch.astype(halves), TEAM, scatter_dimension=0, tiled=True)
    normal_grad = lax.psum_scatter(normal_grad.astype(halves), TEAM, scatter_dimension=0, tiled=True)
    output = (mixed + branch.astype(floats)).astype(halves)[None]
    both_grad = lax.dot_general(team_normal, both_half, first_pair, preferred_element_type=floats)
    down_grad = lax.dot_general(team_outer, hidden_half, first_pair, preferred_element_type=floats)
    grads = jnp.concatenate([both_grad, down_grad], axis=1).astype(halves)
    grads = grads.reshape(z_count, 2, team // z_count, 2, depth, 3 * share)
    grads = lax.psum_scatter(grads, "c", scatter_dimension=3, tiled=True)
    grads = lax.psum_scatter(grads, "x", scatter_dimension=1, tiled=True)
    grads = grads.reshape(team, depth, 3 * share)
    grads = lax.all_to_all(grads, TEAM, split_axis=0, concat_axis=0, tiled=True)
    grads = grads.reshape(team, depth, 3, share).transpose(2, 1, 0, 3)
    grads = grads.reshape(3, depth, hidden_width).astype(floats)

    normal_grad = normal_grad.astype(floats)
    mixed_part, second_local = norm_back(normal_grad, mixed, scale_second, gain_second)
    mixed_grad = outer_grad.astype(floats) + mixed_part
    mixed_half = mixed_grad.astype(halves)
    merge_local = lax.dot_general(
        mixed_half, attended_half, first_pair, preferred_element_type=floats
    )
    attended_grad = jnp.dot(mixed_half, merge_turned, preferred_element_type=floats).astype(halves)
    grad_group = to_groups(attended_grad.reshape(length, HEADS, HEAD_DIM))
    mass_grad = jnp.einsum("krd,nkd->krn", grad_group, value_all, preferred_element_type=floats)
    row_dots = jnp.sum(shares * mass_grad, axis=-1, keepdims=True)
    score_half = (shares * (mass_grad - row_dots)).astype(halves)
    query_sum = (
        jnp.einsum("krn,nkd->krd", score_half, key_all, preferred_element_type=floats) * SCALE
    )
    key_grad = (
        jnp.einsum("krn,krd->nkd", score_half, query_group, preferred_element_type=floats) * SCALE
    )
    value_grad = jnp.einsum("krn,krd->nkd", shares_half, grad_group, preferred_element_type=floats)
    pair_sums = jnp.concatenate(
        [key_grad.reshape(count, KEY_WIDTH), value_grad.reshape(count, KEY_WIDTH)], axis=1
    )
    pair_mine = lax.psum_scatter(
        pair_sums.astype(halves), SEQ, scatter_dimension=0, tiled=True
    ).astype(floats)
    key_back = pair_mine[:, :KEY_WIDTH].reshape(length, KV_HEADS, HEAD_DIM)
    value_back = pair_mine[:, KEY_WIDTH:]
    query_back = from_groups(query_sum, length).reshape(length, HEADS, HEAD_DIM)
    query_back = query_back * cosine + unturn_half(query_back * sine)
    key_back = key_back * cosine + unturn_half(key_back * sine)
    joint_back = jnp.concatenate(
        [query_back.reshape(length, QUERY_WIDTH), key_back.reshape(length, KEY_WIDTH), value_back],
        axis=1,
    ).astype(halves)
    joint_local = lax.dot_general(
        normal_first, joint_back, first_pair, preferred_element_type=floats
    )
    bias_local = jnp.sum(joint_back.astype(floats), axis=0)
    normal_back = lax.dot_general(joint_back, joint_all, last_pair, preferred_element_type=floats)
    residual_part, first_local = norm_back(normal_back, residual, scale_first, gain_first)
    tokens_grad = (mixed_grad + residual_part)[None]

    small_back = jnp.concatenate(
        [
            bias_local.reshape(-1, bias_depth),
            first_local.reshape(-1, depth),
            second_local.reshape(-1, depth),
        ],
        axis=1,
    )
    small_back = jnp.pad(small_back, ((0, 0), (0, depth * small_width - small_back.shape[1])))
    small_back = small_back.reshape(-1, small_width)
    packed_grad = jnp.concatenate([joint_local, merge_local, small_back], axis=1).astype(halves)
    packed_grad = lax.psum_scatter(packed_grad, AXES, scatter_dimension=0, tiled=True).astype(floats)
    joint_grad = packed_grad[:, :joint_width]
    merge_grad = packed_grad[:, joint_width : joint_width + model].T
    small_back = packed_grad[:, joint_width + model :].reshape(-1)
    bias_grad = small_back[:bias_depth]
    first_grad = small_back[bias_depth : bias_depth + depth]
    second_grad = small_back[bias_depth + depth : bias_depth + 2 * depth]
    return (
        output,
        tokens_grad,
        joint_grad,
        bias_grad,
        merge_grad,
        first_grad,
        second_grad,
        grads[0],
        grads[1],
        grads[2].T,
    )


def solution(mesh):
    seq, row = mesh.shape["seq"], mesh.shape["row"]
    fine = Mesh(mesh.devices.reshape(seq // 2, 2, row // 2, 2), AXES)
    whole = ("z", "x", "y", "c")
    placed = (
        P(ROW, SEQ, None),
        P(ROW, SEQ),
        P(whole, None),
        P(whole),
        P(None, whole),
        P(whole),
        P(whole),
        P(whole, None),
        P(whole, None),
        P(None, whole),
        P(ROW, SEQ, None),
    )
    depth = MODEL // mesh.size
    return jax.shard_map(
        body_kernels if depth % 16 == 0 else body_plain,
        mesh=fine,
        in_specs=placed,
        out_specs=(
            P(ROW, SEQ, None),
            P(ROW, SEQ, None),
            P(whole, None),
            P(whole),
            P(None, whole),
            P(whole),
            P(whole),
            P(whole, None),
            P(whole, None),
            P(None, whole),
        ),
        check_vma=False,
    )
```

```python
import functools
import math

import jax
import jax.numpy as jnp
import numpy as np
from jax import lax
from jax.experimental import pallas as pl
from jax.experimental.pallas import tpu as pltpu
from jax.sharding import Mesh, PartitionSpec as P

HEADS = 12
KV_HEADS = 2
HEAD_DIM = 128
MODEL = HEADS * HEAD_DIM
GROUP = HEADS // KV_HEADS
QUERY_WIDTH = HEADS * HEAD_DIM
KEY_WIDTH = KV_HEADS * HEAD_DIM
KV_PIECES = [(QUERY_WIDTH, HEAD_DIM), (QUERY_WIDTH + KEY_WIDTH, HEAD_DIM)]
SCALE = 1.0 / math.sqrt(HEAD_DIM)

eps = 1e-06
theta = 1000000.0
neg = -1e30
last_pair = (((1,), (1,)), ((), ()))
first_pair = (((0,), (0,)), ((), ()))
floats = jnp.float32
halves = jnp.bfloat16

AXES = ("z", "x", "y", "c")
SEQ = ("z", "x")
ROW = ("y", "c")
TEAM = ("z", "y")


def turn_half(values):
    middle = values.shape[-1] // 2
    return jnp.concatenate([-values[..., middle:], values[..., :middle]], axis=-1)


def unturn_half(values):
    middle = values.shape[-1] // 2
    return jnp.concatenate([values[..., middle:], -values[..., :middle]], axis=-1)


def row_positions(labels):
    length = labels.shape[0]
    places = jnp.arange(length, dtype=jnp.int32)
    change = jnp.concatenate([jnp.ones((1,), dtype=jnp.bool_), labels[1:] != labels[:-1]])
    starts = lax.cummax(jnp.where(change, places, 0), axis=0)
    return places - starts


def rotary(positions, width):
    inverse = jnp.power(
        jnp.float32(theta), -(jnp.arange(width // 2, dtype=jnp.float32) * (2.0 / width))
    )
    angle = positions.astype(jnp.float32)[:, None] * inverse[None, :]
    angle = jnp.concatenate([angle, angle], axis=1)[:, None, :]
    return (jnp.cos(angle), jnp.sin(angle))


def to_groups(values):
    length = values.shape[0]
    return (
        values.reshape(length, KV_HEADS, GROUP, HEAD_DIM)
        .transpose(1, 2, 0, 3)
        .reshape(KV_HEADS, GROUP * length, HEAD_DIM)
    )


def from_groups(values, length):
    return (
        values.reshape(KV_HEADS, GROUP, length, HEAD_DIM)
        .transpose(2, 0, 1, 3)
        .reshape(length, QUERY_WIDTH)
    )


def norm_parts(values):
    return lax.rsqrt(jnp.mean(values * values, axis=-1, keepdims=True) + eps)


def norm_back(upstream, values, scale, gain):
    scaled = upstream * gain
    inner = jnp.mean(scaled * values, axis=-1, keepdims=True)
    part = scale * scaled - values * (scale * scale * scale) * inner
    gain_grad = jnp.sum(upstream * values * scale, axis=0, keepdims=True)
    return part, gain_grad


MESH = pl.DeviceIdType.MESH
VMEM_LIMIT = 60 * 2**20


def coordinates():
    return tuple(lax.axis_index(name) for name in AXES)


class Sent:
    def __init__(self, raw, when):
        self.raw, self.when = raw, when

    def under(self, act):
        if self.when is None:
            act()
        else:
            pl.when(self.when)(act)

    def start(self):
        self.under(self.raw.start)

    def wait_recv(self):
        self.under(self.raw.wait_recv)

    def wait_send(self):
        self.under(self.raw.wait_send)


class Courier:
    def __init__(self, sends, receives):
        self.sends, self.receives, self.copies = sends, receives, []

    def make(self, source, target, device, when=None):
        place = len(self.copies)
        raw = pltpu.make_async_remote_copy(
            src_ref=source,
            dst_ref=target,
            send_sem=self.sends.at[place],
            recv_sem=self.receives.at[place],
            device_id=device,
            device_id_type=MESH,
        )
        made = Sent(raw, when)
        self.copies.append(made)
        return made

    def copy(self, source, target, device, when=None):
        made = self.make(source, target, device, when)
        made.start()
        return made

    def finish(self):
        for made in self.copies:
            made.wait_send()


def meet(devices):
    barrier = pltpu.get_barrier_semaphore()
    for device in devices:
        pl.semaphore_signal(barrier, inc=1, device_id=device, device_id_type=MESH)
    pl.semaphore_wait(barrier, len(devices))


def far_first(nz):
    return sorted(range(nz), key=lambda dz: (dz == 0, abs(2 * dz - nz)))


def near_first(nz):
    return [sorted(range(nz), key=lambda group: (abs(group - at), -group)) for at in range(nz)]


def cuts_of(width, step):
    return [(start, min(step, width - start)) for start in range(0, width, step)]


class Line:
    def __init__(self, courier, place, spot):
        self.courier, self.place, self.spot = courier, place, spot
        self.sent = {}

    def items(self):
        p = self.place
        found = [(0, 0, p.z, None)]
        for step in range(1, p.nz):
            found.append((step, 1, lax.max(p.z - step, 0), p.z >= step))
            found.append((step, -1, lax.min(p.z + step, p.nz - 1), p.z + step < p.nz))
        return found

    def send(self, step, way, group, also=None):
        p = self.place
        inside = p.z < p.nz - 1 if way == 1 else p.z > 0
        if also is not None:
            inside = inside & also
        spot = self.spot(group)
        self.sent[step, way] = self.courier.copy(spot, spot, p.line_at(way), inside)

    def start(self):
        self.send(0, 1, self.place.z)
        self.send(0, -1, self.place.z)

    def arrive(self, step, way, group, exists):
        made = self.sent[step - 1, way]

        @pl.when(exists)
        def _():
            made.raw.wait_recv()

        if step < self.place.nz - 1:
            self.send(step, way, group, exists)


class Gather:
    def __init__(self, courier, place, source, buffer):
        self.courier, self.place = courier, place
        self.source, self.buffer = source, buffer
        self.line = Line(courier, place, lambda group: buffer.at[group, :, place.y, place.c])
        self.side, self.core = {}, {}

    def start(self):
        p = self.place
        spot = self.buffer.at[p.z, p.x, p.y, p.c]
        self.cross = [
            self.courier.copy(source, spot.at[:, lanes], p.across["x"])
            for source, lanes in self.source
        ]

    def along(self):
        for made in self.cross:
            made.wait_recv()
        self.line.start()
        self.sideways(self.line.items()[0])

    def sideways(self, item):
        step, way, group, exists = item
        p = self.place
        spot = self.buffer.at[group, :, p.y, p.c]
        self.side[step, way] = self.courier.copy(spot, spot, p.across["y"], exists)

    def pass_on(self, step):
        for item in self.line.items():
            if item[0] == step:
                self.line.arrive(*item)
                self.sideways(item)

    def to_core(self):
        p = self.place
        for item in self.line.items():
            step, way, group, exists = item
            self.side[step, way].wait_recv()
            spot = self.buffer.at[group, :, :, p.c]
            self.core[step, way] = self.courier.copy(spot, spot, p.across["c"], exists)

    def done(self):
        for made in self.core.values():
            made.wait_recv()


class Place:
    def __init__(self, nz):
        self.nz = nz
        self.z, self.x, self.y, self.c = z, x, y, c = coordinates()
        self.across = {"x": (z, 1 - x, y, c), "y": (z, x, 1 - y, c), "c": (z, x, y, 1 - c)}

    def line(self, dz, dy=0):
        y = lax.rem(self.y + dy, 2) if dy else self.y
        return (lax.rem(self.z + dz, self.nz), self.x, y, self.c)

    def line_at(self, way):
        return (lax.rem(self.z + self.nz + way, self.nz), self.x, self.y, self.c)

    def peers(self):
        team = [self.line(dz, dy) for dz in range(self.nz) for dy in range(2)]
        return team[1:] + [self.across["x"], self.across["c"]]


def spread(values, piece, width):
    devices, lanes = values.shape
    at = lax.broadcasted_iota(jnp.int32, (lanes, width), 1)
    inner = lax.broadcasted_iota(jnp.int32, (lanes, width), 0)
    chosen = (lax.rem(at, piece) == inner).astype(floats).astype(halves)
    repeated = jnp.dot(values.astype(halves), chosen, preferred_element_type=floats)
    owner = lax.div(lax.broadcasted_iota(jnp.int32, (devices, width), 1), piece)
    mine = owner == lax.broadcasted_iota(jnp.int32, (devices, width), 0)
    return jnp.sum(jnp.where(mine, repeated, 0.0), axis=0, keepdims=True)


def attention_kernel(
    nz,
    stack_ref,
    joint_ref,
    merge_ref,
    small_ref,
    inverse_ref,
    tokens_ref,
    outer_ref,
    w_ref,
    ct_ref,
    kv_out,
    query_out,
    merge_out,
    xn1_ref,
    xn2_ref,
    mixed_ref,
    gain_ref,
    turn_ref,
    query_ref,
    pair_ref,
    share_ref,
    out_ref,
    joint_kv,
    joint_q,
    merge,
    small,
    bias_mask,
    tokens_all,
    mixed_send,
    mixed_in,
    sends,
    receives,
    locals_,
):
    place = Place(nz)
    z, x, y, c = place.z, place.x, place.y, place.c
    length, model = tokens_ref.shape
    depth, joint_width = joint_ref.shape
    share = w_ref.shape[-1]
    half = GROUP * HEAD_DIM
    both = 2 * length
    total_keys = nz * both
    courier = Courier(sends, receives)
    devices = 8 * nz
    meet(place.peers())

    own_copies = []

    def keep(source, target):
        made = pltpu.make_async_copy(source, target, locals_.at[len(own_copies)])
        made.start()
        own_copies.append(made)
        return made

    def columns(tz, ty):
        return pl.ds(pl.multiple_of((tz * 2 + ty) * share, 128), share)

    gathers, own_waits = {}, {}

    def begin(name, ref, pieces, buffer):
        def from_side(side):
            found = []
            at = 0
            for first, width in pieces:
                lanes = pl.ds(pl.multiple_of(first + side * width, 128), width)
                found.append((ref.at[:, lanes], slice(at, at + width)))
                at += width
            return found

        spot = buffer.at[z, x, y, c]
        own_waits[name] = [keep(own, spot.at[:, lanes]) for own, lanes in from_side(x)]
        gathers[name] = Gather(courier, place, from_side(1 - x), buffer)
        gathers[name].start()

    own_waits["small"] = [keep(small_ref, small.at[z, x, y, c])]
    gathers["small"] = Gather(courier, place, [(small_ref, slice(None))], small)
    gathers["small"].start()
    begin("kv", joint_ref, KV_PIECES, joint_kv)
    token_cross = courier.copy(tokens_ref, tokens_all.at[x], place.across["x"])
    begin("q", joint_ref, [(0, half)], joint_q)
    begin("m", merge_ref, [(0, half)], merge)
    tokens_all[x] = tokens_ref[...]
    w_own = keep(stack_ref.at[:, :, columns(z, y)], w_ref.at[:, z, x, y, c])
    ct_own = keep(outer_ref, ct_ref.at[z, y])

    direct, w_cross, w_hand = {}, {}, {}

    def give(dz, dy):
        device = place.line(dz, dy)
        direct[dz, dy] = courier.copy(
            stack_ref.at[:, :, columns(device[0], device[2])], w_ref.at[:, z, x, y, c], device
        )

    def w_spot(dz, dy, side):
        return w_ref.at[:, lax.rem(z + nz - dz, nz), side, lax.rem(y + dy, 2), c]

    def take(dz, dy):
        if dz or dy:
            direct[dz, dy].wait_recv()
        spot = w_spot(dz, dy, x)
        w_cross[dz, dy] = courier.copy(spot, spot, place.across["x"])
        w_hand[dz, dy, 0] = courier.copy(spot, spot, place.across["c"])

    def hand(dz, dy):
        w_cross[dz, dy].wait_recv()
        spot = w_spot(dz, dy, 1 - x)
        w_hand[dz, dy, 1] = courier.copy(spot, spot, place.across["c"])

    give(0, 1)
    give(1, 0)
    for name in ("small", "kv"):
        for made in own_waits[name]:
            made.wait()
        gathers[name].along()
    token_cross.wait_recv()
    tokens_both = tokens_all[...].reshape(both, model).astype(floats)
    hat = tokens_both * norm_parts(tokens_both)
    for name in ("small", "kv"):
        gathers[name].pass_on(1)
    for made in own_waits["q"] + own_waits["m"]:
        made.wait()
    gathers["q"].along()
    for step in range(2, nz):
        for name in ("small", "kv"):
            gathers[name].pass_on(step)
    for name in ("small", "kv"):
        gathers[name].to_core()
    w_own.wait()
    take(0, 0)
    for step in range(1, nz):
        gathers["q"].pass_on(step)
    for name in ("small", "kv"):
        gathers[name].done()
    take(0, 1)
    give(1, 1)

    pieces = small[...].reshape(devices * 8, 128).astype(halves)

    def row_of(which):
        at = lax.broadcasted_iota(jnp.int32, (devices, devices * 8), 1)
        wanted = lax.broadcasted_iota(jnp.int32, (devices, devices * 8), 0) * 8 + which
        chosen = (at == wanted).astype(floats).astype(halves)
        return jnp.dot(chosen, pieces, preferred_element_type=floats)

    gain_first = spread(row_of(1), depth, model)
    gain_second = spread(row_of(2), depth, model)
    bias = spread(row_of(0), joint_width // devices, joint_width)
    gain_ref[0:1, :] = gain_first
    gain_ref[1:2, :] = gain_second

    def mine(first, width):
        return jnp.where(x == 0, bias[:, first : first + width], bias[:, first + width : first + 2 * width])

    bias_query = mine(0, half)
    bias_key = mine(QUERY_WIDTH, HEAD_DIM)
    bias_value = mine(QUERY_WIDTH + KEY_WIDTH, HEAD_DIM)
    label = jnp.concatenate([small[z, side, y, c].T[:, 3:4] for side in range(2)], axis=0)
    start = jnp.zeros((both, 1), floats)
    rows_at = z * both + lax.broadcasted_iota(jnp.int32, (both, length), 0)
    lanes_at = lax.broadcasted_iota(jnp.int32, (both, length), 1)
    for block in range(2 * nz):
        keys_label = small[block // 2, block % 2, y, c, 3:4, :]
        start = start + jnp.sum((keys_label < label).astype(floats), axis=1, keepdims=True)
        allowed = (keys_label == label) & (rows_at >= block * length + lanes_at)
        bias_mask[:, block * length : (block + 1) * length] = jnp.where(allowed, 0.0, neg)
    place_at = (z * both + lax.broadcasted_iota(jnp.int32, (both, 1), 0)).astype(floats)
    angle = (place_at - start) * inverse_ref[...]
    cosine = jnp.cos(angle)
    lane = lax.broadcasted_iota(jnp.int32, (both, HEAD_DIM), 1)
    sine = jnp.where(lane < HEAD_DIM // 2, -1.0, 1.0) * jnp.sin(angle)
    turn_ref[0] = cosine
    turn_ref[1] = sine

    def turned(values):
        return values * cosine + pltpu.roll(values, HEAD_DIM // 2, 1) * sine

    xn1_ref[...] = (hat * gain_first).astype(halves)
    pair = jnp.dot(
        xn1_ref[...], joint_kv[...].reshape(model, 2 * HEAD_DIM), preferred_element_type=floats
    )
    pair_ref[z, :, :HEAD_DIM] = turned(pair[:, :HEAD_DIM] + bias_key).astype(halves)
    pair_ref[z, :, HEAD_DIM:] = (pair[:, HEAD_DIM:] + bias_value).astype(halves)
    pairs = Line(courier, place, lambda group: pair_ref.at[group])
    pairs.start()
    gathers["q"].to_core()
    gathers["m"].along()
    for item in pairs.items()[1:3]:
        pairs.arrive(*item)
    take(1, 0)
    give(3, 0)
    for item in pairs.items()[3:]:
        pairs.arrive(*item)
    gathers["m"].pass_on(1)
    gathers["q"].done()

    query = jnp.dot(xn1_ref[...], joint_q[...].reshape(model, half), preferred_element_type=floats)
    query = query + bias_query
    for head in range(GROUP):
        query_ref[head] = turned(query[:, head * HEAD_DIM : (head + 1) * HEAD_DIM]).astype(halves)
    for step in range(2, nz):
        gathers["m"].pass_on(step)
    take(1, 1)
    give(3, 1)
    give(2, 0)
    outers = Line(courier, place, lambda group: ct_ref.at[group, y])
    ct_side = {}

    def ct_on(item):
        step, way, group, exists = item
        if step:
            outers.arrive(*item)
        spot = ct_ref.at[group, y]
        ct_side[step, way] = courier.copy(spot, spot, place.across["y"], exists)

    ct_own.wait()
    ct_on(outers.items()[0])
    gathers["m"].to_core()
    hand(0, 0)
    hand(0, 1)

    def attend(first, last):
        @pl.loop(first, last)
        def _(head):
            keys = pair_ref[:, :, :HEAD_DIM].reshape(total_keys, HEAD_DIM)
            values = pair_ref[:, :, HEAD_DIM:].reshape(total_keys, HEAD_DIM)
            scores = lax.dot_general(
                query_ref[head], keys, last_pair, preferred_element_type=floats
            )
            scores = scores * SCALE + bias_mask[...]
            top = jnp.max(scores, axis=-1, keepdims=True)
            raised = jnp.exp(scores - top)
            shares = (raised / jnp.sum(raised, axis=-1, keepdims=True)).astype(halves)
            share_ref[head] = shares
            lanes = pl.ds(pl.multiple_of(head * HEAD_DIM, 128), HEAD_DIM)
            out_ref[:, lanes] = jnp.dot(shares, values, preferred_element_type=floats)

    attend(0, GROUP // 2)
    take(3, 0)
    give(2, 1)
    attend(GROUP // 2, GROUP)
    outers.start()
    gathers["m"].done()
    saves = [keep(joint_kv, kv_out), keep(joint_q, query_out), keep(merge, merge_out)]
    merged = lax.dot_general(
        out_ref[...].astype(halves),
        merge[...].reshape(model, half),
        last_pair,
        preferred_element_type=floats,
    )
    mixed_ref[...] = jnp.where(x == 0, merged[:length], merged[length:])
    mixed_send[...] = jnp.where(x == 0, merged[length:], merged[:length]).astype(halves)
    mixed_cross = courier.copy(mixed_send, mixed_in, place.across["x"])
    take(3, 1)
    hand(1, 0)
    for item in outers.items()[1:3]:
        ct_on(item)
    mixed_cross.wait_recv()
    mixed = tokens_ref[...].astype(floats) + (mixed_ref[...] + mixed_in[...].astype(floats))
    mixed_ref[...] = mixed
    xn2_ref[...] = (mixed * norm_parts(mixed) * gain_second).astype(halves)
    take(2, 0)
    hand(1, 1)
    for item in outers.items()[3:5]:
        ct_on(item)
    hand(3, 0)
    take(2, 1)
    for item in outers.items()[5:]:
        ct_on(item)
    for spot in ((3, 1), (2, 0), (2, 1)):
        hand(*spot)
    for made in w_hand.values():
        made.wait_recv()
    for made in ct_side.values():
        made.wait_recv()
    for made in saves:
        made.wait()
    courier.finish()


def feed_kernel(
    nz,
    w_ref,
    ct_ref,
    normal_ref,
    back_ref,
    branch_ref,
    done_ref,
    grads_ref,
    w,
    xn,
    ct,
    hid,
    gb,
    ub,
    part,
    ybuf,
    zsend,
    zbuf,
    cbuf,
    xbuf,
    sends,
    receives,
    locals_,
):
    place = Place(nz)
    z, x, y, c = place.z, place.x, place.y, place.c
    length, model = normal_ref.shape
    share = w.shape[-1]
    block = model // nz
    lines = 2 * length * nz
    courier = Courier(sends, receives)

    def source(dz):
        return lax.rem(z + nz - dz, nz)

    meet([place.line(dz) for dz in range(1, nz)] + [place.across[name] for name in "xyc"])
    xn[z, y] = normal_ref[...]
    blocks = Line(courier, place, lambda group: xn.at[group, y])
    blocks.start()
    side = {}

    def pass_on(step):
        for item in blocks.items():
            if item[0] == step:
                way, group, exists = item[1:]
                if step:
                    blocks.arrive(*item)
                spot = xn.at[group, y]
                side[step, way] = courier.copy(spot, spot, place.across["y"], exists)

    pass_on(0)
    groups = near_first(nz)

    def group_at(number):
        return sum(jnp.where(z == at, groups[at][number], 0) for at in range(nz))

    def wait_for(number):
        for at in range(nz):
            gap = groups[at][number] - at
            made = side[abs(gap), 0 if gap == 0 else (1 if gap < 0 else -1)]
            pl.when(z == at)(made.raw.wait_recv)

    loads = [
        pltpu.make_async_copy(w_ref.at[which], w.at[which], locals_.at[which])
        for which in range(3)
    ] + [pltpu.make_async_copy(ct_ref, ct, locals_.at[3])]
    for made in loads:
        made.start()
    pass_on(1)
    for made in loads:
        made.wait()

    def weight(which, start, size):
        return w[which, :, :, :, :, :, start : start + size].reshape(model, size)

    half = nz // 2
    scatter = {}

    def scatter_on(dz):
        group = group_at(dz)
        scatter[dz] = courier.copy(
            part.at[group, 1 - y], ybuf.at[group], place.across["y"]
        )

    for dz in range(nz):
        group = group_at(dz)
        wait_for(dz)
        for start, size in cuts_of(share, 256):
            normal = xn[group].reshape(2 * length, model)
            outer = ct[group].reshape(2 * length, model)
            gate = jnp.dot(normal, weight(0, start, size), preferred_element_type=floats)
            upper = jnp.dot(normal, weight(1, start, size), preferred_element_type=floats)
            hidden_back = jnp.dot(outer, weight(2, start, size), preferred_element_type=floats)
            sig = 1.0 / (1.0 + jnp.exp(-gate))
            silu = gate * sig
            spot = (group, slice(None), slice(start, start + size))
            hid[spot] = (silu * upper).astype(halves)
            gb[spot] = (hidden_back * upper * (sig * (1.0 + gate * (1.0 - sig)))).astype(halves)
            ub[spot] = (hidden_back * silu).astype(halves)

        @pl.loop(0, 2)
        def _(step):
            rows = pl.ds(step * half, half)
            lanes = pl.ds(pl.multiple_of(step * (model // 2), 128), model // 2)

            def turned(which):
                return w[which, rows].reshape(model // 2, share)

            both = lax.dot_general(
                gb[group], turned(0), last_pair, preferred_element_type=floats
            ) + lax.dot_general(ub[group], turned(1), last_pair, preferred_element_type=floats)
            part[group, :, :, lanes] = both.astype(halves).reshape(2, length, model // 2)

        if dz:
            scatter_on(dz)
        if dz + 2 < nz:
            pass_on(dz + 2)

    scatter_on(0)

    final = {
        dz: courier.make(
            zsend.at[source(dz)], zbuf.at[dz - 1], (source(dz), x, y, c)
        )
        for dz in range(1, nz)
    }

    def sum_on(dz):
        group = group_at(dz)
        scatter[dz].wait_recv()
        total = part[group, y].astype(floats) + ybuf[group].astype(floats)
        if dz == 0:
            back_ref[...] = total
        else:
            zsend[group] = total.astype(halves)
            for apart, made in final.items():
                pl.when(source(apart) == group)(made.raw.start)

    for group in range(nz):

        @pl.loop(0, 2)
        def _(step):
            rows = pl.ds(step * half, half)
            lanes = pl.ds(pl.multiple_of(step * (model // 2), 128), model // 2)
            product = lax.dot_general(
                hid[group],
                w[2, rows].reshape(model // 2, share),
                last_pair,
                preferred_element_type=floats,
            )
            branch_ref[group, :, :, lanes] = product.astype(halves).reshape(2, length, model // 2)

    orders = far_first(nz)
    early = 2
    handed, crossed, saves = {}, {}, []

    def save(source, target):
        made = pltpu.make_async_copy(source, target, locals_.at[4 + len(saves)])
        made.start()
        saves.append(made)

    def product(dz):
        group = lax.rem(z + dz, nz)
        lanes = pl.ds(pl.multiple_of(group * block, 128), block)
        normal_turned = xn[:, :, :, lanes].reshape(lines, block).T
        outer_turned = ct[:, :, :, lanes].reshape(lines, block).T
        for which, left, right in (
            (0, normal_turned, gb),
            (1, normal_turned, ub),
            (2, outer_turned, hid),
        ):
            for start, size in cuts_of(share, 512):
                w[which, group, :, :, :, :, start : start + size] = (
                    jnp.dot(
                        left,
                        right[:, :, start : start + size].reshape(lines, size),
                        preferred_element_type=floats,
                    )
                    .astype(halves)
                    .reshape(2, 2, 2, -1, size)
                )
        handed[dz] = courier.copy(
            w.at[:, group, :, :, 1 - c], cbuf.at[dz], place.across["c"]
        )

    def settle(position):
        dz = orders[position]
        group = lax.rem(z + dz, nz)
        handed[dz].wait_recv()
        for which in range(3):
            w[which, group, :, :, c] = (
                w[which, group, :, :, c].astype(floats) + cbuf[dz, which].astype(floats)
            ).astype(halves)
        if position < early:
            crossed[position] = courier.copy(
                w.at[:, group, 1 - x, :, c], xbuf.at[position], place.across["x"]
            )
        else:
            save(w.at[:, group, :, :, c], grads_ref.at[:, position - early])

    for position in range(nz):
        product(orders[position])
        sum_on((position + 1) % nz)
        if position:
            settle(position - 1)
    settle(nz - 1)
    for position in range(early):
        group = lax.rem(z + orders[position], nz)
        crossed[position].wait_recv()
        for which in range(3):
            w[which, group, x, :, c] = (
                w[which, group, x, :, c].astype(floats) + xbuf[position, which].astype(floats)
            ).astype(halves)
        save(w.at[:, group, x, :, c], done_ref.at[:, position])
    for dz in range(1, nz):
        final[dz].wait_recv()
        back_ref[...] += zbuf[dz - 1].astype(floats)
    for made in saves:
        made.wait()
    courier.finish()


class LineSum:
    def __init__(self, courier, place, parts, spot, above, below):
        self.courier, self.place, self.parts, self.spot = courier, place, parts, spot
        self.arrivals = {1: above, -1: below}
        self.sent = {}

    def add(self, target, way):
        nz = self.place.nz
        spot = self.spot(target)
        arrived = self.arrivals[way][target - 1 if way == 1 else target]
        self.parts[spot] = (self.parts[spot].astype(floats) + arrived.astype(floats)).astype(
            self.parts.dtype
        )

    def forward(self, target, way):
        p = self.place
        moving = p.z < target if way == 1 else p.z > target
        fed = p.z > 0 if way == 1 else p.z < p.nz - 1
        made = self.courier.make(
            self.parts.at[self.spot(target)],
            self.arrivals[way].at[target - 1 if way == 1 else target],
            p.line_at(way),
            moving,
        )
        self.sent[target, way] = made

        @pl.when(moving & fed)
        def _():
            made.raw.wait_recv()
            self.add(target, way)

        made.start()

    def forward_step(self, step):
        self.forward(self.place.nz - 1 - step, 1)
        self.forward(step, -1)

    def finish(self):
        p = self.place
        for (target, way), made in self.sent.items():
            fed = p.z > 0 if way == 1 else p.z < p.nz - 1

            @pl.when((p.z == target) & fed)
            def _(target=target, way=way, made=made):
                made.raw.wait_recv()
                self.add(target, way)


class Scatter:
    def __init__(self, courier, place, parts, core_in, side_in, above, below, last_in):
        self.courier, self.place, self.parts = courier, place, parts
        self.core_in, self.side_in, self.last_in = core_in, side_in, last_in
        every = slice(None)
        self.line = LineSum(
            courier, place, parts, lambda group: (group, every, place.y, place.c), above, below
        )
        self.groups = []
        for step in range((place.nz + 1) // 2):
            self.groups += [place.nz - 1 - step, step]
        self.core, self.side = {}, {}

    def to_core(self, group):
        p = self.place
        self.core[group] = self.courier.copy(
            self.parts.at[group, :, :, 1 - p.c], self.core_in.at[group], p.across["c"]
        )

    def add(self, spot, arrived):
        self.parts[spot] = (self.parts[spot].astype(floats) + arrived.astype(floats)).astype(
            self.parts.dtype
        )

    def sideways(self):
        p = self.place
        every = slice(None)
        for group in self.groups:
            self.core[group].wait_recv()
            self.add((group, every, every, p.c), self.core_in[group])
            self.side[group] = self.courier.copy(
                self.parts.at[group, :, 1 - p.y, p.c], self.side_in.at[group], p.across["y"]
            )

    def along(self):
        p = self.place
        for group in self.groups:
            self.side[group].wait_recv()
            self.add((group, slice(None), p.y, p.c), self.side_in[group])

    def across(self):
        p = self.place
        self.line.finish()
        self.last = self.courier.copy(
            self.parts.at[p.z, 1 - p.x, p.y, p.c], self.last_in, p.across["x"]
        )

    def own(self):
        p = self.place
        return self.parts[p.z, p.x, p.y, p.c].astype(floats)

    def other(self):
        self.last.wait_recv()
        return self.last_in[...].astype(floats)


def gather_pieces(values, piece, devices):
    width = values.shape[1]
    owner = lax.div(lax.broadcasted_iota(jnp.int32, (devices, width), 1), piece)
    mine = owner == lax.broadcasted_iota(jnp.int32, (devices, width), 0)
    at = lax.broadcasted_iota(jnp.int32, (width, 128), 0)
    inner = lax.broadcasted_iota(jnp.int32, (width, 128), 1)
    chosen = (lax.rem(at, piece) == inner).astype(floats)
    rows = jnp.where(mine, values, 0.0)
    return jnp.dot(rows, chosen, preferred_element_type=floats, precision=lax.Precision.HIGHEST)


def back_kernel(
    nz,
    done_ref,
    grads_in,
    branch_ref,
    kv_ref,
    q_ref,
    m_ref,
    back_ref,
    mixed_ref,
    outer_ref,
    tokens_ref,
    xn1_ref,
    gain_ref,
    turn_ref,
    query_ref,
    pair_ref,
    share_ref,
    out_ref,
    output_ref,
    tokens_grad_ref,
    joint_grad_ref,
    merge_grad_ref,
    small_grad_ref,
    grads_ref,
    weight_m,
    weight_q,
    weight_kv,
    gown,
    gin,
    branch_own,
    branch_in,
    branch_above,
    branch_below,
    *rest,
):
    merge_bufs, query_bufs, kv_bufs, small_bufs = (rest[6 * i : 6 * i + 6] for i in range(4))
    (
        pair_sum,
        pair_half,
        pair_above,
        pair_below,
        joint_back,
        attended_back,
        mixed_both,
        back_send,
        back_in,
        sends,
        receives,
        locals_,
    ) = rest[24:]
    place = Place(nz)
    z, x, y, c = place.z, place.x, place.y, place.c
    length, model = tokens_ref.shape
    share = gown.shape[-1]
    half = GROUP * HEAD_DIM
    both = 2 * length
    block = model // nz
    depth = grads_in.shape[-2]
    devices = 8 * nz
    total_keys = nz * both
    orders = far_first(nz)
    courier = Courier(sends, receives)
    meet(place.peers())

    def group_of(dz):
        return lax.rem(z + dz, nz)

    copies = []

    def load(source, target):
        made = pltpu.make_async_copy(source, target, locals_.at[len(copies)])
        made.start()
        copies.append(made)
        return made

    merge_load = load(m_ref, weight_m)
    branch_load = load(branch_ref.at[:, y], branch_own)
    gown_load = load(grads_in.at[:, :, x], gown)
    early = 2
    late = orders[early:]
    query_load = load(q_ref, weight_q)
    kv_load = load(kv_ref, weight_kv)

    b_cross = {
        group: courier.copy(branch_ref.at[group, 1 - y], branch_in.at[group], place.across["y"])
        for group in range(nz)
    }
    g_cross, g_line, kept = {}, [], []

    def grads_across(dz):
        g_cross[dz] = courier.copy(
            grads_in.at[:, late.index(dz), 1 - x], gin.at[late.index(dz)], place.across["x"]
        )

    mine = pl.ds(pl.multiple_of((z * 2 + y) * share, 128), share)

    def grads_line(dz, rows):
        for dy in range(2):
            ty = lax.rem(y + dy, 2)
            if dz or dy:
                g_line.append(
                    courier.copy(
                        rows.at[:, ty], grads_ref.at[:, :, mine], (group_of(dz), x, ty, c)
                    )
                )
            else:
                kept.append(load(rows.at[:, ty], grads_ref.at[:, :, mine]))

    for position in range(early):
        grads_line(orders[position], done_ref.at[:, position])

    mixed = mixed_ref[...]
    second_scale = norm_parts(mixed)
    part, second_local = norm_back(back_ref[...], mixed, second_scale, gain_ref[1:2, :])
    grad = outer_ref[...].astype(floats) + part
    tokens_grad_ref[...] = grad
    mixed_both[x] = grad.astype(halves)
    mixed_cross = courier.copy(mixed_both.at[x], mixed_both.at[x], place.across["x"])
    mixed_cross.wait_recv()
    for dz in late:
        grads_across(dz)

    merge_load.wait()
    upstream_both = mixed_both[...].reshape(both, model)
    attended_back[...] = jnp.dot(
        upstream_both, weight_m[...].reshape(model, half), preferred_element_type=floats
    ).astype(halves)
    merges = Scatter(courier, place, *merge_bufs)
    queries = Scatter(courier, place, *query_bufs)
    keys_values = Scatter(courier, place, *kv_bufs)
    smalls = Scatter(courier, place, *small_bufs)

    def product_rows(scatter, left, right):
        for group in scatter.groups:
            scatter.parts[group] = (
                jnp.dot(
                    left[group * block : (group + 1) * block], right, preferred_element_type=floats
                )
                .astype(halves)
                .reshape(2, 2, 2, depth, right.shape[1])
            )
            scatter.to_core(group)

    product_rows(merges, upstream_both.T, out_ref[...].astype(halves))

    def attend(first, last):
        @pl.loop(first, last)
        def _(head):
            query = query_ref[head]
            keys = pair_ref[:, :, :HEAD_DIM].reshape(total_keys, HEAD_DIM)
            values = pair_ref[:, :, HEAD_DIM:].reshape(total_keys, HEAD_DIM)
            lanes = pl.ds(pl.multiple_of(head * HEAD_DIM, 128), HEAD_DIM)
            upstream = attended_back[:, lanes]
            delta = jnp.sum(upstream.astype(floats) * out_ref[:, lanes], axis=-1, keepdims=True)
            mass = lax.dot_general(upstream, values, last_pair, preferred_element_type=floats)
            shares = share_ref[head]
            scores = (shares.astype(floats) * (mass - delta)).astype(halves)
            query_sum = jnp.dot(scores, keys, preferred_element_type=floats) * SCALE
            cosine, sine = turn_ref[0], turn_ref[1]
            joint_back[:, lanes] = (
                query_sum * cosine + pltpu.roll(query_sum * sine, HEAD_DIM // 2, 1)
            ).astype(halves)
            pair_sum[:, :HEAD_DIM] += (
                jnp.dot(scores.T, query, preferred_element_type=floats) * SCALE
            )
            pair_sum[:, HEAD_DIM:] += jnp.dot(shares.T, upstream, preferred_element_type=floats)

    def grads_on(dz):
        at = late.index(dz)
        g_cross[dz].wait_recv()
        for which in range(3):
            gown[which, at] = (
                gown[which, at].astype(floats) + gin[at, which].astype(floats)
            ).astype(halves)
        grads_line(dz, gown.at[:, at])

    pair_sum[...] = jnp.zeros_like(pair_sum)
    attend(0, GROUP // 2)
    merges.sideways()

    attend(GROUP // 2, GROUP)

    pair_half[...] = pair_sum[...].astype(halves).reshape(nz, both, 2 * HEAD_DIM)
    pairs = LineSum(courier, place, pair_half, lambda group: (group,), pair_above, pair_below)
    pairs.forward(nz - 1, 1)
    pairs.forward(0, -1)
    turned = xn1_ref[...].T
    product_rows(queries, turned, joint_back[:, :half])
    for step in range(1, nz - 1):
        pairs.forward(nz - 1 - step, 1)
        pairs.forward(step, -1)
    branch_load.wait()
    for group in range(nz):
        b_cross[group].wait_recv()
        branch_own[group] = (
            branch_own[group].astype(floats) + branch_in[group].astype(floats)
        ).astype(halves)
    pairs.finish()
    total = pair_half[z].astype(floats)
    key_total = total[:, :HEAD_DIM]
    joint_back[:, half : half + HEAD_DIM] = (
        key_total * turn_ref[0] + pltpu.roll(key_total * turn_ref[1], HEAD_DIM // 2, 1)
    ).astype(halves)
    joint_back[:, half + HEAD_DIM :] = total[:, HEAD_DIM:].astype(halves)
    product_rows(keys_values, turned, joint_back[:, half:])
    query_load.wait()
    kv_load.wait()
    normal_back = lax.dot_general(
        joint_back[:, :half],
        weight_q[...].reshape(model, half),
        last_pair,
        preferred_element_type=floats,
    ) + lax.dot_general(
        joint_back[:, half:],
        weight_kv[...].reshape(model, 2 * HEAD_DIM),
        last_pair,
        preferred_element_type=floats,
    )
    back_send[...] = jnp.where(x == 0, normal_back[length:], normal_back[:length]).astype(halves)
    back_cross = courier.copy(back_send, back_in, place.across["x"])
    normal_own = jnp.where(x == 0, normal_back[:length], normal_back[length:])
    queries.sideways()
    keys_values.sideways()
    gown_load.wait()
    for dz in late[:1]:
        grads_on(dz)

    local = jnp.sum(joint_back[...].astype(floats), axis=0, keepdims=True)
    pieces_of = []
    for first, width in ((0, half), (half, HEAD_DIM), (half + HEAD_DIM, HEAD_DIM)):
        for side in range(2):
            pieces_of.append(jnp.where(x == side, local[:, first : first + width], 0.0))
    bias_local = jnp.concatenate(pieces_of, axis=1)
    def piece_rows(which, values):
        mine_rows = gather_pieces(values, values.shape[1] // devices, devices)
        at = lax.broadcasted_iota(jnp.int32, (devices * 8, devices), 0)
        wanted = lax.broadcasted_iota(jnp.int32, (devices * 8, devices), 1) * 8 + which
        return jnp.dot(
            (at == wanted).astype(floats),
            mine_rows,
            preferred_element_type=floats,
            precision=lax.Precision.HIGHEST,
        )

    pieces = piece_rows(0, bias_local) + piece_rows(2, second_local)
    branches = LineSum(
        courier, place, branch_own, lambda group: (group,), branch_above, branch_below
    )
    back_cross.wait_recv()
    normal_own = normal_own + back_in[...].astype(floats)
    residual = tokens_ref[...].astype(floats)
    part, first_local = norm_back(normal_own, residual, norm_parts(residual), gain_ref[0:1, :])
    tokens_grad_ref[...] += part

    pieces = pieces + piece_rows(1, first_local)
    smalls.parts[...] = pieces.reshape(nz, 2, 2, 2, 8, 128)
    for group in smalls.groups:
        smalls.to_core(group)
    for made in (merges, queries, keys_values):
        made.along()
    for line in (keys_values.line, queries.line, merges.line, branches):
        line.forward_step(0)
    for line in (keys_values.line, queries.line, merges.line, branches):
        line.forward_step(1)
    for dz in late[1:]:
        grads_on(dz)
    smalls.sideways()
    for line in (keys_values.line, queries.line, merges.line, branches):
        line.forward_step(2)
    smalls.along()
    for step in range(nz - 1):
        smalls.line.forward_step(step)
    for made in (merges, queries, keys_values, smalls):
        made.across()
    branches.finish()
    output_ref[...] = (mixed_ref[...] + branch_own[z].astype(floats)).astype(halves)
    for ref, made, pieces in (
        (merge_grad_ref, merges, [(0, half)]),
        (joint_grad_ref, queries, [(0, half)]),
        (joint_grad_ref, keys_values, KV_PIECES),
    ):
        for side, values in ((x, made.own()), (1 - x, made.other())):
            at = 0
            for first, width in pieces:
                lanes = pl.ds(pl.multiple_of(first + side * width, 128), width)
                ref[:, lanes] = values[:, at : at + width]
                at += width
    small_grad_ref[...] = smalls.own() + smalls.other()
    for made in g_line:
        made.wait_recv()
    for made in kept:
        made.wait()
    courier.finish()


def padded_share(hidden_width, team):
    return -(-hidden_width // (team * 128)) * 128


def body_kernels(
    tokens,
    segments,
    joint_matrix,
    joint_bias,
    merge_matrix,
    norm_first,
    norm_second,
    gate_matrix,
    up_matrix,
    down_matrix,
    cotangent,
):
    length, model = tokens.shape[1:]
    depth, joint_width = joint_matrix.shape
    hidden_width = gate_matrix.shape[1]
    nz = lax.axis_size("z")
    share = padded_share(hidden_width, 2 * nz)
    half = GROUP * HEAD_DIM
    pair_width = 2 * HEAD_DIM
    both = 2 * length
    keys = nz * both
    vmem = pl.BlockSpec(memory_space=pltpu.VMEM)
    anywhere = pl.BlockSpec(memory_space=pl.ANY)
    blocks = (nz, 2, 2, 2)

    def shape(dims, kind=halves):
        return jax.ShapeDtypeStruct(dims, kind)

    def semaphores(count, loads):
        return [
            pltpu.SemaphoreType.DMA((count,)),
            pltpu.SemaphoreType.DMA((count,)),
            pltpu.SemaphoreType.DMA((loads,)),
        ]

    def params(number):
        return pltpu.CompilerParams(
            collective_id=number, has_side_effects=True, vmem_limit_bytes=VMEM_LIMIT
        )

    stack = jnp.stack([gate_matrix, up_matrix, down_matrix.T])
    stack = jnp.pad(stack, ((0, 0), (0, 0), (0, 2 * nz * share - hidden_width)))

    def lane_row(values):
        return jnp.pad(values.astype(floats), (0, 128 - values.shape[0]))

    own_labels = segments[0]
    empty = jnp.zeros((128,), floats)
    small = jnp.stack(
        [lane_row(v) for v in (joint_bias, norm_first, norm_second, own_labels)] + [empty] * 4
    )
    inverse = theta ** -(np.arange(HEAD_DIM // 2) * (2.0 / HEAD_DIM))
    inverse = jnp.asarray(np.tile(inverse, 2)[None], floats)
    outer = cotangent[0]
    (
        w,
        team_outer,
        kv_all,
        q_all,
        m_all,
        xn1,
        xn2,
        mixed,
        gains,
        turns,
        queries,
        pair,
        shares,
        summed,
    ) = pl.pallas_call(
        functools.partial(attention_kernel, nz),
        name="attention_forward",
        out_shape=(
            shape((3,) + blocks + (depth, share)),
            shape((nz, 2, length, model)),
            shape(blocks + (depth, pair_width)),
            shape(blocks + (depth, half)),
            shape(blocks + (depth, half)),
            shape((both, model)),
            shape((length, model)),
            shape((length, model), floats),
            shape((8, model), floats),
            shape((2, both, HEAD_DIM), floats),
            shape((GROUP, both, HEAD_DIM)),
            shape((nz, both, pair_width)),
            shape((GROUP, both, keys)),
            shape((both, half), floats),
        ),
        in_specs=[anywhere] * 3 + [vmem] * 4,
        out_specs=(anywhere,) * 5 + (vmem,) * 9,
        scratch_shapes=[
            pltpu.VMEM(blocks + (depth, pair_width), halves),
            pltpu.VMEM(blocks + (depth, half), halves),
            pltpu.VMEM(blocks + (depth, half), halves),
            pltpu.VMEM(blocks + (8, 128), floats),
            pltpu.VMEM((both, keys), floats),
            pltpu.VMEM((2, length, model), halves),
            pltpu.VMEM((length, model), halves),
            pltpu.VMEM((length, model), halves),
        ]
        + semaphores(137, 10),
        compiler_params=params(0),
    )(stack, joint_matrix, merge_matrix.T, small, inverse, tokens[0], outer)

    lines = 2 * length
    back, branch, done, grads = pl.pallas_call(
        functools.partial(feed_kernel, nz),
        name="feed_forward",
        out_shape=(
            shape((length, model), floats),
            shape((nz, 2, length, model)),
            shape((3, 2, 2, depth, share)),
            shape((3, nz - 2, 2, 2, depth, share)),
        ),
        in_specs=[anywhere, anywhere, vmem],
        out_specs=(vmem, vmem, anywhere, anywhere),
        scratch_shapes=[
            pltpu.VMEM((3,) + blocks + (depth, share), halves),
            pltpu.VMEM((nz, 2, length, model), halves),
            pltpu.VMEM((nz, 2, length, model), halves),
            pltpu.VMEM((nz, lines, share), halves),
            pltpu.VMEM((nz, lines, share), halves),
            pltpu.VMEM((nz, lines, share), halves),
            pltpu.VMEM((nz, 2, length, model), halves),
            pltpu.VMEM((nz, length, model), halves),
            pltpu.VMEM((nz, length, model), halves),
            pltpu.VMEM((nz - 1, length, model), halves),
            pltpu.VMEM((nz, 3, 2, 2, depth, share), halves),
            pltpu.VMEM((2, 3, 2, depth, share), halves),
        ]
        + semaphores(30, 8),
        compiler_params=params(1),
    )(w, team_outer, xn2)

    def sums(rows, width, kind=halves):
        return [
            pltpu.VMEM(blocks + (rows, width), kind),
            pltpu.VMEM((nz, 2, 2, rows, width), kind),
            pltpu.VMEM((nz, 2, rows, width), kind),
            pltpu.VMEM((nz - 1, 2, rows, width), kind),
            pltpu.VMEM((nz - 1, 2, rows, width), kind),
            pltpu.VMEM((rows, width), kind),
        ]

    output, tokens_grad, joint_grad, merge_grad, small_grad, grads = pl.pallas_call(
        functools.partial(back_kernel, nz),
        name="attention_backward",
        out_shape=(
            shape((length, model)),
            shape((length, model), floats),
            shape((depth, joint_width), floats),
            shape((depth, QUERY_WIDTH), floats),
            shape((8, 128), floats),
            shape((3, depth, 2 * nz * share)),
        ),
        in_specs=[anywhere] * 6 + [vmem] * 11,
        out_specs=(vmem,) * 5 + (anywhere,),
        scratch_shapes=[
            pltpu.VMEM(blocks + (depth, half), halves),
            pltpu.VMEM(blocks + (depth, half), halves),
            pltpu.VMEM(blocks + (depth, pair_width), halves),
            pltpu.VMEM((3, nz - 2, 2, depth, share), halves),
            pltpu.VMEM((nz - 2, 3, 2, depth, share), halves),
            pltpu.VMEM((nz, length, model), halves),
            pltpu.VMEM((nz, length, model), halves),
            pltpu.VMEM((nz - 1, length, model), halves),
            pltpu.VMEM((nz - 1, length, model), halves),
        ]
        + sums(depth, half)
        + sums(depth, half)
        + sums(depth, pair_width)
        + sums(8, 128, floats)
        + [
            pltpu.VMEM((keys, pair_width), floats),
            pltpu.VMEM((nz, both, pair_width), halves),
            pltpu.VMEM((nz - 1, both, pair_width), halves),
            pltpu.VMEM((nz - 1, both, pair_width), halves),
            pltpu.VMEM((both, half + pair_width), halves),
            pltpu.VMEM((both, half), halves),
            pltpu.VMEM((2, length, model), halves),
            pltpu.VMEM((length, model), halves),
            pltpu.VMEM((length, model), halves),
        ]
        + semaphores(90, 6),
        compiler_params=params(2),
    )(
        done,
        grads,
        branch,
        kv_all,
        q_all,
        m_all,
        back,
        mixed,
        outer,
        tokens[0],
        xn1,
        gains,
        turns,
        queries,
        pair,
        shares,
        summed,
    )
    grads = [grads[which, :, :hidden_width].astype(floats) for which in range(3)]
    return (
        output[None],
        tokens_grad[None],
        joint_grad,
        small_grad[0, : joint_bias.shape[0]],
        merge_grad.T,
        small_grad[1, :depth],
        small_grad[2, :depth],
        grads[0],
        grads[1],
        grads[2].T,
    )


def body_plain(
    tokens,
    segments,
    joint_matrix,
    joint_bias,
    merge_matrix,
    norm_first,
    norm_second,
    gate_matrix,
    up_matrix,
    down_matrix,
    cotangent,
):
    residual = tokens[0].astype(floats)
    length, model = residual.shape
    depth = joint_matrix.shape[0]
    joint_width = joint_matrix.shape[1]
    hidden_width = gate_matrix.shape[1]
    z_count = lax.axis_size("z")
    team = lax.axis_size(TEAM)
    share = hidden_width // team
    own_labels = segments[0]
    labels = lax.all_gather(own_labels, SEQ, axis=0, tiled=True)
    offset = lax.axis_index(SEQ) * length
    places = offset + jnp.arange(length, dtype=jnp.int32)
    positions = lax.dynamic_slice_in_dim(row_positions(labels), offset, length, 0)
    cosine, sine = rotary(positions, HEAD_DIM)

    small = jnp.concatenate([joint_bias, norm_first, norm_second])
    small = jnp.pad(small, (0, -small.shape[0] % depth)).reshape(depth, -1)
    small_width = small.shape[1]
    packed = jnp.concatenate([joint_matrix, merge_matrix.T, small], axis=1)
    packed = lax.all_gather(packed, AXES, axis=0, tiled=True)
    joint_all = packed[:, :joint_width]
    merge_turned = packed[:, joint_width : joint_width + model]
    small = packed[:, joint_width + model :].reshape(-1, depth * small_width).astype(floats)
    bias_depth = joint_bias.shape[0]
    bias_all = small[:, :bias_depth].reshape(-1)
    gain_first = small[:, bias_depth : bias_depth + depth].reshape(-1)
    gain_second = small[:, bias_depth + depth : bias_depth + 2 * depth].reshape(-1)

    stacked = jnp.stack([gate_matrix, up_matrix, down_matrix.T], axis=1)
    stacked = stacked.reshape(depth, 3, team, share).transpose(2, 0, 1, 3)
    stacked = stacked.reshape(team, depth, 3 * share)
    stacked = lax.all_to_all(stacked, TEAM, split_axis=0, concat_axis=0, tiled=True)
    stacked = stacked.reshape(z_count, 1, team // z_count, 1, depth, 3 * share)
    stacked = lax.all_gather(stacked, "x", axis=1, tiled=True)
    stacked = lax.all_gather(stacked, "c", axis=3, tiled=True)
    stacked = stacked.reshape(model, 3 * share)
    both_all, down_turned = stacked[:, : 2 * share], stacked[:, 2 * share :]
    outer_grad = cotangent[0]
    team_outer = lax.all_gather(outer_grad, TEAM, axis=0, tiled=True)

    scale_first = norm_parts(residual)
    normal_first = (residual * scale_first * gain_first).astype(halves)
    joint = jnp.dot(normal_first, joint_all, preferred_element_type=floats) + bias_all
    query = joint[:, :QUERY_WIDTH].reshape(length, HEADS, HEAD_DIM)
    keys = joint[:, QUERY_WIDTH : QUERY_WIDTH + KEY_WIDTH].reshape(length, KV_HEADS, HEAD_DIM)
    values = joint[:, QUERY_WIDTH + KEY_WIDTH :].astype(halves)
    query = (query * cosine + turn_half(query) * sine).astype(halves)
    keys = (keys * cosine + turn_half(keys) * sine).astype(halves).reshape(length, KEY_WIDTH)
    query_group = to_groups(query)
    pair = lax.all_gather(jnp.concatenate([keys, values], axis=1), SEQ, axis=0, tiled=True)
    count = pair.shape[0]
    key_all = pair[:, :KEY_WIDTH].reshape(count, KV_HEADS, HEAD_DIM)
    value_all = pair[:, KEY_WIDTH:].reshape(count, KV_HEADS, HEAD_DIM)
    allowed = (places[:, None] >= jnp.arange(count, dtype=jnp.int32)[None, :]) & (
        own_labels[:, None] == labels[None, :]
    )
    allowed = jnp.tile(allowed, (GROUP, 1))[None]
    scores = jnp.einsum("krd,nkd->krn", query_group, key_all, preferred_element_type=floats)
    scores = jnp.where(allowed, scores * SCALE, neg)
    top = jnp.max(scores, axis=-1, keepdims=True)
    weights = jnp.where(allowed, jnp.exp(scores - top), 0.0)
    total = jnp.sum(weights, axis=-1, keepdims=True)
    shares = weights / total
    shares_half = shares.astype(halves)
    attended = jnp.einsum("krn,nkd->krd", shares_half, value_all, preferred_element_type=floats)
    attended_half = from_groups(attended, length).astype(halves)
    mixed = residual + lax.dot_general(
        attended_half, merge_turned, last_pair, preferred_element_type=floats
    )
    scale_second = norm_parts(mixed)
    normal_half = (mixed * scale_second * gain_second).astype(halves)

    team_normal = lax.all_gather(normal_half, TEAM, axis=0, tiled=True)
    both = jnp.dot(team_normal, both_all, preferred_element_type=floats)
    gate, upper = both[:, :share], both[:, share:]
    sig = jax.nn.sigmoid(gate)
    silu = gate * sig
    hidden_half = (silu * upper).astype(halves)
    branch = lax.dot_general(hidden_half, down_turned, last_pair, preferred_element_type=floats)
    hidden_grad = jnp.dot(team_outer, down_turned, preferred_element_type=floats)
    gate_half = (hidden_grad * upper * sig * (1.0 + gate * (1.0 - sig))).astype(halves)
    upper_half = (hidden_grad * silu).astype(halves)
    both_half = jnp.concatenate([gate_half, upper_half], axis=1)
    normal_grad = lax.dot_general(both_half, both_all, last_pair, preferred_element_type=floats)
    branch = lax.psum_scatter(branch.astype(halves), TEAM, scatter_dimension=0, tiled=True)
    normal_grad = lax.psum_scatter(normal_grad.astype(halves), TEAM, scatter_dimension=0, tiled=True)
    output = (mixed + branch.astype(floats)).astype(halves)[None]
    both_grad = lax.dot_general(team_normal, both_half, first_pair, preferred_element_type=floats)
    down_grad = lax.dot_general(team_outer, hidden_half, first_pair, preferred_element_type=floats)
    grads = jnp.concatenate([both_grad, down_grad], axis=1).astype(halves)
    grads = grads.reshape(z_count, 2, team // z_count, 2, depth, 3 * share)
    grads = lax.psum_scatter(grads, "c", scatter_dimension=3, tiled=True)
    grads = lax.psum_scatter(grads, "x", scatter_dimension=1, tiled=True)
    grads = grads.reshape(team, depth, 3 * share)
    grads = lax.all_to_all(grads, TEAM, split_axis=0, concat_axis=0, tiled=True)
    grads = grads.reshape(team, depth, 3, share).transpose(2, 1, 0, 3)
    grads = grads.reshape(3, depth, hidden_width).astype(floats)

    normal_grad = normal_grad.astype(floats)
    mixed_part, second_local = norm_back(normal_grad, mixed, scale_second, gain_second)
    mixed_grad = outer_grad.astype(floats) + mixed_part
    mixed_half = mixed_grad.astype(halves)
    merge_local = lax.dot_general(
        mixed_half, attended_half, first_pair, preferred_element_type=floats
    )
    attended_grad = jnp.dot(mixed_half, merge_turned, preferred_element_type=floats).astype(halves)
    grad_group = to_groups(attended_grad.reshape(length, HEADS, HEAD_DIM))
    mass_grad = jnp.einsum("krd,nkd->krn", grad_group, value_all, preferred_element_type=floats)
    row_dots = jnp.sum(shares * mass_grad, axis=-1, keepdims=True)
    score_half = (shares * (mass_grad - row_dots)).astype(halves)
    query_sum = (
        jnp.einsum("krn,nkd->krd", score_half, key_all, preferred_element_type=floats) * SCALE
    )
    key_grad = (
        jnp.einsum("krn,krd->nkd", score_half, query_group, preferred_element_type=floats) * SCALE
    )
    value_grad = jnp.einsum("krn,krd->nkd", shares_half, grad_group, preferred_element_type=floats)
    pair_sums = jnp.concatenate(
        [key_grad.reshape(count, KEY_WIDTH), value_grad.reshape(count, KEY_WIDTH)], axis=1
    )
    pair_mine = lax.psum_scatter(
        pair_sums.astype(halves), SEQ, scatter_dimension=0, tiled=True
    ).astype(floats)
    key_back = pair_mine[:, :KEY_WIDTH].reshape(length, KV_HEADS, HEAD_DIM)
    value_back = pair_mine[:, KEY_WIDTH:]
    query_back = from_groups(query_sum, length).reshape(length, HEADS, HEAD_DIM)
    query_back = query_back * cosine + unturn_half(query_back * sine)
    key_back = key_back * cosine + unturn_half(key_back * sine)
    joint_back = jnp.concatenate(
        [query_back.reshape(length, QUERY_WIDTH), key_back.reshape(length, KEY_WIDTH), value_back],
        axis=1,
    ).astype(halves)
    joint_local = lax.dot_general(
        normal_first, joint_back, first_pair, preferred_element_type=floats
    )
    bias_local = jnp.sum(joint_back.astype(floats), axis=0)
    normal_back = lax.dot_general(joint_back, joint_all, last_pair, preferred_element_type=floats)
    residual_part, first_local = norm_back(normal_back, residual, scale_first, gain_first)
    tokens_grad = (mixed_grad + residual_part)[None]

    small_back = jnp.concatenate(
        [
            bias_local.reshape(-1, bias_depth),
            first_local.reshape(-1, depth),
            second_local.reshape(-1, depth),
        ],
        axis=1,
    )
    small_back = jnp.pad(small_back, ((0, 0), (0, depth * small_width - small_back.shape[1])))
    small_back = small_back.reshape(-1, small_width)
    packed_grad = jnp.concatenate([joint_local, merge_local, small_back], axis=1).astype(halves)
    packed_grad = lax.psum_scatter(packed_grad, AXES, scatter_dimension=0, tiled=True).astype(floats)
    joint_grad = packed_grad[:, :joint_width]
    merge_grad = packed_grad[:, joint_width : joint_width + model].T
    small_back = packed_grad[:, joint_width + model :].reshape(-1)
    bias_grad = small_back[:bias_depth]
    first_grad = small_back[bias_depth : bias_depth + depth]
    second_grad = small_back[bias_depth + depth : bias_depth + 2 * depth]
    return (
        output,
        tokens_grad,
        joint_grad,
        bias_grad,
        merge_grad,
        first_grad,
        second_grad,
        grads[0],
        grads[1],
        grads[2].T,
    )


def solution(mesh):
    seq, row = mesh.shape["seq"], mesh.shape["row"]
    fine = Mesh(mesh.devices.reshape(seq // 2, 2, row // 2, 2), AXES)
    whole = ("z", "x", "y", "c")
    placed = (
        P(ROW, SEQ, None),
        P(ROW, SEQ),
        P(whole, None),
        P(whole),
        P(None, whole),
        P(whole),
        P(whole),
        P(whole, None),
        P(whole, None),
        P(None, whole),
        P(ROW, SEQ, None),
    )
    depth = MODEL // mesh.size
    return jax.shard_map(
        body_kernels if depth % 16 == 0 else body_plain,
        mesh=fine,
        in_specs=placed,
        out_specs=(
            P(ROW, SEQ, None),
            P(ROW, SEQ, None),
            P(whole, None),
            P(whole),
            P(None, whole),
            P(whole),
            P(whole),
            P(whole, None),
            P(whole, None),
            P(None, whole),
        ),
        check_vma=False,
    )
```

```python
import functools
import math

import jax
import jax.numpy as jnp
import numpy as np
from jax import lax
from jax.experimental import pallas as pl
from jax.experimental.pallas import tpu as pltpu
from jax.sharding import Mesh, PartitionSpec as P

HEADS = 12
KV_HEADS = 2
HEAD_DIM = 128
MODEL = HEADS * HEAD_DIM
GROUP = HEADS // KV_HEADS
QUERY_WIDTH = HEADS * HEAD_DIM
KEY_WIDTH = KV_HEADS * HEAD_DIM
KV_PIECES = [(QUERY_WIDTH, HEAD_DIM), (QUERY_WIDTH + KEY_WIDTH, HEAD_DIM)]
SCALE = 1.0 / math.sqrt(HEAD_DIM)

eps = 1e-06
theta = 1000000.0
neg = -1e30
last_pair = (((1,), (1,)), ((), ()))
first_pair = (((0,), (0,)), ((), ()))
floats = jnp.float32
halves = jnp.bfloat16

AXES = ("z", "x", "y", "c")
SEQ = ("z", "x")
ROW = ("y", "c")
TEAM = ("z", "y")


def turn_half(values):
    middle = values.shape[-1] // 2
    return jnp.concatenate([-values[..., middle:], values[..., :middle]], axis=-1)


def unturn_half(values):
    middle = values.shape[-1] // 2
    return jnp.concatenate([values[..., middle:], -values[..., :middle]], axis=-1)


def row_positions(labels):
    length = labels.shape[0]
    places = jnp.arange(length, dtype=jnp.int32)
    change = jnp.concatenate([jnp.ones((1,), dtype=jnp.bool_), labels[1:] != labels[:-1]])
    starts = lax.cummax(jnp.where(change, places, 0), axis=0)
    return places - starts


def rotary(positions, width):
    inverse = jnp.power(
        jnp.float32(theta), -(jnp.arange(width // 2, dtype=jnp.float32) * (2.0 / width))
    )
    angle = positions.astype(jnp.float32)[:, None] * inverse[None, :]
    angle = jnp.concatenate([angle, angle], axis=1)[:, None, :]
    return (jnp.cos(angle), jnp.sin(angle))


def to_groups(values):
    length = values.shape[0]
    return (
        values.reshape(length, KV_HEADS, GROUP, HEAD_DIM)
        .transpose(1, 2, 0, 3)
        .reshape(KV_HEADS, GROUP * length, HEAD_DIM)
    )


def from_groups(values, length):
    return (
        values.reshape(KV_HEADS, GROUP, length, HEAD_DIM)
        .transpose(2, 0, 1, 3)
        .reshape(length, QUERY_WIDTH)
    )


def norm_parts(values):
    return lax.rsqrt(jnp.mean(values * values, axis=-1, keepdims=True) + eps)


def norm_back(upstream, values, scale, gain):
    scaled = upstream * gain
    inner = jnp.mean(scaled * values, axis=-1, keepdims=True)
    part = scale * scaled - values * (scale * scale * scale) * inner
    gain_grad = jnp.sum(upstream * values * scale, axis=0, keepdims=True)
    return part, gain_grad


MESH = pl.DeviceIdType.MESH
VMEM_LIMIT = 60 * 2**20


def coordinates():
    return tuple(lax.axis_index(name) for name in AXES)


class Sent:
    def __init__(self, raw, when):
        self.raw, self.when = raw, when

    def under(self, act):
        if self.when is None:
            act()
        else:
            pl.when(self.when)(act)

    def start(self):
        self.under(self.raw.start)

    def wait_recv(self):
        self.under(self.raw.wait_recv)

    def wait_send(self):
        self.under(self.raw.wait_send)


class Courier:
    def __init__(self, sends, receives):
        self.sends, self.receives, self.copies = sends, receives, []

    def make(self, source, target, device, when=None):
        place = len(self.copies)
        raw = pltpu.make_async_remote_copy(
            src_ref=source,
            dst_ref=target,
            send_sem=self.sends.at[place],
            recv_sem=self.receives.at[place],
            device_id=device,
            device_id_type=MESH,
        )
        made = Sent(raw, when)
        self.copies.append(made)
        return made

    def copy(self, source, target, device, when=None):
        made = self.make(source, target, device, when)
        made.start()
        return made

    def finish(self):
        for made in self.copies:
            made.wait_send()


def meet(devices):
    barrier = pltpu.get_barrier_semaphore()
    for device in devices:
        pl.semaphore_signal(barrier, inc=1, device_id=device, device_id_type=MESH)
    pl.semaphore_wait(barrier, len(devices))


def far_first(nz):
    return sorted(range(nz), key=lambda dz: (dz == 0, abs(2 * dz - nz)))


def near_first(nz):
    return [sorted(range(nz), key=lambda group: (abs(group - at), -group)) for at in range(nz)]


def cuts_of(width, step):
    return [(start, min(step, width - start)) for start in range(0, width, step)]


class Line:
    def __init__(self, courier, place, spot):
        self.courier, self.place, self.spot = courier, place, spot
        self.sent = {}

    def items(self):
        p = self.place
        found = [(0, 0, p.z, None)]
        for step in range(1, p.nz):
            found.append((step, 1, lax.max(p.z - step, 0), p.z >= step))
            found.append((step, -1, lax.min(p.z + step, p.nz - 1), p.z + step < p.nz))
        return found

    def send(self, step, way, group, also=None):
        p = self.place
        inside = p.z < p.nz - 1 if way == 1 else p.z > 0
        if also is not None:
            inside = inside & also
        spot = self.spot(group)
        self.sent[step, way] = self.courier.copy(spot, spot, p.line_at(way), inside)

    def start(self):
        self.send(0, 1, self.place.z)
        self.send(0, -1, self.place.z)

    def arrive(self, step, way, group, exists):
        made = self.sent[step - 1, way]

        @pl.when(exists)
        def _():
            made.raw.wait_recv()

        if step < self.place.nz - 1:
            self.send(step, way, group, exists)


class Gather:
    def __init__(self, courier, place, source, buffer):
        self.courier, self.place = courier, place
        self.source, self.buffer = source, buffer
        self.line = Line(courier, place, lambda group: buffer.at[group, :, place.y, place.c])
        self.side, self.core = {}, {}

    def start(self):
        p = self.place
        spot = self.buffer.at[p.z, p.x, p.y, p.c]
        self.cross = [
            self.courier.copy(source, spot.at[:, lanes], p.across["x"])
            for source, lanes in self.source
        ]

    def along(self):
        for made in self.cross:
            made.wait_recv()
        self.line.start()
        self.sideways(self.line.items()[0])

    def sideways(self, item):
        step, way, group, exists = item
        p = self.place
        spot = self.buffer.at[group, :, p.y, p.c]
        self.side[step, way] = self.courier.copy(spot, spot, p.across["y"], exists)

    def pass_on(self, step):
        for item in self.line.items():
            if item[0] == step:
                self.line.arrive(*item)
                self.sideways(item)

    def to_core(self):
        p = self.place
        for item in self.line.items():
            step, way, group, exists = item
            self.side[step, way].wait_recv()
            spot = self.buffer.at[group, :, :, p.c]
            self.core[step, way] = self.courier.copy(spot, spot, p.across["c"], exists)

    def done(self):
        for made in self.core.values():
            made.wait_recv()


class Place:
    def __init__(self, nz):
        self.nz = nz
        self.z, self.x, self.y, self.c = z, x, y, c = coordinates()
        self.across = {"x": (z, 1 - x, y, c), "y": (z, x, 1 - y, c), "c": (z, x, y, 1 - c)}

    def line(self, dz, dy=0):
        y = lax.rem(self.y + dy, 2) if dy else self.y
        return (lax.rem(self.z + dz, self.nz), self.x, y, self.c)

    def line_at(self, way):
        return (lax.rem(self.z + self.nz + way, self.nz), self.x, self.y, self.c)

    def peers(self):
        team = [self.line(dz, dy) for dz in range(self.nz) for dy in range(2)]
        return team[1:] + [self.across["x"], self.across["c"]]


def spread(values, piece, width):
    devices, lanes = values.shape
    at = lax.broadcasted_iota(jnp.int32, (lanes, width), 1)
    inner = lax.broadcasted_iota(jnp.int32, (lanes, width), 0)
    chosen = (lax.rem(at, piece) == inner).astype(floats).astype(halves)
    repeated = jnp.dot(values.astype(halves), chosen, preferred_element_type=floats)
    owner = lax.div(lax.broadcasted_iota(jnp.int32, (devices, width), 1), piece)
    mine = owner == lax.broadcasted_iota(jnp.int32, (devices, width), 0)
    return jnp.sum(jnp.where(mine, repeated, 0.0), axis=0, keepdims=True)


def attention_kernel(
    nz,
    stack_ref,
    joint_ref,
    merge_ref,
    small_ref,
    inverse_ref,
    tokens_ref,
    outer_ref,
    w_ref,
    ct_ref,
    kv_out,
    query_out,
    merge_out,
    xn1_ref,
    xn2_ref,
    mixed_ref,
    gain_ref,
    turn_ref,
    query_ref,
    pair_ref,
    share_ref,
    out_ref,
    joint_kv,
    joint_q,
    merge,
    small,
    bias_mask,
    tokens_all,
    mixed_send,
    mixed_in,
    sends,
    receives,
    locals_,
):
    place = Place(nz)
    z, x, y, c = place.z, place.x, place.y, place.c
    length, model = tokens_ref.shape
    depth, joint_width = joint_ref.shape
    share = w_ref.shape[-1]
    half = GROUP * HEAD_DIM
    both = 2 * length
    total_keys = nz * both
    courier = Courier(sends, receives)
    devices = 8 * nz
    meet(place.peers())

    own_copies = []

    def keep(source, target):
        made = pltpu.make_async_copy(source, target, locals_.at[len(own_copies)])
        made.start()
        own_copies.append(made)
        return made

    def columns(tz, ty):
        return pl.ds(pl.multiple_of((tz * 2 + ty) * share, 128), share)

    gathers, own_waits = {}, {}

    def begin(name, ref, pieces, buffer):
        def from_side(side):
            found = []
            at = 0
            for first, width in pieces:
                lanes = pl.ds(pl.multiple_of(first + side * width, 128), width)
                found.append((ref.at[:, lanes], slice(at, at + width)))
                at += width
            return found

        spot = buffer.at[z, x, y, c]
        own_waits[name] = [keep(own, spot.at[:, lanes]) for own, lanes in from_side(x)]
        gathers[name] = Gather(courier, place, from_side(1 - x), buffer)
        gathers[name].start()

    own_waits["small"] = [keep(small_ref, small.at[z, x, y, c])]
    gathers["small"] = Gather(courier, place, [(small_ref, slice(None))], small)
    gathers["small"].start()
    begin("kv", joint_ref, KV_PIECES, joint_kv)
    token_cross = courier.copy(tokens_ref, tokens_all.at[x], place.across["x"])
    begin("q", joint_ref, [(0, half)], joint_q)
    begin("m", merge_ref, [(0, half)], merge)
    tokens_all[x] = tokens_ref[...]
    w_own = keep(stack_ref.at[:, :, columns(z, y)], w_ref.at[:, z, x, y, c])
    ct_own = keep(outer_ref, ct_ref.at[z, y])

    direct, w_cross, w_hand = {}, {}, {}

    def give(dz, dy):
        device = place.line(dz, dy)
        direct[dz, dy] = courier.copy(
            stack_ref.at[:, :, columns(device[0], device[2])], w_ref.at[:, z, x, y, c], device
        )

    def w_spot(dz, dy, side):
        return w_ref.at[:, lax.rem(z + nz - dz, nz), side, lax.rem(y + dy, 2), c]

    def take(dz, dy):
        if dz or dy:
            direct[dz, dy].wait_recv()
        spot = w_spot(dz, dy, x)
        w_cross[dz, dy] = courier.copy(spot, spot, place.across["x"])
        w_hand[dz, dy, 0] = courier.copy(spot, spot, place.across["c"])

    def hand(dz, dy):
        w_cross[dz, dy].wait_recv()
        spot = w_spot(dz, dy, 1 - x)
        w_hand[dz, dy, 1] = courier.copy(spot, spot, place.across["c"])

    give(0, 1)
    give(1, 0)
    for name in ("small", "kv"):
        for made in own_waits[name]:
            made.wait()
        gathers[name].along()
    token_cross.wait_recv()
    tokens_both = tokens_all[...].reshape(both, model).astype(floats)
    hat = tokens_both * norm_parts(tokens_both)
    for name in ("small", "kv"):
        gathers[name].pass_on(1)
    for made in own_waits["q"] + own_waits["m"]:
        made.wait()
    gathers["q"].along()
    for step in range(2, nz):
        for name in ("small", "kv"):
            gathers[name].pass_on(step)
    for name in ("small", "kv"):
        gathers[name].to_core()
    w_own.wait()
    take(0, 0)
    for step in range(1, nz):
        gathers["q"].pass_on(step)
    for name in ("small", "kv"):
        gathers[name].done()
    take(0, 1)
    give(1, 1)

    pieces = small[...].reshape(devices * 8, 128).astype(halves)

    def row_of(which):
        at = lax.broadcasted_iota(jnp.int32, (devices, devices * 8), 1)
        wanted = lax.broadcasted_iota(jnp.int32, (devices, devices * 8), 0) * 8 + which
        chosen = (at == wanted).astype(floats).astype(halves)
        return jnp.dot(chosen, pieces, preferred_element_type=floats)

    gain_first = spread(row_of(1), depth, model)
    gain_second = spread(row_of(2), depth, model)
    bias = spread(row_of(0), joint_width // devices, joint_width)
    gain_ref[0:1, :] = gain_first
    gain_ref[1:2, :] = gain_second

    def mine(first, width):
        return jnp.where(x == 0, bias[:, first : first + width], bias[:, first + width : first + 2 * width])

    bias_query = mine(0, half)
    bias_key = mine(QUERY_WIDTH, HEAD_DIM)
    bias_value = mine(QUERY_WIDTH + KEY_WIDTH, HEAD_DIM)
    label = jnp.concatenate([small[z, side, y, c].T[:, 3:4] for side in range(2)], axis=0)
    start = jnp.zeros((both, 1), floats)
    rows_at = z * both + lax.broadcasted_iota(jnp.int32, (both, length), 0)
    lanes_at = lax.broadcasted_iota(jnp.int32, (both, length), 1)
    for block in range(2 * nz):
        keys_label = small[block // 2, block % 2, y, c, 3:4, :]
        start = start + jnp.sum((keys_label < label).astype(floats), axis=1, keepdims=True)
        allowed = (keys_label == label) & (rows_at >= block * length + lanes_at)
        bias_mask[:, block * length : (block + 1) * length] = jnp.where(allowed, 0.0, neg)
    place_at = (z * both + lax.broadcasted_iota(jnp.int32, (both, 1), 0)).astype(floats)
    angle = (place_at - start) * inverse_ref[...]
    cosine = jnp.cos(angle)
    lane = lax.broadcasted_iota(jnp.int32, (both, HEAD_DIM), 1)
    sine = jnp.where(lane < HEAD_DIM // 2, -1.0, 1.0) * jnp.sin(angle)
    turn_ref[0] = cosine
    turn_ref[1] = sine

    def turned(values):
        return values * cosine + pltpu.roll(values, HEAD_DIM // 2, 1) * sine

    xn1_ref[...] = (hat * gain_first).astype(halves)
    pair = jnp.dot(
        xn1_ref[...], joint_kv[...].reshape(model, 2 * HEAD_DIM), preferred_element_type=floats
    )
    pair_ref[z, :, :HEAD_DIM] = turned(pair[:, :HEAD_DIM] + bias_key).astype(halves)
    pair_ref[z, :, HEAD_DIM:] = (pair[:, HEAD_DIM:] + bias_value).astype(halves)
    pairs = Line(courier, place, lambda group: pair_ref.at[group])
    pairs.start()
    gathers["q"].to_core()
    gathers["m"].along()
    for item in pairs.items()[1:3]:
        pairs.arrive(*item)
    take(1, 0)
    give(3, 0)
    for item in pairs.items()[3:]:
        pairs.arrive(*item)
    gathers["m"].pass_on(1)
    gathers["q"].done()

    query = jnp.dot(xn1_ref[...], joint_q[...].reshape(model, half), preferred_element_type=floats)
    query = query + bias_query
    for head in range(GROUP):
        query_ref[head] = turned(query[:, head * HEAD_DIM : (head + 1) * HEAD_DIM]).astype(halves)
    for step in range(2, nz):
        gathers["m"].pass_on(step)
    take(1, 1)
    give(3, 1)
    give(2, 0)
    outers = Line(courier, place, lambda group: ct_ref.at[group, y])
    ct_side = {}

    def ct_on(item):
        step, way, group, exists = item
        if step:
            outers.arrive(*item)
        spot = ct_ref.at[group, y]
        ct_side[step, way] = courier.copy(spot, spot, place.across["y"], exists)

    ct_own.wait()
    ct_on(outers.items()[0])
    gathers["m"].to_core()
    hand(0, 0)
    hand(0, 1)

    def attend(first, last):
        @pl.loop(first, last)
        def _(head):
            keys = pair_ref[:, :, :HEAD_DIM].reshape(total_keys, HEAD_DIM)
            values = pair_ref[:, :, HEAD_DIM:].reshape(total_keys, HEAD_DIM)
            scores = lax.dot_general(
                query_ref[head], keys, last_pair, preferred_element_type=floats
            )
            scores = scores * SCALE + bias_mask[...]
            top = jnp.max(scores, axis=-1, keepdims=True)
            raised = jnp.exp(scores - top)
            shares = (raised / jnp.sum(raised, axis=-1, keepdims=True)).astype(halves)
            share_ref[head] = shares
            lanes = pl.ds(pl.multiple_of(head * HEAD_DIM, 128), HEAD_DIM)
            out_ref[:, lanes] = jnp.dot(shares, values, preferred_element_type=floats)

    attend(0, GROUP // 2)
    take(3, 0)
    give(2, 1)
    attend(GROUP // 2, GROUP)
    outers.start()
    gathers["m"].done()
    saves = [keep(joint_kv, kv_out), keep(joint_q, query_out), keep(merge, merge_out)]
    merged = lax.dot_general(
        out_ref[...].astype(halves),
        merge[...].reshape(model, half),
        last_pair,
        preferred_element_type=floats,
    )
    mixed_ref[...] = jnp.where(x == 0, merged[:length], merged[length:])
    mixed_send[...] = jnp.where(x == 0, merged[length:], merged[:length]).astype(halves)
    mixed_cross = courier.copy(mixed_send, mixed_in, place.across["x"])
    take(3, 1)
    hand(1, 0)
    for item in outers.items()[1:3]:
        ct_on(item)
    mixed_cross.wait_recv()
    mixed = tokens_ref[...].astype(floats) + (mixed_ref[...] + mixed_in[...].astype(floats))
    mixed_ref[...] = mixed
    xn2_ref[...] = (mixed * norm_parts(mixed) * gain_second).astype(halves)
    take(2, 0)
    hand(1, 1)
    for item in outers.items()[3:5]:
        ct_on(item)
    hand(3, 0)
    take(2, 1)
    for item in outers.items()[5:]:
        ct_on(item)
    for spot in ((3, 1), (2, 0), (2, 1)):
        hand(*spot)
    for made in w_hand.values():
        made.wait_recv()
    for made in ct_side.values():
        made.wait_recv()
    for made in saves:
        made.wait()
    courier.finish()


def feed_kernel(
    nz,
    w_ref,
    ct_ref,
    normal_ref,
    back_ref,
    branch_ref,
    done_ref,
    grads_ref,
    w,
    xn,
    ct,
    hid,
    gb,
    ub,
    part,
    ybuf,
    zsend,
    zbuf,
    cbuf,
    xbuf,
    sends,
    receives,
    locals_,
):
    place = Place(nz)
    z, x, y, c = place.z, place.x, place.y, place.c
    length, model = normal_ref.shape
    share = w.shape[-1]
    block = model // nz
    lines = 2 * length * nz
    courier = Courier(sends, receives)

    def source(dz):
        return lax.rem(z + nz - dz, nz)

    meet([place.line(dz) for dz in range(1, nz)] + [place.across[name] for name in "xyc"])
    xn[z, y] = normal_ref[...]
    blocks = Line(courier, place, lambda group: xn.at[group, y])
    blocks.start()
    side = {}

    def pass_on(step):
        for item in blocks.items():
            if item[0] == step:
                way, group, exists = item[1:]
                if step:
                    blocks.arrive(*item)
                spot = xn.at[group, y]
                side[step, way] = courier.copy(spot, spot, place.across["y"], exists)

    pass_on(0)
    groups = near_first(nz)

    def group_at(number):
        return sum(jnp.where(z == at, groups[at][number], 0) for at in range(nz))

    def wait_for(number):
        for at in range(nz):
            gap = groups[at][number] - at
            made = side[abs(gap), 0 if gap == 0 else (1 if gap < 0 else -1)]
            pl.when(z == at)(made.raw.wait_recv)

    loads = [
        pltpu.make_async_copy(w_ref.at[which], w.at[which], locals_.at[which])
        for which in range(3)
    ] + [pltpu.make_async_copy(ct_ref, ct, locals_.at[3])]
    for made in loads:
        made.start()
    pass_on(1)
    for made in loads:
        made.wait()

    def weight(which, start, size):
        return w[which, :, :, :, :, :, start : start + size].reshape(model, size)

    half = nz // 2
    scatter = {}

    def scatter_on(dz):
        group = group_at(dz)
        scatter[dz] = courier.copy(
            part.at[group, 1 - y], ybuf.at[group], place.across["y"]
        )

    for dz in range(nz):
        group = group_at(dz)
        wait_for(dz)
        for start, size in cuts_of(share, 256):
            normal = xn[group].reshape(2 * length, model)
            outer = ct[group].reshape(2 * length, model)
            gate = jnp.dot(normal, weight(0, start, size), preferred_element_type=floats)
            upper = jnp.dot(normal, weight(1, start, size), preferred_element_type=floats)
            hidden_back = jnp.dot(outer, weight(2, start, size), preferred_element_type=floats)
            sig = 1.0 / (1.0 + jnp.exp(-gate))
            silu = gate * sig
            spot = (group, slice(None), slice(start, start + size))
            hid[spot] = (silu * upper).astype(halves)
            gb[spot] = (hidden_back * upper * (sig * (1.0 + gate * (1.0 - sig)))).astype(halves)
            ub[spot] = (hidden_back * silu).astype(halves)

        @pl.loop(0, 2)
        def _(step):
            rows = pl.ds(step * half, half)
            lanes = pl.ds(pl.multiple_of(step * (model // 2), 128), model // 2)

            def turned(which):
                return w[which, rows].reshape(model // 2, share)

            both = lax.dot_general(
                gb[group], turned(0), last_pair, preferred_element_type=floats
            ) + lax.dot_general(ub[group], turned(1), last_pair, preferred_element_type=floats)
            part[group, :, :, lanes] = both.astype(halves).reshape(2, length, model // 2)

        if dz:
            scatter_on(dz)
        if dz + 2 < nz:
            pass_on(dz + 2)

        @pl.loop(0, 2)
        def _(step):
            rows = pl.ds(step * half, half)
            lanes = pl.ds(pl.multiple_of(step * (model // 2), 128), model // 2)
            product = lax.dot_general(
                hid[group],
                w[2, rows].reshape(model // 2, share),
                last_pair,
                preferred_element_type=floats,
            )
            branch_ref[group, :, :, lanes] = product.astype(halves).reshape(2, length, model // 2)


    scatter_on(0)

    final = {
        dz: courier.make(
            zsend.at[source(dz)], zbuf.at[dz - 1], (source(dz), x, y, c)
        )
        for dz in range(1, nz)
    }

    def sum_on(dz):
        group = group_at(dz)
        scatter[dz].wait_recv()
        total = part[group, y].astype(floats) + ybuf[group].astype(floats)
        if dz == 0:
            back_ref[...] = total
        else:
            zsend[group] = total.astype(halves)
            for apart, made in final.items():
                pl.when(source(apart) == group)(made.raw.start)

    orders = far_first(nz)
    early = 2
    handed, crossed, saves = {}, {}, []

    def save(source, target):
        made = pltpu.make_async_copy(source, target, locals_.at[4 + len(saves)])
        made.start()
        saves.append(made)

    def product(dz):
        group = lax.rem(z + dz, nz)
        lanes = pl.ds(pl.multiple_of(group * block, 128), block)
        normal_turned = xn[:, :, :, lanes].reshape(lines, block).T
        outer_turned = ct[:, :, :, lanes].reshape(lines, block).T
        for which, left, right in (
            (0, normal_turned, gb),
            (1, normal_turned, ub),
            (2, outer_turned, hid),
        ):
            for start, size in cuts_of(share, 512):
                w[which, group, :, :, :, :, start : start + size] = (
                    jnp.dot(
                        left,
                        right[:, :, start : start + size].reshape(lines, size),
                        preferred_element_type=floats,
                    )
                    .astype(halves)
                    .reshape(2, 2, 2, -1, size)
                )
        handed[dz] = courier.copy(
            w.at[:, group, :, :, 1 - c], cbuf.at[dz], place.across["c"]
        )

    def settle(position):
        dz = orders[position]
        group = lax.rem(z + dz, nz)
        handed[dz].wait_recv()
        for which in range(3):
            w[which, group, :, :, c] = (
                w[which, group, :, :, c].astype(floats) + cbuf[dz, which].astype(floats)
            ).astype(halves)
        if position < early:
            crossed[position] = courier.copy(
                w.at[:, group, 1 - x, :, c], xbuf.at[position], place.across["x"]
            )
        else:
            save(w.at[:, group, :, :, c], grads_ref.at[:, position - early])

    for position in range(nz):
        product(orders[position])
        sum_on((position + 1) % nz)
        if position:
            settle(position - 1)
    settle(nz - 1)
    for position in range(early):
        group = lax.rem(z + orders[position], nz)
        crossed[position].wait_recv()
        for which in range(3):
            w[which, group, x, :, c] = (
                w[which, group, x, :, c].astype(floats) + xbuf[position, which].astype(floats)
            ).astype(halves)
        save(w.at[:, group, x, :, c], done_ref.at[:, position])
    for dz in range(1, nz):
        final[dz].wait_recv()
        back_ref[...] += zbuf[dz - 1].astype(floats)
    for made in saves:
        made.wait()
    courier.finish()


class LineSum:
    def __init__(self, courier, place, parts, spot, above, below):
        self.courier, self.place, self.parts, self.spot = courier, place, parts, spot
        self.arrivals = {1: above, -1: below}
        self.sent = {}

    def add(self, target, way):
        nz = self.place.nz
        spot = self.spot(target)
        arrived = self.arrivals[way][target - 1 if way == 1 else target]
        self.parts[spot] = (self.parts[spot].astype(floats) + arrived.astype(floats)).astype(
            self.parts.dtype
        )

    def forward(self, target, way):
        p = self.place
        moving = p.z < target if way == 1 else p.z > target
        fed = p.z > 0 if way == 1 else p.z < p.nz - 1
        made = self.courier.make(
            self.parts.at[self.spot(target)],
            self.arrivals[way].at[target - 1 if way == 1 else target],
            p.line_at(way),
            moving,
        )
        self.sent[target, way] = made

        @pl.when(moving & fed)
        def _():
            made.raw.wait_recv()
            self.add(target, way)

        made.start()

    def forward_step(self, step):
        self.forward(self.place.nz - 1 - step, 1)
        self.forward(step, -1)

    def finish(self):
        p = self.place
        for (target, way), made in self.sent.items():
            fed = p.z > 0 if way == 1 else p.z < p.nz - 1

            @pl.when((p.z == target) & fed)
            def _(target=target, way=way, made=made):
                made.raw.wait_recv()
                self.add(target, way)


class Scatter:
    def __init__(self, courier, place, parts, core_in, side_in, above, below, last_in):
        self.courier, self.place, self.parts = courier, place, parts
        self.core_in, self.side_in, self.last_in = core_in, side_in, last_in
        every = slice(None)
        self.line = LineSum(
            courier, place, parts, lambda group: (group, every, place.y, place.c), above, below
        )
        self.groups = []
        for step in range((place.nz + 1) // 2):
            self.groups += [place.nz - 1 - step, step]
        self.core, self.side = {}, {}

    def to_core(self, group):
        p = self.place
        self.core[group] = self.courier.copy(
            self.parts.at[group, :, :, 1 - p.c], self.core_in.at[group], p.across["c"]
        )

    def add(self, spot, arrived):
        self.parts[spot] = (self.parts[spot].astype(floats) + arrived.astype(floats)).astype(
            self.parts.dtype
        )

    def sideways(self):
        p = self.place
        every = slice(None)
        for group in self.groups:
            self.core[group].wait_recv()
            self.add((group, every, every, p.c), self.core_in[group])
            self.side[group] = self.courier.copy(
                self.parts.at[group, :, 1 - p.y, p.c], self.side_in.at[group], p.across["y"]
            )

    def along(self):
        p = self.place
        for group in self.groups:
            self.side[group].wait_recv()
            self.add((group, slice(None), p.y, p.c), self.side_in[group])

    def across(self):
        p = self.place
        self.line.finish()
        self.last = self.courier.copy(
            self.parts.at[p.z, 1 - p.x, p.y, p.c], self.last_in, p.across["x"]
        )

    def own(self):
        p = self.place
        return self.parts[p.z, p.x, p.y, p.c].astype(floats)

    def other(self):
        self.last.wait_recv()
        return self.last_in[...].astype(floats)


def gather_pieces(values, piece, devices):
    width = values.shape[1]
    owner = lax.div(lax.broadcasted_iota(jnp.int32, (devices, width), 1), piece)
    mine = owner == lax.broadcasted_iota(jnp.int32, (devices, width), 0)
    at = lax.broadcasted_iota(jnp.int32, (width, 128), 0)
    inner = lax.broadcasted_iota(jnp.int32, (width, 128), 1)
    chosen = (lax.rem(at, piece) == inner).astype(floats)
    rows = jnp.where(mine, values, 0.0)
    return jnp.dot(rows, chosen, preferred_element_type=floats, precision=lax.Precision.HIGHEST)


def back_kernel(
    nz,
    done_ref,
    grads_in,
    branch_ref,
    kv_ref,
    q_ref,
    m_ref,
    back_ref,
    mixed_ref,
    outer_ref,
    tokens_ref,
    xn1_ref,
    gain_ref,
    turn_ref,
    query_ref,
    pair_ref,
    share_ref,
    out_ref,
    output_ref,
    tokens_grad_ref,
    joint_grad_ref,
    merge_grad_ref,
    small_grad_ref,
    grads_ref,
    weight_m,
    weight_q,
    weight_kv,
    gown,
    gin,
    branch_own,
    branch_in,
    branch_above,
    branch_below,
    *rest,
):
    merge_bufs, query_bufs, kv_bufs, small_bufs = (rest[6 * i : 6 * i + 6] for i in range(4))
    (
        pair_sum,
        pair_half,
        pair_above,
        pair_below,
        joint_back,
        attended_back,
        mixed_both,
        back_send,
        back_in,
        sends,
        receives,
        locals_,
    ) = rest[24:]
    place = Place(nz)
    z, x, y, c = place.z, place.x, place.y, place.c
    length, model = tokens_ref.shape
    share = gown.shape[-1]
    half = GROUP * HEAD_DIM
    both = 2 * length
    block = model // nz
    depth = grads_in.shape[-2]
    devices = 8 * nz
    total_keys = nz * both
    orders = far_first(nz)
    courier = Courier(sends, receives)
    meet(place.peers())

    def group_of(dz):
        return lax.rem(z + dz, nz)

    copies = []

    def load(source, target):
        made = pltpu.make_async_copy(source, target, locals_.at[len(copies)])
        made.start()
        copies.append(made)
        return made

    merge_load = load(m_ref, weight_m)
    branch_load = load(branch_ref.at[:, y], branch_own)
    gown_load = load(grads_in.at[:, :, x], gown)
    early = 2
    late = orders[early:]
    query_load = load(q_ref, weight_q)
    kv_load = load(kv_ref, weight_kv)

    b_cross = {
        group: courier.copy(branch_ref.at[group, 1 - y], branch_in.at[group], place.across["y"])
        for group in range(nz)
    }
    g_cross, g_line, kept = {}, [], []

    def grads_across(dz):
        g_cross[dz] = courier.copy(
            grads_in.at[:, late.index(dz), 1 - x], gin.at[late.index(dz)], place.across["x"]
        )

    mine = pl.ds(pl.multiple_of((z * 2 + y) * share, 128), share)

    def grads_line(dz, rows):
        for dy in range(2):
            ty = lax.rem(y + dy, 2)
            if dz or dy:
                g_line.append(
                    courier.copy(
                        rows.at[:, ty], grads_ref.at[:, :, mine], (group_of(dz), x, ty, c)
                    )
                )
            else:
                kept.append(load(rows.at[:, ty], grads_ref.at[:, :, mine]))

    for position in range(early):
        grads_line(orders[position], done_ref.at[:, position])

    mixed = mixed_ref[...]
    second_scale = norm_parts(mixed)
    part, second_local = norm_back(back_ref[...], mixed, second_scale, gain_ref[1:2, :])
    grad = outer_ref[...].astype(floats) + part
    tokens_grad_ref[...] = grad
    mixed_both[x] = grad.astype(halves)
    mixed_cross = courier.copy(mixed_both.at[x], mixed_both.at[x], place.across["x"])
    mixed_cross.wait_recv()
    for dz in late:
        grads_across(dz)

    merge_load.wait()
    upstream_both = mixed_both[...].reshape(both, model)
    attended_back[...] = jnp.dot(
        upstream_both, weight_m[...].reshape(model, half), preferred_element_type=floats
    ).astype(halves)
    merges = Scatter(courier, place, *merge_bufs)
    queries = Scatter(courier, place, *query_bufs)
    keys_values = Scatter(courier, place, *kv_bufs)
    smalls = Scatter(courier, place, *small_bufs)

    def product_rows(scatter, left, right):
        for group in scatter.groups:
            scatter.parts[group] = (
                jnp.dot(
                    left[group * block : (group + 1) * block], right, preferred_element_type=floats
                )
                .astype(halves)
                .reshape(2, 2, 2, depth, right.shape[1])
            )
            scatter.to_core(group)

    product_rows(merges, upstream_both.T, out_ref[...].astype(halves))

    def attend(first, last):
        @pl.loop(first, last)
        def _(head):
            query = query_ref[head]
            keys = pair_ref[:, :, :HEAD_DIM].reshape(total_keys, HEAD_DIM)
            values = pair_ref[:, :, HEAD_DIM:].reshape(total_keys, HEAD_DIM)
            lanes = pl.ds(pl.multiple_of(head * HEAD_DIM, 128), HEAD_DIM)
            upstream = attended_back[:, lanes]
            delta = jnp.sum(upstream.astype(floats) * out_ref[:, lanes], axis=-1, keepdims=True)
            mass = lax.dot_general(upstream, values, last_pair, preferred_element_type=floats)
            shares = share_ref[head]
            scores = (shares.astype(floats) * (mass - delta)).astype(halves)
            query_sum = jnp.dot(scores, keys, preferred_element_type=floats) * SCALE
            cosine, sine = turn_ref[0], turn_ref[1]
            joint_back[:, lanes] = (
                query_sum * cosine + pltpu.roll(query_sum * sine, HEAD_DIM // 2, 1)
            ).astype(halves)
            pair_sum[:, :HEAD_DIM] += (
                jnp.dot(scores.T, query, preferred_element_type=floats) * SCALE
            )
            pair_sum[:, HEAD_DIM:] += jnp.dot(shares.T, upstream, preferred_element_type=floats)

    def grads_on(dz):
        at = late.index(dz)
        g_cross[dz].wait_recv()
        for which in range(3):
            gown[which, at] = (
                gown[which, at].astype(floats) + gin[at, which].astype(floats)
            ).astype(halves)
        grads_line(dz, gown.at[:, at])

    pair_sum[...] = jnp.zeros_like(pair_sum)
    attend(0, GROUP // 2)
    merges.sideways()

    attend(GROUP // 2, GROUP)

    pair_half[...] = pair_sum[...].astype(halves).reshape(nz, both, 2 * HEAD_DIM)
    pairs = LineSum(courier, place, pair_half, lambda group: (group,), pair_above, pair_below)
    pairs.forward(nz - 1, 1)
    pairs.forward(0, -1)
    turned = xn1_ref[...].T
    product_rows(queries, turned, joint_back[:, :half])
    for step in range(1, nz - 1):
        pairs.forward(nz - 1 - step, 1)
        pairs.forward(step, -1)
    branch_load.wait()
    for group in range(nz):
        b_cross[group].wait_recv()
        branch_own[group] = (
            branch_own[group].astype(floats) + branch_in[group].astype(floats)
        ).astype(halves)
    pairs.finish()
    total = pair_half[z].astype(floats)
    key_total = total[:, :HEAD_DIM]
    joint_back[:, half : half + HEAD_DIM] = (
        key_total * turn_ref[0] + pltpu.roll(key_total * turn_ref[1], HEAD_DIM // 2, 1)
    ).astype(halves)
    joint_back[:, half + HEAD_DIM :] = total[:, HEAD_DIM:].astype(halves)
    product_rows(keys_values, turned, joint_back[:, half:])
    query_load.wait()
    kv_load.wait()
    normal_back = lax.dot_general(
        joint_back[:, :half],
        weight_q[...].reshape(model, half),
        last_pair,
        preferred_element_type=floats,
    ) + lax.dot_general(
        joint_back[:, half:],
        weight_kv[...].reshape(model, 2 * HEAD_DIM),
        last_pair,
        preferred_element_type=floats,
    )
    back_send[...] = jnp.where(x == 0, normal_back[length:], normal_back[:length]).astype(halves)
    back_cross = courier.copy(back_send, back_in, place.across["x"])
    normal_own = jnp.where(x == 0, normal_back[:length], normal_back[length:])
    queries.sideways()
    keys_values.sideways()
    gown_load.wait()
    for dz in late[:1]:
        grads_on(dz)

    local = jnp.sum(joint_back[...].astype(floats), axis=0, keepdims=True)
    pieces_of = []
    for first, width in ((0, half), (half, HEAD_DIM), (half + HEAD_DIM, HEAD_DIM)):
        for side in range(2):
            pieces_of.append(jnp.where(x == side, local[:, first : first + width], 0.0))
    bias_local = jnp.concatenate(pieces_of, axis=1)
    def piece_rows(which, values):
        mine_rows = gather_pieces(values, values.shape[1] // devices, devices)
        at = lax.broadcasted_iota(jnp.int32, (devices * 8, devices), 0)
        wanted = lax.broadcasted_iota(jnp.int32, (devices * 8, devices), 1) * 8 + which
        return jnp.dot(
            (at == wanted).astype(floats),
            mine_rows,
            preferred_element_type=floats,
            precision=lax.Precision.HIGHEST,
        )

    pieces = piece_rows(0, bias_local) + piece_rows(2, second_local)
    branches = LineSum(
        courier, place, branch_own, lambda group: (group,), branch_above, branch_below
    )
    back_cross.wait_recv()
    normal_own = normal_own + back_in[...].astype(floats)
    residual = tokens_ref[...].astype(floats)
    part, first_local = norm_back(normal_own, residual, norm_parts(residual), gain_ref[0:1, :])
    tokens_grad_ref[...] += part

    pieces = pieces + piece_rows(1, first_local)
    smalls.parts[...] = pieces.reshape(nz, 2, 2, 2, 8, 128)
    for group in smalls.groups:
        smalls.to_core(group)
    for made in (merges, queries, keys_values):
        made.along()
    for line in (keys_values.line, queries.line, merges.line, branches):
        line.forward_step(0)
    for line in (keys_values.line, queries.line, merges.line, branches):
        line.forward_step(1)
    for dz in late[1:]:
        grads_on(dz)
    smalls.sideways()
    for line in (keys_values.line, queries.line, merges.line, branches):
        line.forward_step(2)
    smalls.along()
    for step in range(nz - 1):
        smalls.line.forward_step(step)
    for made in (merges, queries, keys_values, smalls):
        made.across()
    branches.finish()
    output_ref[...] = (mixed_ref[...] + branch_own[z].astype(floats)).astype(halves)
    for ref, made, pieces in (
        (merge_grad_ref, merges, [(0, half)]),
        (joint_grad_ref, queries, [(0, half)]),
        (joint_grad_ref, keys_values, KV_PIECES),
    ):
        for side, values in ((x, made.own()), (1 - x, made.other())):
            at = 0
            for first, width in pieces:
                lanes = pl.ds(pl.multiple_of(first + side * width, 128), width)
                ref[:, lanes] = values[:, at : at + width]
                at += width
    small_grad_ref[...] = smalls.own() + smalls.other()
    for made in g_line:
        made.wait_recv()
    for made in kept:
        made.wait()
    courier.finish()


def padded_share(hidden_width, team):
    return -(-hidden_width // (team * 128)) * 128


def body_kernels(
    tokens,
    segments,
    joint_matrix,
    joint_bias,
    merge_matrix,
    norm_first,
    norm_second,
    gate_matrix,
    up_matrix,
    down_matrix,
    cotangent,
):
    length, model = tokens.shape[1:]
    depth, joint_width = joint_matrix.shape
    hidden_width = gate_matrix.shape[1]
    nz = lax.axis_size("z")
    share = padded_share(hidden_width, 2 * nz)
    half = GROUP * HEAD_DIM
    pair_width = 2 * HEAD_DIM
    both = 2 * length
    keys = nz * both
    vmem = pl.BlockSpec(memory_space=pltpu.VMEM)
    anywhere = pl.BlockSpec(memory_space=pl.ANY)
    blocks = (nz, 2, 2, 2)

    def shape(dims, kind=halves):
        return jax.ShapeDtypeStruct(dims, kind)

    def semaphores(count, loads):
        return [
            pltpu.SemaphoreType.DMA((count,)),
            pltpu.SemaphoreType.DMA((count,)),
            pltpu.SemaphoreType.DMA((loads,)),
        ]

    def params(number):
        return pltpu.CompilerParams(
            collective_id=number, has_side_effects=True, vmem_limit_bytes=VMEM_LIMIT
        )

    stack = jnp.stack([gate_matrix, up_matrix, down_matrix.T])
    stack = jnp.pad(stack, ((0, 0), (0, 0), (0, 2 * nz * share - hidden_width)))

    def lane_row(values):
        return jnp.pad(values.astype(floats), (0, 128 - values.shape[0]))

    own_labels = segments[0]
    at = lax.broadcasted_iota(jnp.int32, (8, 128), 0)
    small = jnp.zeros((8, 128), floats)
    for which, values in enumerate((joint_bias, norm_first, norm_second, own_labels)):
        small = jnp.where(at == which, lane_row(values)[None], small)
    inverse = theta ** -(np.arange(HEAD_DIM // 2) * (2.0 / HEAD_DIM))
    inverse = jnp.asarray(np.tile(inverse, 2)[None], floats)
    outer = cotangent[0]
    (
        w,
        team_outer,
        kv_all,
        q_all,
        m_all,
        xn1,
        xn2,
        mixed,
        gains,
        turns,
        queries,
        pair,
        shares,
        summed,
    ) = pl.pallas_call(
        functools.partial(attention_kernel, nz),
        name="attention_forward",
        out_shape=(
            shape((3,) + blocks + (depth, share)),
            shape((nz, 2, length, model)),
            shape(blocks + (depth, pair_width)),
            shape(blocks + (depth, half)),
            shape(blocks + (depth, half)),
            shape((both, model)),
            shape((length, model)),
            shape((length, model), floats),
            shape((8, model), floats),
            shape((2, both, HEAD_DIM), floats),
            shape((GROUP, both, HEAD_DIM)),
            shape((nz, both, pair_width)),
            shape((GROUP, both, keys)),
            shape((both, half), floats),
        ),
        in_specs=[anywhere] * 3 + [vmem] * 4,
        out_specs=(anywhere,) * 5 + (vmem,) * 9,
        scratch_shapes=[
            pltpu.VMEM(blocks + (depth, pair_width), halves),
            pltpu.VMEM(blocks + (depth, half), halves),
            pltpu.VMEM(blocks + (depth, half), halves),
            pltpu.VMEM(blocks + (8, 128), floats),
            pltpu.VMEM((both, keys), floats),
            pltpu.VMEM((2, length, model), halves),
            pltpu.VMEM((length, model), halves),
            pltpu.VMEM((length, model), halves),
        ]
        + semaphores(137, 10),
        compiler_params=params(0),
    )(stack, joint_matrix, merge_matrix.T, small, inverse, tokens[0], outer)

    lines = 2 * length
    back, branch, done, grads = pl.pallas_call(
        functools.partial(feed_kernel, nz),
        name="feed_forward",
        out_shape=(
            shape((length, model), floats),
            shape((nz, 2, length, model)),
            shape((3, 2, 2, depth, share)),
            shape((3, nz - 2, 2, 2, depth, share)),
        ),
        in_specs=[anywhere, anywhere, vmem],
        out_specs=(vmem, vmem, anywhere, anywhere),
        scratch_shapes=[
            pltpu.VMEM((3,) + blocks + (depth, share), halves),
            pltpu.VMEM((nz, 2, length, model), halves),
            pltpu.VMEM((nz, 2, length, model), halves),
            pltpu.VMEM((nz, lines, share), halves),
            pltpu.VMEM((nz, lines, share), halves),
            pltpu.VMEM((nz, lines, share), halves),
            pltpu.VMEM((nz, 2, length, model), halves),
            pltpu.VMEM((nz, length, model), halves),
            pltpu.VMEM((nz, length, model), halves),
            pltpu.VMEM((nz - 1, length, model), halves),
            pltpu.VMEM((nz, 3, 2, 2, depth, share), halves),
            pltpu.VMEM((2, 3, 2, depth, share), halves),
        ]
        + semaphores(30, 8),
        compiler_params=params(1),
    )(w, team_outer, xn2)

    def sums(rows, width, kind=halves):
        return [
            pltpu.VMEM(blocks + (rows, width), kind),
            pltpu.VMEM((nz, 2, 2, rows, width), kind),
            pltpu.VMEM((nz, 2, rows, width), kind),
            pltpu.VMEM((nz - 1, 2, rows, width), kind),
            pltpu.VMEM((nz - 1, 2, rows, width), kind),
            pltpu.VMEM((rows, width), kind),
        ]

    output, tokens_grad, joint_grad, merge_grad, small_grad, grads = pl.pallas_call(
        functools.partial(back_kernel, nz),
        name="attention_backward",
        out_shape=(
            shape((length, model)),
            shape((length, model), floats),
            shape((depth, joint_width), floats),
            shape((depth, QUERY_WIDTH), floats),
            shape((8, 128), floats),
            shape((3, depth, 2 * nz * share)),
        ),
        in_specs=[anywhere] * 6 + [vmem] * 11,
        out_specs=(vmem,) * 5 + (anywhere,),
        scratch_shapes=[
            pltpu.VMEM(blocks + (depth, half), halves),
            pltpu.VMEM(blocks + (depth, half), halves),
            pltpu.VMEM(blocks + (depth, pair_width), halves),
            pltpu.VMEM((3, nz - 2, 2, depth, share), halves),
            pltpu.VMEM((nz - 2, 3, 2, depth, share), halves),
            pltpu.VMEM((nz, length, model), halves),
            pltpu.VMEM((nz, length, model), halves),
            pltpu.VMEM((nz - 1, length, model), halves),
            pltpu.VMEM((nz - 1, length, model), halves),
        ]
        + sums(depth, half)
        + sums(depth, half)
        + sums(depth, pair_width)
        + sums(8, 128, floats)
        + [
            pltpu.VMEM((keys, pair_width), floats),
            pltpu.VMEM((nz, both, pair_width), halves),
            pltpu.VMEM((nz - 1, both, pair_width), halves),
            pltpu.VMEM((nz - 1, both, pair_width), halves),
            pltpu.VMEM((both, half + pair_width), halves),
            pltpu.VMEM((both, half), halves),
            pltpu.VMEM((2, length, model), halves),
            pltpu.VMEM((length, model), halves),
            pltpu.VMEM((length, model), halves),
        ]
        + semaphores(90, 6),
        compiler_params=params(2),
    )(
        done,
        grads,
        branch,
        kv_all,
        q_all,
        m_all,
        back,
        mixed,
        outer,
        tokens[0],
        xn1,
        gains,
        turns,
        queries,
        pair,
        shares,
        summed,
    )
    grads = [grads[which, :, :hidden_width].astype(floats) for which in range(3)]
    return (
        output[None],
        tokens_grad[None],
        joint_grad,
        small_grad[0, : joint_bias.shape[0]],
        merge_grad.T,
        small_grad[1, :depth],
        small_grad[2, :depth],
        grads[0],
        grads[1],
        grads[2].T,
    )


def body_plain(
    tokens,
    segments,
    joint_matrix,
    joint_bias,
    merge_matrix,
    norm_first,
    norm_second,
    gate_matrix,
    up_matrix,
    down_matrix,
    cotangent,
):
    residual = tokens[0].astype(floats)
    length, model = residual.shape
    depth = joint_matrix.shape[0]
    joint_width = joint_matrix.shape[1]
    hidden_width = gate_matrix.shape[1]
    z_count = lax.axis_size("z")
    team = lax.axis_size(TEAM)
    share = hidden_width // team
    own_labels = segments[0]
    labels = lax.all_gather(own_labels, SEQ, axis=0, tiled=True)
    offset = lax.axis_index(SEQ) * length
    places = offset + jnp.arange(length, dtype=jnp.int32)
    positions = lax.dynamic_slice_in_dim(row_positions(labels), offset, length, 0)
    cosine, sine = rotary(positions, HEAD_DIM)

    small = jnp.concatenate([joint_bias, norm_first, norm_second])
    small = jnp.pad(small, (0, -small.shape[0] % depth)).reshape(depth, -1)
    small_width = small.shape[1]
    packed = jnp.concatenate([joint_matrix, merge_matrix.T, small], axis=1)
    packed = lax.all_gather(packed, AXES, axis=0, tiled=True)
    joint_all = packed[:, :joint_width]
    merge_turned = packed[:, joint_width : joint_width + model]
    small = packed[:, joint_width + model :].reshape(-1, depth * small_width).astype(floats)
    bias_depth = joint_bias.shape[0]
    bias_all = small[:, :bias_depth].reshape(-1)
    gain_first = small[:, bias_depth : bias_depth + depth].reshape(-1)
    gain_second = small[:, bias_depth + depth : bias_depth + 2 * depth].reshape(-1)

    stacked = jnp.stack([gate_matrix, up_matrix, down_matrix.T], axis=1)
    stacked = stacked.reshape(depth, 3, team, share).transpose(2, 0, 1, 3)
    stacked = stacked.reshape(team, depth, 3 * share)
    stacked = lax.all_to_all(stacked, TEAM, split_axis=0, concat_axis=0, tiled=True)
    stacked = stacked.reshape(z_count, 1, team // z_count, 1, depth, 3 * share)
    stacked = lax.all_gather(stacked, "x", axis=1, tiled=True)
    stacked = lax.all_gather(stacked, "c", axis=3, tiled=True)
    stacked = stacked.reshape(model, 3 * share)
    both_all, down_turned = stacked[:, : 2 * share], stacked[:, 2 * share :]
    outer_grad = cotangent[0]
    team_outer = lax.all_gather(outer_grad, TEAM, axis=0, tiled=True)

    scale_first = norm_parts(residual)
    normal_first = (residual * scale_first * gain_first).astype(halves)
    joint = jnp.dot(normal_first, joint_all, preferred_element_type=floats) + bias_all
    query = joint[:, :QUERY_WIDTH].reshape(length, HEADS, HEAD_DIM)
    keys = joint[:, QUERY_WIDTH : QUERY_WIDTH + KEY_WIDTH].reshape(length, KV_HEADS, HEAD_DIM)
    values = joint[:, QUERY_WIDTH + KEY_WIDTH :].astype(halves)
    query = (query * cosine + turn_half(query) * sine).astype(halves)
    keys = (keys * cosine + turn_half(keys) * sine).astype(halves).reshape(length, KEY_WIDTH)
    query_group = to_groups(query)
    pair = lax.all_gather(jnp.concatenate([keys, values], axis=1), SEQ, axis=0, tiled=True)
    count = pair.shape[0]
    key_all = pair[:, :KEY_WIDTH].reshape(count, KV_HEADS, HEAD_DIM)
    value_all = pair[:, KEY_WIDTH:].reshape(count, KV_HEADS, HEAD_DIM)
    allowed = (places[:, None] >= jnp.arange(count, dtype=jnp.int32)[None, :]) & (
        own_labels[:, None] == labels[None, :]
    )
    allowed = jnp.tile(allowed, (GROUP, 1))[None]
    scores = jnp.einsum("krd,nkd->krn", query_group, key_all, preferred_element_type=floats)
    scores = jnp.where(allowed, scores * SCALE, neg)
    top = jnp.max(scores, axis=-1, keepdims=True)
    weights = jnp.where(allowed, jnp.exp(scores - top), 0.0)
    total = jnp.sum(weights, axis=-1, keepdims=True)
    shares = weights / total
    shares_half = shares.astype(halves)
    attended = jnp.einsum("krn,nkd->krd", shares_half, value_all, preferred_element_type=floats)
    attended_half = from_groups(attended, length).astype(halves)
    mixed = residual + lax.dot_general(
        attended_half, merge_turned, last_pair, preferred_element_type=floats
    )
    scale_second = norm_parts(mixed)
    normal_half = (mixed * scale_second * gain_second).astype(halves)

    team_normal = lax.all_gather(normal_half, TEAM, axis=0, tiled=True)
    both = jnp.dot(team_normal, both_all, preferred_element_type=floats)
    gate, upper = both[:, :share], both[:, share:]
    sig = jax.nn.sigmoid(gate)
    silu = gate * sig
    hidden_half = (silu * upper).astype(halves)
    branch = lax.dot_general(hidden_half, down_turned, last_pair, preferred_element_type=floats)
    hidden_grad = jnp.dot(team_outer, down_turned, preferred_element_type=floats)
    gate_half = (hidden_grad * upper * sig * (1.0 + gate * (1.0 - sig))).astype(halves)
    upper_half = (hidden_grad * silu).astype(halves)
    both_half = jnp.concatenate([gate_half, upper_half], axis=1)
    normal_grad = lax.dot_general(both_half, both_all, last_pair, preferred_element_type=floats)
    branch = lax.psum_scatter(branch.astype(halves), TEAM, scatter_dimension=0, tiled=True)
    normal_grad = lax.psum_scatter(normal_grad.astype(halves), TEAM, scatter_dimension=0, tiled=True)
    output = (mixed + branch.astype(floats)).astype(halves)[None]
    both_grad = lax.dot_general(team_normal, both_half, first_pair, preferred_element_type=floats)
    down_grad = lax.dot_general(team_outer, hidden_half, first_pair, preferred_element_type=floats)
    grads = jnp.concatenate([both_grad, down_grad], axis=1).astype(halves)
    grads = grads.reshape(z_count, 2, team // z_count, 2, depth, 3 * share)
    grads = lax.psum_scatter(grads, "c", scatter_dimension=3, tiled=True)
    grads = lax.psum_scatter(grads, "x", scatter_dimension=1, tiled=True)
    grads = grads.reshape(team, depth, 3 * share)
    grads = lax.all_to_all(grads, TEAM, split_axis=0, concat_axis=0, tiled=True)
    grads = grads.reshape(team, depth, 3, share).transpose(2, 1, 0, 3)
    grads = grads.reshape(3, depth, hidden_width).astype(floats)

    normal_grad = normal_grad.astype(floats)
    mixed_part, second_local = norm_back(normal_grad, mixed, scale_second, gain_second)
    mixed_grad = outer_grad.astype(floats) + mixed_part
    mixed_half = mixed_grad.astype(halves)
    merge_local = lax.dot_general(
        mixed_half, attended_half, first_pair, preferred_element_type=floats
    )
    attended_grad = jnp.dot(mixed_half, merge_turned, preferred_element_type=floats).astype(halves)
    grad_group = to_groups(attended_grad.reshape(length, HEADS, HEAD_DIM))
    mass_grad = jnp.einsum("krd,nkd->krn", grad_group, value_all, preferred_element_type=floats)
    row_dots = jnp.sum(shares * mass_grad, axis=-1, keepdims=True)
    score_half = (shares * (mass_grad - row_dots)).astype(halves)
    query_sum = (
        jnp.einsum("krn,nkd->krd", score_half, key_all, preferred_element_type=floats) * SCALE
    )
    key_grad = (
        jnp.einsum("krn,krd->nkd", score_half, query_group, preferred_element_type=floats) * SCALE
    )
    value_grad = jnp.einsum("krn,krd->nkd", shares_half, grad_group, preferred_element_type=floats)
    pair_sums = jnp.concatenate(
        [key_grad.reshape(count, KEY_WIDTH), value_grad.reshape(count, KEY_WIDTH)], axis=1
    )
    pair_mine = lax.psum_scatter(
        pair_sums.astype(halves), SEQ, scatter_dimension=0, tiled=True
    ).astype(floats)
    key_back = pair_mine[:, :KEY_WIDTH].reshape(length, KV_HEADS, HEAD_DIM)
    value_back = pair_mine[:, KEY_WIDTH:]
    query_back = from_groups(query_sum, length).reshape(length, HEADS, HEAD_DIM)
    query_back = query_back * cosine + unturn_half(query_back * sine)
    key_back = key_back * cosine + unturn_half(key_back * sine)
    joint_back = jnp.concatenate(
        [query_back.reshape(length, QUERY_WIDTH), key_back.reshape(length, KEY_WIDTH), value_back],
        axis=1,
    ).astype(halves)
    joint_local = lax.dot_general(
        normal_first, joint_back, first_pair, preferred_element_type=floats
    )
    bias_local = jnp.sum(joint_back.astype(floats), axis=0)
    normal_back = lax.dot_general(joint_back, joint_all, last_pair, preferred_element_type=floats)
    residual_part, first_local = norm_back(normal_back, residual, scale_first, gain_first)
    tokens_grad = (mixed_grad + residual_part)[None]

    small_back = jnp.concatenate(
        [
            bias_local.reshape(-1, bias_depth),
            first_local.reshape(-1, depth),
            second_local.reshape(-1, depth),
        ],
        axis=1,
    )
    small_back = jnp.pad(small_back, ((0, 0), (0, depth * small_width - small_back.shape[1])))
    small_back = small_back.reshape(-1, small_width)
    packed_grad = jnp.concatenate([joint_local, merge_local, small_back], axis=1).astype(halves)
    packed_grad = lax.psum_scatter(packed_grad, AXES, scatter_dimension=0, tiled=True).astype(floats)
    joint_grad = packed_grad[:, :joint_width]
    merge_grad = packed_grad[:, joint_width : joint_width + model].T
    small_back = packed_grad[:, joint_width + model :].reshape(-1)
    bias_grad = small_back[:bias_depth]
    first_grad = small_back[bias_depth : bias_depth + depth]
    second_grad = small_back[bias_depth + depth : bias_depth + 2 * depth]
    return (
        output,
        tokens_grad,
        joint_grad,
        bias_grad,
        merge_grad,
        first_grad,
        second_grad,
        grads[0],
        grads[1],
        grads[2].T,
    )


def solution(mesh):
    seq, row = mesh.shape["seq"], mesh.shape["row"]
    fine = Mesh(mesh.devices.reshape(seq // 2, 2, row // 2, 2), AXES)
    whole = ("z", "x", "y", "c")
    placed = (
        P(ROW, SEQ, None),
        P(ROW, SEQ),
        P(whole, None),
        P(whole),
        P(None, whole),
        P(whole),
        P(whole),
        P(whole, None),
        P(whole, None),
        P(None, whole),
        P(ROW, SEQ, None),
    )
    depth = MODEL // mesh.size
    return jax.shard_map(
        body_kernels if depth % 16 == 0 else body_plain,
        mesh=fine,
        in_specs=placed,
        out_specs=(
            P(ROW, SEQ, None),
            P(ROW, SEQ, None),
            P(whole, None),
            P(whole),
            P(None, whole),
            P(whole),
            P(whole),
            P(whole, None),
            P(whole, None),
            P(None, whole),
        ),
        check_vma=False,
    )
```

```python
import functools
import math

import jax
import jax.numpy as jnp
import numpy as np
from jax import lax
from jax.experimental import pallas as pl
from jax.experimental.pallas import tpu as pltpu
from jax.sharding import Mesh, PartitionSpec as P

HEADS = 12
KV_HEADS = 2
HEAD_DIM = 128
MODEL = HEADS * HEAD_DIM
GROUP = HEADS // KV_HEADS
QUERY_WIDTH = HEADS * HEAD_DIM
KEY_WIDTH = KV_HEADS * HEAD_DIM
KV_PIECES = [(QUERY_WIDTH, HEAD_DIM), (QUERY_WIDTH + KEY_WIDTH, HEAD_DIM)]
SCALE = 1.0 / math.sqrt(HEAD_DIM)

eps = 1e-06
theta = 1000000.0
neg = -1e30
last_pair = (((1,), (1,)), ((), ()))
first_pair = (((0,), (0,)), ((), ()))
floats = jnp.float32
halves = jnp.bfloat16

AXES = ("z", "x", "y", "c")
SEQ = ("z", "x")
ROW = ("y", "c")
TEAM = ("z", "y")


def turn_half(values):
    middle = values.shape[-1] // 2
    return jnp.concatenate([-values[..., middle:], values[..., :middle]], axis=-1)


def unturn_half(values):
    middle = values.shape[-1] // 2
    return jnp.concatenate([values[..., middle:], -values[..., :middle]], axis=-1)


def row_positions(labels):
    length = labels.shape[0]
    places = jnp.arange(length, dtype=jnp.int32)
    change = jnp.concatenate([jnp.ones((1,), dtype=jnp.bool_), labels[1:] != labels[:-1]])
    starts = lax.cummax(jnp.where(change, places, 0), axis=0)
    return places - starts


def rotary(positions, width):
    inverse = jnp.power(
        jnp.float32(theta), -(jnp.arange(width // 2, dtype=jnp.float32) * (2.0 / width))
    )
    angle = positions.astype(jnp.float32)[:, None] * inverse[None, :]
    angle = jnp.concatenate([angle, angle], axis=1)[:, None, :]
    return (jnp.cos(angle), jnp.sin(angle))


def to_groups(values):
    length = values.shape[0]
    return (
        values.reshape(length, KV_HEADS, GROUP, HEAD_DIM)
        .transpose(1, 2, 0, 3)
        .reshape(KV_HEADS, GROUP * length, HEAD_DIM)
    )


def from_groups(values, length):
    return (
        values.reshape(KV_HEADS, GROUP, length, HEAD_DIM)
        .transpose(2, 0, 1, 3)
        .reshape(length, QUERY_WIDTH)
    )


def norm_parts(values):
    return lax.rsqrt(jnp.mean(values * values, axis=-1, keepdims=True) + eps)


def norm_back(upstream, values, scale, gain):
    scaled = upstream * gain
    inner = jnp.mean(scaled * values, axis=-1, keepdims=True)
    part = scale * scaled - values * (scale * scale * scale) * inner
    gain_grad = jnp.sum(upstream * values * scale, axis=0, keepdims=True)
    return part, gain_grad


MESH = pl.DeviceIdType.MESH
VMEM_LIMIT = 60 * 2**20


def coordinates():
    return tuple(lax.axis_index(name) for name in AXES)


class Sent:
    def __init__(self, raw, when):
        self.raw, self.when = raw, when

    def under(self, act):
        if self.when is None:
            act()
        else:
            pl.when(self.when)(act)

    def start(self):
        self.under(self.raw.start)

    def wait_recv(self):
        self.under(self.raw.wait_recv)

    def wait_send(self):
        self.under(self.raw.wait_send)


class Courier:
    def __init__(self, sends, receives):
        self.sends, self.receives, self.copies = sends, receives, []

    def make(self, source, target, device, when=None):
        place = len(self.copies)
        raw = pltpu.make_async_remote_copy(
            src_ref=source,
            dst_ref=target,
            send_sem=self.sends.at[place],
            recv_sem=self.receives.at[place],
            device_id=device,
            device_id_type=MESH,
        )
        made = Sent(raw, when)
        self.copies.append(made)
        return made

    def copy(self, source, target, device, when=None):
        made = self.make(source, target, device, when)
        made.start()
        return made

    def finish(self):
        for made in self.copies:
            made.wait_send()


def meet(devices):
    barrier = pltpu.get_barrier_semaphore()
    for device in devices:
        pl.semaphore_signal(barrier, inc=1, device_id=device, device_id_type=MESH)
    pl.semaphore_wait(barrier, len(devices))


def far_first(nz):
    return sorted(range(nz), key=lambda dz: (dz == 0, -abs(2 * dz - nz)))


def near_first(nz):
    return [sorted(range(nz), key=lambda group: (abs(group - at), -group)) for at in range(nz)]


def cuts_of(width, step):
    return [(start, min(step, width - start)) for start in range(0, width, step)]


class Line:
    def __init__(self, courier, place, spot):
        self.courier, self.place, self.spot = courier, place, spot
        self.sent = {}

    def items(self):
        p = self.place
        found = [(0, 0, p.z, None)]
        for step in range(1, p.nz):
            found.append((step, 1, lax.max(p.z - step, 0), p.z >= step))
            found.append((step, -1, lax.min(p.z + step, p.nz - 1), p.z + step < p.nz))
        return found

    def send(self, step, way, group, also=None):
        p = self.place
        inside = p.z < p.nz - 1 if way == 1 else p.z > 0
        if also is not None:
            inside = inside & also
        spot = self.spot(group)
        self.sent[step, way] = self.courier.copy(spot, spot, p.line_at(way), inside)

    def start(self):
        self.send(0, 1, self.place.z)
        self.send(0, -1, self.place.z)

    def arrive(self, step, way, group, exists):
        made = self.sent[step - 1, way]

        @pl.when(exists)
        def _():
            made.raw.wait_recv()

        if step < self.place.nz - 1:
            self.send(step, way, group, exists)


class Gather:
    def __init__(self, courier, place, source, buffer):
        self.courier, self.place = courier, place
        self.source, self.buffer = source, buffer
        self.line = Line(courier, place, lambda group: buffer.at[group, :, place.y, place.c])
        self.side, self.core = {}, {}

    def start(self):
        p = self.place
        spot = self.buffer.at[p.z, p.x, p.y, p.c]
        self.cross = [
            self.courier.copy(source, spot.at[:, lanes], p.across["x"])
            for source, lanes in self.source
        ]

    def along(self):
        for made in self.cross:
            made.wait_recv()
        self.line.start()
        self.sideways(self.line.items()[0])

    def sideways(self, item):
        step, way, group, exists = item
        p = self.place
        spot = self.buffer.at[group, :, p.y, p.c]
        self.side[step, way] = self.courier.copy(spot, spot, p.across["y"], exists)

    def pass_on(self, step):
        for item in self.line.items():
            if item[0] == step:
                self.line.arrive(*item)
                self.sideways(item)

    def to_core(self):
        p = self.place
        for item in self.line.items():
            step, way, group, exists = item
            self.side[step, way].wait_recv()
            spot = self.buffer.at[group, :, :, p.c]
            self.core[step, way] = self.courier.copy(spot, spot, p.across["c"], exists)

    def done(self):
        for made in self.core.values():
            made.wait_recv()


class Place:
    def __init__(self, nz):
        self.nz = nz
        self.z, self.x, self.y, self.c = z, x, y, c = coordinates()
        self.across = {"x": (z, 1 - x, y, c), "y": (z, x, 1 - y, c), "c": (z, x, y, 1 - c)}

    def line(self, dz, dy=0):
        y = lax.rem(self.y + dy, 2) if dy else self.y
        return (lax.rem(self.z + dz, self.nz), self.x, y, self.c)

    def line_at(self, way):
        return (lax.rem(self.z + self.nz + way, self.nz), self.x, self.y, self.c)

    def peers(self):
        team = [self.line(dz, dy) for dz in range(self.nz) for dy in range(2)]
        return team[1:] + [self.across["x"], self.across["c"]]


def spread(values, piece, width):
    devices, lanes = values.shape
    at = lax.broadcasted_iota(jnp.int32, (lanes, width), 1)
    inner = lax.broadcasted_iota(jnp.int32, (lanes, width), 0)
    chosen = (lax.rem(at, piece) == inner).astype(floats).astype(halves)
    repeated = jnp.dot(values.astype(halves), chosen, preferred_element_type=floats)
    owner = lax.div(lax.broadcasted_iota(jnp.int32, (devices, width), 1), piece)
    mine = owner == lax.broadcasted_iota(jnp.int32, (devices, width), 0)
    return jnp.sum(jnp.where(mine, repeated, 0.0), axis=0, keepdims=True)


def attention_kernel(
    nz,
    stack_ref,
    joint_ref,
    merge_ref,
    small_ref,
    inverse_ref,
    tokens_ref,
    outer_ref,
    w_ref,
    ct_ref,
    kv_out,
    query_out,
    merge_out,
    xn1_ref,
    xn2_ref,
    mixed_ref,
    gain_ref,
    turn_ref,
    query_ref,
    pair_ref,
    share_ref,
    out_ref,
    joint_kv,
    joint_q,
    merge,
    small,
    bias_mask,
    tokens_all,
    mixed_send,
    mixed_in,
    sends,
    receives,
    locals_,
):
    place = Place(nz)
    z, x, y, c = place.z, place.x, place.y, place.c
    length, model = tokens_ref.shape
    depth, joint_width = joint_ref.shape
    share = w_ref.shape[-1]
    half = GROUP * HEAD_DIM
    both = 2 * length
    total_keys = nz * both
    courier = Courier(sends, receives)
    devices = 8 * nz
    meet(place.peers())

    own_copies = []

    def keep(source, target):
        made = pltpu.make_async_copy(source, target, locals_.at[len(own_copies)])
        made.start()
        own_copies.append(made)
        return made

    def columns(tz, ty):
        return pl.ds(pl.multiple_of((tz * 2 + ty) * share, 128), share)

    gathers, own_waits = {}, {}

    def begin(name, ref, pieces, buffer):
        def from_side(side):
            found = []
            at = 0
            for first, width in pieces:
                lanes = pl.ds(pl.multiple_of(first + side * width, 128), width)
                found.append((ref.at[:, lanes], slice(at, at + width)))
                at += width
            return found

        spot = buffer.at[z, x, y, c]
        own_waits[name] = [keep(own, spot.at[:, lanes]) for own, lanes in from_side(x)]
        gathers[name] = Gather(courier, place, from_side(1 - x), buffer)
        gathers[name].start()

    own_waits["small"] = [keep(small_ref, small.at[z, x, y, c])]
    gathers["small"] = Gather(courier, place, [(small_ref, slice(None))], small)
    gathers["small"].start()
    begin("kv", joint_ref, KV_PIECES, joint_kv)
    token_cross = courier.copy(tokens_ref, tokens_all.at[x], place.across["x"])
    begin("q", joint_ref, [(0, half)], joint_q)
    begin("m", merge_ref, [(0, half)], merge)
    tokens_all[x] = tokens_ref[...]
    w_own = keep(stack_ref.at[:, :, columns(z, y)], w_ref.at[:, z, x, y, c])
    ct_own = keep(outer_ref, ct_ref.at[z, y])

    direct, w_cross, w_hand = {}, {}, {}

    def give(dz, dy):
        device = place.line(dz, dy)
        direct[dz, dy] = courier.copy(
            stack_ref.at[:, :, columns(device[0], device[2])], w_ref.at[:, z, x, y, c], device
        )

    def w_spot(dz, dy, side):
        return w_ref.at[:, lax.rem(z + nz - dz, nz), side, lax.rem(y + dy, 2), c]

    def take(dz, dy):
        if dz or dy:
            direct[dz, dy].wait_recv()
        spot = w_spot(dz, dy, x)
        w_cross[dz, dy] = courier.copy(spot, spot, place.across["x"])
        w_hand[dz, dy, 0] = courier.copy(spot, spot, place.across["c"])

    def hand(dz, dy):
        w_cross[dz, dy].wait_recv()
        spot = w_spot(dz, dy, 1 - x)
        w_hand[dz, dy, 1] = courier.copy(spot, spot, place.across["c"])

    give(0, 1)
    give(1, 0)
    for name in ("small", "kv"):
        for made in own_waits[name]:
            made.wait()
        gathers[name].along()
    token_cross.wait_recv()
    tokens_both = tokens_all[...].reshape(both, model).astype(floats)
    hat = tokens_both * norm_parts(tokens_both)
    for name in ("small", "kv"):
        gathers[name].pass_on(1)
    for made in own_waits["q"] + own_waits["m"]:
        made.wait()
    gathers["q"].along()
    for step in range(2, nz):
        for name in ("small", "kv"):
            gathers[name].pass_on(step)
    for name in ("small", "kv"):
        gathers[name].to_core()
    w_own.wait()
    take(0, 0)
    for step in range(1, nz):
        gathers["q"].pass_on(step)
    for name in ("small", "kv"):
        gathers[name].done()
    take(0, 1)
    give(1, 1)

    pieces = small[...].reshape(devices * 8, 128).astype(halves)

    def row_of(which):
        at = lax.broadcasted_iota(jnp.int32, (devices, devices * 8), 1)
        wanted = lax.broadcasted_iota(jnp.int32, (devices, devices * 8), 0) * 8 + which
        chosen = (at == wanted).astype(floats).astype(halves)
        return jnp.dot(chosen, pieces, preferred_element_type=floats)

    gain_first = spread(row_of(1), depth, model)
    gain_second = spread(row_of(2), depth, model)
    bias = spread(row_of(0), joint_width // devices, joint_width)
    gain_ref[0:1, :] = gain_first
    gain_ref[1:2, :] = gain_second

    def mine(first, width):
        return jnp.where(x == 0, bias[:, first : first + width], bias[:, first + width : first + 2 * width])

    bias_query = mine(0, half)
    bias_key = mine(QUERY_WIDTH, HEAD_DIM)
    bias_value = mine(QUERY_WIDTH + KEY_WIDTH, HEAD_DIM)
    label = jnp.concatenate([small[z, side, y, c].T[:, 3:4] for side in range(2)], axis=0)
    start = jnp.zeros((both, 1), floats)
    rows_at = z * both + lax.broadcasted_iota(jnp.int32, (both, length), 0)
    lanes_at = lax.broadcasted_iota(jnp.int32, (both, length), 1)
    for block in range(2 * nz):
        keys_label = small[block // 2, block % 2, y, c, 3:4, :]
        start = start + jnp.sum((keys_label < label).astype(floats), axis=1, keepdims=True)
        allowed = (keys_label == label) & (rows_at >= block * length + lanes_at)
        bias_mask[:, block * length : (block + 1) * length] = jnp.where(allowed, 0.0, neg)
    place_at = (z * both + lax.broadcasted_iota(jnp.int32, (both, 1), 0)).astype(floats)
    angle = (place_at - start) * inverse_ref[...]
    cosine = jnp.cos(angle)
    lane = lax.broadcasted_iota(jnp.int32, (both, HEAD_DIM), 1)
    sine = jnp.where(lane < HEAD_DIM // 2, -1.0, 1.0) * jnp.sin(angle)
    turn_ref[0] = cosine
    turn_ref[1] = sine

    def turned(values):
        return values * cosine + pltpu.roll(values, HEAD_DIM // 2, 1) * sine

    xn1_ref[...] = (hat * gain_first).astype(halves)
    pair = jnp.dot(
        xn1_ref[...], joint_kv[...].reshape(model, 2 * HEAD_DIM), preferred_element_type=floats
    )
    pair_ref[z, :, :HEAD_DIM] = turned(pair[:, :HEAD_DIM] + bias_key).astype(halves)
    pair_ref[z, :, HEAD_DIM:] = (pair[:, HEAD_DIM:] + bias_value).astype(halves)
    pairs = Line(courier, place, lambda group: pair_ref.at[group])
    pairs.start()
    gathers["q"].to_core()
    gathers["m"].along()
    for item in pairs.items()[1:3]:
        pairs.arrive(*item)
    take(1, 0)
    give(3, 0)
    for item in pairs.items()[3:]:
        pairs.arrive(*item)
    gathers["m"].pass_on(1)
    gathers["q"].done()

    query = jnp.dot(xn1_ref[...], joint_q[...].reshape(model, half), preferred_element_type=floats)
    query = query + bias_query
    for head in range(GROUP):
        query_ref[head] = turned(query[:, head * HEAD_DIM : (head + 1) * HEAD_DIM]).astype(halves)
    for step in range(2, nz):
        gathers["m"].pass_on(step)
    take(1, 1)
    give(3, 1)
    give(2, 0)
    outers = Line(courier, place, lambda group: ct_ref.at[group, y])
    ct_side = {}

    def ct_on(item):
        step, way, group, exists = item
        if step:
            outers.arrive(*item)
        spot = ct_ref.at[group, y]
        ct_side[step, way] = courier.copy(spot, spot, place.across["y"], exists)

    ct_own.wait()
    ct_on(outers.items()[0])
    gathers["m"].to_core()
    hand(0, 0)
    hand(0, 1)

    def attend(first, last):
        @pl.loop(first, last)
        def _(head):
            keys = pair_ref[:, :, :HEAD_DIM].reshape(total_keys, HEAD_DIM)
            values = pair_ref[:, :, HEAD_DIM:].reshape(total_keys, HEAD_DIM)
            scores = lax.dot_general(
                query_ref[head], keys, last_pair, preferred_element_type=floats
            )
            scores = scores * SCALE + bias_mask[...]
            top = jnp.max(scores, axis=-1, keepdims=True)
            raised = jnp.exp(scores - top)
            shares = (raised / jnp.sum(raised, axis=-1, keepdims=True)).astype(halves)
            share_ref[head] = shares
            lanes = pl.ds(pl.multiple_of(head * HEAD_DIM, 128), HEAD_DIM)
            out_ref[:, lanes] = jnp.dot(shares, values, preferred_element_type=floats)

    attend(0, GROUP // 2)
    take(3, 0)
    give(2, 1)
    attend(GROUP // 2, GROUP)
    outers.start()
    gathers["m"].done()
    saves = [keep(joint_kv, kv_out), keep(joint_q, query_out), keep(merge, merge_out)]
    merged = lax.dot_general(
        out_ref[...].astype(halves),
        merge[...].reshape(model, half),
        last_pair,
        preferred_element_type=floats,
    )
    mixed_ref[...] = jnp.where(x == 0, merged[:length], merged[length:])
    mixed_send[...] = jnp.where(x == 0, merged[length:], merged[:length]).astype(halves)
    mixed_cross = courier.copy(mixed_send, mixed_in, place.across["x"])
    take(3, 1)
    hand(1, 0)
    for item in outers.items()[1:3]:
        ct_on(item)
    mixed_cross.wait_recv()
    mixed = tokens_ref[...].astype(floats) + (mixed_ref[...] + mixed_in[...].astype(floats))
    mixed_ref[...] = mixed
    xn2_ref[...] = (mixed * norm_parts(mixed) * gain_second).astype(halves)
    take(2, 0)
    hand(1, 1)
    for item in outers.items()[3:5]:
        ct_on(item)
    hand(3, 0)
    take(2, 1)
    for item in outers.items()[5:]:
        ct_on(item)
    for spot in ((3, 1), (2, 0), (2, 1)):
        hand(*spot)
    for made in w_hand.values():
        made.wait_recv()
    for made in ct_side.values():
        made.wait_recv()
    for made in saves:
        made.wait()
    courier.finish()


def feed_kernel(
    nz,
    w_ref,
    ct_ref,
    normal_ref,
    back_ref,
    branch_ref,
    done_ref,
    grads_ref,
    w,
    xn,
    ct,
    hid,
    gb,
    ub,
    part,
    ybuf,
    zsend,
    zbuf,
    cbuf,
    xbuf,
    sends,
    receives,
    locals_,
):
    place = Place(nz)
    z, x, y, c = place.z, place.x, place.y, place.c
    length, model = normal_ref.shape
    share = w.shape[-1]
    block = model // nz
    lines = 2 * length * nz
    courier = Courier(sends, receives)

    def source(dz):
        return lax.rem(z + nz - dz, nz)

    meet([place.line(dz) for dz in range(1, nz)] + [place.across[name] for name in "xyc"])
    xn[z, y] = normal_ref[...]
    blocks = Line(courier, place, lambda group: xn.at[group, y])
    blocks.start()
    side = {}

    def pass_on(step):
        for item in blocks.items():
            if item[0] == step:
                way, group, exists = item[1:]
                if step:
                    blocks.arrive(*item)
                spot = xn.at[group, y]
                side[step, way] = courier.copy(spot, spot, place.across["y"], exists)

    pass_on(0)
    groups = near_first(nz)

    def group_at(number):
        return sum(jnp.where(z == at, groups[at][number], 0) for at in range(nz))

    def wait_for(number):
        for at in range(nz):
            gap = groups[at][number] - at
            made = side[abs(gap), 0 if gap == 0 else (1 if gap < 0 else -1)]
            pl.when(z == at)(made.raw.wait_recv)

    loads = [
        pltpu.make_async_copy(w_ref.at[which], w.at[which], locals_.at[which])
        for which in range(3)
    ] + [pltpu.make_async_copy(ct_ref, ct, locals_.at[3])]
    for made in loads:
        made.start()
    pass_on(1)
    for made in loads:
        made.wait()

    def weight(which, start, size):
        return w[which, :, :, :, :, :, start : start + size].reshape(model, size)

    half = nz // 2
    scatter = {}

    def scatter_on(dz):
        group = group_at(dz)
        scatter[dz] = courier.copy(
            part.at[group, 1 - y], ybuf.at[group], place.across["y"]
        )

    for dz in range(nz):
        group = group_at(dz)
        wait_for(dz)
        for start, size in cuts_of(share, 256):
            normal = xn[group].reshape(2 * length, model)
            outer = ct[group].reshape(2 * length, model)
            gate = jnp.dot(normal, weight(0, start, size), preferred_element_type=floats)
            upper = jnp.dot(normal, weight(1, start, size), preferred_element_type=floats)
            hidden_back = jnp.dot(outer, weight(2, start, size), preferred_element_type=floats)
            sig = 1.0 / (1.0 + jnp.exp(-gate))
            silu = gate * sig
            spot = (group, slice(None), slice(start, start + size))
            hid[spot] = (silu * upper).astype(halves)
            gb[spot] = (hidden_back * upper * (sig * (1.0 + gate * (1.0 - sig)))).astype(halves)
            ub[spot] = (hidden_back * silu).astype(halves)

        @pl.loop(0, 2)
        def _(step):
            rows = pl.ds(step * half, half)
            lanes = pl.ds(pl.multiple_of(step * (model // 2), 128), model // 2)

            def turned(which):
                return w[which, rows].reshape(model // 2, share)

            both = lax.dot_general(
                gb[group], turned(0), last_pair, preferred_element_type=floats
            ) + lax.dot_general(ub[group], turned(1), last_pair, preferred_element_type=floats)
            part[group, :, :, lanes] = both.astype(halves).reshape(2, length, model // 2)

        if dz:
            scatter_on(dz)
        if dz + 2 < nz:
            pass_on(dz + 2)

        @pl.loop(0, 2)
        def _(step):
            rows = pl.ds(step * half, half)
            lanes = pl.ds(pl.multiple_of(step * (model // 2), 128), model // 2)
            product = lax.dot_general(
                hid[group],
                w[2, rows].reshape(model // 2, share),
                last_pair,
                preferred_element_type=floats,
            )
            branch_ref[group, :, :, lanes] = product.astype(halves).reshape(2, length, model // 2)


    scatter_on(0)

    final = {
        dz: courier.make(
            zsend.at[source(dz)], zbuf.at[dz - 1], (source(dz), x, y, c)
        )
        for dz in range(1, nz)
    }

    def sum_on(dz):
        group = group_at(dz)
        scatter[dz].wait_recv()
        total = part[group, y].astype(floats) + ybuf[group].astype(floats)
        if dz == 0:
            back_ref[...] = total
        else:
            zsend[group] = total.astype(halves)
            for apart, made in final.items():
                pl.when(source(apart) == group)(made.raw.start)

    orders = far_first(nz)
    early = 2
    handed, crossed, saves = {}, {}, []

    def save(source, target):
        made = pltpu.make_async_copy(source, target, locals_.at[4 + len(saves)])
        made.start()
        saves.append(made)

    def product(dz):
        group = lax.rem(z + dz, nz)
        lanes = pl.ds(pl.multiple_of(group * block, 128), block)
        normal_turned = xn[:, :, :, lanes].reshape(lines, block).T
        outer_turned = ct[:, :, :, lanes].reshape(lines, block).T
        for which, left, right in (
            (0, normal_turned, gb),
            (1, normal_turned, ub),
            (2, outer_turned, hid),
        ):
            for start, size in cuts_of(share, 512):
                w[which, group, :, :, :, :, start : start + size] = (
                    jnp.dot(
                        left,
                        right[:, :, start : start + size].reshape(lines, size),
                        preferred_element_type=floats,
                    )
                    .astype(halves)
                    .reshape(2, 2, 2, -1, size)
                )
        handed[dz] = courier.copy(
            w.at[:, group, :, :, 1 - c], cbuf.at[dz], place.across["c"]
        )

    def settle(position):
        dz = orders[position]
        group = lax.rem(z + dz, nz)
        handed[dz].wait_recv()
        for which in range(3):
            w[which, group, :, :, c] = (
                w[which, group, :, :, c].astype(floats) + cbuf[dz, which].astype(floats)
            ).astype(halves)
        if position < early:
            crossed[position] = courier.copy(
                w.at[:, group, 1 - x, :, c], xbuf.at[position], place.across["x"]
            )
        else:
            save(w.at[:, group, :, :, c], grads_ref.at[:, position - early])

    for position in range(nz):
        product(orders[position])
        sum_on((position + 1) % nz)
        if position:
            settle(position - 1)
    settle(nz - 1)
    for position in range(early):
        group = lax.rem(z + orders[position], nz)
        crossed[position].wait_recv()
        for which in range(3):
            w[which, group, x, :, c] = (
                w[which, group, x, :, c].astype(floats) + xbuf[position, which].astype(floats)
            ).astype(halves)
        save(w.at[:, group, x, :, c], done_ref.at[:, position])
    for dz in range(1, nz):
        final[dz].wait_recv()
        back_ref[...] += zbuf[dz - 1].astype(floats)
    for made in saves:
        made.wait()
    courier.finish()


class LineSum:
    def __init__(self, courier, place, parts, spot, above, below):
        self.courier, self.place, self.parts, self.spot = courier, place, parts, spot
        self.arrivals = {1: above, -1: below}
        self.sent = {}

    def add(self, target, way):
        nz = self.place.nz
        spot = self.spot(target)
        arrived = self.arrivals[way][target - 1 if way == 1 else target]
        self.parts[spot] = (self.parts[spot].astype(floats) + arrived.astype(floats)).astype(
            self.parts.dtype
        )

    def forward(self, target, way):
        p = self.place
        moving = p.z < target if way == 1 else p.z > target
        fed = p.z > 0 if way == 1 else p.z < p.nz - 1
        made = self.courier.make(
            self.parts.at[self.spot(target)],
            self.arrivals[way].at[target - 1 if way == 1 else target],
            p.line_at(way),
            moving,
        )
        self.sent[target, way] = made

        @pl.when(moving & fed)
        def _():
            made.raw.wait_recv()
            self.add(target, way)

        made.start()

    def forward_step(self, step):
        self.forward(self.place.nz - 1 - step, 1)
        self.forward(step, -1)

    def finish(self):
        p = self.place
        for (target, way), made in self.sent.items():
            fed = p.z > 0 if way == 1 else p.z < p.nz - 1

            @pl.when((p.z == target) & fed)
            def _(target=target, way=way, made=made):
                made.raw.wait_recv()
                self.add(target, way)


class Scatter:
    def __init__(self, courier, place, parts, core_in, side_in, above, below, last_in):
        self.courier, self.place, self.parts = courier, place, parts
        self.core_in, self.side_in, self.last_in = core_in, side_in, last_in
        every = slice(None)
        self.line = LineSum(
            courier, place, parts, lambda group: (group, every, place.y, place.c), above, below
        )
        self.groups = []
        for step in range((place.nz + 1) // 2):
            self.groups += [place.nz - 1 - step, step]
        self.core, self.side = {}, {}

    def to_core(self, group):
        p = self.place
        self.core[group] = self.courier.copy(
            self.parts.at[group, :, :, 1 - p.c], self.core_in.at[group], p.across["c"]
        )

    def add(self, spot, arrived):
        self.parts[spot] = (self.parts[spot].astype(floats) + arrived.astype(floats)).astype(
            self.parts.dtype
        )

    def sideways(self):
        p = self.place
        every = slice(None)
        for group in self.groups:
            self.core[group].wait_recv()
            self.add((group, every, every, p.c), self.core_in[group])
            self.side[group] = self.courier.copy(
                self.parts.at[group, :, 1 - p.y, p.c], self.side_in.at[group], p.across["y"]
            )

    def along(self):
        p = self.place
        for group in self.groups:
            self.side[group].wait_recv()
            self.add((group, slice(None), p.y, p.c), self.side_in[group])

    def across(self):
        p = self.place
        self.line.finish()
        self.last = self.courier.copy(
            self.parts.at[p.z, 1 - p.x, p.y, p.c], self.last_in, p.across["x"]
        )

    def own(self):
        p = self.place
        return self.parts[p.z, p.x, p.y, p.c].astype(floats)

    def other(self):
        self.last.wait_recv()
        return self.last_in[...].astype(floats)


def gather_pieces(values, piece, devices):
    width = values.shape[1]
    owner = lax.div(lax.broadcasted_iota(jnp.int32, (devices, width), 1), piece)
    mine = owner == lax.broadcasted_iota(jnp.int32, (devices, width), 0)
    at = lax.broadcasted_iota(jnp.int32, (width, 128), 0)
    inner = lax.broadcasted_iota(jnp.int32, (width, 128), 1)
    chosen = (lax.rem(at, piece) == inner).astype(floats)
    rows = jnp.where(mine, values, 0.0)
    return jnp.dot(rows, chosen, preferred_element_type=floats, precision=lax.Precision.HIGHEST)


def back_kernel(
    nz,
    done_ref,
    grads_in,
    branch_ref,
    kv_ref,
    q_ref,
    m_ref,
    back_ref,
    mixed_ref,
    outer_ref,
    tokens_ref,
    xn1_ref,
    gain_ref,
    turn_ref,
    query_ref,
    pair_ref,
    share_ref,
    out_ref,
    output_ref,
    tokens_grad_ref,
    joint_grad_ref,
    merge_grad_ref,
    small_grad_ref,
    grads_ref,
    weight_m,
    weight_q,
    weight_kv,
    gown,
    gin,
    branch_own,
    branch_in,
    branch_above,
    branch_below,
    *rest,
):
    merge_bufs, query_bufs, kv_bufs, small_bufs = (rest[6 * i : 6 * i + 6] for i in range(4))
    (
        pair_sum,
        pair_half,
        pair_above,
        pair_below,
        joint_back,
        attended_back,
        mixed_both,
        back_send,
        back_in,
        sends,
        receives,
        locals_,
    ) = rest[24:]
    place = Place(nz)
    z, x, y, c = place.z, place.x, place.y, place.c
    length, model = tokens_ref.shape
    share = gown.shape[-1]
    half = GROUP * HEAD_DIM
    both = 2 * length
    block = model // nz
    depth = grads_in.shape[-2]
    devices = 8 * nz
    total_keys = nz * both
    orders = far_first(nz)
    courier = Courier(sends, receives)
    meet(place.peers())

    def group_of(dz):
        return lax.rem(z + dz, nz)

    copies = []

    def load(source, target):
        made = pltpu.make_async_copy(source, target, locals_.at[len(copies)])
        made.start()
        copies.append(made)
        return made

    merge_load = load(m_ref, weight_m)
    branch_load = load(branch_ref.at[:, y], branch_own)
    gown_load = load(grads_in.at[:, :, x], gown)
    early = 2
    late = orders[early:]
    query_load = load(q_ref, weight_q)
    kv_load = load(kv_ref, weight_kv)

    b_cross = {
        group: courier.copy(branch_ref.at[group, 1 - y], branch_in.at[group], place.across["y"])
        for group in range(nz)
    }
    g_cross, g_line, kept = {}, [], []

    def grads_across(dz):
        g_cross[dz] = courier.copy(
            grads_in.at[:, late.index(dz), 1 - x], gin.at[late.index(dz)], place.across["x"]
        )

    mine = pl.ds(pl.multiple_of((z * 2 + y) * share, 128), share)

    def grads_line(dz, rows):
        for dy in range(2):
            ty = lax.rem(y + dy, 2)
            if dz or dy:
                g_line.append(
                    courier.copy(
                        rows.at[:, ty], grads_ref.at[:, :, mine], (group_of(dz), x, ty, c)
                    )
                )
            else:
                kept.append(load(rows.at[:, ty], grads_ref.at[:, :, mine]))

    for position in range(early):
        grads_line(orders[position], done_ref.at[:, position])

    mixed = mixed_ref[...]
    second_scale = norm_parts(mixed)
    part, second_local = norm_back(back_ref[...], mixed, second_scale, gain_ref[1:2, :])
    grad = outer_ref[...].astype(floats) + part
    tokens_grad_ref[...] = grad
    mixed_both[x] = grad.astype(halves)
    mixed_cross = courier.copy(mixed_both.at[x], mixed_both.at[x], place.across["x"])
    mixed_cross.wait_recv()
    for dz in late:
        grads_across(dz)

    merge_load.wait()
    upstream_both = mixed_both[...].reshape(both, model)
    attended_back[...] = jnp.dot(
        upstream_both, weight_m[...].reshape(model, half), preferred_element_type=floats
    ).astype(halves)
    merges = Scatter(courier, place, *merge_bufs)
    queries = Scatter(courier, place, *query_bufs)
    keys_values = Scatter(courier, place, *kv_bufs)
    smalls = Scatter(courier, place, *small_bufs)

    def product_rows(scatter, left, right):
        for group in scatter.groups:
            scatter.parts[group] = (
                jnp.dot(
                    left[group * block : (group + 1) * block], right, preferred_element_type=floats
                )
                .astype(halves)
                .reshape(2, 2, 2, depth, right.shape[1])
            )
            scatter.to_core(group)

    product_rows(merges, upstream_both.T, out_ref[...].astype(halves))

    def attend(first, last):
        @pl.loop(first, last)
        def _(head):
            query = query_ref[head]
            keys = pair_ref[:, :, :HEAD_DIM].reshape(total_keys, HEAD_DIM)
            values = pair_ref[:, :, HEAD_DIM:].reshape(total_keys, HEAD_DIM)
            lanes = pl.ds(pl.multiple_of(head * HEAD_DIM, 128), HEAD_DIM)
            upstream = attended_back[:, lanes]
            delta = jnp.sum(upstream.astype(floats) * out_ref[:, lanes], axis=-1, keepdims=True)
            mass = lax.dot_general(upstream, values, last_pair, preferred_element_type=floats)
            shares = share_ref[head]
            scores = (shares.astype(floats) * (mass - delta)).astype(halves)
            query_sum = jnp.dot(scores, keys, preferred_element_type=floats) * SCALE
            cosine, sine = turn_ref[0], turn_ref[1]
            joint_back[:, lanes] = (
                query_sum * cosine + pltpu.roll(query_sum * sine, HEAD_DIM // 2, 1)
            ).astype(halves)
            pair_sum[:, :HEAD_DIM] += (
                jnp.dot(scores.T, query, preferred_element_type=floats) * SCALE
            )
            pair_sum[:, HEAD_DIM:] += jnp.dot(shares.T, upstream, preferred_element_type=floats)

    def grads_on(dz):
        at = late.index(dz)
        g_cross[dz].wait_recv()
        for which in range(3):
            gown[which, at] = (
                gown[which, at].astype(floats) + gin[at, which].astype(floats)
            ).astype(halves)
        grads_line(dz, gown.at[:, at])

    pair_sum[...] = jnp.zeros_like(pair_sum)
    attend(0, GROUP // 2)
    merges.sideways()

    attend(GROUP // 2, GROUP)

    pair_half[...] = pair_sum[...].astype(halves).reshape(nz, both, 2 * HEAD_DIM)
    pairs = LineSum(courier, place, pair_half, lambda group: (group,), pair_above, pair_below)
    pairs.forward(nz - 1, 1)
    pairs.forward(0, -1)
    turned = xn1_ref[...].T
    product_rows(queries, turned, joint_back[:, :half])
    for step in range(1, nz - 1):
        pairs.forward(nz - 1 - step, 1)
        pairs.forward(step, -1)
    branch_load.wait()
    for group in range(nz):
        b_cross[group].wait_recv()
        branch_own[group] = (
            branch_own[group].astype(floats) + branch_in[group].astype(floats)
        ).astype(halves)
    pairs.finish()
    total = pair_half[z].astype(floats)
    key_total = total[:, :HEAD_DIM]
    joint_back[:, half : half + HEAD_DIM] = (
        key_total * turn_ref[0] + pltpu.roll(key_total * turn_ref[1], HEAD_DIM // 2, 1)
    ).astype(halves)
    joint_back[:, half + HEAD_DIM :] = total[:, HEAD_DIM:].astype(halves)
    product_rows(keys_values, turned, joint_back[:, half:])
    query_load.wait()
    kv_load.wait()
    normal_back = lax.dot_general(
        joint_back[:, :half],
        weight_q[...].reshape(model, half),
        last_pair,
        preferred_element_type=floats,
    ) + lax.dot_general(
        joint_back[:, half:],
        weight_kv[...].reshape(model, 2 * HEAD_DIM),
        last_pair,
        preferred_element_type=floats,
    )
    back_send[...] = jnp.where(x == 0, normal_back[length:], normal_back[:length]).astype(halves)
    back_cross = courier.copy(back_send, back_in, place.across["x"])
    normal_own = jnp.where(x == 0, normal_back[:length], normal_back[length:])
    queries.sideways()
    keys_values.sideways()
    gown_load.wait()
    for dz in late[:1]:
        grads_on(dz)

    local = jnp.sum(joint_back[...].astype(floats), axis=0, keepdims=True)
    pieces_of = []
    for first, width in ((0, half), (half, HEAD_DIM), (half + HEAD_DIM, HEAD_DIM)):
        for side in range(2):
            pieces_of.append(jnp.where(x == side, local[:, first : first + width], 0.0))
    bias_local = jnp.concatenate(pieces_of, axis=1)
    def piece_rows(which, values):
        mine_rows = gather_pieces(values, values.shape[1] // devices, devices)
        at = lax.broadcasted_iota(jnp.int32, (devices * 8, devices), 0)
        wanted = lax.broadcasted_iota(jnp.int32, (devices * 8, devices), 1) * 8 + which
        return jnp.dot(
            (at == wanted).astype(floats),
            mine_rows,
            preferred_element_type=floats,
            precision=lax.Precision.HIGHEST,
        )

    pieces = piece_rows(0, bias_local) + piece_rows(2, second_local)
    branches = LineSum(
        courier, place, branch_own, lambda group: (group,), branch_above, branch_below
    )
    back_cross.wait_recv()
    normal_own = normal_own + back_in[...].astype(floats)
    residual = tokens_ref[...].astype(floats)
    part, first_local = norm_back(normal_own, residual, norm_parts(residual), gain_ref[0:1, :])
    tokens_grad_ref[...] += part

    pieces = pieces + piece_rows(1, first_local)
    smalls.parts[...] = pieces.reshape(nz, 2, 2, 2, 8, 128)
    for group in smalls.groups:
        smalls.to_core(group)
    for made in (merges, queries, keys_values):
        made.along()
    for line in (keys_values.line, queries.line, merges.line, branches):
        line.forward_step(0)
    for line in (keys_values.line, queries.line, merges.line, branches):
        line.forward_step(1)
    for dz in late[1:]:
        grads_on(dz)
    smalls.sideways()
    for line in (keys_values.line, queries.line, merges.line, branches):
        line.forward_step(2)
    smalls.along()
    for step in range(nz - 1):
        smalls.line.forward_step(step)
    for made in (smalls, keys_values, queries, merges):
        made.across()
    branches.finish()
    output_ref[...] = (mixed_ref[...] + branch_own[z].astype(floats)).astype(halves)
    for ref, made, pieces in (
        (merge_grad_ref, merges, [(0, half)]),
        (joint_grad_ref, queries, [(0, half)]),
        (joint_grad_ref, keys_values, KV_PIECES),
    ):
        for side, values in ((x, made.own()), (1 - x, made.other())):
            at = 0
            for first, width in pieces:
                lanes = pl.ds(pl.multiple_of(first + side * width, 128), width)
                ref[:, lanes] = values[:, at : at + width]
                at += width
    small_grad_ref[...] = smalls.own() + smalls.other()
    for made in g_line:
        made.wait_recv()
    for made in kept:
        made.wait()
    courier.finish()


def padded_share(hidden_width, team):
    return -(-hidden_width // (team * 128)) * 128


def body_kernels(
    tokens,
    segments,
    joint_matrix,
    joint_bias,
    merge_matrix,
    norm_first,
    norm_second,
    gate_matrix,
    up_matrix,
    down_matrix,
    cotangent,
):
    length, model = tokens.shape[1:]
    depth, joint_width = joint_matrix.shape
    hidden_width = gate_matrix.shape[1]
    nz = lax.axis_size("z")
    share = padded_share(hidden_width, 2 * nz)
    half = GROUP * HEAD_DIM
    pair_width = 2 * HEAD_DIM
    both = 2 * length
    keys = nz * both
    vmem = pl.BlockSpec(memory_space=pltpu.VMEM)
    anywhere = pl.BlockSpec(memory_space=pl.ANY)
    blocks = (nz, 2, 2, 2)

    def shape(dims, kind=halves):
        return jax.ShapeDtypeStruct(dims, kind)

    def semaphores(count, loads):
        return [
            pltpu.SemaphoreType.DMA((count,)),
            pltpu.SemaphoreType.DMA((count,)),
            pltpu.SemaphoreType.DMA((loads,)),
        ]

    def params(number):
        return pltpu.CompilerParams(
            collective_id=number, has_side_effects=True, vmem_limit_bytes=VMEM_LIMIT
        )

    stack = jnp.stack([gate_matrix, up_matrix, down_matrix.T])
    stack = jnp.pad(stack, ((0, 0), (0, 0), (0, 2 * nz * share - hidden_width)))

    def lane_row(values):
        return jnp.pad(values.astype(floats), (0, 128 - values.shape[0]))

    own_labels = segments[0]
    at = lax.broadcasted_iota(jnp.int32, (8, 128), 0)
    small = jnp.zeros((8, 128), floats)
    for which, values in enumerate((joint_bias, norm_first, norm_second, own_labels)):
        small = jnp.where(at == which, lane_row(values)[None], small)
    inverse = theta ** -(np.arange(HEAD_DIM // 2) * (2.0 / HEAD_DIM))
    inverse = jnp.asarray(np.tile(inverse, 2)[None], floats)
    outer = cotangent[0]
    (
        w,
        team_outer,
        kv_all,
        q_all,
        m_all,
        xn1,
        xn2,
        mixed,
        gains,
        turns,
        queries,
        pair,
        shares,
        summed,
    ) = pl.pallas_call(
        functools.partial(attention_kernel, nz),
        name="attention_forward",
        out_shape=(
            shape((3,) + blocks + (depth, share)),
            shape((nz, 2, length, model)),
            shape(blocks + (depth, pair_width)),
            shape(blocks + (depth, half)),
            shape(blocks + (depth, half)),
            shape((both, model)),
            shape((length, model)),
            shape((length, model), floats),
            shape((8, model), floats),
            shape((2, both, HEAD_DIM), floats),
            shape((GROUP, both, HEAD_DIM)),
            shape((nz, both, pair_width)),
            shape((GROUP, both, keys)),
            shape((both, half), floats),
        ),
        in_specs=[anywhere] * 3 + [vmem] * 4,
        out_specs=(anywhere,) * 5 + (vmem,) * 9,
        scratch_shapes=[
            pltpu.VMEM(blocks + (depth, pair_width), halves),
            pltpu.VMEM(blocks + (depth, half), halves),
            pltpu.VMEM(blocks + (depth, half), halves),
            pltpu.VMEM(blocks + (8, 128), floats),
            pltpu.VMEM((both, keys), floats),
            pltpu.VMEM((2, length, model), halves),
            pltpu.VMEM((length, model), halves),
            pltpu.VMEM((length, model), halves),
        ]
        + semaphores(137, 10),
        compiler_params=params(0),
    )(stack, joint_matrix, merge_matrix.T, small, inverse, tokens[0], outer)

    lines = 2 * length
    back, branch, done, grads = pl.pallas_call(
        functools.partial(feed_kernel, nz),
        name="feed_forward",
        out_shape=(
            shape((length, model), floats),
            shape((nz, 2, length, model)),
            shape((3, 2, 2, depth, share)),
            shape((3, nz - 2, 2, 2, depth, share)),
        ),
        in_specs=[anywhere, anywhere, vmem],
        out_specs=(vmem, vmem, anywhere, anywhere),
        scratch_shapes=[
            pltpu.VMEM((3,) + blocks + (depth, share), halves),
            pltpu.VMEM((nz, 2, length, model), halves),
            pltpu.VMEM((nz, 2, length, model), halves),
            pltpu.VMEM((nz, lines, share), halves),
            pltpu.VMEM((nz, lines, share), halves),
            pltpu.VMEM((nz, lines, share), halves),
            pltpu.VMEM((nz, 2, length, model), halves),
            pltpu.VMEM((nz, length, model), halves),
            pltpu.VMEM((nz, length, model), halves),
            pltpu.VMEM((nz - 1, length, model), halves),
            pltpu.VMEM((nz, 3, 2, 2, depth, share), halves),
            pltpu.VMEM((2, 3, 2, depth, share), halves),
        ]
        + semaphores(30, 8),
        compiler_params=params(1),
    )(w, team_outer, xn2)

    def sums(rows, width, kind=halves):
        return [
            pltpu.VMEM(blocks + (rows, width), kind),
            pltpu.VMEM((nz, 2, 2, rows, width), kind),
            pltpu.VMEM((nz, 2, rows, width), kind),
            pltpu.VMEM((nz - 1, 2, rows, width), kind),
            pltpu.VMEM((nz - 1, 2, rows, width), kind),
            pltpu.VMEM((rows, width), kind),
        ]

    output, tokens_grad, joint_grad, merge_grad, small_grad, grads = pl.pallas_call(
        functools.partial(back_kernel, nz),
        name="attention_backward",
        out_shape=(
            shape((length, model)),
            shape((length, model), floats),
            shape((depth, joint_width), floats),
            shape((depth, QUERY_WIDTH), floats),
            shape((8, 128), floats),
            shape((3, depth, 2 * nz * share)),
        ),
        in_specs=[anywhere] * 6 + [vmem] * 11,
        out_specs=(vmem,) * 5 + (anywhere,),
        scratch_shapes=[
            pltpu.VMEM(blocks + (depth, half), halves),
            pltpu.VMEM(blocks + (depth, half), halves),
            pltpu.VMEM(blocks + (depth, pair_width), halves),
            pltpu.VMEM((3, nz - 2, 2, depth, share), halves),
            pltpu.VMEM((nz - 2, 3, 2, depth, share), halves),
            pltpu.VMEM((nz, length, model), halves),
            pltpu.VMEM((nz, length, model), halves),
            pltpu.VMEM((nz - 1, length, model), halves),
            pltpu.VMEM((nz - 1, length, model), halves),
        ]
        + sums(depth, half)
        + sums(depth, half)
        + sums(depth, pair_width)
        + sums(8, 128, floats)
        + [
            pltpu.VMEM((keys, pair_width), floats),
            pltpu.VMEM((nz, both, pair_width), halves),
            pltpu.VMEM((nz - 1, both, pair_width), halves),
            pltpu.VMEM((nz - 1, both, pair_width), halves),
            pltpu.VMEM((both, half + pair_width), halves),
            pltpu.VMEM((both, half), halves),
            pltpu.VMEM((2, length, model), halves),
            pltpu.VMEM((length, model), halves),
            pltpu.VMEM((length, model), halves),
        ]
        + semaphores(90, 6),
        compiler_params=params(2),
    )(
        done,
        grads,
        branch,
        kv_all,
        q_all,
        m_all,
        back,
        mixed,
        outer,
        tokens[0],
        xn1,
        gains,
        turns,
        queries,
        pair,
        shares,
        summed,
    )
    grads = [grads[which, :, :hidden_width].astype(floats) for which in range(3)]
    return (
        output[None],
        tokens_grad[None],
        joint_grad,
        small_grad[0, : joint_bias.shape[0]],
        merge_grad.T,
        small_grad[1, :depth],
        small_grad[2, :depth],
        grads[0],
        grads[1],
        grads[2].T,
    )


def body_plain(
    tokens,
    segments,
    joint_matrix,
    joint_bias,
    merge_matrix,
    norm_first,
    norm_second,
    gate_matrix,
    up_matrix,
    down_matrix,
    cotangent,
):
    residual = tokens[0].astype(floats)
    length, model = residual.shape
    depth = joint_matrix.shape[0]
    joint_width = joint_matrix.shape[1]
    hidden_width = gate_matrix.shape[1]
    z_count = lax.axis_size("z")
    team = lax.axis_size(TEAM)
    share = hidden_width // team
    own_labels = segments[0]
    labels = lax.all_gather(own_labels, SEQ, axis=0, tiled=True)
    offset = lax.axis_index(SEQ) * length
    places = offset + jnp.arange(length, dtype=jnp.int32)
    positions = lax.dynamic_slice_in_dim(row_positions(labels), offset, length, 0)
    cosine, sine = rotary(positions, HEAD_DIM)

    small = jnp.concatenate([joint_bias, norm_first, norm_second])
    small = jnp.pad(small, (0, -small.shape[0] % depth)).reshape(depth, -1)
    small_width = small.shape[1]
    packed = jnp.concatenate([joint_matrix, merge_matrix.T, small], axis=1)
    packed = lax.all_gather(packed, AXES, axis=0, tiled=True)
    joint_all = packed[:, :joint_width]
    merge_turned = packed[:, joint_width : joint_width + model]
    small = packed[:, joint_width + model :].reshape(-1, depth * small_width).astype(floats)
    bias_depth = joint_bias.shape[0]
    bias_all = small[:, :bias_depth].reshape(-1)
    gain_first = small[:, bias_depth : bias_depth + depth].reshape(-1)
    gain_second = small[:, bias_depth + depth : bias_depth + 2 * depth].reshape(-1)

    stacked = jnp.stack([gate_matrix, up_matrix, down_matrix.T], axis=1)
    stacked = stacked.reshape(depth, 3, team, share).transpose(2, 0, 1, 3)
    stacked = stacked.reshape(team, depth, 3 * share)
    stacked = lax.all_to_all(stacked, TEAM, split_axis=0, concat_axis=0, tiled=True)
    stacked = stacked.reshape(z_count, 1, team // z_count, 1, depth, 3 * share)
    stacked = lax.all_gather(stacked, "x", axis=1, tiled=True)
    stacked = lax.all_gather(stacked, "c", axis=3, tiled=True)
    stacked = stacked.reshape(model, 3 * share)
    both_all, down_turned = stacked[:, : 2 * share], stacked[:, 2 * share :]
    outer_grad = cotangent[0]
    team_outer = lax.all_gather(outer_grad, TEAM, axis=0, tiled=True)

    scale_first = norm_parts(residual)
    normal_first = (residual * scale_first * gain_first).astype(halves)
    joint = jnp.dot(normal_first, joint_all, preferred_element_type=floats) + bias_all
    query = joint[:, :QUERY_WIDTH].reshape(length, HEADS, HEAD_DIM)
    keys = joint[:, QUERY_WIDTH : QUERY_WIDTH + KEY_WIDTH].reshape(length, KV_HEADS, HEAD_DIM)
    values = joint[:, QUERY_WIDTH + KEY_WIDTH :].astype(halves)
    query = (query * cosine + turn_half(query) * sine).astype(halves)
    keys = (keys * cosine + turn_half(keys) * sine).astype(halves).reshape(length, KEY_WIDTH)
    query_group = to_groups(query)
    pair = lax.all_gather(jnp.concatenate([keys, values], axis=1), SEQ, axis=0, tiled=True)
    count = pair.shape[0]
    key_all = pair[:, :KEY_WIDTH].reshape(count, KV_HEADS, HEAD_DIM)
    value_all = pair[:, KEY_WIDTH:].reshape(count, KV_HEADS, HEAD_DIM)
    allowed = (places[:, None] >= jnp.arange(count, dtype=jnp.int32)[None, :]) & (
        own_labels[:, None] == labels[None, :]
    )
    allowed = jnp.tile(allowed, (GROUP, 1))[None]
    scores = jnp.einsum("krd,nkd->krn", query_group, key_all, preferred_element_type=floats)
    scores = jnp.where(allowed, scores * SCALE, neg)
    top = jnp.max(scores, axis=-1, keepdims=True)
    weights = jnp.where(allowed, jnp.exp(scores - top), 0.0)
    total = jnp.sum(weights, axis=-1, keepdims=True)
    shares = weights / total
    shares_half = shares.astype(halves)
    attended = jnp.einsum("krn,nkd->krd", shares_half, value_all, preferred_element_type=floats)
    attended_half = from_groups(attended, length).astype(halves)
    mixed = residual + lax.dot_general(
        attended_half, merge_turned, last_pair, preferred_element_type=floats
    )
    scale_second = norm_parts(mixed)
    normal_half = (mixed * scale_second * gain_second).astype(halves)

    team_normal = lax.all_gather(normal_half, TEAM, axis=0, tiled=True)
    both = jnp.dot(team_normal, both_all, preferred_element_type=floats)
    gate, upper = both[:, :share], both[:, share:]
    sig = jax.nn.sigmoid(gate)
    silu = gate * sig
    hidden_half = (silu * upper).astype(halves)
    branch = lax.dot_general(hidden_half, down_turned, last_pair, preferred_element_type=floats)
    hidden_grad = jnp.dot(team_outer, down_turned, preferred_element_type=floats)
    gate_half = (hidden_grad * upper * sig * (1.0 + gate * (1.0 - sig))).astype(halves)
    upper_half = (hidden_grad * silu).astype(halves)
    both_half = jnp.concatenate([gate_half, upper_half], axis=1)
    normal_grad = lax.dot_general(both_half, both_all, last_pair, preferred_element_type=floats)
    branch = lax.psum_scatter(branch.astype(halves), TEAM, scatter_dimension=0, tiled=True)
    normal_grad = lax.psum_scatter(normal_grad.astype(halves), TEAM, scatter_dimension=0, tiled=True)
    output = (mixed + branch.astype(floats)).astype(halves)[None]
    both_grad = lax.dot_general(team_normal, both_half, first_pair, preferred_element_type=floats)
    down_grad = lax.dot_general(team_outer, hidden_half, first_pair, preferred_element_type=floats)
    grads = jnp.concatenate([both_grad, down_grad], axis=1).astype(halves)
    grads = grads.reshape(z_count, 2, team // z_count, 2, depth, 3 * share)
    grads = lax.psum_scatter(grads, "c", scatter_dimension=3, tiled=True)
    grads = lax.psum_scatter(grads, "x", scatter_dimension=1, tiled=True)
    grads = grads.reshape(team, depth, 3 * share)
    grads = lax.all_to_all(grads, TEAM, split_axis=0, concat_axis=0, tiled=True)
    grads = grads.reshape(team, depth, 3, share).transpose(2, 1, 0, 3)
    grads = grads.reshape(3, depth, hidden_width).astype(floats)

    normal_grad = normal_grad.astype(floats)
    mixed_part, second_local = norm_back(normal_grad, mixed, scale_second, gain_second)
    mixed_grad = outer_grad.astype(floats) + mixed_part
    mixed_half = mixed_grad.astype(halves)
    merge_local = lax.dot_general(
        mixed_half, attended_half, first_pair, preferred_element_type=floats
    )
    attended_grad = jnp.dot(mixed_half, merge_turned, preferred_element_type=floats).astype(halves)
    grad_group = to_groups(attended_grad.reshape(length, HEADS, HEAD_DIM))
    mass_grad = jnp.einsum("krd,nkd->krn", grad_group, value_all, preferred_element_type=floats)
    row_dots = jnp.sum(shares * mass_grad, axis=-1, keepdims=True)
    score_half = (shares * (mass_grad - row_dots)).astype(halves)
    query_sum = (
        jnp.einsum("krn,nkd->krd", score_half, key_all, preferred_element_type=floats) * SCALE
    )
    key_grad = (
        jnp.einsum("krn,krd->nkd", score_half, query_group, preferred_element_type=floats) * SCALE
    )
    value_grad = jnp.einsum("krn,krd->nkd", shares_half, grad_group, preferred_element_type=floats)
    pair_sums = jnp.concatenate(
        [key_grad.reshape(count, KEY_WIDTH), value_grad.reshape(count, KEY_WIDTH)], axis=1
    )
    pair_mine = lax.psum_scatter(
        pair_sums.astype(halves), SEQ, scatter_dimension=0, tiled=True
    ).astype(floats)
    key_back = pair_mine[:, :KEY_WIDTH].reshape(length, KV_HEADS, HEAD_DIM)
    value_back = pair_mine[:, KEY_WIDTH:]
    query_back = from_groups(query_sum, length).reshape(length, HEADS, HEAD_DIM)
    query_back = query_back * cosine + unturn_half(query_back * sine)
    key_back = key_back * cosine + unturn_half(key_back * sine)
    joint_back = jnp.concatenate(
        [query_back.reshape(length, QUERY_WIDTH), key_back.reshape(length, KEY_WIDTH), value_back],
        axis=1,
    ).astype(halves)
    joint_local = lax.dot_general(
        normal_first, joint_back, first_pair, preferred_element_type=floats
    )
    bias_local = jnp.sum(joint_back.astype(floats), axis=0)
    normal_back = lax.dot_general(joint_back, joint_all, last_pair, preferred_element_type=floats)
    residual_part, first_local = norm_back(normal_back, residual, scale_first, gain_first)
    tokens_grad = (mixed_grad + residual_part)[None]

    small_back = jnp.concatenate(
        [
            bias_local.reshape(-1, bias_depth),
            first_local.reshape(-1, depth),
            second_local.reshape(-1, depth),
        ],
        axis=1,
    )
    small_back = jnp.pad(small_back, ((0, 0), (0, depth * small_width - small_back.shape[1])))
    small_back = small_back.reshape(-1, small_width)
    packed_grad = jnp.concatenate([joint_local, merge_local, small_back], axis=1).astype(halves)
    packed_grad = lax.psum_scatter(packed_grad, AXES, scatter_dimension=0, tiled=True).astype(floats)
    joint_grad = packed_grad[:, :joint_width]
    merge_grad = packed_grad[:, joint_width : joint_width + model].T
    small_back = packed_grad[:, joint_width + model :].reshape(-1)
    bias_grad = small_back[:bias_depth]
    first_grad = small_back[bias_depth : bias_depth + depth]
    second_grad = small_back[bias_depth + depth : bias_depth + 2 * depth]
    return (
        output,
        tokens_grad,
        joint_grad,
        bias_grad,
        merge_grad,
        first_grad,
        second_grad,
        grads[0],
        grads[1],
        grads[2].T,
    )


def solution(mesh):
    seq, row = mesh.shape["seq"], mesh.shape["row"]
    fine = Mesh(mesh.devices.reshape(seq // 2, 2, row // 2, 2), AXES)
    whole = ("z", "x", "y", "c")
    placed = (
        P(ROW, SEQ, None),
        P(ROW, SEQ),
        P(whole, None),
        P(whole),
        P(None, whole),
        P(whole),
        P(whole),
        P(whole, None),
        P(whole, None),
        P(None, whole),
        P(ROW, SEQ, None),
    )
    depth = MODEL // mesh.size
    return jax.shard_map(
        body_kernels if depth % 16 == 0 else body_plain,
        mesh=fine,
        in_specs=placed,
        out_specs=(
            P(ROW, SEQ, None),
            P(ROW, SEQ, None),
            P(whole, None),
            P(whole),
            P(None, whole),
            P(whole),
            P(whole),
            P(whole, None),
            P(whole, None),
            P(None, whole),
        ),
        check_vma=False,
    )
```
